32 devices in a mesh: dp: 16 (over z, y, core), mp: 2 (over x).
Axes of the slice: x: 2, y: 2, z: 4, core: 2. Of those that a mesh axis runs over, the one named last changes fastest.
Arguments:
- hidden_in: bfloat16 [16384, 1536], P(('dp', 'mp')), may hold values from -6 to 6
- positions: int32 [16384], P('dp'), may hold values from 0 to 511, as said below
- query_weight: bfloat16 [1536, 1536], P('dp', 'mp'), may hold values from -0.15625 to 0.15625
- query_bias: float32 [1536], replicated, may hold values from -3 to 3
- key_weight: bfloat16 [1536, 256], P('dp', 'mp'), may hold values from -0.15625 to 0.15625
- key_bias: float32 [256], replicated, may hold values from -3 to 3
- value_weight: bfloat16 [1536, 256], P('dp', 'mp'), may hold values from -0.15625 to 0.15625
- value_bias: float32 [256], replicated, may hold values from -3 to 3
- out_weight: bfloat16 [1536, 1536], P('mp', 'dp'), may hold values from -1.75 to 1.75
- gate_weight: bfloat16 [1536, 8960], P('dp', 'mp'), may hold values from -0.15625 to 0.15625
- up_weight: bfloat16 [1536, 8960], P('dp', 'mp'), may hold values from -0.15625 to 0.15625
- down_weight: bfloat16 [8960, 1536], P('mp', 'dp'), may hold values from -0.0625 to 0.0625
- attn_gain: float32 [1536], replicated, may hold values from 0.5 to 1.5
- ffn_gain: float32 [1536], replicated, may hold values from 0.5 to 1.5
- cotangent: bfloat16 [16384, 1536], P(('dp', 'mp')), may hold values from -6 to 6
Outputs:
- layer_out: bfloat16 [16384, 1536], P(('dp', 'mp'))
- grad_input: bfloat16 [16384, 1536], P(('dp', 'mp'))
- grad_query_weight: float32 [1536, 1536], P('dp', 'mp')
- grad_query_bias: float32 [1536], replicated
- grad_key_weight: float32 [1536, 256], P('dp', 'mp')
- grad_key_bias: float32 [256], replicated
- grad_value_weight: float32 [1536, 256], P('dp', 'mp')
- grad_value_bias: float32 [256], replicated
- grad_out_weight: float32 [1536, 1536], P('mp', 'dp')
- grad_gate_weight: float32 [1536, 8960], P('dp', 'mp')
- grad_up_weight: float32 [1536, 8960], P('dp', 'mp')
- grad_down_weight: float32 [8960, 1536], P('mp', 'dp')
- grad_attn_gain: float32 [1536], replicated
- grad_ffn_gain: float32 [1536], replicated
The draws below stay inside these ranges and needn't reach their ends.
Inputs may be any that keep to these rules, and one draw needn't show every extreme that they name: `positions`: positions count up by one from 0 within each packed document; each sequence of 1024 tokens begins with a position 0, and its longest document has 512 tokens.
All inputs are finite; a program needn't handle non-finite values.
Results may differ from the reference program's by a relative error of at most 0.02.
Values may be sent and summed in bfloat16 or wider, within the bound.
A program may use at most 320 MiB of HBM per device.

```python
import math
import jax
import jax.numpy as jnp
from jax import lax

D = 1536
H = 12
KV = 2
HD = 128
FF = 8960
SEQ_LEN = 1024
TOKENS = 16384


def draw_positions(key, part):
    key = jax.random.fold_in(key, 7)
    keys = jax.random.split(key, 4)
    count = TOKENS // SEQ_LEN
    first = jax.random.randint(keys[0], (count, 1), 2, SEQ_LEN // 4 + 1)
    early = jax.random.randint(keys[1], (count, 1), 0, 1 << 20) % (first - 1) + 1
    last = first + SEQ_LEN // 2
    late = last + 1 + jax.random.randint(keys[3], (count, 1), 0, 1 << 20) % (SEQ_LEN - 1 - last)
    starts = jnp.concatenate([jnp.zeros((count, 1), jnp.int32), early, first, last, late], axis=1).astype(jnp.int32)
    steps = jnp.arange(SEQ_LEN, dtype=jnp.int32)
    begin = jnp.max(jnp.where(starts[:, None, :] <= steps[None, :, None], starts[:, None, :], 0), axis=-1)
    return (steps[None, :] - begin).reshape(TOKENS).astype(jnp.int32)


def spiked(values, key, source, target, parts, factor):
    def block_of(position):
        return (jnp.arange(values.shape[position]) // (values.shape[position] // parts)).reshape((-1,) + (1,) * (values.ndim - 1 - position))

    near = jax.random.permutation(key, parts)[block_of(target)]
    second = (block_of(target) + parts // 2) % parts
    return jnp.where((block_of(source) == near) | (block_of(source) == second), factor * values, values)


def shard_levels(key, dims, cuts, low, largest):
    def one(dim, shards_of):
        draws = jax.random.uniform(jax.random.fold_in(jax.random.fold_in(key, 6), dim), (shards_of,), jnp.float32, low / len(cuts), largest / len(cuts))
        return jnp.repeat(jnp.exp(draws), dims[dim] // shards_of).reshape((-1,) + (1,) * (len(dims) - dim - 1))

    factor_of = one(*cuts[0])
    for cut in cuts[1:]:
        factor_of = factor_of * one(*cut)
    return factor_of


def noise(own_key, extent, width, bound, cuts=(), kind=jnp.bfloat16):
    result = jax.random.normal(own_key, extent, jnp.float32) * width
    if len(cuts) > 0:
        result = shard_levels(own_key, extent, cuts, -0.22, 0.18) * result
    return jnp.clip(result, min=-bound, max=bound).astype(kind)


def bell_draw_with(stream_key, extent, width, limit, cuts, heavy, held_as=jnp.bfloat16):
    values = width * jax.random.normal(stream_key, extent, jnp.float32)
    if cuts:
        values = values * shard_levels(stream_key, extent, cuts, -0.22, 0.18)
    return jnp.clip(spiked(values, jax.random.fold_in(stream_key, 3), *heavy), -limit, limit).astype(held_as)


def setup_inputs(seed: int = 0) -> dict:
    streams_of = jax.random.split(jax.random.key(seed), 16)
    return {
        "hidden_in": noise(streams_of[0], (TOKENS, D), 1.0, 6.0, ((0, 32),)),
        "positions": draw_positions(jax.random.fold_in(streams_of[15], 71), 0),
        "query_weight": noise(streams_of[2], (D, H * HD), D ** -0.5, 0.15625, ((0, 16), (1, 2))),
        "query_bias": noise(streams_of[3], (H * HD,), 0.5, 3.0, (), jnp.float32),
        "key_weight": noise(streams_of[4], (D, KV * HD), D ** -0.5, 0.15625, ((0, 16), (1, 2))),
        "key_bias": noise(streams_of[5], (KV * HD,), 0.5, 3.0, (), jnp.float32),
        "value_weight": noise(streams_of[6], (D, KV * HD), D ** -0.5, 0.15625, ((0, 16), (1, 2))),
        "value_bias": noise(streams_of[7], (KV * HD,), 0.5, 3.0, (), jnp.float32),
        "out_weight": noise(streams_of[8], (H * HD, D), (max(H * HD // 128, 1)) ** -0.5, 1.75, ((0, 2), (1, 16))),
        "gate_weight": noise(streams_of[9], (D, FF), D ** -0.5, 0.15625, ((0, 16), (1, 2))),
        "up_weight": noise(streams_of[10], (D, FF), D ** -0.5, 0.15625, ((0, 16), (1, 2))),
        "down_weight": noise(streams_of[11], (FF, D), FF ** -0.5, 0.0625, ((0, 2), (1, 16))),
        "attn_gain": jnp.clip(1.0 + 0.1 * jax.random.normal(streams_of[12], (D,), jnp.float32), 0.5, 1.5),
        "ffn_gain": jnp.clip(1.0 + 0.1 * jax.random.normal(streams_of[13], (D,), jnp.float32), 0.5, 1.5),
        "cotangent": bell_draw_with(streams_of[14], (TOKENS, D), 1.0, 6.0, ((0, 32),), (0, 1, 32, 2.75)),
    }


EPS = 1e-06
ROPE_BASE = 1000000.0

@jax.custom_vjp
def low(v):
    return lax.optimization_barrier(v.astype(jnp.bfloat16)).astype(jnp.float32)

@jax.custom_vjp
def low_back(v):
    return v

def low_keep(v):
    return (low(v), None)

def low_pass(kept, grad):
    return (grad,)

def back_keep(v):
    return (v, None)

def back_low(kept, grad):
    return (low(grad),)
low.defvjp(low_keep, low_pass)
low_back.defvjp(back_keep, back_low)

def matmul(left, right):
    return jnp.dot(left, right, preferred_element_type=jnp.float32, precision=lax.Precision.HIGHEST)

def normalize(values, gain):
    return values * lax.rsqrt(lax.optimization_barrier(jnp.mean(values * values, axis=-1, keepdims=True)) + EPS) * gain

def rotary(positions):
    half = HD // 2
    freq = jnp.power(ROPE_BASE, -2.0 * jnp.arange(half, dtype=jnp.float32) / HD)
    angles = positions.astype(jnp.float32)[:, None] * freq[None, :]
    return (jnp.cos(angles)[:, None, :], jnp.sin(angles)[:, None, :])

def rotate(values, cosines, sines):
    half = values.shape[-1] // 2
    first = values[..., :half]
    second = values[..., half:]
    return jnp.concatenate([first * cosines - second * sines, second * cosines + first * sines], axis=-1)

def attend(queries, keys, values, docs):
    block = min(512, SEQ_LEN)
    count = SEQ_LEN // block
    columns = jnp.arange(SEQ_LEN, dtype=jnp.int32)

    def one_block(index):
        start = index * block
        query_block = lax.dynamic_slice_in_dim(queries, start, block, 0)
        scores = low_back(1.0 / math.sqrt(HD) * jnp.einsum('qcgd,kcd->cgqk', query_block, keys, precision=lax.Precision.HIGHEST))
        rows = start + jnp.arange(block, dtype=jnp.int32)
        doc_rows = lax.dynamic_slice_in_dim(docs, start, block, 0)
        visible = (doc_rows[:, None] == docs[None, :]) & (columns[None, :] <= rows[:, None])
        masked = jnp.where(visible, scores, -1e+30)
        top = lax.optimization_barrier(jnp.max(masked, axis=-1, keepdims=True))
        weights = jnp.exp(masked - top)
        probs = low(weights / lax.optimization_barrier(jnp.sum(weights, axis=-1, keepdims=True)))
        return jnp.einsum('cgqk,kcd->qcgd', probs, values, precision=lax.Precision.HIGHEST).reshape(block, H * HD)
    mixed = lax.map(jax.checkpoint(one_block), jnp.arange(count, dtype=jnp.int32))
    return mixed.reshape(SEQ_LEN, H * HD)

def layer(params, hidden, positions):
    query_weight, query_bias, key_weight, key_bias, value_weight, value_bias, out_weight, gate_weight, up_weight, down_weight, attn_gain, ffn_gain = params
    cosines, sines = rotary(positions)
    docs = jnp.cumsum((positions == 0).astype(jnp.int32)).astype(jnp.int32)
    inputs_one = low(normalize(hidden, attn_gain))
    queries = low_back(matmul(inputs_one, query_weight) + query_bias)
    keys = low_back(matmul(inputs_one, key_weight) + key_bias)
    values = low(low_back(matmul(inputs_one, value_weight) + value_bias))
    queries = low(rotate(queries.reshape(SEQ_LEN, H, HD), cosines, sines)).reshape(SEQ_LEN, KV, H // KV, HD)
    keys = low(rotate(keys.reshape(SEQ_LEN, KV, HD), cosines, sines))
    values = values.reshape(SEQ_LEN, KV, HD)
    mixed = low(low_back(attend(queries, keys, values, docs)))
    middle = hidden + low_back(matmul(mixed, out_weight))
    inputs_two = low(normalize(middle, ffn_gain))
    gate = low_back(matmul(inputs_two, gate_weight))
    up = low_back(matmul(inputs_two, up_weight))
    hidden_ffn = low(gate * jax.nn.sigmoid(gate) * up)
    return middle + low_back(matmul(hidden_ffn, down_weight))

def reference(hidden_in, positions, query_weight, query_bias, key_weight, key_bias, value_weight, value_bias, out_weight, gate_weight, up_weight, down_weight, attn_gain, ffn_gain, cotangent):
    params = tuple((p.astype(jnp.float32) for p in (query_weight, query_bias, key_weight, key_bias, value_weight, value_bias, out_weight, gate_weight, up_weight, down_weight, attn_gain, ffn_gain)))
    count = TOKENS // SEQ_LEN
    inputs = hidden_in.astype(jnp.float32).reshape(count, SEQ_LEN, D)
    places = positions.astype(jnp.int32).reshape(count, SEQ_LEN)
    grads_in = cotangent.astype(jnp.float32).reshape(count, SEQ_LEN, D)

    def step(totals, item):
        inputs_seq, places_seq, grads_seq = item
        output, pull = jax.vjp(lambda pr, hv: layer(pr, hv, places_seq), params, inputs_seq)
        grad_params, grad_hidden = pull(grads_seq)
        totals = jax.tree.map(jnp.add, totals, grad_params)
        return (totals, (output.astype(jnp.bfloat16), grad_hidden.astype(jnp.bfloat16)))
    zeros = tuple((jnp.zeros_like(p) for p in params))
    totals, (outputs, grad_hidden) = lax.scan(step, zeros, (inputs, places, grads_in))
    return (outputs.reshape(TOKENS, D), grad_hidden.reshape(TOKENS, D), totals[0], totals[1], totals[2], totals[3], totals[4], totals[5], totals[6], totals[7], totals[8], totals[9], totals[10], totals[11])
```

```python
import functools
import math

import jax
import jax.numpy as jnp
from jax import lax
from jax.experimental import pallas as pl
from jax.experimental.pallas import tpu as pltpu
from jax.sharding import PartitionSpec as P

HD = 128
SEQ_LEN = 1024
DOC_MAX = 512
EPS = 1e-06
ROPE_BASE = 1000000.0
BLOCK = 256
SCALE = 1.0 / math.sqrt(HD)
F32 = jnp.float32
BF16 = jnp.bfloat16


def contract(left, right, left_dim, right_dim):
    return lax.dot_general(
        left, right, (((left_dim,), (right_dim,)), ((), ())), preferred_element_type=F32
    )


def key_range(block_id):
    low = max(0, block_id * BLOCK - (DOC_MAX - 1)) // BLOCK * BLOCK
    return low, (block_id + 1) * BLOCK


def visible(start_row, low, high, block_id):
    keys = low + lax.broadcasted_iota(jnp.int32, (high - low, BLOCK), 0)
    queries = block_id * BLOCK + lax.broadcasted_iota(jnp.int32, (high - low, BLOCK), 1)
    return (keys >= start_row) & (keys <= queries)


def turn(values, cosines, sines):
    return values * cosines + pltpu.roll(values, HD // 2, 1) * sines


def attend_kernel(
    q_ref, k_ref, v_ref, bq_ref, bk_ref, bv_ref, cos_ref, sin_ref, start_ref,
    mixed_ref, qrot_ref, krot_ref, vlow_ref, lse_ref,
):
    head = pl.program_id(0)

    @pl.when(head == 0)
    def _():
        krot_ref[...] = turn(k_ref[...] + bk_ref[...], cos_ref[...], sin_ref[...]).astype(BF16)
        vlow_ref[...] = (v_ref[...] + bv_ref[...]).astype(BF16)

    qrot_ref[...] = turn(q_ref[...] + bq_ref[...], cos_ref[...], sin_ref[...]).astype(BF16)
    for i in range(SEQ_LEN // BLOCK):
        low, high = key_range(i)
        rows = pl.ds(i * BLOCK, BLOCK)
        start_row = start_ref[0:1, rows]
        scores = contract(krot_ref[low:high, :], qrot_ref[rows, :], 1, 1) * SCALE
        scores = jnp.where(visible(start_row, low, high, i), scores, -1e30)
        top = jnp.max(scores, axis=0, keepdims=True)
        weights = jnp.exp(scores - top)
        total = jnp.sum(weights, axis=0, keepdims=True)
        probs = (weights * (1.0 / total)).astype(BF16)
        mixed_ref[rows, :] = contract(probs, vlow_ref[low:high, :], 0, 0).astype(BF16)
        lse_ref[0, 0:1, rows] = top + jnp.log(total)


def attend(qkv, bias, cos2, sin2, start, heads):
    seq = SEQ_LEN
    full = lambda shape: pl.BlockSpec(shape, lambda h: (0,) * len(shape))
    col = lambda: pl.BlockSpec((seq, HD), lambda h: (0, h))
    at = lambda j: pl.BlockSpec((seq, HD), lambda h: (0, j))
    bat = lambda j: pl.BlockSpec((1, HD), lambda h: (0, j))
    return pl.pallas_call(
        attend_kernel,
        grid=(heads,),
        in_specs=[
            col(), at(heads), at(heads + 1),
            pl.BlockSpec((1, HD), lambda h: (0, h)), bat(heads), bat(heads + 1),
            full((seq, HD)), full((seq, HD)), full((1, seq)),
        ],
        out_specs=[
            col(), col(), full((seq, HD)), full((seq, HD)),
            pl.BlockSpec((1, 8, seq), lambda h: (h, 0, 0)),
        ],
        out_shape=[
            jax.ShapeDtypeStruct((seq, heads * HD), BF16),
            jax.ShapeDtypeStruct((seq, heads * HD), BF16),
            jax.ShapeDtypeStruct((seq, HD), BF16),
            jax.ShapeDtypeStruct((seq, HD), BF16),
            jax.ShapeDtypeStruct((heads, 8, seq), F32),
        ],
        compiler_params=pltpu.CompilerParams(vmem_limit_bytes=40 * 2**20),
        cost_estimate=pl.CostEstimate(
            flops=4 * heads * seq * seq * HD, bytes_accessed=10 * 2**20,
            transcendentals=heads * seq * seq // 2,
        ),
        name="attend",
    )(qkv, qkv, qkv, bias, bias, bias, cos2, sin2, start)


def attend_back_kernel(
    heads, qrot_ref, krot_ref, vlow_ref, lse_ref, grad_ref, cos_ref, sin_ref, start_ref,
    out_ref, gk_ref, gv_ref,
):
    head = pl.program_id(0)

    @pl.when(head == 0)
    def _():
        gk_ref[...] = jnp.zeros_like(gk_ref)
        gv_ref[...] = jnp.zeros_like(gv_ref)

    for i in range(SEQ_LEN // BLOCK):
        low, high = key_range(i)
        rows = pl.ds(i * BLOCK, BLOCK)
        start_row = start_ref[0:1, rows]
        query, grad = qrot_ref[rows, :], grad_ref[rows, :]
        keys = krot_ref[low:high, :]
        scores = contract(keys, query, 1, 1) * SCALE
        probs = jnp.where(
            visible(start_row, low, high, i), jnp.exp(scores - lse_ref[0, 0:1, rows]), 0.0
        )
        grad_probs = contract(vlow_ref[low:high, :], grad, 1, 1)
        row_term = jnp.sum(probs * grad_probs, axis=0, keepdims=True)
        grad_scores = (probs * (grad_probs - row_term)).astype(BF16)
        gk_ref[low:high, :] += contract(grad_scores, query, 1, 0)
        gv_ref[low:high, :] += contract(probs.astype(BF16), grad, 1, 0)
        grad_query = contract(grad_scores, keys, 0, 0) * SCALE
        out_ref[rows, pl.ds(pl.multiple_of(head * HD, HD), HD)] = turn(
            grad_query, cos_ref[rows, :], -sin_ref[rows, :]
        ).astype(BF16)

    @pl.when(head == heads - 1)
    def _():
        out_ref[:, heads * HD : (heads + 1) * HD] = turn(
            gk_ref[...] * SCALE, cos_ref[...], -sin_ref[...]
        ).astype(BF16)
        out_ref[:, (heads + 1) * HD :] = gv_ref[...].astype(BF16)


def attend_back(qrot, krot, vlow, lse, grad_mixed, cos2, sin2, start, heads):
    seq = SEQ_LEN
    full = lambda shape: pl.BlockSpec(shape, lambda h: (0,) * len(shape))
    col = lambda: pl.BlockSpec((seq, HD), lambda h: (0, h))
    return pl.pallas_call(
        functools.partial(attend_back_kernel, heads),
        grid=(heads,),
        in_specs=[
            col(), full((seq, HD)), full((seq, HD)),
            pl.BlockSpec((1, 8, seq), lambda h: (h, 0, 0)), col(),
            full((seq, HD)), full((seq, HD)), full((1, seq)),
        ],
        out_specs=full((seq, (heads + 2) * HD)),
        out_shape=jax.ShapeDtypeStruct((seq, (heads + 2) * HD), BF16),
        scratch_shapes=[pltpu.VMEM((seq, HD), F32), pltpu.VMEM((seq, HD), F32)],
        compiler_params=pltpu.CompilerParams(vmem_limit_bytes=40 * 2**20),
        cost_estimate=pl.CostEstimate(
            flops=10 * heads * seq * seq * HD, bytes_accessed=10 * 2**20,
            transcendentals=heads * seq * seq // 2,
        ),
        name="attend_back",
    )(qrot, krot, vlow, lse, grad_mixed, cos2, sin2, start)


class Ring:
    def __init__(self, members):
        self.members = members
        self.chips = members // 2
        self.half = self.chips // 2
        n = self.chips
        self.path = [2 * r if r < n // 2 else 2 * (n - 1 - r) + 1 for r in range(n)]
        self.offsets = [self.half]
        for k in range(self.half - 1, 0, -1):
            self.offsets += [k, n - k]
        self.offsets += [0]
        self.place = {k: i for i, k in enumerate(self.offsets)}

    def pairs(self, shift):
        n, path = self.chips, self.path
        return [
            (path[r] * 2 + c, path[(r + shift) % n] * 2 + c) for r in range(n) for c in range(2)
        ]

    def up(self, block):
        return lax.ppermute(block, "dp", self.pairs(1))

    def down(self, block):
        return lax.ppermute(block, "dp", self.pairs(-1))

    def across(self, block):
        return lax.ppermute(block, "dp", [(i, i ^ 1) for i in range(self.members)])

    def order(self):
        me = lax.axis_index("dp")
        path = jnp.array(self.path, jnp.int32)
        spot = jnp.zeros((self.chips,), jnp.int32).at[path].set(jnp.arange(self.chips, dtype=jnp.int32))
        mine = spot[me // 2]
        offsets = jnp.array(self.offsets, jnp.int32)
        chips = path[(mine + offsets) % self.chips]
        core = me % 2
        return jnp.concatenate([chips * 2 + core, chips * 2 + (1 - core)])

    def gather(self, block):
        n, h = self.chips, self.half
        rows = block.shape[0]
        got = {0: block}
        for k in range(1, h):
            got[n - k] = self.up(got[(n - k + 1) % n])
            got[k] = self.down(got[k - 1])
        first = self.up(got[h + 1][: rows // 2])
        second = self.down(got[h - 1][rows // 2 :])
        other = {k: self.across(got[k]) for k in got}
        got_half = [first, second]
        other_half = [self.across(first), self.across(second)]
        blocks = []
        for side, halves in ((got, got_half), (other, other_half)):
            for k in self.offsets:
                blocks.append(tuple(halves) if k == h else (side[k],))
        return blocks, first

    def reduce(self, own, rows):
        def term(k):
            begin = self.place[k] * rows
            return jnp.concatenate([o[begin : begin + rows] for o in own], axis=1)

        return self.reduce_terms(term, rows)

    def reduce_terms(self, term, rows):
        n, h = self.chips, self.half
        up = self.up(term(h)[: rows // 2])
        down = self.down(term(h)[rows // 2 :])
        for k in range(h - 1, 0, -1):
            mine_up, mine_down = term(k), term(n - k)
            if k == h - 1:
                sent_up = jnp.concatenate([
                    (up.astype(F32) + mine_up[: rows // 2].astype(F32)).astype(BF16),
                    mine_up[rows // 2 :],
                ])
                sent_down = jnp.concatenate([
                    mine_down[: rows // 2],
                    (down.astype(F32) + mine_down[rows // 2 :].astype(F32)).astype(BF16),
                ])
            else:
                sent_up = (up.astype(F32) + mine_up.astype(F32)).astype(BF16)
                sent_down = (down.astype(F32) + mine_down.astype(F32)).astype(BF16)
            up, down = self.up(sent_up), self.down(sent_down)
        return term(0).astype(F32) + up.astype(F32) + down.astype(F32)


def stack(blocks, begin, stop):
    return jnp.concatenate([part[:, begin:stop] for block in blocks for part in block], axis=0)


def swap(block):
    return lax.ppermute(block, "mp", [(0, 1), (1, 0)])


def rms(values):
    return lax.rsqrt(jnp.mean(values * values, axis=-1, keepdims=True) + EPS)


def after(value, *earlier):
    return lax.optimization_barrier((value, *earlier))[0]


def split_hidden(width, parts):
    tiles = width // HD
    cuts = [round(tiles * i / parts) * HD for i in range(parts + 1)]
    return list(zip(cuts[:-1], cuts[1:]))


def body_general(
    hidden_in, positions, query_weight, query_bias, key_weight, key_bias, value_weight, value_bias,
    out_weight, gate_weight, up_weight, down_weight, attn_gain, ffn_gain, cotangent,
):
    ring = Ring(lax.axis_size("dp"))
    rows = query_weight.shape[0]
    width = rows * ring.members
    side_rows = rows * ring.chips
    heads = query_weight.shape[1] // HD
    width_q = heads * HD
    width_qkv = width_q + 2 * HD
    own_tokens = hidden_in.shape[0]
    shard = lax.axis_index("mp")

    def whole(own, other):
        first = jnp.where(shard == 0, own, other)
        second = jnp.where(shard == 0, other, own)
        return jnp.concatenate([first, second], axis=0)

    def own_half(values):
        return lax.dynamic_slice_in_dim(values, shard * own_tokens, own_tokens, 0)

    def other_half(values):
        return lax.dynamic_slice_in_dim(values, (1 - shard) * own_tokens, own_tokens, 0)

    hidden_other = swap(hidden_in)
    attn_pack = jnp.concatenate([query_weight, key_weight, value_weight, out_weight.T], axis=1)
    attn_blocks, attn_last = ring.gather(attn_pack)
    cotangent_other = swap(after(cotangent, hidden_other))
    down_t = down_weight.T
    spans = split_hidden(gate_weight.shape[1], 2)
    ffn_blocks = []
    last = attn_last
    for begin, stop in spans:
        pack = jnp.concatenate(
            [gate_weight[:, begin:stop], up_weight[:, begin:stop], down_t[:, begin:stop]], axis=1
        )
        blocks, last = ring.gather(after(pack, last))
        ffn_blocks.append(blocks)

    order = ring.order()
    feature = (order[:, None] * rows + jnp.arange(rows, dtype=jnp.int32)[None, :]).reshape(width)
    shuffle = (jnp.arange(width, dtype=jnp.int32)[:, None] == feature[None, :]).astype(BF16)

    def to_order(values):
        return contract(values, shuffle, 1, 0).astype(BF16)

    def from_order(values):
        return contract(values, shuffle, 1, 1).astype(BF16)

    def vector_to_order(values):
        return jnp.sum(jnp.where(shuffle > 0, values[:, None], 0.0), axis=0)

    def vector_from_order(values):
        return jnp.sum(jnp.where(shuffle > 0, values[None, :], 0.0), axis=1)

    gain_attn, gain_ffn = vector_to_order(attn_gain), vector_to_order(ffn_gain)

    hidden_all = to_order(whole(hidden_in, hidden_other))
    resid_all = hidden_all.astype(F32)
    factor_one = rms(resid_all)
    inputs_one = (resid_all * factor_one * gain_attn).astype(BF16)
    half = HD // 2
    freq = jnp.power(ROPE_BASE, -2.0 * jnp.arange(half, dtype=F32) / HD)
    angles = positions.astype(F32)[:, None] * freq[None, :]
    cosines, sines = jnp.cos(angles), jnp.sin(angles)
    cos2 = jnp.concatenate([cosines, cosines], axis=1)
    sin2 = jnp.concatenate([-sines, sines], axis=1)
    start = (jnp.arange(SEQ_LEN, dtype=jnp.int32) - positions)[None, :]
    bias = jnp.concatenate([
        lax.dynamic_slice_in_dim(query_bias, shard * width_q, width_q, 0),
        lax.dynamic_slice_in_dim(key_bias, shard * HD, HD, 0),
        lax.dynamic_slice_in_dim(value_bias, shard * HD, HD, 0),
    ])[None, :]
    qkv_full = stack(attn_blocks, 0, width_qkv)
    out_full = stack(attn_blocks, width_qkv, width_qkv + width_q)
    qkv = contract(inputs_one, qkv_full, 1, 0)
    mixed, qrot, krot, vlow, lse = attend(qkv, bias, cos2, sin2, start, heads)
    out_other = swap(contract(other_half(mixed), out_full, 1, 1).astype(BF16))
    middle = (
        own_half(hidden_all).astype(F32)
        + contract(own_half(mixed), out_full, 1, 1)
        + out_other.astype(F32)
    )
    factor_two = rms(middle)
    in_two_own = (middle * factor_two * gain_ffn).astype(BF16)
    inputs_two = whole(in_two_own, swap(in_two_own))
    grad_ffn = to_order(whole(cotangent, cotangent_other))

    hiddens, grads_gate, grads_up, weights = [], [], [], []
    for (begin, stop), blocks in zip(spans, ffn_blocks):
        wide = stop - begin
        gate_full = stack(blocks, 0, wide)
        up_full = stack(blocks, wide, 2 * wide)
        down_full = stack(blocks, 2 * wide, 3 * wide)
        grad_hidden = contract(grad_ffn, down_full, 1, 0)
        gate = contract(inputs_two, gate_full, 1, 0)
        up = contract(inputs_two, up_full, 1, 0)
        sig = jax.nn.sigmoid(gate)
        swish = gate * sig
        hiddens.append((swish * up).astype(BF16))
        grads_gate.append((grad_hidden * up * sig * (1.0 + gate * (1.0 - sig))).astype(BF16))
        grads_up.append((grad_hidden * swish).astype(BF16))
        weights.append((gate_full, up_full, down_full))

    def side(values, index):
        return values[:, index * side_rows : (index + 1) * side_rows]

    def chip_sum(left, right):
        sent = contract(side(left, 1), right, 0, 0).astype(BF16)
        return (contract(side(left, 0), right, 0, 0) + ring.across(sent).astype(F32)).astype(BF16)

    sums = []
    for index in range(len(spans)):
        own = [
            chip_sum(inputs_two, grads_gate[index]),
            chip_sum(inputs_two, grads_up[index]),
            chip_sum(grad_ffn, hiddens[index]),
        ]
        sums.append(ring.reduce(own, rows))

    def back_two(take):
        total = None
        for (gate_full, up_full, _), g, u in zip(weights, grads_gate, grads_up):
            term = contract(take(g), gate_full, 1, 1) + contract(take(u), up_full, 1, 1)
            total = term if total is None else total + term
        return total

    def forward_out(take):
        total = None
        for (_, _, down_full), h in zip(weights, hiddens):
            term = contract(take(h), down_full, 1, 1)
            total = term if total is None else total + term
        return total

    back_other = swap(back_two(other_half).astype(BF16))
    grad_normed_two = back_two(own_half) + back_other.astype(F32)
    ffn_other = swap(forward_out(other_half).astype(BF16))
    layer_out = from_order(
        (middle + forward_out(own_half) + ffn_other.astype(F32)).astype(BF16)
    )

    unit_two = middle * factor_two
    scaled = grad_normed_two * gain_ffn
    gain_two = jnp.sum(grad_normed_two * unit_two, axis=0)
    inner = jnp.mean(scaled * unit_two, axis=-1, keepdims=True)
    grad_middle = own_half(grad_ffn).astype(F32) + factor_two * (scaled - unit_two * inner)

    grad_attn_own = grad_middle.astype(BF16)
    grad_attn = whole(grad_attn_own, swap(grad_attn_own))
    grad_mixed = contract(grad_attn, out_full, 1, 0).astype(BF16)
    grad_qkv = attend_back(qrot, krot, vlow, lse, grad_mixed, cos2, sin2, start, heads)
    sum_out = ring.reduce([chip_sum(grad_attn, mixed)], rows)
    sum_qkv = ring.reduce([chip_sum(inputs_one, grad_qkv)], rows)

    back_one_other = contract(other_half(grad_qkv), qkv_full, 1, 1)
    one_other = swap(back_one_other.astype(BF16))
    back_one_own = contract(own_half(grad_qkv), qkv_full, 1, 1)
    unit_all = resid_all * factor_one
    unit_one = own_half(unit_all)
    gain_one = jnp.sum(back_one_own * unit_one, axis=0) + jnp.sum(
        back_one_other * other_half(unit_all), axis=0
    )
    grad_normed_one = back_one_own + one_other.astype(F32)
    scaled_one = grad_normed_one * gain_attn
    inner_one = jnp.mean(scaled_one * unit_one, axis=-1, keepdims=True)
    through_one = own_half(factor_one) * (scaled_one - unit_one * inner_one)
    grad_input = from_order((grad_middle + through_one).astype(BF16))

    bias_part = jnp.sum(grad_qkv.astype(F32), axis=0)

    def place(part, total):
        return lax.dynamic_update_slice_in_dim(
            jnp.zeros((total,), F32), part, shard * part.shape[0], 0
        )

    small = jnp.concatenate([
        vector_from_order(gain_one),
        vector_from_order(gain_two),
        place(bias_part[:width_q], query_bias.shape[0]),
        place(bias_part[width_q : width_q + HD], key_bias.shape[0]),
        place(bias_part[width_q + HD :], value_bias.shape[0]),
    ])
    small = small + swap(small)
    bit = 1
    while bit < ring.members:
        small = small + lax.ppermute(small, "dp", [(i, i ^ bit) for i in range(ring.members)])
        bit *= 2
    cuts = [width, width, query_bias.shape[0], key_bias.shape[0], value_bias.shape[0]]
    pieces, begin = [], 0
    for cut in cuts:
        pieces.append(small[begin : begin + cut])
        begin += cut

    def gather_cols(index):
        parts = []
        for (begin, stop), total in zip(spans, sums):
            wide = stop - begin
            parts.append(total[:, index * wide : (index + 1) * wide])
        return jnp.concatenate(parts, axis=1)

    return (
        layer_out,
        grad_input,
        sum_qkv[:, :width_q],
        pieces[2],
        sum_qkv[:, width_q : width_q + HD],
        pieces[3],
        sum_qkv[:, width_q + HD :],
        pieces[4],
        sum_out.T,
        gather_cols(0),
        gather_cols(1),
        gather_cols(2).T,
        pieces[0],
        pieces[1],
    )


CHIPS = 8
HALF = CHIPS // 2
CHUNK = 512
TILE = 256
MESH = pl.DeviceIdType.MESH


class Spot:
    def __init__(self, rows):
        self.rows = rows
        self.me = lax.axis_index("dp")
        self.shard = lax.axis_index("mp")
        self.core = lax.rem(self.me, 2)
        chip = lax.div(self.me, 2)
        line, back = lax.div(chip, 2), lax.rem(chip, 2)
        self.spot = line * (1 - back) + (CHIPS - 1 - line) * back
        self.sibling = self.me + 1 - 2 * self.core
        self.next = (self.chip(1) * 2 + self.core, self.chip(CHIPS - 1) * 2 + self.core)

    def chip(self, offset):
        place = lax.rem(self.spot + offset, CHIPS)
        back = lax.div(place, HALF)
        return (1 - back) * (2 * place) + back * (2 * (CHIPS - 1 - place) + 1)

    def greet(self):
        barrier = pltpu.get_barrier_semaphore()
        for target in (
            {"dp": self.sibling}, {"dp": self.next[0]}, {"dp": self.next[1]}, {"mp": 1 - self.shard}
        ):
            pl.semaphore_signal(barrier, inc=1, device_id=target, device_id_type=MESH)
        pl.semaphore_wait(barrier, 4)

    def part(self, block, half=None):
        begin, size = block * self.rows, self.rows
        if half is not None:
            size = self.rows // 2
            begin = begin + half * size
        return pl.ds(pl.multiple_of(begin, 16), size)


def tile_of(index, size=TILE):
    return pl.ds(pl.multiple_of(index * size, size), size)


def small_inputs(ref, width_qkv, width):
    gains = width_qkv + width, width_qkv + 2 * width

    def start_of(block):
        begin = gains[1] + block * BLOCK
        return ref[0:1, begin : begin + BLOCK]

    return (
        ref[0:1, 0:width_qkv], ref[0:1, width_qkv : gains[0]], ref[0:1, gains[0] : gains[1]], start_of
    )


def visible_keys(start_row, low, high, block_id):
    shape = (high - low, BLOCK)
    keys = low + lax.broadcasted_iota(jnp.int32, shape, 0)
    queries = block_id * BLOCK + lax.broadcasted_iota(jnp.int32, shape, 1)
    return (keys.astype(F32) >= start_row) & (keys <= queries)


class Gather:
    def __init__(self, here, held, home, landed, hop_send, hop_recv, side_send, side_recv, store_sem):
        self.here, self.held, self.home, self.landed = here, held, home, landed
        self.hop_send, self.hop_recv = hop_send, hop_recv
        self.side_send, self.side_recv, self.store_sem = side_send, side_recv, store_sem

    def member(self, step, way, sibling=False):
        here = self.here
        chip = here.chip((CHIPS - step) % CHIPS if way == 0 else step)
        return chip * 2 + (1 - here.core if sibling else here.core)

    def hop(self, unit, step, way, arrival=False):
        half = way if step == HALF else None
        source = self.held(unit, step if arrival else step - 1, way, half)
        target = source if arrival or self.landed(unit) else self.held(unit, step, way, half)
        return pltpu.make_async_remote_copy(
            src_ref=source, dst_ref=target, send_sem=self.hop_send.at[unit, step - 1, way],
            recv_sem=self.hop_recv.at[unit, step - 1, way],
            device_id={"dp": self.here.next[way]}, device_id_type=MESH,
        )

    def index(self, step, way):
        return 0 if step == 0 else 2 * step - 1 + way

    def across(self, unit, step, way, arrival=False):
        half = way if step == HALF else None
        target = self.home(unit, self.member(step, way, sibling=arrival), half)
        source = target if arrival else self.held(unit, step, way, half)
        index = self.index(step, way)
        return pltpu.make_async_remote_copy(
            src_ref=source, dst_ref=target, send_sem=self.side_send.at[unit, index],
            recv_sem=self.side_recv.at[unit, index],
            device_id={"dp": self.here.sibling}, device_id_type=MESH,
        )

    def store(self, unit, step, way):
        half = way if step == HALF else None
        return pltpu.make_async_copy(
            self.held(unit, step, way, half), self.home(unit, self.member(step, way), half),
            self.store_sem.at[unit, self.index(step, way)],
        )

    def start(self, unit):
        for way in range(2):
            self.hop(unit, 1, way).start()
        self.across(unit, 0, 0).start()
        if not self.landed(unit):
            self.store(unit, 0, 0).start()

    def step(self, unit, step):
        for way in range(2):
            self.hop(unit, step - 1, way, arrival=True).wait_recv()
            if step <= HALF:
                self.hop(unit, step, way).start()
            self.across(unit, step - 1, way).start()
            if not self.landed(unit):
                self.store(unit, step - 1, way).start()

    def pieces(self):
        return [(0, 0)] + [(step, way) for step in range(1, HALF + 1) for way in range(2)]

    def end(self, unit):
        for step, way in self.pieces():
            self.across(unit, step, way, arrival=True).wait_recv()

    def sent(self, unit):
        for step, way in self.pieces():
            self.across(unit, step, way).wait_send()
            if step:
                self.hop(unit, step, way).wait_send()
            if not self.landed(unit):
                self.store(unit, step, way).wait()


def units_of(chunk, total):
    return min(CHUNK, total - chunk * CHUNK)


def pack_copies(weights, pack, chunks, sem):
    copies = []
    for i, chunk in enumerate(chunks):
        begin, size = chunk * CHUNK, units_of(chunk, weights[0].shape[1])
        for m, ref in enumerate(weights):
            copies.append(pltpu.make_async_copy(
                ref.at[:, begin : begin + size], pack.at[i, :, m * size : (m + 1) * size],
                sem.at[i, m],
            ))
    return copies


LATER = 3
PAIRS = 2
QUARTERS = 4


def forward_kernel(
    cfg, hid, cot, turns, places, bias_q, bias_k, bias_v, gain_a, gain_f,
    wq, wk, wv, wo, wg, wu, wd,
    w_ffn, w_attn, hid_all, cot_all, in_one_t, qrot, krot, vlow, mixed, lse, middle, in_two, vec_ref,
    cos_ref, sin_ref, in_two_t, cot_t,
    wa, qkv, psend, precv, pack, slots, in_one, cots, turned, turned_cot,
    local_sem, pack_sem, store_sem, hop_send, hop_recv, side_send, side_recv, x_send, x_recv, t_sem,
):
    rows, heads, units = cfg
    own_tokens, width = hid.shape
    tokens = 2 * own_tokens
    width_q = heads * HD
    width_qkv = width_q + 2 * HD
    here = Spot(rows)
    shard = here.shard

    own_rows = pl.ds(pl.multiple_of(shard * own_tokens, TILE), own_tokens)
    other_rows = pl.ds(pl.multiple_of((1 - shard) * own_tokens, TILE), own_tokens)
    quarter = own_tokens // QUARTERS

    def quarter_rows(index, side):
        return pl.ds(pl.multiple_of(side * own_tokens + index * quarter, quarter), quarter)

    mine = here.part(here.me)
    attn_copies, column = [], 0
    for i, ref in enumerate((wq, wk, wv, wo)):
        wide = ref.shape[1]
        attn_copies.append(
            pltpu.make_async_copy(ref, wa.at[mine, column : column + wide], local_sem.at[i])
        )
        column += wide
    ffn_copies = pack_copies((wg, wu, wd), pack, range(PAIRS * units), pack_sem)
    own_copies = [
        pltpu.make_async_copy(hid, hid_all.at[own_rows, :], local_sem.at[4]),
        pltpu.make_async_copy(cot, cots.at[own_rows, :], local_sem.at[5]),
    ]
    for copy in attn_copies + own_copies + ffn_copies:
        copy.start()

    column = 0
    for ref in (bias_q, bias_k, bias_v):
        size = ref.shape[0] // 2
        row = ref[...].reshape(1, 2 * size)
        vec_ref[:, column : column + size] = jnp.where(shard == 0, row[:, :size], row[:, size:])
        column += size
    for ref in (gain_a, gain_f):
        vec_ref[:, column : column + width] = ref[...].reshape(1, width)
        column += width
    vec_ref[:, column : column + tokens] = (
        lax.broadcasted_iota(jnp.int32, (1, tokens), 1) - places[...].reshape(1, tokens)
    ).astype(F32)
    bias, gain_one, gain_two, start_of = small_inputs(vec_ref, width_qkv, width)

    here.greet()

    def swap_copy(index, src, dst):
        return pltpu.make_async_remote_copy(
            src_ref=src, dst_ref=dst, send_sem=x_send.at[index], recv_sem=x_recv.at[index],
            device_id={"mp": 1 - shard}, device_id_type=MESH,
        )

    hid_swap = (swap_copy(0, hid, hid_all.at[own_rows, :]), swap_copy(0, hid, hid_all.at[other_rows, :]))
    mix_swap = swap_copy(1, psend, precv)
    two_swap = (
        swap_copy(2, in_two.at[own_rows, :], in_two.at[own_rows, :]),
        swap_copy(2, in_two.at[other_rows, :], in_two.at[other_rows, :]),
    )

    def cot_swap(index, arrival=False):
        ref = cots.at[quarter_rows(index, 1 - shard if arrival else shard), :]
        return swap_copy(3 + index, ref, ref)

    def home(unit, member, half):
        part = here.part(member, half)
        if unit == 0:
            return wa.at[part, :]
        return w_ffn.at[(unit - 1) * PAIRS : unit * PAIRS, part, :]

    def held(unit, step, way, half):
        if unit == 0:
            return home(0, gather.member(step, way), half)
        part = slice(0, rows) if half is None else slice(half * rows // 2, (half + 1) * rows // 2)
        if step == 0:
            return pack.at[(unit - 1) * PAIRS : unit * PAIRS, part, :]
        slot = 2 * HALF - 2 if step == HALF else 2 * (step - 1) + way
        return slots.at[unit - 1, slot, :, part, :]

    gather = Gather(
        here, held, home, lambda unit: unit == 0, hop_send, hop_recv, side_send, side_recv, store_sem
    )
    ffn_units = range(1, units + 1)

    hid_swap[0].start()
    for copy in attn_copies:
        copy.wait()
    gather.start(0)
    at = jnp.broadcast_to(places[...].reshape(1, tokens).astype(F32), (HD, tokens)).T
    angles = at * turns[...].reshape(1, HD)
    cos_ref[...] = jnp.cos(angles)
    lanes = lax.broadcasted_iota(jnp.int32, (tokens, HD), 1)
    sin_ref[...] = jnp.where(lanes < HD // 2, -1.0, 1.0) * jnp.sin(angles)

    for step in range(2, HALF + 1):
        gather.step(0, step)
    for copy in ffn_copies:
        copy.wait()
    for unit in ffn_units:
        gather.start(unit)
    gather.step(0, HALF + 1)

    for copy in own_copies:
        copy.wait()
    hid_swap[1].wait_recv()
    for index in range(QUARTERS - 1):
        cot_swap(index).start()

    @pl.loop(0, tokens // TILE)
    def _(t):
        v = hid_all[tile_of(t), :].astype(F32)
        factor = lax.rsqrt(jnp.mean(v * v, axis=-1, keepdims=True) + EPS)
        in_one[tile_of(t), :] = (v * factor * gain_one).astype(BF16)

    gather.end(0)
    wa_out = pltpu.make_async_copy(wa, w_attn, local_sem.at[6])
    wa_out.start()

    @pl.loop(0, tokens // TILE)
    def _(t):
        part = tile_of(t)
        qkv[part, :] = contract(in_one[part, :], wa[:, 0:width_qkv], 1, 0) + bias
        cosines, sines = cos_ref[part, :], sin_ref[part, :]
        for h in range(heads):
            columns = slice(h * HD, (h + 1) * HD)
            qrot[part, columns] = turn(qkv[part, columns], cosines, sines).astype(BF16)
        krot[part, :] = turn(qkv[part, width_q : width_q + HD], cosines, sines).astype(BF16)
        vlow[part, :] = qkv[part, width_q + HD :].astype(BF16)

    def attend(blocks):
        @pl.loop(0, heads)
        def _(h):
            columns = tile_of(h, HD)
            for i in blocks:
                low, high = key_range(i)
                part = pl.ds(i * BLOCK, BLOCK)
                scores = contract(krot[low:high, :], qrot[part, columns], 1, 1) * SCALE
                scores = jnp.where(visible_keys(start_of(i), low, high, i), scores, -1e30)
                top = jnp.max(scores, axis=0, keepdims=True)
                weights = jnp.exp(scores - top)
                total = jnp.sum(weights, axis=0, keepdims=True)
                probs = (weights * (1.0 / total)).astype(BF16)
                mixed[part, columns] = contract(probs, vlow[low:high, :], 0, 0).astype(BF16)
                lse[h, 0:1, part] = top + jnp.log(total)

    halves = (range(own_tokens // BLOCK), range(own_tokens // BLOCK, tokens // BLOCK))
    for index in range(2):
        @pl.when(shard == index)
        def _():
            attend(halves[1 - index])

    @pl.loop(0, width // TILE)
    def _(n):
        weight = wa[tile_of(n), width_qkv:]
        psend[:, tile_of(n)] = contract(mixed[other_rows, :], weight, 1, 1).astype(BF16)

    mix_swap.start()
    for index in range(2):
        @pl.when(shard == index)
        def _():
            attend(halves[index])

    @pl.loop(0, width // TILE)
    def _(n):
        weight = wa[tile_of(n), width_qkv:]
        middle[:, tile_of(n)] = (
            contract(mixed[own_rows, :], weight, 1, 1) + hid[:, tile_of(n)].astype(F32)
        )

    for unit in ffn_units:
        gather.step(unit, 2)

    def transpose(source, target, first, begin, count):
        @pl.loop(0, width // TILE)
        def _(n):
            for t in range(count):
                part = pl.ds(pl.multiple_of(begin + t * TILE, TILE), TILE)
                target[tile_of(n), part] = source[part, tile_of(n)].T

    transpose(in_one, turned, 0, 0, tokens // TILE)
    one_turned = pltpu.make_async_copy(turned, in_one_t, t_sem.at[0])
    one_turned.start()
    mine_begin, theirs_begin = shard * own_tokens, (1 - shard) * own_tokens
    transpose(cots, turned_cot, 0, mine_begin, own_tokens // TILE)
    for index in range(QUARTERS // 2):
        cot_swap(index, arrival=True).wait_recv()
    transpose(cots, turned_cot, 0, theirs_begin, own_tokens // TILE // 2)

    mix_swap.wait_recv()

    @pl.loop(0, own_tokens // TILE)
    def _(t):
        part = tile_of(t)
        v = middle[part, :] + precv[part, :].astype(F32)
        middle[part, :] = v
        factor = lax.rsqrt(jnp.mean(v * v, axis=-1, keepdims=True) + EPS)
        to = pl.ds(pl.multiple_of(shard * own_tokens + t * TILE, TILE), TILE)
        in_two[to, :] = (v * factor * gain_two).astype(BF16)

    two_swap[0].start()
    cot_swap(QUARTERS - 1).start()
    one_turned.wait()
    for unit in ffn_units:
        gather.step(unit, 3)
    transpose(in_two, turned, 0, mine_begin, own_tokens // TILE)
    for unit in list(ffn_units)[:1]:
        gather.step(unit, 4)
    two_swap[1].wait_recv()
    transpose(in_two, turned, 0, theirs_begin, own_tokens // TILE)
    two_turned = pltpu.make_async_copy(turned, in_two_t, t_sem.at[1])
    two_turned.start()
    for unit in list(ffn_units)[1:]:
        gather.step(unit, 4)
    for index in range(QUARTERS // 2, QUARTERS):
        cot_swap(index, arrival=True).wait_recv()
    transpose(cots, turned_cot, 0, theirs_begin + own_tokens // 2, own_tokens // TILE // 2)
    cot_copies = [
        pltpu.make_async_copy(cots, cot_all, t_sem.at[2]),
        pltpu.make_async_copy(turned_cot, cot_t, t_sem.at[3]),
    ]
    for copy in cot_copies:
        copy.start()
    for unit in ffn_units:
        gather.step(unit, 5)
    for unit in ffn_units:
        gather.end(unit)
    for unit in range(units + 1):
        gather.sent(unit)
    hid_swap[0].wait_send()
    mix_swap.wait_send()
    two_swap[0].wait_send()
    for index in range(QUARTERS):
        cot_swap(index).wait_send()
    for copy in [wa_out, two_turned] + cot_copies:
        copy.wait()


def forward_attention(hidden_in, cotangent, vectors, weights, heads):
    own_tokens, width = hidden_in.shape
    tokens = 2 * own_tokens
    rows = weights[0].shape[0]
    chunks = -(-weights[4].shape[1] // CHUNK)
    units = (chunks - LATER) // PAIRS
    early = units * PAIRS
    width_q = heads * HD
    width_attn = 2 * width_q + 2 * HD
    wide = 3 * CHUNK
    vmem = pl.BlockSpec(memory_space=pltpu.VMEM)
    hbm = pl.BlockSpec(memory_space=pl.ANY)
    dma = pltpu.SemaphoreType.DMA
    shape = jax.ShapeDtypeStruct
    pieces = 2 * HALF + 1
    return pl.pallas_call(
        functools.partial(forward_kernel, (rows, heads, units)),
        in_specs=[vmem, hbm] + [vmem] * 7 + [hbm] * 7,
        out_specs=[hbm, hbm, vmem, hbm, hbm] + [vmem] * 10 + [hbm, hbm],
        out_shape=[
            shape((early, width, wide), BF16),
            shape((width, width_attn), BF16),
            shape((tokens, width), BF16),
            shape((tokens, width), BF16),
            shape((width, tokens), BF16),
            shape((tokens, width_q), BF16),
            shape((tokens, HD), BF16),
            shape((tokens, HD), BF16),
            shape((tokens, width_q), BF16),
            shape((heads, 8, tokens), F32),
            shape((own_tokens, width), F32),
            shape((tokens, width), BF16),
            shape((1, width_q + 2 * HD + 2 * width + tokens), F32),
            shape((tokens, HD), F32),
            shape((tokens, HD), F32),
            shape((width, tokens), BF16),
            shape((width, tokens), BF16),
        ],
        scratch_shapes=[
            pltpu.VMEM((width, width_attn), BF16),
            pltpu.VMEM((tokens, width_q + 2 * HD), F32),
            pltpu.VMEM((own_tokens, width), BF16),
            pltpu.VMEM((own_tokens, width), BF16),
            pltpu.VMEM((early, rows, wide), BF16),
            pltpu.VMEM((units, 2 * HALF - 1, PAIRS, rows, wide), BF16),
            pltpu.VMEM((tokens, width), BF16),
            pltpu.VMEM((tokens, width), BF16),
            pltpu.VMEM((width, tokens), BF16),
            pltpu.VMEM((width, tokens), BF16),
            dma((7,)), dma((early, 3)), dma((units + 1, pieces)),
            dma((units + 1, HALF, 2)), dma((units + 1, HALF, 2)),
            dma((units + 1, pieces)), dma((units + 1, pieces)),
            dma((3 + QUARTERS,)), dma((3 + QUARTERS,)), dma((4,)),
        ],
        compiler_params=pltpu.CompilerParams(
            collective_id=1, has_side_effects=True, vmem_limit_bytes=63 * 2**20
        ),
        cost_estimate=pl.CostEstimate(
            flops=6 * tokens * width * width_attn, bytes_accessed=120 * 2**20, transcendentals=0
        ),
        name="forward_attention",
    )(hidden_in, cotangent, *vectors, *weights)


class Sums:
    def __init__(self, here, own, places, send_sem, recv_sem):
        self.here, self.own, self.places = here, own, places
        self.send_sem, self.recv_sem = send_sem, recv_sem

    def chip(self, step, way):
        distance = HALF - step
        return self.here.chip(distance if way == 0 else CHIPS - distance)

    def copy(self, o, p, step, way, m, columns):
        here, rows = self.here, self.here.rows
        return pltpu.make_async_remote_copy(
            src_ref=self.own.at[o, here.part(self.chip(step, way), way if step == 0 else None), columns],
            dst_ref=self.places.at[p, step, way, 0 : rows // 2 if step == 0 else rows, columns],
            send_sem=self.send_sem.at[p, step, way, m],
            recv_sem=self.recv_sem.at[p, step, way, m],
            device_id={"dp": here.next[way]},
            device_id_type=MESH,
        )

    def columns(self, pieces, m):
        count, size = pieces
        return pl.ds(pl.multiple_of(m * size, HD), size)

    def start(self, o, p, pieces):
        @pl.loop(0, pieces[0])
        def _(m):
            for way in range(2):
                self.copy(o, p, 0, way, m, self.columns(pieces, m)).start()

    def step(self, o, p, step, pieces):
        here, own = self.here, self.own

        @pl.loop(0, pieces[0])
        def _(m):
            columns = self.columns(pieces, m)
            for way in range(2):
                self.copy(o, p, step - 1, way, m, columns).wait()
            for way in range(2):
                part = here.part(self.chip(step, way), way if step == 1 else None)
                size = here.rows // 2 if step == 1 else here.rows
                own[o, part, columns] = (
                    own[o, part, columns].astype(F32)
                    + self.places[p, step - 1, way, 0:size, columns].astype(F32)
                ).astype(BF16)
                self.copy(o, p, step, way, m, columns).start()

    def end(self, o, p, pieces, target):
        own, last = self.own, HALF - 1
        part = self.here.part(self.here.chip(0))

        @pl.loop(0, pieces[0])
        def _(m):
            columns = self.columns(pieces, m)
            for way in range(2):
                self.copy(o, p, last, way, m, columns).wait()
            target[:, columns] = (
                own[o, part, columns].astype(F32)
                + self.places[p, last, 0, :, columns].astype(F32)
                + self.places[p, last, 1, :, columns].astype(F32)
            )


EVENTS = {
    (0, "a"): "G11 G21",
    (0, "c"): "G02",
    (0, "f"): "G12",
    (1, "a"): "R00",
    (1, "b"): "G22",
    (1, "e"): "G03",
    (2, "a"): "R10",
    (2, "b"): "G13",
    (2, "c"): "R01 G23",
    (3, "a"): "G04 R11",
    (3, "c"): "G14",
    (4, "a"): "R02",
    (4, "b"): "G24",
    (4, "c"): "G05",
    (4, "e"): "R12",
    (4, "f"): "G15",
    (5, "a"): "R03 R20",
    (5, "c"): "G25 R13",
    (6, "0a"): "R04 R21",
    (6, "1a"): "R14 R22",
    (6, "1b"): "R30",
    (6, "2b"): "R23",
    (7, "0a"): "R31",
    (7, "1a"): "R24 R32 R40",
    (7, "2a"): "R33",
    (7, "2b"): "R41",
    (8, "1a"): "R34 R42",
    (8, "1b"): "R43",
    (8, "2b"): "R44",
}
SETS = 3


def ffn_kernel(
    cfg, in2_hbm, cot_hbm, in2t_hbm, cott_hbm, w_ffn, w_attn, wg, wu, wd,
    hiddens, gin_own, later, grad_g, grad_u, grad_d, w_other, w_late,
    in2, cot, in2t, cott, wbuf, acts, gin, own, sent, sib, ring, stage, pack,
    in_sem, w_sem, sib_send, sib_recv, ring_send, ring_recv, out_sem, g_sem, end_sem, free_sem,
    pack_sem, store_sem, hop_send, hop_recv, side_send, side_recv, park_sem, fetch_sem, hid_sem,
):
    rows, chunks, total = cfg
    grads = (grad_g, grad_u, grad_d)
    tokens, width = in2.shape
    side_rows = CHIPS * rows
    own_tokens = tokens // 2
    first = chunks - LATER
    rings = first - 1
    here = Spot(rows)
    shard = here.shard
    sums = Sums(here, own, ring, ring_send, ring_recv)
    ring_pieces = (3, CHUNK)
    own_rows = pl.ds(pl.multiple_of(shard * own_tokens, TILE), own_tokens)
    other_rows = pl.ds(pl.multiple_of((1 - shard) * own_tokens, TILE), own_tokens)

    def load(chunk, m):
        columns = (slice(0, 2 * CHUNK), slice(2 * CHUNK, 3 * CHUNK))[m]
        return pltpu.make_async_copy(
            w_ffn.at[chunk, :, columns], wbuf.at[:, columns], w_sem.at[m]
        )

    def size_of(i):
        return units_of(first + i, total)

    def load_late(i, m):
        size = size_of(i)
        columns = (slice(0, 2 * size), slice(2 * size, 3 * size))[m]
        return pltpu.make_async_copy(
            w_late.at[i, :, columns], wbuf.at[:, columns], w_sem.at[m]
        )

    def home(unit, member, half):
        return w_late.at[unit, here.part(member, half), 0 : 3 * size_of(unit)]

    def held(unit, step, way, half):
        size = rows if half is None else rows // 2
        columns = slice(0, 3 * size_of(unit))
        if step == 0:
            return pack.at[unit, :, columns]
        slot = 2 * (step - 1) + way
        whole = 2 * HALF - 2
        if unit < 2:
            buffer, begin = 1 + unit, (whole if step == HALF else slot) * rows
            offset = 0
            if half is not None:
                offset = half * size
        else:
            base = (whole + 1) * rows
            if step == HALF:
                buffer, begin, offset = 1 + way, base + whole // 2 * rows, 0
            else:
                buffer, begin = 1 + slot // (whole // 2), base + slot % (whole // 2) * rows
                offset = 0 if half is None else half * size
        return acts.at[buffer, begin + offset : begin + offset + size, columns]

    gather = Gather(
        here, held, home, lambda unit: False, hop_send, hop_recv, side_send, side_recv, store_sem
    )
    own_blocks = pack_copies((wg, wu, wd), pack, range(first, chunks), pack_sem)

    inputs = [
        pltpu.make_async_copy(in2_hbm, in2, in_sem.at[0]),
        pltpu.make_async_copy(cot_hbm, cot, in_sem.at[1]),
    ]
    turned = []
    for i, (source, target) in enumerate(((in2t_hbm, in2t), (cott_hbm, cott))):
        for side in range(2):
            for chip in range(CHIPS):
                member = 2 * chip + (here.core if side == 0 else 1 - here.core)
                begin = side * side_rows + chip * rows
                turned.append(pltpu.make_async_copy(
                    source.at[here.part(member), :], target.at[begin : begin + rows, :],
                    in_sem.at[2 + i],
                ))
    for copy in own_blocks + [load(0, m) for m in range(2)] + inputs:
        copy.start()
    here.greet()
    for copy in own_blocks:
        copy.wait()
    gather.start(0)

    def result_copies(chunk):
        return [
            pltpu.make_async_copy(
                stage.at[:, m * CHUNK : (m + 1) * CHUNK],
                grads[m].at[:, tile_of(chunk, CHUNK)],
                out_sem.at[m],
            )
            for m in range(3)
        ]

    def fetch(chunk):
        return pltpu.make_async_copy(
            later.at[chunk - SETS], own.at[chunk % SETS], fetch_sem.at[chunk % SETS]
        )

    def park(chunk, p, early, size=CHUNK):
        columns = slice(0, 3 * size)
        target = own.at[chunk] if early else later.at[chunk - SETS, :, columns]
        return pltpu.make_async_copy(sib.at[p, :, columns], target, park_sem.at[p])

    def ring_event(chunk, step):
        o, p = chunk % SETS, chunk % 2
        if step == 0:
            if chunk >= SETS:
                fetch(chunk).wait()
            sums.start(o, p, ring_pieces)
        elif step < HALF:
            sums.step(o, p, step, ring_pieces)
        else:
            if chunk:
                for copy in result_copies(chunk - 1):
                    copy.wait()
            sums.end(o, p, ring_pieces, stage)
            for copy in result_copies(chunk):
                copy.start()
            if chunk + SETS < rings:
                fetch(chunk + SETS).start()

    def run(events):
        for event in events.split():
            index, step = int(event[1]), int(event[2])
            if event[0] == "R":
                ring_event(index, step)
            elif step == 1:
                gather.start(index)
            else:
                gather.step(index, step)

    def sib_copy(p, m, size):
        columns = slice(m * size, (m + 1) * size)
        return pltpu.make_async_remote_copy(
            src_ref=sent.at[:, columns],
            dst_ref=sib.at[p, :, columns],
            send_sem=sib_send.at[m],
            recv_sem=sib_recv.at[p, m],
            device_id={"dp": here.sibling},
            device_id_type=MESH,
        )

    def weight_copy():
        return pltpu.make_async_remote_copy(
            src_ref=w_attn.at[:, 0 : w_other.shape[1]], dst_ref=w_other,
            send_sem=g_sem.at[2], recv_sem=g_sem.at[3],
            device_id={"mp": 1 - shard}, device_id_type=MESH,
        )

    def gin_copy():
        return pltpu.make_async_remote_copy(
            src_ref=in2.at[other_rows, :], dst_ref=cot.at[own_rows, :],
            send_sem=g_sem.at[0], recv_sem=g_sem.at[1],
            device_id={"mp": 1 - shard}, device_id_type=MESH,
        )

    def hidden_copy(index, chunk, size=CHUNK):
        return pltpu.make_async_copy(
            acts.at[index, :, 2 * size : 3 * size], hiddens.at[chunk, :, 0:size], hid_sem.at[index]
        )

    def forward(index, part, size=CHUNK):
        for begin in range(0, size, TILE):
            stop = min(begin + TILE, size)
            gates, ups, downs = (slice(m * size + begin, m * size + stop) for m in range(3))
            gate = contract(in2[part, :], wbuf[:, gates], 1, 0)
            up = contract(in2[part, :], wbuf[:, ups], 1, 0)
            grad = contract(cot[part, :], wbuf[:, downs], 1, 0)
            sig = 0.5 * jnp.tanh(0.5 * gate) + 0.5
            swish = gate * sig
            acts[index, part, downs] = (swish * up).astype(BF16)
            acts[index, part, gates] = (grad * up * (sig + swish - swish * sig)).astype(BF16)
            acts[index, part, ups] = (grad * swish).astype(BF16)

    def back_gin(index, part, size=CHUNK):
        @pl.loop(0, width // TILE)
        def _(n):
            gin[part, tile_of(n)] += contract(
                acts[index, part, 0 : 2 * size], wbuf[tile_of(n), 0 : 2 * size], 1, 1
            )

    def weight_grads(index, p, between, size=CHUNK):
        for m, left in enumerate((in2t, in2t, cott)):
            columns = slice(m * size, (m + 1) * size)
            sent[:, columns] = contract(
                left[side_rows:, :], acts[index, :, columns], 1, 0
            ).astype(BF16)
            sib_copy(p, m, size).start()
        between()
        for m, left in enumerate((in2t, in2t, cott)):
            columns = slice(m * size, (m + 1) * size)
            sib_copy(p, m, size).wait()
            sib[p, :, columns] = (
                contract(left[0:side_rows, :], acts[index, :, columns], 1, 0)
                + sib[p, :, columns].astype(F32)
            ).astype(BF16)

    gin[...] = jnp.zeros_like(gin)
    for copy in inputs:
        copy.wait()
    for copy in turned:
        copy.start()

    def at_point(j, point):
        for chunk in range(first):
            if (chunk, point) in EVENTS:
                @pl.when(j == chunk)
                def _():
                    run(EVENTS[chunk, point])

    weight_copy().start()

    @pl.loop(0, first)
    def _(j):
        p = lax.rem(j, 2)
        for m in range(2):
            load(j, m).wait()

        @pl.when(j >= 1)
        def _():
            hidden_copy(0, j - 1).wait()

        forward(0, slice(0, own_tokens))

        @pl.when((j >= 1) & (j <= SETS))
        def _():
            park(j - 1, 1 - p, True).wait()

        @pl.when(j > SETS)
        def _():
            park(j - 1, 1 - p, False).wait()

        at_point(j, "a")
        forward(0, slice(own_tokens, tokens))
        hidden_copy(0, j).start()
        at_point(j, "b")

        @pl.when(j == first - 1)
        def _():
            gather.end(0)
            gather.sent(0)

        @pl.when(j + 1 < first)
        def _():
            load(j + 1, 1).start()

        @pl.when(j == first - 1)
        def _():
            load_late(0, 1).start()

        back_gin(0, slice(0, tokens))

        @pl.when(j + 1 < first)
        def _():
            load(j + 1, 0).start()

        @pl.when(j == first - 1)
        def _():
            load_late(0, 0).start()

        at_point(j, "c")

        @pl.when(j == 0)
        def _():
            for i, ref in enumerate((in2t, cott)):
                pltpu.make_async_copy(ref, ref, in_sem.at[2 + i]).wait()

        weight_grads(0, p, lambda: at_point(j, "e"))

        @pl.when(j < SETS)
        def _():
            park(j, p, True).start()

        @pl.when(j >= SETS)
        def _():
            park(j, p, False).start()

        at_point(j, "f")

    hidden_copy(0, first - 1).wait()
    for unit in range(1, LATER):
        gather.end(unit)
        gather.sent(unit)

    for half in range(2):
        part = (other_rows, own_rows)[half]
        for i in range(LATER):
            size = size_of(i)
            for m in range(2):
                load_late(i, m).wait()
            forward(i, part, size)
            if half == 1:
                hidden_copy(i, first + i, size).start()
            run(EVENTS.get((first + half, f"{i}a"), ""))
            following = i + 1 if i + 1 < LATER else 0
            same = size_of(following) == size
            more = half == 0 or i + 1 < LATER
            if more and same:
                load_late(following, 1).start()
            back_gin(i, part, size)
            if more:
                load_late(following, 0).start()
            if more and not same:
                load_late(following, 1).start()
            run(EVENTS.get((first + half, f"{i}b"), ""))
        if half == 0:
            pl.semaphore_signal(
                free_sem, inc=1, device_id={"mp": 1 - shard}, device_id_type=MESH
            )

            @pl.loop(0, own_tokens // TILE)
            def _(t):
                of = pl.ds(pl.multiple_of((1 - shard) * own_tokens + t * TILE, TILE), TILE)
                in2[of, :] = gin[of, :].astype(BF16)

            pl.semaphore_wait(free_sem, 1)
            gin_copy().start()

    for i in range(LATER):
        chunk, size = first + i, size_of(i)
        p = chunk % 2
        park(chunk - 1, 1 - p, False).wait()
        weight_grads(i, p, lambda: run(EVENTS.get((first + 2, f"{i}a"), "")), size)
        park(chunk, p, False, size).start()
        run(EVENTS.get((first + 2, f"{i}b"), ""))
    gin_copy().wait()

    @pl.loop(0, own_tokens // TILE)
    def _(t):
        of = pl.ds(pl.multiple_of(shard * own_tokens + t * TILE, TILE), TILE)
        at = pl.ds(pl.multiple_of((1 - shard) * own_tokens + t * TILE, TILE), TILE)
        gin[of, :] = gin[of, :] + cot[at, :].astype(F32)

    gin_out = pltpu.make_async_copy(gin.at[own_rows, :], gin_own, end_sem.at[0])
    gin_out.start()
    weight_copy().wait()
    last_park = park(chunks - 1, (chunks - 1) % 2, False, size_of(LATER - 1))
    for copy in [gin_out, last_park] + result_copies(rings - 1):
        copy.wait()
    for i in range(LATER):
        hidden_copy(i, first + i, size_of(i)).wait()


def feed_forward(inputs_two, grad_ffn, in_two_t, cot_t, w_ffn, w_attn, width_qkv, weights):
    tokens, width = inputs_two.shape
    rows = weights[0].shape[0]
    chunks = w_ffn.shape[0] + LATER
    pieces = 2 * HALF + 1
    hbm = pl.BlockSpec(memory_space=pl.ANY)
    side_rows, wide = CHIPS * rows, 3 * CHUNK
    dma = pltpu.SemaphoreType.DMA
    shape = jax.ShapeDtypeStruct
    half = (tokens // 2, width)
    return pl.pallas_call(
        functools.partial(ffn_kernel, (rows, chunks, weights[0].shape[1])),
        in_specs=[hbm] * 9,
        out_specs=[hbm] * 8,
        out_shape=[
            shape((chunks, tokens, CHUNK), BF16), shape(half, F32),
            shape((chunks - SETS, side_rows, wide), BF16),
        ] + [shape((rows, (chunks - LATER - 1) * CHUNK), F32)] * 3 + [
            shape((width, width_qkv), BF16),
            shape((LATER, width, wide), BF16),
        ],
        scratch_shapes=[
            pltpu.VMEM((tokens, width), BF16),
            pltpu.VMEM((tokens, width), BF16),
            pltpu.VMEM((width, tokens), BF16),
            pltpu.VMEM((width, tokens), BF16),
            pltpu.VMEM((width, wide), BF16),
            pltpu.VMEM((LATER, tokens, wide), BF16),
            pltpu.VMEM((tokens, width), F32),
            pltpu.VMEM((SETS, side_rows, wide), BF16),
            pltpu.VMEM((side_rows, wide), BF16),
            pltpu.VMEM((2, side_rows, wide), BF16),
            pltpu.VMEM((2, HALF, 2, rows, wide), BF16),
            pltpu.VMEM((rows, wide), F32),
            pltpu.VMEM((LATER, rows, wide), BF16),
            dma((4,)), dma((2,)), dma((3,)), dma((2, 3)),
            dma((2, HALF, 2, 3)), dma((2, HALF, 2, 3)), dma((3,)), dma((4,)), dma((1,)),
            pltpu.SemaphoreType.REGULAR,
            dma((LATER, 3)), dma((LATER, pieces)), dma((LATER, HALF, 2)), dma((LATER, HALF, 2)),
            dma((LATER, pieces)), dma((LATER, pieces)), dma((2,)), dma((SETS,)), dma((LATER,)),
        ],
        compiler_params=pltpu.CompilerParams(
            collective_id=2, has_side_effects=True, vmem_limit_bytes=63 * 2**20
        ),
        cost_estimate=pl.CostEstimate(
            flops=18 * tokens * width * chunks * CHUNK, bytes_accessed=80 * 2**20,
            transcendentals=tokens * chunks * CHUNK,
        ),
        name="feed_forward",
    )(inputs_two, grad_ffn, in_two_t, cot_t, w_ffn, w_attn, *weights)


JOBS = 1 + LATER


BACK_EVENTS = {
    "w0": "01 11",
    "w1": "20",
    "w2": "02",
    "w4": "12",
    "w6": "21",
    "w8": "03",
    "w9": "13",
    "h0": "22",
    "h3": "04",
    "h4": "30",
    "h5": "14",
    "o": "23 31",
    "q1": "40",
    "t1": "24",
    "t2": "32",
    "t3": "41",
    "g": "33",
    "b": "42",
    "u1": "50 34 43",
    "l0": "51",
    "l2": "44 52 53",
    "z1": "54",
}


def backward_kernel(
    cfg, later, gin_hbm, middle_hbm, cot_hbm, hiddens, w_ffn, w_late, w_other, w_attn, qrot_hbm, krot_hbm,
    vlow_hbm, lse_hbm, mixed_hbm, in_one_t, hid_hbm, cos_ref, sin_ref, vec_ref,
    layer_out, grad_input, small_out, grad_g, grad_u, grad_d, grad_qkv, grad_out, kept,
    own, ring, sent, sib, lefts, gin, middle, tall, wa, qrot, krot, vlow, lse, mixed,
    gmix, dqkv, gk, gv, osend, orecv, cots, got, stage, small, small_got,
    in_sem, ring_send, ring_recv, sib_send, sib_recv, x_send, x_recv, out_sem, s_send, s_recv, down_sem, hid_sem,
):
    rows, heads, skip, tail = cfg
    grads = (grad_g, grad_u, grad_d)
    own_tokens, width = gin.shape
    tokens = 2 * own_tokens
    width_q = heads * HD
    width_qkv = width_q + 2 * HD
    side_rows = CHIPS * rows
    _, gain_one, gain_two, start_of = small_inputs(vec_ref, width_qkv, width)
    here = Spot(rows)
    shard, me = here.shard, here.me
    sums = Sums(here, own, ring, ring_send, ring_recv)
    wide_qkv, wide_out = (2, width_qkv // 2), (2, width_q // 2)
    pieces = [(3, CHUNK)] * (JOBS - 1) + [(3, tail), wide_qkv, wide_out]
    own_rows = pl.ds(pl.multiple_of(shard * own_tokens, TILE), own_tokens)
    other_rows = pl.ds(pl.multiple_of((1 - shard) * own_tokens, TILE), own_tokens)

    def at_own(t, size=TILE):
        return pl.ds(pl.multiple_of(shard * own_tokens + t * size, size), size)

    def at_other(t, size=TILE):
        return pl.ds(pl.multiple_of((1 - shard) * own_tokens + t * size, size), size)

    def get(index, source, target):
        return pltpu.make_async_copy(source, target, in_sem.at[index])

    sums_in = [get(i, later.at[skip + i], own.at[i]) for i in range(3)]
    norm_in = [get(3, gin_hbm, gin), get(4, middle_hbm, middle), get(5, cot_hbm, cots)]
    rest_in = [
        get(7, w_attn, wa), get(8, qrot_hbm, qrot), get(9, krot_hbm, krot), get(10, vlow_hbm, vlow),
        get(11, lse_hbm, lse), get(12, mixed_hbm, mixed),
    ]
    for copy in sums_in[:2] + norm_in + sums_in[2:] + rest_in:
        copy.start()
    for side in range(2):
        for chip in range(CHIPS):
            member = 2 * chip + (here.core if side == 0 else 1 - here.core)
            begin = side * side_rows + chip * rows
            get(13, in_one_t.at[here.part(member), :], lefts.at[0, begin : begin + rows, :]).start()

    def bit(value):
        return lax.rem(lax.div(me, value), 2)

    def flipped(*values):
        return me + sum(value - 2 * value * bit(value) for value in values)

    ranks = (here.core + 2 * shard, bit(2) + 2 * bit(4), bit(8))
    partners = (
        ({"dp": flipped(1)}, {"mp": 1 - shard}, {"dp": flipped(1), "mp": 1 - shard}),
        ({"dp": flipped(2)}, {"dp": flipped(4)}, {"dp": flipped(2, 4)}),
        ({"dp": flipped(8)},),
    )

    def rank_of(group, k):
        rank = ranks[group]
        return (rank + 1 - 2 * lax.rem(rank, 2), rank + 2 - 4 * lax.div(rank, 2), 3 - rank)[k]

    barrier = pltpu.get_barrier_semaphore()
    greeted = [p for group in partners for p in group] + [{"dp": n} for n in here.next]
    for target in greeted:
        pl.semaphore_signal(barrier, inc=1, device_id=target, device_id_type=MESH)
    pl.semaphore_wait(barrier, len(greeted))

    def swap_copy(index, src, dst):
        return pltpu.make_async_remote_copy(
            src_ref=src, dst_ref=dst, send_sem=x_send.at[index], recv_sem=x_recv.at[index],
            device_id={"mp": 1 - shard}, device_id_type=MESH,
        )

    some = own_tokens // 2

    def out_swap(index):
        part = slice(index * some, (index + 1) * some)
        return swap_copy(index, osend.at[part, :], orecv.at[part, :])

    half_tiles = own_tokens // TILE

    def attn_swap(t):
        return swap_copy(2 + t, tall.at[at_own(t), :], tall.at[at_own(t), :])

    def attn_got(t):
        return swap_copy(2 + t, tall.at[at_other(t), :], tall.at[at_other(t), :])

    one_swap = swap_copy(2 + half_tiles, dqkv.at[other_rows, :], got)

    def result_copies(job):
        if job < JOBS:
            count, size = pieces[job]
            return [
                pltpu.make_async_copy(
                    stage.at[:, m * size : (m + 1) * size],
                    grads[m].at[:, job * CHUNK : job * CHUNK + size], out_sem.at[m],
                )
                for m in range(count)
            ]
        target = (grad_qkv, grad_out)[job - JOBS]
        return [pltpu.make_async_copy(stage.at[:, 0 : target.shape[1]], target, out_sem.at[0])]

    last_in = get(0, later.at[skip + 3, :, 0 : 3 * tail], own.at[0, :, 0 : 3 * tail])

    def run(point):
        for event in BACK_EVENTS.get(point, "").split():
            job, step = int(event[0]), int(event[1])
            o = p = job % 3
            if step == 0:
                if job == 2:
                    sums_in[2].wait()
                if job == 3:
                    last_in.wait()
                sums.start(o, p, pieces[job])
            elif step < HALF:
                sums.step(o, p, step, pieces[job])
            else:
                if job:
                    for copy in result_copies(job - 1):
                        copy.wait()
                sums.end(o, p, pieces[job], stage)
                for copy in result_copies(job):
                    copy.start()
                if job == 0:
                    last_in.start()

    for i in range(2):
        sums_in[i].wait()
        sums.start(i, i, pieces[i])

    for copy in norm_in:
        copy.wait()
    small[0, :, :] = jnp.zeros_like(small[0])

    @pl.loop(0, half_tiles)
    def _(t):
        part = tile_of(t)
        v = middle[part, :]
        factor = lax.rsqrt(jnp.mean(v * v, axis=-1, keepdims=True) + EPS)
        unit = v * factor
        e = gin[part, :]
        scaled = e * gain_two
        inner = jnp.mean(scaled * unit, axis=-1, keepdims=True)
        total = cots[part, :].astype(F32) + factor * (scaled - unit * inner)
        middle[part, :] = total
        gin[part, :] = v
        tall[at_own(t), :] = total.astype(BF16)
        attn_swap(t).start()
        small[0, 1:2, :] += jnp.sum(e * unit, axis=0, keepdims=True)

    keep = pltpu.make_async_copy(middle, kept, out_sem.at[5])
    keep.start()
    keep.wait()
    middle[...] = jnp.zeros_like(middle)
    early = w_ffn.shape[0]
    chunks = early + w_late.shape[0]

    def down_in(chunk):
        size = CHUNK if chunk + 1 < chunks else tail
        slot = chunk % 2 * CHUNK
        source = w_ffn.at[chunk] if chunk < early else w_late.at[chunk - early]
        return [
            pltpu.make_async_copy(
                source.at[:, 2 * size : 3 * size], lefts.at[1, :, slot : slot + size],
                down_sem.at[chunk % 2],
            ),
            pltpu.make_async_copy(
                hiddens.at[chunk, :, 0:size], dqkv.at[:, slot : slot + size], hid_sem.at[chunk % 2]
            ),
        ]

    for copy in down_in(0):
        copy.start()
    for chunk in range(chunks):
        if chunk + 1 < chunks:
            for copy in down_in(chunk + 1):
                copy.start()
        for copy in down_in(chunk):
            copy.wait()
        begin = chunk % 2 * CHUNK
        columns = slice(begin, begin + (CHUNK if chunk + 1 < chunks else tail))

        @pl.loop(0, width // TILE)
        def _(n):
            weight = lefts[1, tile_of(n), columns]
            middle[:, tile_of(n)] += contract(dqkv[other_rows, columns], weight, 1, 1)
            gin[:, tile_of(n)] += contract(dqkv[own_rows, columns], weight, 1, 1)

        run(f"w{chunk}")

    osend[...] = middle[...].astype(BF16)
    out_swap(0).start()
    run("w9")

    for copy in rest_in:
        copy.wait()
    for t in range(half_tiles):
        attn_got(t).wait_recv()

    @pl.loop(0, tokens // TILE)
    def _(t):
        gmix[tile_of(t), :] = contract(tall[tile_of(t), :], wa[:, width_qkv:], 1, 0).astype(BF16)

    gk[...] = jnp.zeros_like(gk)
    gv[...] = jnp.zeros_like(gv)

    @pl.loop(0, heads)
    def _(h):
        columns = tile_of(h, HD)
        for i in range(SEQ_LEN // BLOCK):
            low, high = key_range(i)
            part = pl.ds(i * BLOCK, BLOCK)
            query, grad = qrot[part, columns], gmix[part, columns]
            keys = krot[low:high, :]
            scores = contract(keys, query, 1, 1) * SCALE
            seen = visible_keys(start_of(i), low, high, i)
            probs = jnp.where(seen, jnp.exp(scores - lse[h, 0:1, part]), 0.0)
            grad_probs = contract(vlow[low:high, :], grad, 1, 1)
            row_term = jnp.sum(probs * grad_probs, axis=0, keepdims=True)
            grad_scores = (probs * (grad_probs - row_term)).astype(BF16)
            gk[low:high, :] += contract(grad_scores, query, 1, 0)
            gv[low:high, :] += contract(probs.astype(BF16), grad, 1, 0)
            dqkv[part, columns] = turn(
                contract(grad_scores, keys, 0, 0) * SCALE, cos_ref[part, :], -sin_ref[part, :]
            ).astype(BF16)

        for head in range(heads):
            if f"h{head}" in BACK_EVENTS:
                @pl.when(h == head)
                def _():
                    run(f"h{head}")

    dqkv[:, width_q : width_q + HD] = turn(gk[...] * SCALE, cos_ref[...], -sin_ref[...]).astype(BF16)
    dqkv[:, width_q + HD :] = gv[...].astype(BF16)

    one_swap.start()
    out_swap(1).start()
    run("o")

    side_sent = (sent, gmix.at[0:side_rows, :])
    side_got = (sib, qrot.at[0:side_rows, :])

    def side_copy(job, m, columns):
        return pltpu.make_async_remote_copy(
            src_ref=side_sent[job].at[:, columns],
            dst_ref=side_got[job].at[:, columns],
            send_sem=sib_send.at[job, m],
            recv_sem=sib_recv.at[job, m],
            device_id={"dp": here.sibling},
            device_id_type=MESH,
        )

    get(13, lefts.at[0], lefts.at[0]).wait()

    def send_side(job, left, right, pieces):
        for m in range(pieces[0]):
            columns = slice(m * pieces[1], (m + 1) * pieces[1])
            side_sent[job][:, columns] = contract(
                lefts[left, side_rows:, :], right[:, columns], 1, 0
            ).astype(BF16)
            side_copy(job, m, columns).start()

    def own_side(job, left, right, pieces, o):
        for m in range(pieces[0]):
            columns = slice(m * pieces[1], (m + 1) * pieces[1])
            side_copy(job, m, columns).wait()
            own[o, :, columns] = (
                contract(lefts[left, 0:side_rows, :], right[:, columns], 1, 0)
                + side_got[job][:, columns].astype(F32)
            ).astype(BF16)

    send_side(0, 0, dqkv, wide_qkv)
    run("q0")
    own_side(0, 0, dqkv, wide_qkv, 1)
    other_in = get(6, w_other, lefts.at[0])
    other_in.start()
    run("q1")

    for group in range(width // (4 * rows)):
        @pl.loop(0, tokens // TILE)
        def _(t):
            part = tile_of(t)
            turned = tall[part, group * 4 * rows : (group + 1) * 4 * rows].T
            for k in range(4):
                chip, odd = (4 * group + k) // 2, k % 2
                side = odd + here.core - 2 * odd * here.core
                to = pl.ds(pl.multiple_of(side * side_rows + chip * rows, 16), rows)
                lefts[1, to, part] = turned[k * rows : (k + 1) * rows, :]

        run(f"t{group}")

    for t in range(half_tiles):
        attn_swap(t).wait_send()
    hid_in = get(15, hid_hbm, tall)
    hid_in.start()

    fac = gk
    hid_in.wait()

    @pl.loop(0, tokens // TILE)
    def _(t):
        v = tall[tile_of(t), :].astype(F32)
        factor = lax.rsqrt(jnp.mean(v * v, axis=-1, keepdims=True) + EPS)
        fac[tile_of(t), :] = jnp.broadcast_to(factor, (TILE, HD))

    run("f")

    @pl.loop(0, width // TILE)
    def _(n):
        e = contract(dqkv[other_rows, :], wa[tile_of(n), 0:width_qkv], 1, 1)
        unit = tall[other_rows, tile_of(n)].astype(F32) * fac[other_rows, 0:1]
        small[0, 0:1, tile_of(n)] += jnp.sum(e * unit, axis=0, keepdims=True)

    run("g")

    @pl.loop(0, width // TILE)
    def _(n):
        e = contract(dqkv[own_rows, :], wa[tile_of(n), 0:width_qkv], 1, 1)
        middle[:, tile_of(n)] = e
        unit = tall[own_rows, tile_of(n)].astype(F32) * fac[own_rows, 0:1]
        small[0, 0:1, tile_of(n)] += jnp.sum(e * unit, axis=0, keepdims=True)

    @pl.loop(0, tokens // TILE)
    def _(t):
        bias = jnp.sum(dqkv[tile_of(t), :].astype(F32), axis=0, keepdims=True)
        at_query = pl.ds(pl.multiple_of(shard * width_q, HD), width_q)
        small[0, 2:3, at_query] += bias[:, 0:width_q]
        small[0, 3:4, tile_of(shard, HD)] += bias[:, width_q : width_q + HD]
        small[0, 3:4, tile_of(shard + 2, HD)] += bias[:, width_q + HD :]

    run("b")

    def small_copy(group, k):
        return pltpu.make_async_remote_copy(
            src_ref=small.at[group], dst_ref=small_got.at[group, ranks[group]],
            send_sem=s_send.at[group, k], recv_sem=s_recv.at[group, ranks[group]],
            device_id=partners[group][k], device_id_type=MESH,
        )

    def small_start(group):
        for k in range(len(partners[group])):
            small_copy(group, k).start()
        small_got[group, ranks[group]] = small[group]

    def small_end(group):
        count = len(partners[group])
        for k in range(count):
            ref = small_got.at[group, rank_of(group, k)]
            pltpu.make_async_remote_copy(
                src_ref=ref, dst_ref=ref, send_sem=s_send.at[group, k],
                recv_sem=s_recv.at[group, rank_of(group, k)],
                device_id=partners[group][k], device_id_type=MESH,
            ).wait_recv()
            small_copy(group, k).wait_send()
        total = small_got[group, 0]
        for rank in range(1, count + 1):
            total = total + small_got[group, rank]
        small[group + 1] = total

    small_start(0)
    send_side(1, 1, mixed, wide_out)
    run("u0")
    own_side(1, 1, mixed, wide_out, 2)
    small_end(0)
    small_start(1)
    run("u1")

    def layer_rows(index):
        part = slice(index * some, (index + 1) * some)
        out_swap(index).wait()
        orecv[part, :] = (gin[part, :] + orecv[part, :].astype(F32)).astype(BF16)
        copy = pltpu.make_async_copy(
            orecv.at[part, :], layer_out.at[part, :], out_sem.at[(3, 6)[index]]
        )
        copy.start()
        return copy

    def keep_in(index):
        part = slice(index * some, (index + 1) * some)
        return get(14, kept.at[part, :], gin.at[0:some, :])

    layer_copies = [layer_rows(0)]
    keep_in(0).start()
    run("l0")
    small_end(1)
    small_start(2)
    run("l1")
    small_end(2)
    run("l2")
    small_out[...] = small[3]

    one_swap.wait()
    other_in.wait()

    @pl.loop(0, width // TILE)
    def _(n):
        middle[:, tile_of(n)] += contract(got[...], lefts[0, tile_of(n), :], 1, 1)

    for index in range(2):
        part = slice(index * some, (index + 1) * some)
        of = pl.ds(pl.multiple_of(shard * own_tokens + index * some, some), some)
        if index:
            keep_in(index).start()
        keep_in(index).wait()
        factor = fac[of, 0:1]
        unit = tall[of, :].astype(F32) * factor
        scaled = middle[part, :] * gain_one
        inner = jnp.mean(scaled * unit, axis=-1, keepdims=True)
        cots[part, :] = (gin[0:some, :] + factor * (scaled - unit * inner)).astype(BF16)

    input_copy = pltpu.make_async_copy(cots, grad_input, out_sem.at[4])
    input_copy.start()
    layer_copies.append(layer_rows(1))
    run("z1")
    for copy in [input_copy] + layer_copies + result_copies(JOBS + 1):
        copy.wait()


def attention_back(
    later, gin, middle, cot, hiddens, w_ffn, w_late, w_other, forward, cos2, sin2, vector, tail
):
    w_attn, qrot, krot, vlow, lse, mixed, in_one_t, hid_all = forward
    own_tokens, width = cot.shape
    tokens = 2 * own_tokens
    heads = lse.shape[0]
    width_q = heads * HD
    width_qkv = width_q + 2 * HD
    side_rows, wide = later.shape[1:]
    rows = side_rows // CHIPS
    vmem = pl.BlockSpec(memory_space=pltpu.VMEM)
    hbm = pl.BlockSpec(memory_space=pl.ANY)
    dma = pltpu.SemaphoreType.DMA
    shape = jax.ShapeDtypeStruct
    half = (own_tokens, width)
    n_swaps = own_tokens // TILE + 3
    return pl.pallas_call(
        functools.partial(backward_kernel, (rows, heads, later.shape[0] - JOBS, tail)),
        in_specs=[hbm] * 16 + [vmem] * 3,
        out_specs=[hbm, hbm, vmem] + [hbm] * 6,
        out_shape=[
            shape(half, BF16), shape(half, BF16), shape((8, width), F32),
        ] + [shape((rows, (JOBS - 1) * CHUNK + tail), F32)] * 3 + [
            shape((rows, width_qkv), F32), shape((rows, width_q), F32), shape(half, F32),
        ],
        scratch_shapes=[
            pltpu.VMEM((3, side_rows, wide), BF16),
            pltpu.VMEM((3, HALF, 2, rows, wide), BF16),
            pltpu.VMEM((side_rows, width_qkv), BF16),
            pltpu.VMEM((side_rows, width_qkv), BF16),
            pltpu.VMEM((2, width, tokens), BF16),
            pltpu.VMEM(half, F32),
            pltpu.VMEM(half, F32),
            pltpu.VMEM((tokens, width), BF16),
            pltpu.VMEM(w_attn.shape, BF16),
            pltpu.VMEM((tokens, width_q), BF16),
            pltpu.VMEM((tokens, HD), BF16),
            pltpu.VMEM((tokens, HD), BF16),
            pltpu.VMEM(lse.shape, F32),
            pltpu.VMEM((tokens, width_q), BF16),
            pltpu.VMEM((tokens, width_q), BF16),
            pltpu.VMEM((tokens, width_qkv), BF16),
            pltpu.VMEM((tokens, HD), F32),
            pltpu.VMEM((tokens, HD), F32),
            pltpu.VMEM(half, BF16),
            pltpu.VMEM(half, BF16),
            pltpu.VMEM(half, BF16),
            pltpu.VMEM((own_tokens, width_qkv), BF16),
            pltpu.VMEM((rows, wide), F32),
            pltpu.VMEM((4, 8, width), F32),
            pltpu.VMEM((3, 4, 8, width), F32),
            dma((16,)), dma((3, HALF, 2, 3)), dma((3, HALF, 2, 3)), dma((2, 2)), dma((2, 2)),
            dma((n_swaps,)), dma((n_swaps,)), dma((7,)), dma((3, 3)), dma((3, 4)), dma((2,)), dma((2,)),
        ],
        compiler_params=pltpu.CompilerParams(
            collective_id=3, has_side_effects=True, vmem_limit_bytes=63 * 2**20
        ),
        cost_estimate=pl.CostEstimate(
            flops=10 * heads * tokens * tokens * HD, bytes_accessed=50 * 2**20, transcendentals=0
        ),
        name="attention_back",
    )(
        later, gin, middle, cot, hiddens, w_ffn, w_late, w_other, w_attn, qrot, krot, vlow, lse, mixed, in_one_t,
        hid_all, cos2, sin2, vector,
    )


def finish_kernel(
    layer_in, input_in, first_g, first_u, first_d, last_g, last_u, last_d, qkv_in, out_in, small_in,
    layer_out, grad_input, grad_q, grad_k, grad_v, grad_out, grad_g, grad_u, grad_d, vec_one, vec_two,
    bias_q, bias_k, bias_v,
    layer, grad, gates, ups, downs, qkv, out, in_sem, out_sem,
):
    early = first_g.shape[1]
    moves = [
        (layer_in, layer, layer_out), (input_in, grad, grad_input),
        (first_g, gates.at[:, 0:early], None), (last_g, gates.at[:, early:], None),
        (first_u, ups.at[:, 0:early], None), (last_u, ups.at[:, early:], None),
        (first_d, downs.at[:, 0:early], None), (last_d, downs.at[:, early:], None),
        (qkv_in, qkv, None), (out_in, out, grad_out),
    ]
    loads = [
        pltpu.make_async_copy(source, buffer, in_sem.at[i]) for i, (source, buffer, _) in enumerate(moves)
    ]
    for copy in loads:
        copy.start()
    stores = []

    def store(buffer, target):
        copy = pltpu.make_async_copy(buffer, target, out_sem.at[len(stores)])
        copy.start()
        stores.append(copy)

    for i, (_, buffer, target) in enumerate(moves):
        loads[i].wait()
        if target is not None:
            store(buffer, target)
        if i in (3, 5, 7):
            store(*((gates, grad_g), (ups, grad_u), (downs, grad_d))[i // 2 - 1])
    begin = 0
    for target in (grad_q, grad_k, grad_v):
        store(qkv.at[:, begin : begin + target.shape[1]], target)
        begin += target.shape[1]
    for i, target in enumerate((vec_one, vec_two, bias_q)):
        target[...] = small_in[i : i + 1, :].reshape(target.shape[0])
    wide = bias_k.shape[0]
    bias_k[...] = small_in[3:4, 0:wide].reshape(wide)
    bias_v[...] = small_in[3:4, wide : 2 * wide].reshape(wide)
    for copy in stores:
        copy.wait()


def finish(layer_out, grad_input, first, last, sum_qkv, sum_out, small, width_q):
    vmem = pl.BlockSpec(memory_space=pltpu.VMEM)
    hbm = pl.BlockSpec(memory_space=pl.ANY)
    shape = jax.ShapeDtypeStruct
    rows, width_qkv = sum_qkv.shape
    width_k = (width_qkv - width_q) // 2
    width = layer_out.shape[1]
    ffn = (rows, first[0].shape[1] + last[0].shape[1])
    dma = pltpu.SemaphoreType.DMA
    return pl.pallas_call(
        finish_kernel,
        in_specs=[hbm] * 10 + [vmem],
        out_specs=[hbm] * 9 + [vmem] * 5,
        out_shape=[
            shape(layer_out.shape, BF16), shape(grad_input.shape, BF16),
            shape((rows, width_q), F32), shape((rows, width_k), F32), shape((rows, width_k), F32),
            shape(sum_out.shape, F32), shape(ffn, F32), shape(ffn, F32), shape(ffn, F32),
            shape((width,), F32), shape((width,), F32), shape((2 * width_q,), F32),
            shape((2 * width_k,), F32), shape((2 * width_k,), F32),
        ],
        scratch_shapes=[
            pltpu.VMEM(layer_out.shape, BF16), pltpu.VMEM(grad_input.shape, BF16),
            pltpu.VMEM(ffn, F32), pltpu.VMEM(ffn, F32), pltpu.VMEM(ffn, F32),
            pltpu.VMEM(sum_qkv.shape, F32), pltpu.VMEM(sum_out.shape, F32), dma((10,)), dma((9,)),
        ],
        compiler_params=pltpu.CompilerParams(vmem_limit_bytes=62 * 2**20),
        name="finish",
    )(layer_out, grad_input, *first, *last, sum_qkv, sum_out, small)


def body_fused(
    hidden_in, positions, query_weight, query_bias, key_weight, key_bias, value_weight, value_bias,
    out_weight, gate_weight, up_weight, down_weight, attn_gain, ffn_gain, cotangent,
):
    rows, width_q = query_weight.shape
    heads = width_q // HD
    hidden_units = gate_weight.shape[1]
    own_tokens, width = hidden_in.shape
    half = HD // 2
    lanes = jnp.arange(HD, dtype=jnp.int32)
    freq = jnp.power(ROPE_BASE, -2.0 * (lanes % half).astype(F32) / HD)
    ffn_weights = (gate_weight, up_weight, down_weight.T)
    (w_ffn, w_attn, hidden_all, grad_ffn, in_one_t, qrot, krot, vlow, mixed, lse, middle,
     inputs_two, vector, cos2, sin2, in_two_t, cot_t) = forward_attention(
        hidden_in, cotangent,
        (freq, positions, query_bias, key_bias, value_bias, attn_gain, ffn_gain),
        (query_weight, key_weight, value_weight, out_weight.T, *ffn_weights),
        heads,
    )
    hiddens, grad_normed_two, later, *first_sums, w_other, w_late = feed_forward(
        inputs_two, grad_ffn, in_two_t, cot_t, w_ffn, w_attn, width_q + 2 * HD, ffn_weights
    )
    tail = units_of(-(-hidden_units // CHUNK) - 1, hidden_units)
    layer_out, grad_input, small, *sums = attention_back(
        later, grad_normed_two, middle, cotangent, hiddens, w_ffn, w_late, w_other,
        (w_attn, qrot, krot, vlow, lse, mixed, in_one_t, hidden_all), cos2, sin2, vector, tail,
    )
    (layer_out, grad_input, sum_q, sum_k, sum_v, sum_out, sum_gate, sum_up, sum_down, gain_one,
     gain_two, sum_bias_q, sum_bias_k, sum_bias_v) = finish(
        layer_out, grad_input, first_sums, sums[:3], *sums[3:5], small, width_q
    )
    return (
        layer_out,
        grad_input,
        sum_q,
        sum_bias_q,
        sum_k,
        sum_bias_k,
        sum_v,
        sum_bias_v,
        sum_out.T,
        sum_gate,
        sum_up,
        sum_down.T,
        gain_one,
        gain_two,
    )


def body(*arrays):
    rows = arrays[2].shape[0]
    if lax.axis_size("dp") == 2 * CHIPS and rows % 32 == 0 and -(-arrays[9].shape[1] // CHUNK) == 9:
        return body_fused(*arrays)
    return body_general(*arrays)


def solution(mesh):
    tokens, weight, weight_t = P(("dp", "mp"), None), P("dp", "mp"), P("mp", "dp")
    return jax.shard_map(
        body,
        mesh=mesh,
        in_specs=(
            tokens, P("dp"), weight, P(), weight, P(), weight, P(), weight_t,
            weight, weight, weight_t, P(), P(), tokens,
        ),
        out_specs=(
            tokens, tokens, weight, P(), weight, P(), weight, P(), weight_t,
            weight, weight, weight_t, P(), P(),
        ),
        check_vma=False,
    )
```

```python
import functools
import math

import jax
import jax.numpy as jnp
from jax import lax
from jax.experimental import pallas as pl
from jax.experimental.pallas import tpu as pltpu
from jax.sharding import PartitionSpec as P

HD = 128
SEQ_LEN = 1024
DOC_MAX = 512
EPS = 1e-06
ROPE_BASE = 1000000.0
BLOCK = 256
SCALE = 1.0 / math.sqrt(HD)
F32 = jnp.float32
BF16 = jnp.bfloat16


def contract(left, right, left_dim, right_dim):
    return lax.dot_general(
        left, right, (((left_dim,), (right_dim,)), ((), ())), preferred_element_type=F32
    )


def key_range(block_id):
    low = max(0, block_id * BLOCK - (DOC_MAX - 1)) // BLOCK * BLOCK
    return low, (block_id + 1) * BLOCK


def visible(start_row, low, high, block_id):
    keys = low + lax.broadcasted_iota(jnp.int32, (high - low, BLOCK), 0)
    queries = block_id * BLOCK + lax.broadcasted_iota(jnp.int32, (high - low, BLOCK), 1)
    return (keys >= start_row) & (keys <= queries)


def turn(values, cosines, sines):
    return values * cosines + pltpu.roll(values, HD // 2, 1) * sines


def attend_kernel(
    q_ref, k_ref, v_ref, bq_ref, bk_ref, bv_ref, cos_ref, sin_ref, start_ref,
    mixed_ref, qrot_ref, krot_ref, vlow_ref, lse_ref,
):
    head = pl.program_id(0)

    @pl.when(head == 0)
    def _():
        krot_ref[...] = turn(k_ref[...] + bk_ref[...], cos_ref[...], sin_ref[...]).astype(BF16)
        vlow_ref[...] = (v_ref[...] + bv_ref[...]).astype(BF16)

    qrot_ref[...] = turn(q_ref[...] + bq_ref[...], cos_ref[...], sin_ref[...]).astype(BF16)
    for i in range(SEQ_LEN // BLOCK):
        low, high = key_range(i)
        rows = pl.ds(i * BLOCK, BLOCK)
        start_row = start_ref[0:1, rows]
        scores = contract(krot_ref[low:high, :], qrot_ref[rows, :], 1, 1) * SCALE
        scores = jnp.where(visible(start_row, low, high, i), scores, -1e30)
        top = jnp.max(scores, axis=0, keepdims=True)
        weights = jnp.exp(scores - top)
        total = jnp.sum(weights, axis=0, keepdims=True)
        probs = (weights * (1.0 / total)).astype(BF16)
        mixed_ref[rows, :] = contract(probs, vlow_ref[low:high, :], 0, 0).astype(BF16)
        lse_ref[0, 0:1, rows] = top + jnp.log(total)


def attend(qkv, bias, cos2, sin2, start, heads):
    seq = SEQ_LEN
    full = lambda shape: pl.BlockSpec(shape, lambda h: (0,) * len(shape))
    col = lambda: pl.BlockSpec((seq, HD), lambda h: (0, h))
    at = lambda j: pl.BlockSpec((seq, HD), lambda h: (0, j))
    bat = lambda j: pl.BlockSpec((1, HD), lambda h: (0, j))
    return pl.pallas_call(
        attend_kernel,
        grid=(heads,),
        in_specs=[
            col(), at(heads), at(heads + 1),
            pl.BlockSpec((1, HD), lambda h: (0, h)), bat(heads), bat(heads + 1),
            full((seq, HD)), full((seq, HD)), full((1, seq)),
        ],
        out_specs=[
            col(), col(), full((seq, HD)), full((seq, HD)),
            pl.BlockSpec((1, 8, seq), lambda h: (h, 0, 0)),
        ],
        out_shape=[
            jax.ShapeDtypeStruct((seq, heads * HD), BF16),
            jax.ShapeDtypeStruct((seq, heads * HD), BF16),
            jax.ShapeDtypeStruct((seq, HD), BF16),
            jax.ShapeDtypeStruct((seq, HD), BF16),
            jax.ShapeDtypeStruct((heads, 8, seq), F32),
        ],
        compiler_params=pltpu.CompilerParams(vmem_limit_bytes=40 * 2**20),
        cost_estimate=pl.CostEstimate(
            flops=4 * heads * seq * seq * HD, bytes_accessed=10 * 2**20,
            transcendentals=heads * seq * seq // 2,
        ),
        name="attend",
    )(qkv, qkv, qkv, bias, bias, bias, cos2, sin2, start)


def attend_back_kernel(
    heads, qrot_ref, krot_ref, vlow_ref, lse_ref, grad_ref, cos_ref, sin_ref, start_ref,
    out_ref, gk_ref, gv_ref,
):
    head = pl.program_id(0)

    @pl.when(head == 0)
    def _():
        gk_ref[...] = jnp.zeros_like(gk_ref)
        gv_ref[...] = jnp.zeros_like(gv_ref)

    for i in range(SEQ_LEN // BLOCK):
        low, high = key_range(i)
        rows = pl.ds(i * BLOCK, BLOCK)
        start_row = start_ref[0:1, rows]
        query, grad = qrot_ref[rows, :], grad_ref[rows, :]
        keys = krot_ref[low:high, :]
        scores = contract(keys, query, 1, 1) * SCALE
        probs = jnp.where(
            visible(start_row, low, high, i), jnp.exp(scores - lse_ref[0, 0:1, rows]), 0.0
        )
        grad_probs = contract(vlow_ref[low:high, :], grad, 1, 1)
        row_term = jnp.sum(probs * grad_probs, axis=0, keepdims=True)
        grad_scores = (probs * (grad_probs - row_term)).astype(BF16)
        gk_ref[low:high, :] += contract(grad_scores, query, 1, 0)
        gv_ref[low:high, :] += contract(probs.astype(BF16), grad, 1, 0)
        grad_query = contract(grad_scores, keys, 0, 0) * SCALE
        out_ref[rows, pl.ds(pl.multiple_of(head * HD, HD), HD)] = turn(
            grad_query, cos_ref[rows, :], -sin_ref[rows, :]
        ).astype(BF16)

    @pl.when(head == heads - 1)
    def _():
        out_ref[:, heads * HD : (heads + 1) * HD] = turn(
            gk_ref[...] * SCALE, cos_ref[...], -sin_ref[...]
        ).astype(BF16)
        out_ref[:, (heads + 1) * HD :] = gv_ref[...].astype(BF16)


def attend_back(qrot, krot, vlow, lse, grad_mixed, cos2, sin2, start, heads):
    seq = SEQ_LEN
    full = lambda shape: pl.BlockSpec(shape, lambda h: (0,) * len(shape))
    col = lambda: pl.BlockSpec((seq, HD), lambda h: (0, h))
    return pl.pallas_call(
        functools.partial(attend_back_kernel, heads),
        grid=(heads,),
        in_specs=[
            col(), full((seq, HD)), full((seq, HD)),
            pl.BlockSpec((1, 8, seq), lambda h: (h, 0, 0)), col(),
            full((seq, HD)), full((seq, HD)), full((1, seq)),
        ],
        out_specs=full((seq, (heads + 2) * HD)),
        out_shape=jax.ShapeDtypeStruct((seq, (heads + 2) * HD), BF16),
        scratch_shapes=[pltpu.VMEM((seq, HD), F32), pltpu.VMEM((seq, HD), F32)],
        compiler_params=pltpu.CompilerParams(vmem_limit_bytes=40 * 2**20),
        cost_estimate=pl.CostEstimate(
            flops=10 * heads * seq * seq * HD, bytes_accessed=10 * 2**20,
            transcendentals=heads * seq * seq // 2,
        ),
        name="attend_back",
    )(qrot, krot, vlow, lse, grad_mixed, cos2, sin2, start)


class Ring:
    def __init__(self, members):
        self.members = members
        self.chips = members // 2
        self.half = self.chips // 2
        n = self.chips
        self.path = [2 * r if r < n // 2 else 2 * (n - 1 - r) + 1 for r in range(n)]
        self.offsets = [self.half]
        for k in range(self.half - 1, 0, -1):
            self.offsets += [k, n - k]
        self.offsets += [0]
        self.place = {k: i for i, k in enumerate(self.offsets)}

    def pairs(self, shift):
        n, path = self.chips, self.path
        return [
            (path[r] * 2 + c, path[(r + shift) % n] * 2 + c) for r in range(n) for c in range(2)
        ]

    def up(self, block):
        return lax.ppermute(block, "dp", self.pairs(1))

    def down(self, block):
        return lax.ppermute(block, "dp", self.pairs(-1))

    def across(self, block):
        return lax.ppermute(block, "dp", [(i, i ^ 1) for i in range(self.members)])

    def order(self):
        me = lax.axis_index("dp")
        path = jnp.array(self.path, jnp.int32)
        spot = jnp.zeros((self.chips,), jnp.int32).at[path].set(jnp.arange(self.chips, dtype=jnp.int32))
        mine = spot[me // 2]
        offsets = jnp.array(self.offsets, jnp.int32)
        chips = path[(mine + offsets) % self.chips]
        core = me % 2
        return jnp.concatenate([chips * 2 + core, chips * 2 + (1 - core)])

    def gather(self, block):
        n, h = self.chips, self.half
        rows = block.shape[0]
        got = {0: block}
        for k in range(1, h):
            got[n - k] = self.up(got[(n - k + 1) % n])
            got[k] = self.down(got[k - 1])
        first = self.up(got[h + 1][: rows // 2])
        second = self.down(got[h - 1][rows // 2 :])
        other = {k: self.across(got[k]) for k in got}
        got_half = [first, second]
        other_half = [self.across(first), self.across(second)]
        blocks = []
        for side, halves in ((got, got_half), (other, other_half)):
            for k in self.offsets:
                blocks.append(tuple(halves) if k == h else (side[k],))
        return blocks, first

    def reduce(self, own, rows):
        def term(k):
            begin = self.place[k] * rows
            return jnp.concatenate([o[begin : begin + rows] for o in own], axis=1)

        return self.reduce_terms(term, rows)

    def reduce_terms(self, term, rows):
        n, h = self.chips, self.half
        up = self.up(term(h)[: rows // 2])
        down = self.down(term(h)[rows // 2 :])
        for k in range(h - 1, 0, -1):
            mine_up, mine_down = term(k), term(n - k)
            if k == h - 1:
                sent_up = jnp.concatenate([
                    (up.astype(F32) + mine_up[: rows // 2].astype(F32)).astype(BF16),
                    mine_up[rows // 2 :],
                ])
                sent_down = jnp.concatenate([
                    mine_down[: rows // 2],
                    (down.astype(F32) + mine_down[rows // 2 :].astype(F32)).astype(BF16),
                ])
            else:
                sent_up = (up.astype(F32) + mine_up.astype(F32)).astype(BF16)
                sent_down = (down.astype(F32) + mine_down.astype(F32)).astype(BF16)
            up, down = self.up(sent_up), self.down(sent_down)
        return term(0).astype(F32) + up.astype(F32) + down.astype(F32)


def stack(blocks, begin, stop):
    return jnp.concatenate([part[:, begin:stop] for block in blocks for part in block], axis=0)


def swap(block):
    return lax.ppermute(block, "mp", [(0, 1), (1, 0)])


def rms(values):
    return lax.rsqrt(jnp.mean(values * values, axis=-1, keepdims=True) + EPS)


def after(value, *earlier):
    return lax.optimization_barrier((value, *earlier))[0]


def split_hidden(width, parts):
    tiles = width // HD
    cuts = [round(tiles * i / parts) * HD for i in range(parts + 1)]
    return list(zip(cuts[:-1], cuts[1:]))


def body_general(
    hidden_in, positions, query_weight, query_bias, key_weight, key_bias, value_weight, value_bias,
    out_weight, gate_weight, up_weight, down_weight, attn_gain, ffn_gain, cotangent,
):
    ring = Ring(lax.axis_size("dp"))
    rows = query_weight.shape[0]
    width = rows * ring.members
    side_rows = rows * ring.chips
    heads = query_weight.shape[1] // HD
    width_q = heads * HD
    width_qkv = width_q + 2 * HD
    own_tokens = hidden_in.shape[0]
    shard = lax.axis_index("mp")

    def whole(own, other):
        first = jnp.where(shard == 0, own, other)
        second = jnp.where(shard == 0, other, own)
        return jnp.concatenate([first, second], axis=0)

    def own_half(values):
        return lax.dynamic_slice_in_dim(values, shard * own_tokens, own_tokens, 0)

    def other_half(values):
        return lax.dynamic_slice_in_dim(values, (1 - shard) * own_tokens, own_tokens, 0)

    hidden_other = swap(hidden_in)
    attn_pack = jnp.concatenate([query_weight, key_weight, value_weight, out_weight.T], axis=1)
    attn_blocks, attn_last = ring.gather(attn_pack)
    cotangent_other = swap(after(cotangent, hidden_other))
    down_t = down_weight.T
    spans = split_hidden(gate_weight.shape[1], 2)
    ffn_blocks = []
    last = attn_last
    for begin, stop in spans:
        pack = jnp.concatenate(
            [gate_weight[:, begin:stop], up_weight[:, begin:stop], down_t[:, begin:stop]], axis=1
        )
        blocks, last = ring.gather(after(pack, last))
        ffn_blocks.append(blocks)

    order = ring.order()
    feature = (order[:, None] * rows + jnp.arange(rows, dtype=jnp.int32)[None, :]).reshape(width)
    shuffle = (jnp.arange(width, dtype=jnp.int32)[:, None] == feature[None, :]).astype(BF16)

    def to_order(values):
        return contract(values, shuffle, 1, 0).astype(BF16)

    def from_order(values):
        return contract(values, shuffle, 1, 1).astype(BF16)

    def vector_to_order(values):
        return jnp.sum(jnp.where(shuffle > 0, values[:, None], 0.0), axis=0)

    def vector_from_order(values):
        return jnp.sum(jnp.where(shuffle > 0, values[None, :], 0.0), axis=1)

    gain_attn, gain_ffn = vector_to_order(attn_gain), vector_to_order(ffn_gain)

    hidden_all = to_order(whole(hidden_in, hidden_other))
    resid_all = hidden_all.astype(F32)
    factor_one = rms(resid_all)
    inputs_one = (resid_all * factor_one * gain_attn).astype(BF16)
    half = HD // 2
    freq = jnp.power(ROPE_BASE, -2.0 * jnp.arange(half, dtype=F32) / HD)
    angles = positions.astype(F32)[:, None] * freq[None, :]
    cosines, sines = jnp.cos(angles), jnp.sin(angles)
    cos2 = jnp.concatenate([cosines, cosines], axis=1)
    sin2 = jnp.concatenate([-sines, sines], axis=1)
    start = (jnp.arange(SEQ_LEN, dtype=jnp.int32) - positions)[None, :]
    bias = jnp.concatenate([
        lax.dynamic_slice_in_dim(query_bias, shard * width_q, width_q, 0),
        lax.dynamic_slice_in_dim(key_bias, shard * HD, HD, 0),
        lax.dynamic_slice_in_dim(value_bias, shard * HD, HD, 0),
    ])[None, :]
    qkv_full = stack(attn_blocks, 0, width_qkv)
    out_full = stack(attn_blocks, width_qkv, width_qkv + width_q)
    qkv = contract(inputs_one, qkv_full, 1, 0)
    mixed, qrot, krot, vlow, lse = attend(qkv, bias, cos2, sin2, start, heads)
    out_other = swap(contract(other_half(mixed), out_full, 1, 1).astype(BF16))
    middle = (
        own_half(hidden_all).astype(F32)
        + contract(own_half(mixed), out_full, 1, 1)
        + out_other.astype(F32)
    )
    factor_two = rms(middle)
    in_two_own = (middle * factor_two * gain_ffn).astype(BF16)
    inputs_two = whole(in_two_own, swap(in_two_own))
    grad_ffn = to_order(whole(cotangent, cotangent_other))

    hiddens, grads_gate, grads_up, weights = [], [], [], []
    for (begin, stop), blocks in zip(spans, ffn_blocks):
        wide = stop - begin
        gate_full = stack(blocks, 0, wide)
        up_full = stack(blocks, wide, 2 * wide)
        down_full = stack(blocks, 2 * wide, 3 * wide)
        grad_hidden = contract(grad_ffn, down_full, 1, 0)
        gate = contract(inputs_two, gate_full, 1, 0)
        up = contract(inputs_two, up_full, 1, 0)
        sig = jax.nn.sigmoid(gate)
        swish = gate * sig
        hiddens.append((swish * up).astype(BF16))
        grads_gate.append((grad_hidden * up * sig * (1.0 + gate * (1.0 - sig))).astype(BF16))
        grads_up.append((grad_hidden * swish).astype(BF16))
        weights.append((gate_full, up_full, down_full))

    def side(values, index):
        return values[:, index * side_rows : (index + 1) * side_rows]

    def chip_sum(left, right):
        sent = contract(side(left, 1), right, 0, 0).astype(BF16)
        return (contract(side(left, 0), right, 0, 0) + ring.across(sent).astype(F32)).astype(BF16)

    sums = []
    for index in range(len(spans)):
        own = [
            chip_sum(inputs_two, grads_gate[index]),
            chip_sum(inputs_two, grads_up[index]),
            chip_sum(grad_ffn, hiddens[index]),
        ]
        sums.append(ring.reduce(own, rows))

    def back_two(take):
        total = None
        for (gate_full, up_full, _), g, u in zip(weights, grads_gate, grads_up):
            term = contract(take(g), gate_full, 1, 1) + contract(take(u), up_full, 1, 1)
            total = term if total is None else total + term
        return total

    def forward_out(take):
        total = None
        for (_, _, down_full), h in zip(weights, hiddens):
            term = contract(take(h), down_full, 1, 1)
            total = term if total is None else total + term
        return total

    back_other = swap(back_two(other_half).astype(BF16))
    grad_normed_two = back_two(own_half) + back_other.astype(F32)
    ffn_other = swap(forward_out(other_half).astype(BF16))
    layer_out = from_order(
        (middle + forward_out(own_half) + ffn_other.astype(F32)).astype(BF16)
    )

    unit_two = middle * factor_two
    scaled = grad_normed_two * gain_ffn
    gain_two = jnp.sum(grad_normed_two * unit_two, axis=0)
    inner = jnp.mean(scaled * unit_two, axis=-1, keepdims=True)
    grad_middle = own_half(grad_ffn).astype(F32) + factor_two * (scaled - unit_two * inner)

    grad_attn_own = grad_middle.astype(BF16)
    grad_attn = whole(grad_attn_own, swap(grad_attn_own))
    grad_mixed = contract(grad_attn, out_full, 1, 0).astype(BF16)
    grad_qkv = attend_back(qrot, krot, vlow, lse, grad_mixed, cos2, sin2, start, heads)
    sum_out = ring.reduce([chip_sum(grad_attn, mixed)], rows)
    sum_qkv = ring.reduce([chip_sum(inputs_one, grad_qkv)], rows)

    back_one_other = contract(other_half(grad_qkv), qkv_full, 1, 1)
    one_other = swap(back_one_other.astype(BF16))
    back_one_own = contract(own_half(grad_qkv), qkv_full, 1, 1)
    unit_all = resid_all * factor_one
    unit_one = own_half(unit_all)
    gain_one = jnp.sum(back_one_own * unit_one, axis=0) + jnp.sum(
        back_one_other * other_half(unit_all), axis=0
    )
    grad_normed_one = back_one_own + one_other.astype(F32)
    scaled_one = grad_normed_one * gain_attn
    inner_one = jnp.mean(scaled_one * unit_one, axis=-1, keepdims=True)
    through_one = own_half(factor_one) * (scaled_one - unit_one * inner_one)
    grad_input = from_order((grad_middle + through_one).astype(BF16))

    bias_part = jnp.sum(grad_qkv.astype(F32), axis=0)

    def place(part, total):
        return lax.dynamic_update_slice_in_dim(
            jnp.zeros((total,), F32), part, shard * part.shape[0], 0
        )

    small = jnp.concatenate([
        vector_from_order(gain_one),
        vector_from_order(gain_two),
        place(bias_part[:width_q], query_bias.shape[0]),
        place(bias_part[width_q : width_q + HD], key_bias.shape[0]),
        place(bias_part[width_q + HD :], value_bias.shape[0]),
    ])
    small = small + swap(small)
    bit = 1
    while bit < ring.members:
        small = small + lax.ppermute(small, "dp", [(i, i ^ bit) for i in range(ring.members)])
        bit *= 2
    cuts = [width, width, query_bias.shape[0], key_bias.shape[0], value_bias.shape[0]]
    pieces, begin = [], 0
    for cut in cuts:
        pieces.append(small[begin : begin + cut])
        begin += cut

    def gather_cols(index):
        parts = []
        for (begin, stop), total in zip(spans, sums):
            wide = stop - begin
            parts.append(total[:, index * wide : (index + 1) * wide])
        return jnp.concatenate(parts, axis=1)

    return (
        layer_out,
        grad_input,
        sum_qkv[:, :width_q],
        pieces[2],
        sum_qkv[:, width_q : width_q + HD],
        pieces[3],
        sum_qkv[:, width_q + HD :],
        pieces[4],
        sum_out.T,
        gather_cols(0),
        gather_cols(1),
        gather_cols(2).T,
        pieces[0],
        pieces[1],
    )


CHIPS = 8
HALF = CHIPS // 2
CHUNK = 512
TILE = 256
MESH = pl.DeviceIdType.MESH


class Spot:
    def __init__(self, rows):
        self.rows = rows
        self.me = lax.axis_index("dp")
        self.shard = lax.axis_index("mp")
        self.core = lax.rem(self.me, 2)
        chip = lax.div(self.me, 2)
        line, back = lax.div(chip, 2), lax.rem(chip, 2)
        self.spot = line * (1 - back) + (CHIPS - 1 - line) * back
        self.sibling = self.me + 1 - 2 * self.core
        self.next = (self.chip(1) * 2 + self.core, self.chip(CHIPS - 1) * 2 + self.core)

    def chip(self, offset):
        place = lax.rem(self.spot + offset, CHIPS)
        back = lax.div(place, HALF)
        return (1 - back) * (2 * place) + back * (2 * (CHIPS - 1 - place) + 1)

    def greet(self):
        barrier = pltpu.get_barrier_semaphore()
        for target in (
            {"dp": self.sibling}, {"dp": self.next[0]}, {"dp": self.next[1]}, {"mp": 1 - self.shard}
        ):
            pl.semaphore_signal(barrier, inc=1, device_id=target, device_id_type=MESH)
        pl.semaphore_wait(barrier, 4)

    def part(self, block, half=None):
        begin, size = block * self.rows, self.rows
        if half is not None:
            size = self.rows // 2
            begin = begin + half * size
        return pl.ds(pl.multiple_of(begin, 16), size)


def tile_of(index, size=TILE):
    return pl.ds(pl.multiple_of(index * size, size), size)


def small_inputs(ref, width_qkv, width):
    gains = width_qkv + width, width_qkv + 2 * width

    def start_of(block):
        begin = gains[1] + block * BLOCK
        return ref[0:1, begin : begin + BLOCK]

    return (
        ref[0:1, 0:width_qkv], ref[0:1, width_qkv : gains[0]], ref[0:1, gains[0] : gains[1]], start_of
    )


def visible_keys(start_row, low, high, block_id):
    shape = (high - low, BLOCK)
    keys = low + lax.broadcasted_iota(jnp.int32, shape, 0)
    queries = block_id * BLOCK + lax.broadcasted_iota(jnp.int32, shape, 1)
    return (keys.astype(F32) >= start_row) & (keys <= queries)


class Gather:
    def __init__(self, here, held, home, landed, hop_send, hop_recv, side_send, side_recv, store_sem):
        self.here, self.held, self.home, self.landed = here, held, home, landed
        self.hop_send, self.hop_recv = hop_send, hop_recv
        self.side_send, self.side_recv, self.store_sem = side_send, side_recv, store_sem

    def member(self, step, way, sibling=False):
        here = self.here
        chip = here.chip((CHIPS - step) % CHIPS if way == 0 else step)
        return chip * 2 + (1 - here.core if sibling else here.core)

    def hop(self, unit, step, way, arrival=False):
        half = way if step == HALF else None
        source = self.held(unit, step if arrival else step - 1, way, half)
        target = source if arrival or self.landed(unit) else self.held(unit, step, way, half)
        return pltpu.make_async_remote_copy(
            src_ref=source, dst_ref=target, send_sem=self.hop_send.at[unit, step - 1, way],
            recv_sem=self.hop_recv.at[unit, step - 1, way],
            device_id={"dp": self.here.next[way]}, device_id_type=MESH,
        )

    def index(self, step, way):
        return 0 if step == 0 else 2 * step - 1 + way

    def across(self, unit, step, way, arrival=False):
        half = way if step == HALF else None
        target = self.home(unit, self.member(step, way, sibling=arrival), half)
        source = target if arrival else self.held(unit, step, way, half)
        index = self.index(step, way)
        return pltpu.make_async_remote_copy(
            src_ref=source, dst_ref=target, send_sem=self.side_send.at[unit, index],
            recv_sem=self.side_recv.at[unit, index],
            device_id={"dp": self.here.sibling}, device_id_type=MESH,
        )

    def store(self, unit, step, way):
        half = way if step == HALF else None
        return pltpu.make_async_copy(
            self.held(unit, step, way, half), self.home(unit, self.member(step, way), half),
            self.store_sem.at[unit, self.index(step, way)],
        )

    def start(self, unit):
        for way in range(2):
            self.hop(unit, 1, way).start()
        self.across(unit, 0, 0).start()
        if not self.landed(unit):
            self.store(unit, 0, 0).start()

    def step(self, unit, step):
        for way in range(2):
            self.hop(unit, step - 1, way, arrival=True).wait_recv()
            if step <= HALF:
                self.hop(unit, step, way).start()
            self.across(unit, step - 1, way).start()
            if not self.landed(unit):
                self.store(unit, step - 1, way).start()

    def pieces(self):
        return [(0, 0)] + [(step, way) for step in range(1, HALF + 1) for way in range(2)]

    def end(self, unit):
        for step, way in self.pieces():
            self.across(unit, step, way, arrival=True).wait_recv()

    def sent(self, unit):
        for step, way in self.pieces():
            self.across(unit, step, way).wait_send()
            if step:
                self.hop(unit, step, way).wait_send()
            if not self.landed(unit):
                self.store(unit, step, way).wait()


def units_of(chunk, total):
    return min(CHUNK, total - chunk * CHUNK)


def pack_copies(weights, pack, chunks, sem):
    copies = []
    for i, chunk in enumerate(chunks):
        begin, size = chunk * CHUNK, units_of(chunk, weights[0].shape[1])
        for m, ref in enumerate(weights):
            copies.append(pltpu.make_async_copy(
                ref.at[:, begin : begin + size], pack.at[i, :, m * size : (m + 1) * size],
                sem.at[i, m],
            ))
    return copies


LATER = 3
PAIRS = 2
QUARTERS = 4


def forward_kernel(
    cfg, hid, cot, turns, places, bias_q, bias_k, bias_v, gain_a, gain_f,
    wq, wk, wv, wo, wg, wu, wd,
    w_ffn, w_attn, hid_all, cot_all, in_one_t, qrot, krot, vlow, mixed, lse, middle, in_two, vec_ref,
    cos_ref, sin_ref, in_two_t, cot_t,
    wa, qkv, psend, precv, pack, slots, in_one, cots, turned, turned_cot,
    local_sem, pack_sem, store_sem, hop_send, hop_recv, side_send, side_recv, x_send, x_recv, t_sem,
):
    rows, heads, units = cfg
    own_tokens, width = hid.shape
    tokens = 2 * own_tokens
    width_q = heads * HD
    width_qkv = width_q + 2 * HD
    here = Spot(rows)
    shard = here.shard

    own_rows = pl.ds(pl.multiple_of(shard * own_tokens, TILE), own_tokens)
    other_rows = pl.ds(pl.multiple_of((1 - shard) * own_tokens, TILE), own_tokens)
    quarter = own_tokens // QUARTERS

    def quarter_rows(index, side):
        return pl.ds(pl.multiple_of(side * own_tokens + index * quarter, quarter), quarter)

    mine = here.part(here.me)
    attn_copies, column = [], 0
    for i, ref in enumerate((wq, wk, wv, wo)):
        wide = ref.shape[1]
        attn_copies.append(
            pltpu.make_async_copy(ref, wa.at[mine, column : column + wide], local_sem.at[i])
        )
        column += wide
    ffn_copies = pack_copies((wg, wu, wd), pack, range(PAIRS * units), pack_sem)
    own_copies = [
        pltpu.make_async_copy(hid, hid_all.at[own_rows, :], local_sem.at[4]),
        pltpu.make_async_copy(cot, cots.at[own_rows, :], local_sem.at[5]),
    ]
    for copy in attn_copies + own_copies + ffn_copies:
        copy.start()

    column = 0
    for ref in (bias_q, bias_k, bias_v):
        size = ref.shape[0] // 2
        row = ref[...].reshape(1, 2 * size)
        vec_ref[:, column : column + size] = jnp.where(shard == 0, row[:, :size], row[:, size:])
        column += size
    for ref in (gain_a, gain_f):
        vec_ref[:, column : column + width] = ref[...].reshape(1, width)
        column += width
    vec_ref[:, column : column + tokens] = (
        lax.broadcasted_iota(jnp.int32, (1, tokens), 1) - places[...].reshape(1, tokens)
    ).astype(F32)
    bias, gain_one, gain_two, start_of = small_inputs(vec_ref, width_qkv, width)

    here.greet()

    def swap_copy(index, src, dst):
        return pltpu.make_async_remote_copy(
            src_ref=src, dst_ref=dst, send_sem=x_send.at[index], recv_sem=x_recv.at[index],
            device_id={"mp": 1 - shard}, device_id_type=MESH,
        )

    hid_swap = (swap_copy(0, hid, hid_all.at[own_rows, :]), swap_copy(0, hid, hid_all.at[other_rows, :]))
    mix_swap = swap_copy(1, psend, precv)
    two_swap = (
        swap_copy(2, in_two.at[own_rows, :], in_two.at[own_rows, :]),
        swap_copy(2, in_two.at[other_rows, :], in_two.at[other_rows, :]),
    )

    def cot_swap(index, arrival=False):
        ref = cots.at[quarter_rows(index, 1 - shard if arrival else shard), :]
        return swap_copy(3 + index, ref, ref)

    def home(unit, member, half):
        part = here.part(member, half)
        if unit == 0:
            return wa.at[part, :]
        return w_ffn.at[(unit - 1) * PAIRS : unit * PAIRS, part, :]

    def held(unit, step, way, half):
        if unit == 0:
            return home(0, gather.member(step, way), half)
        part = slice(0, rows) if half is None else slice(half * rows // 2, (half + 1) * rows // 2)
        if step == 0:
            return pack.at[(unit - 1) * PAIRS : unit * PAIRS, part, :]
        slot = 2 * HALF - 2 if step == HALF else 2 * (step - 1) + way
        return slots.at[unit - 1, slot, :, part, :]

    gather = Gather(
        here, held, home, lambda unit: unit == 0, hop_send, hop_recv, side_send, side_recv, store_sem
    )
    ffn_units = range(1, units + 1)

    hid_swap[0].start()
    for copy in attn_copies:
        copy.wait()
    gather.start(0)
    at = jnp.broadcast_to(places[...].reshape(1, tokens).astype(F32), (HD, tokens)).T
    angles = at * turns[...].reshape(1, HD)
    cos_ref[...] = jnp.cos(angles)
    lanes = lax.broadcasted_iota(jnp.int32, (tokens, HD), 1)
    sin_ref[...] = jnp.where(lanes < HD // 2, -1.0, 1.0) * jnp.sin(angles)

    for step in range(2, HALF + 1):
        gather.step(0, step)
    for copy in ffn_copies:
        copy.wait()
    for unit in ffn_units:
        gather.start(unit)
    gather.step(0, HALF + 1)

    for copy in own_copies:
        copy.wait()
    hid_swap[1].wait_recv()
    for index in range(QUARTERS - 1):
        cot_swap(index).start()

    @pl.loop(0, tokens // TILE)
    def _(t):
        v = hid_all[tile_of(t), :].astype(F32)
        factor = lax.rsqrt(jnp.mean(v * v, axis=-1, keepdims=True) + EPS)
        in_one[tile_of(t), :] = (v * factor * gain_one).astype(BF16)

    gather.end(0)
    wa_out = pltpu.make_async_copy(wa, w_attn, local_sem.at[6])
    wa_out.start()

    @pl.loop(0, tokens // TILE)
    def _(t):
        part = tile_of(t)
        qkv[part, :] = contract(in_one[part, :], wa[:, 0:width_qkv], 1, 0) + bias
        cosines, sines = cos_ref[part, :], sin_ref[part, :]
        for h in range(heads):
            columns = slice(h * HD, (h + 1) * HD)
            qrot[part, columns] = turn(qkv[part, columns], cosines, sines).astype(BF16)
        krot[part, :] = turn(qkv[part, width_q : width_q + HD], cosines, sines).astype(BF16)
        vlow[part, :] = qkv[part, width_q + HD :].astype(BF16)

    def attend(blocks):
        @pl.loop(0, heads)
        def _(h):
            columns = tile_of(h, HD)
            for i in blocks:
                low, high = key_range(i)
                part = pl.ds(i * BLOCK, BLOCK)
                scores = contract(krot[low:high, :], qrot[part, columns], 1, 1) * SCALE
                scores = jnp.where(visible_keys(start_of(i), low, high, i), scores, -1e30)
                top = jnp.max(scores, axis=0, keepdims=True)
                weights = jnp.exp(scores - top)
                total = jnp.sum(weights, axis=0, keepdims=True)
                probs = (weights * (1.0 / total)).astype(BF16)
                mixed[part, columns] = contract(probs, vlow[low:high, :], 0, 0).astype(BF16)
                lse[h, 0:1, part] = top + jnp.log(total)

    halves = (range(own_tokens // BLOCK), range(own_tokens // BLOCK, tokens // BLOCK))
    for index in range(2):
        @pl.when(shard == index)
        def _():
            attend(halves[1 - index])

    @pl.loop(0, width // TILE)
    def _(n):
        weight = wa[tile_of(n), width_qkv:]
        psend[:, tile_of(n)] = contract(mixed[other_rows, :], weight, 1, 1).astype(BF16)

    mix_swap.start()
    for index in range(2):
        @pl.when(shard == index)
        def _():
            attend(halves[index])

    @pl.loop(0, width // TILE)
    def _(n):
        weight = wa[tile_of(n), width_qkv:]
        middle[:, tile_of(n)] = (
            contract(mixed[own_rows, :], weight, 1, 1) + hid[:, tile_of(n)].astype(F32)
        )

    for unit in ffn_units:
        gather.step(unit, 2)

    def transpose(source, target, first, begin, count):
        @pl.loop(0, width // TILE)
        def _(n):
            for t in range(count):
                part = pl.ds(pl.multiple_of(begin + t * TILE, TILE), TILE)
                target[tile_of(n), part] = source[part, tile_of(n)].T

    transpose(in_one, turned, 0, 0, tokens // TILE)
    one_turned = pltpu.make_async_copy(turned, in_one_t, t_sem.at[0])
    one_turned.start()
    mine_begin, theirs_begin = shard * own_tokens, (1 - shard) * own_tokens
    transpose(cots, turned_cot, 0, mine_begin, own_tokens // TILE)
    for index in range(QUARTERS // 2):
        cot_swap(index, arrival=True).wait_recv()
    transpose(cots, turned_cot, 0, theirs_begin, own_tokens // TILE // 2)

    mix_swap.wait_recv()

    @pl.loop(0, own_tokens // TILE)
    def _(t):
        part = tile_of(t)
        v = middle[part, :] + precv[part, :].astype(F32)
        middle[part, :] = v
        factor = lax.rsqrt(jnp.mean(v * v, axis=-1, keepdims=True) + EPS)
        to = pl.ds(pl.multiple_of(shard * own_tokens + t * TILE, TILE), TILE)
        in_two[to, :] = (v * factor * gain_two).astype(BF16)

    two_swap[0].start()
    cot_swap(QUARTERS - 1).start()
    one_turned.wait()
    for unit in ffn_units:
        gather.step(unit, 3)
    transpose(in_two, turned, 0, mine_begin, own_tokens // TILE)
    for unit in list(ffn_units)[:1]:
        gather.step(unit, 4)
    two_swap[1].wait_recv()
    transpose(in_two, turned, 0, theirs_begin, own_tokens // TILE)
    two_turned = pltpu.make_async_copy(turned, in_two_t, t_sem.at[1])
    two_turned.start()
    for unit in list(ffn_units)[1:]:
        gather.step(unit, 4)
    for index in range(QUARTERS // 2, QUARTERS):
        cot_swap(index, arrival=True).wait_recv()
    transpose(cots, turned_cot, 0, theirs_begin + own_tokens // 2, own_tokens // TILE // 2)
    cot_copies = [
        pltpu.make_async_copy(cots, cot_all, t_sem.at[2]),
        pltpu.make_async_copy(turned_cot, cot_t, t_sem.at[3]),
    ]
    for copy in cot_copies:
        copy.start()
    for unit in ffn_units:
        gather.step(unit, 5)
    for unit in ffn_units:
        gather.end(unit)
    for unit in range(units + 1):
        gather.sent(unit)
    hid_swap[0].wait_send()
    mix_swap.wait_send()
    two_swap[0].wait_send()
    for index in range(QUARTERS):
        cot_swap(index).wait_send()
    for copy in [wa_out, two_turned] + cot_copies:
        copy.wait()


def forward_attention(hidden_in, cotangent, vectors, weights, heads):
    own_tokens, width = hidden_in.shape
    tokens = 2 * own_tokens
    rows = weights[0].shape[0]
    chunks = -(-weights[4].shape[1] // CHUNK)
    units = (chunks - LATER) // PAIRS
    early = units * PAIRS
    width_q = heads * HD
    width_attn = 2 * width_q + 2 * HD
    wide = 3 * CHUNK
    vmem = pl.BlockSpec(memory_space=pltpu.VMEM)
    hbm = pl.BlockSpec(memory_space=pl.ANY)
    dma = pltpu.SemaphoreType.DMA
    shape = jax.ShapeDtypeStruct
    pieces = 2 * HALF + 1
    return pl.pallas_call(
        functools.partial(forward_kernel, (rows, heads, units)),
        in_specs=[vmem, hbm] + [vmem] * 7 + [hbm] * 7,
        out_specs=[hbm, hbm, vmem, hbm, hbm] + [vmem] * 10 + [hbm, hbm],
        out_shape=[
            shape((early, width, wide), BF16),
            shape((width, width_attn), BF16),
            shape((tokens, width), BF16),
            shape((tokens, width), BF16),
            shape((width, tokens), BF16),
            shape((tokens, width_q), BF16),
            shape((tokens, HD), BF16),
            shape((tokens, HD), BF16),
            shape((tokens, width_q), BF16),
            shape((heads, 8, tokens), F32),
            shape((own_tokens, width), F32),
            shape((tokens, width), BF16),
            shape((1, width_q + 2 * HD + 2 * width + tokens), F32),
            shape((tokens, HD), F32),
            shape((tokens, HD), F32),
            shape((width, tokens), BF16),
            shape((width, tokens), BF16),
        ],
        scratch_shapes=[
            pltpu.VMEM((width, width_attn), BF16),
            pltpu.VMEM((tokens, width_q + 2 * HD), F32),
            pltpu.VMEM((own_tokens, width), BF16),
            pltpu.VMEM((own_tokens, width), BF16),
            pltpu.VMEM((early, rows, wide), BF16),
            pltpu.VMEM((units, 2 * HALF - 1, PAIRS, rows, wide), BF16),
            pltpu.VMEM((tokens, width), BF16),
            pltpu.VMEM((tokens, width), BF16),
            pltpu.VMEM((width, tokens), BF16),
            pltpu.VMEM((width, tokens), BF16),
            dma((7,)), dma((early, 3)), dma((units + 1, pieces)),
            dma((units + 1, HALF, 2)), dma((units + 1, HALF, 2)),
            dma((units + 1, pieces)), dma((units + 1, pieces)),
            dma((3 + QUARTERS,)), dma((3 + QUARTERS,)), dma((4,)),
        ],
        compiler_params=pltpu.CompilerParams(
            collective_id=1, has_side_effects=True, vmem_limit_bytes=63 * 2**20
        ),
        cost_estimate=pl.CostEstimate(
            flops=6 * tokens * width * width_attn, bytes_accessed=120 * 2**20, transcendentals=0
        ),
        name="forward_attention",
    )(hidden_in, cotangent, *vectors, *weights)


class Sums:
    def __init__(self, here, own, places, send_sem, recv_sem):
        self.here, self.own, self.places = here, own, places
        self.send_sem, self.recv_sem = send_sem, recv_sem

    def chip(self, step, way):
        distance = HALF - step
        return self.here.chip(distance if way == 0 else CHIPS - distance)

    def copy(self, o, p, step, way, m, columns):
        here, rows = self.here, self.here.rows
        return pltpu.make_async_remote_copy(
            src_ref=self.own.at[o, here.part(self.chip(step, way), way if step == 0 else None), columns],
            dst_ref=self.places.at[p, step, way, 0 : rows // 2 if step == 0 else rows, columns],
            send_sem=self.send_sem.at[p, step, way, m],
            recv_sem=self.recv_sem.at[p, step, way, m],
            device_id={"dp": here.next[way]},
            device_id_type=MESH,
        )

    def columns(self, pieces, m):
        count, size = pieces
        return pl.ds(pl.multiple_of(m * size, HD), size)

    def start(self, o, p, pieces):
        @pl.loop(0, pieces[0])
        def _(m):
            for way in range(2):
                self.copy(o, p, 0, way, m, self.columns(pieces, m)).start()

    def step(self, o, p, step, pieces):
        here, own = self.here, self.own

        @pl.loop(0, pieces[0])
        def _(m):
            columns = self.columns(pieces, m)
            for way in range(2):
                self.copy(o, p, step - 1, way, m, columns).wait()
            for way in range(2):
                part = here.part(self.chip(step, way), way if step == 1 else None)
                size = here.rows // 2 if step == 1 else here.rows
                own[o, part, columns] = (
                    own[o, part, columns].astype(F32)
                    + self.places[p, step - 1, way, 0:size, columns].astype(F32)
                ).astype(BF16)
                self.copy(o, p, step, way, m, columns).start()

    def end(self, o, p, pieces, target):
        own, last = self.own, HALF - 1
        part = self.here.part(self.here.chip(0))

        @pl.loop(0, pieces[0])
        def _(m):
            columns = self.columns(pieces, m)
            for way in range(2):
                self.copy(o, p, last, way, m, columns).wait()
            target[:, columns] = (
                own[o, part, columns].astype(F32)
                + self.places[p, last, 0, :, columns].astype(F32)
                + self.places[p, last, 1, :, columns].astype(F32)
            )


EVENTS = {
    (0, "a"): "G11 G21",
    (0, "c"): "G02",
    (0, "f"): "G12",
    (1, "a"): "R00",
    (1, "b"): "G22",
    (1, "e"): "G03",
    (2, "a"): "R10",
    (2, "b"): "G13",
    (2, "c"): "R01 G23",
    (3, "a"): "G04 R11",
    (3, "c"): "G14",
    (4, "a"): "R02",
    (4, "b"): "G24",
    (4, "c"): "G05",
    (4, "e"): "R12",
    (4, "f"): "G15",
    (5, "a"): "R03 R20",
    (5, "c"): "G25 R13",
    (6, "0a"): "R04 R21",
    (6, "1a"): "R14 R22",
    (6, "1b"): "R30",
    (6, "2b"): "R23",
    (7, "0a"): "R31",
    (7, "1a"): "R24 R32 R40",
    (7, "2a"): "R33",
    (7, "2b"): "R41",
    (8, "1a"): "R34 R42",
    (8, "1b"): "R43",
    (8, "2b"): "R44",
}
SETS = 3


def ffn_kernel(
    cfg, in2_hbm, cot_hbm, in2t_hbm, cott_hbm, w_ffn, w_attn, wg, wu, wd,
    hiddens, w_down, gin_own, later, grad_g, grad_u, grad_d, w_other, w_late,
    in2, cot, in2t, cott, wbuf, acts, gin, own, sent, sib, ring, stage, pack,
    in_sem, w_sem, sib_send, sib_recv, ring_send, ring_recv, out_sem, g_sem, end_sem, free_sem,
    pack_sem, store_sem, hop_send, hop_recv, side_send, side_recv, park_sem, fetch_sem, hid_sem, down_sem,
):
    rows, chunks, total = cfg
    grads = (grad_g, grad_u, grad_d)
    tokens, width = in2.shape
    side_rows = CHIPS * rows
    own_tokens = tokens // 2
    first = chunks - LATER
    rings = first - 1
    here = Spot(rows)
    shard = here.shard
    sums = Sums(here, own, ring, ring_send, ring_recv)
    ring_pieces = (3, CHUNK)
    own_rows = pl.ds(pl.multiple_of(shard * own_tokens, TILE), own_tokens)
    other_rows = pl.ds(pl.multiple_of((1 - shard) * own_tokens, TILE), own_tokens)

    def size_of(i):
        return units_of(first + i, total)

    def load(chunk, s):
        return pltpu.make_async_copy(w_ffn.at[chunk], wbuf.at[s], w_sem.at[s])

    def load_late(i, s):
        columns = slice(0, 3 * size_of(i))
        return pltpu.make_async_copy(w_late.at[i, :, columns], wbuf.at[s, :, columns], w_sem.at[s])

    def down_copies(chunk, s, size=CHUNK):
        top = width // 2
        return [
            pltpu.make_async_copy(
                wbuf.at[s, h * top : (h + 1) * top, 2 * size : 3 * size],
                w_down.at[chunk, :, h * CHUNK : h * CHUNK + size], down_sem.at[s, h],
            )
            for h in range(2)
        ]

    def hidden_copies(index, chunk, size=CHUNK):
        return [
            pltpu.make_async_copy(
                acts.at[index, h * own_tokens : (h + 1) * own_tokens, 2 * size : 3 * size],
                hiddens.at[chunk, :, h * CHUNK : h * CHUNK + size], hid_sem.at[index, h],
            )
            for h in range(2)
        ]

    def home(unit, member, half):
        return w_late.at[unit, here.part(member, half), 0 : 3 * size_of(unit)]

    def held(unit, step, way, half):
        size = rows if half is None else rows // 2
        columns = slice(0, 3 * size_of(unit))
        if step == 0:
            return pack.at[unit, :, columns]
        slot = 2 * (step - 1) + way
        whole = 2 * HALF - 2
        if unit < 2:
            buffer, begin = 1 + unit, (whole if step == HALF else slot) * rows
            offset = 0
            if half is not None:
                offset = half * size
        else:
            base = (whole + 1) * rows
            if step == HALF:
                buffer, begin, offset = 1 + way, base + whole // 2 * rows, 0
            else:
                buffer, begin = 1 + slot // (whole // 2), base + slot % (whole // 2) * rows
                offset = 0 if half is None else half * size
        return acts.at[buffer, begin + offset : begin + offset + size, columns]

    gather = Gather(
        here, held, home, lambda unit: False, hop_send, hop_recv, side_send, side_recv, store_sem
    )
    own_blocks = pack_copies((wg, wu, wd), pack, range(first, chunks), pack_sem)

    inputs = [
        pltpu.make_async_copy(in2_hbm, in2, in_sem.at[0]),
        pltpu.make_async_copy(cot_hbm, cot, in_sem.at[1]),
    ]
    turned = []
    for i, (source, target) in enumerate(((in2t_hbm, in2t), (cott_hbm, cott))):
        for side in range(2):
            for chip in range(CHIPS):
                member = 2 * chip + (here.core if side == 0 else 1 - here.core)
                begin = side * side_rows + chip * rows
                turned.append(pltpu.make_async_copy(
                    source.at[here.part(member), :], target.at[begin : begin + rows, :],
                    in_sem.at[2 + i],
                ))
    for copy in own_blocks + [load(0, 0)] + inputs:
        copy.start()
    here.greet()
    for copy in own_blocks:
        copy.wait()
    gather.start(0)

    def result_copies(chunk):
        return [
            pltpu.make_async_copy(
                stage.at[:, m * CHUNK : (m + 1) * CHUNK],
                grads[m].at[:, tile_of(chunk, CHUNK)],
                out_sem.at[m],
            )
            for m in range(3)
        ]

    def fetch(chunk):
        return pltpu.make_async_copy(
            later.at[chunk - SETS], own.at[chunk % SETS], fetch_sem.at[chunk % SETS]
        )

    def park(chunk, p, early, size=CHUNK):
        columns = slice(0, 3 * size)
        target = own.at[chunk] if early else later.at[chunk - SETS, :, columns]
        return pltpu.make_async_copy(sib.at[p, :, columns], target, park_sem.at[p])

    def ring_event(chunk, step):
        o, p = chunk % SETS, chunk % 2
        if step == 0:
            if chunk >= SETS:
                fetch(chunk).wait()
            sums.start(o, p, ring_pieces)
        elif step < HALF:
            sums.step(o, p, step, ring_pieces)
        else:
            if chunk:
                for copy in result_copies(chunk - 1):
                    copy.wait()
            sums.end(o, p, ring_pieces, stage)
            for copy in result_copies(chunk):
                copy.start()
            if chunk + SETS < rings:
                fetch(chunk + SETS).start()

    def run(events):
        for event in events.split():
            index, step = int(event[1]), int(event[2])
            if event[0] == "R":
                ring_event(index, step)
            elif step == 1:
                gather.start(index)
            else:
                gather.step(index, step)

    def sib_copy(p, m, size):
        columns = slice(m * size, (m + 1) * size)
        return pltpu.make_async_remote_copy(
            src_ref=sent.at[:, columns],
            dst_ref=sib.at[p, :, columns],
            send_sem=sib_send.at[m],
            recv_sem=sib_recv.at[p, m],
            device_id={"dp": here.sibling},
            device_id_type=MESH,
        )

    def weight_copy():
        return pltpu.make_async_remote_copy(
            src_ref=w_attn.at[:, 0 : w_other.shape[1]], dst_ref=w_other,
            send_sem=g_sem.at[2], recv_sem=g_sem.at[3],
            device_id={"mp": 1 - shard}, device_id_type=MESH,
        )

    def gin_copy():
        return pltpu.make_async_remote_copy(
            src_ref=in2.at[other_rows, :], dst_ref=cot.at[own_rows, :],
            send_sem=g_sem.at[0], recv_sem=g_sem.at[1],
            device_id={"mp": 1 - shard}, device_id_type=MESH,
        )

    def forward(index, part, s, size=CHUNK):
        for begin in range(0, size, TILE):
            stop = min(begin + TILE, size)
            gates, ups, downs = (slice(m * size + begin, m * size + stop) for m in range(3))
            gate = contract(in2[part, :], wbuf[s, :, gates], 1, 0)
            up = contract(in2[part, :], wbuf[s, :, ups], 1, 0)
            grad = contract(cot[part, :], wbuf[s, :, downs], 1, 0)
            sig = 0.5 * jnp.tanh(0.5 * gate) + 0.5
            swish = gate * sig
            acts[index, part, downs] = (swish * up).astype(BF16)
            acts[index, part, gates] = (grad * up * (sig + swish - swish * sig)).astype(BF16)
            acts[index, part, ups] = (grad * swish).astype(BF16)

    def back_gin(index, part, s, size=CHUNK):
        @pl.loop(0, width // TILE)
        def _(n):
            gin[part, tile_of(n)] += contract(
                acts[index, part, 0 : 2 * size], wbuf[s, tile_of(n), 0 : 2 * size], 1, 1
            )

    def weight_grads(index, p, between, size=CHUNK):
        for m, left in enumerate((in2t, in2t, cott)):
            columns = slice(m * size, (m + 1) * size)
            sent[:, columns] = contract(
                left[side_rows:, :], acts[index, :, columns], 1, 0
            ).astype(BF16)
            sib_copy(p, m, size).start()
        between()
        for m, left in enumerate((in2t, in2t, cott)):
            columns = slice(m * size, (m + 1) * size)
            sib_copy(p, m, size).wait()
            sib[p, :, columns] = (
                contract(left[0:side_rows, :], acts[index, :, columns], 1, 0)
                + sib[p, :, columns].astype(F32)
            ).astype(BF16)

    gin[...] = jnp.zeros_like(gin)
    for copy in inputs:
        copy.wait()
    for copy in turned:
        copy.start()

    def at_point(j, point):
        for chunk in range(first):
            if (chunk, point) in EVENTS:
                @pl.when(j == chunk)
                def _():
                    run(EVENTS[chunk, point])

    weight_copy().start()

    def start(copies):
        for copy in copies:
            copy.start()

    def wait(copies):
        for copy in copies:
            copy.wait()

    @pl.loop(0, first)
    def _(j):
        p = lax.rem(j, 2)
        load(j, p).wait()
        start(down_copies(j, p))

        @pl.when(j >= 1)
        def _():
            wait(down_copies(j - 1, 1 - p))
            wait(hidden_copies(0, j - 1))

        @pl.when(j + 1 < first)
        def _():
            load(j + 1, 1 - p).start()

        @pl.when(j == first - 1)
        def _():
            gather.end(0)
            gather.sent(0)
            load_late(0, 1 - p).start()

        forward(0, slice(0, own_tokens), p)

        @pl.when((j >= 1) & (j <= SETS))
        def _():
            park(j - 1, 1 - p, True).wait()

        @pl.when(j > SETS)
        def _():
            park(j - 1, 1 - p, False).wait()

        at_point(j, "a")
        forward(0, slice(own_tokens, tokens), p)
        start(hidden_copies(0, j))
        at_point(j, "b")
        back_gin(0, slice(0, tokens), p)
        at_point(j, "c")

        @pl.when(j == 0)
        def _():
            for i, ref in enumerate((in2t, cott)):
                pltpu.make_async_copy(ref, ref, in_sem.at[2 + i]).wait()

        weight_grads(0, p, lambda: at_point(j, "e"))

        @pl.when(j < SETS)
        def _():
            park(j, p, True).start()

        @pl.when(j >= SETS)
        def _():
            park(j, p, False).start()

        at_point(j, "f")

    wait(hidden_copies(0, first - 1))
    wait(down_copies(first - 1, (first - 1) % 2))
    for unit in range(1, LATER):
        gather.end(unit)
        gather.sent(unit)

    for half in range(2):
        part = (other_rows, own_rows)[half]
        for i in range(LATER):
            size = size_of(i)
            turn = half * LATER + i
            s = (first + turn) % 2
            load_late(i, s).wait()
            if half == 0:
                start(down_copies(first + i, s, size))
            if 0 < turn <= LATER:
                wait(down_copies(first + turn - 1, 1 - s, size_of(turn - 1)))
            if turn + 1 < 2 * LATER:
                load_late((i + 1) % LATER, 1 - s).start()
            forward(i, part, s, size)
            if half == 1:
                start(hidden_copies(i, first + i, size))
            run(EVENTS.get((first + half, f"{i}a"), ""))
            back_gin(i, part, s, size)
            run(EVENTS.get((first + half, f"{i}b"), ""))
        if half == 0:
            pl.semaphore_signal(
                free_sem, inc=1, device_id={"mp": 1 - shard}, device_id_type=MESH
            )

            @pl.loop(0, own_tokens // TILE)
            def _(t):
                of = pl.ds(pl.multiple_of((1 - shard) * own_tokens + t * TILE, TILE), TILE)
                in2[of, :] = gin[of, :].astype(BF16)

            pl.semaphore_wait(free_sem, 1)
            gin_copy().start()

    for i in range(LATER):
        chunk, size = first + i, size_of(i)
        p = chunk % 2
        park(chunk - 1, 1 - p, False).wait()
        weight_grads(i, p, lambda: run(EVENTS.get((first + 2, f"{i}a"), "")), size)
        park(chunk, p, False, size).start()
        run(EVENTS.get((first + 2, f"{i}b"), ""))
    gin_copy().wait()

    @pl.loop(0, own_tokens // TILE)
    def _(t):
        of = pl.ds(pl.multiple_of(shard * own_tokens + t * TILE, TILE), TILE)
        at = pl.ds(pl.multiple_of((1 - shard) * own_tokens + t * TILE, TILE), TILE)
        gin[of, :] = gin[of, :] + cot[at, :].astype(F32)

    gin_out = pltpu.make_async_copy(gin.at[own_rows, :], gin_own, end_sem.at[0])
    gin_out.start()
    weight_copy().wait()
    last_park = park(chunks - 1, (chunks - 1) % 2, False, size_of(LATER - 1))
    for copy in [gin_out, last_park] + result_copies(rings - 1):
        copy.wait()
    for i in range(LATER):
        wait(hidden_copies(i, first + i, size_of(i)))


def feed_forward(inputs_two, grad_ffn, in_two_t, cot_t, w_ffn, w_attn, width_qkv, weights):
    tokens, width = inputs_two.shape
    rows = weights[0].shape[0]
    chunks = w_ffn.shape[0] + LATER
    pieces = 2 * HALF + 1
    hbm = pl.BlockSpec(memory_space=pl.ANY)
    side_rows, wide = CHIPS * rows, 3 * CHUNK
    dma = pltpu.SemaphoreType.DMA
    shape = jax.ShapeDtypeStruct
    half = (tokens // 2, width)
    return pl.pallas_call(
        functools.partial(ffn_kernel, (rows, chunks, weights[0].shape[1])),
        in_specs=[hbm] * 9,
        out_specs=[hbm] * 9,
        out_shape=[
            shape((chunks, tokens // 2, 2 * CHUNK), BF16),
            shape((chunks, width // 2, 2 * CHUNK), BF16), shape(half, F32),
            shape((chunks - SETS, side_rows, wide), BF16),
        ] + [shape((rows, (chunks - LATER - 1) * CHUNK), F32)] * 3 + [
            shape((width, width_qkv), BF16),
            shape((LATER, width, wide), BF16),
        ],
        scratch_shapes=[
            pltpu.VMEM((tokens, width), BF16),
            pltpu.VMEM((tokens, width), BF16),
            pltpu.VMEM((width, tokens), BF16),
            pltpu.VMEM((width, tokens), BF16),
            pltpu.VMEM((2, width, wide), BF16),
            pltpu.VMEM((LATER, tokens, wide), BF16),
            pltpu.VMEM((tokens, width), F32),
            pltpu.VMEM((SETS, side_rows, wide), BF16),
            pltpu.VMEM((side_rows, wide), BF16),
            pltpu.VMEM((2, side_rows, wide), BF16),
            pltpu.VMEM((2, HALF, 2, rows, wide), BF16),
            pltpu.VMEM((rows, wide), F32),
            pltpu.VMEM((LATER, rows, wide), BF16),
            dma((4,)), dma((2,)), dma((3,)), dma((2, 3)),
            dma((2, HALF, 2, 3)), dma((2, HALF, 2, 3)), dma((3,)), dma((4,)), dma((1,)),
            pltpu.SemaphoreType.REGULAR,
            dma((LATER, 3)), dma((LATER, pieces)), dma((LATER, HALF, 2)), dma((LATER, HALF, 2)),
            dma((LATER, pieces)), dma((LATER, pieces)), dma((2,)), dma((SETS,)), dma((LATER, 2)), dma((2, 2)),
        ],
        compiler_params=pltpu.CompilerParams(
            collective_id=2, has_side_effects=True, vmem_limit_bytes=63 * 2**20
        ),
        cost_estimate=pl.CostEstimate(
            flops=18 * tokens * width * chunks * CHUNK, bytes_accessed=80 * 2**20,
            transcendentals=tokens * chunks * CHUNK,
        ),
        name="feed_forward",
    )(inputs_two, grad_ffn, in_two_t, cot_t, w_ffn, w_attn, *weights)


JOBS = 1 + LATER


BACK_EVENTS = {
    "w0": "01 11",
    "w1": "20",
    "w2": "02",
    "w4": "12",
    "w6": "21",
    "w8": "03",
    "w9": "13",
    "h0": "22",
    "h3": "04",
    "h4": "30",
    "h5": "14",
    "o": "23 31",
    "q1": "40",
    "t1": "24",
    "t2": "32",
    "t3": "41",
    "g": "33",
    "b": "42",
    "u1": "50 34 43",
    "l0": "51",
    "l2": "44 52 53",
    "z1": "54",
}


def backward_kernel(
    cfg, later, gin_hbm, middle_hbm, cot_hbm, hiddens, w_down, w_other, w_attn, qrot_hbm, krot_hbm,
    vlow_hbm, lse_hbm, mixed_hbm, in_one_t, hid_hbm, cos_ref, sin_ref, vec_ref,
    layer_out, grad_input, small_out, grad_g, grad_u, grad_d, grad_qkv, grad_out, kept,
    own, ring, sent, sib, lefts, gin, middle, tall, wa, qrot, krot, vlow, lse, mixed,
    gmix, dqkv, gk, gv, osend, orecv, cots, got, stage, small, small_got,
    in_sem, ring_send, ring_recv, sib_send, sib_recv, x_send, x_recv, out_sem, s_send, s_recv, down_sem, hid_sem,
):
    rows, heads, skip, tail = cfg
    grads = (grad_g, grad_u, grad_d)
    own_tokens, width = gin.shape
    tokens = 2 * own_tokens
    width_q = heads * HD
    width_qkv = width_q + 2 * HD
    side_rows = CHIPS * rows
    _, gain_one, gain_two, start_of = small_inputs(vec_ref, width_qkv, width)
    here = Spot(rows)
    shard, me = here.shard, here.me
    sums = Sums(here, own, ring, ring_send, ring_recv)
    wide_qkv, wide_out = (2, width_qkv // 2), (2, width_q // 2)
    pieces = [(3, CHUNK)] * (JOBS - 1) + [(3, tail), wide_qkv, wide_out]
    own_rows = pl.ds(pl.multiple_of(shard * own_tokens, TILE), own_tokens)
    other_rows = pl.ds(pl.multiple_of((1 - shard) * own_tokens, TILE), own_tokens)

    def at_own(t, size=TILE):
        return pl.ds(pl.multiple_of(shard * own_tokens + t * size, size), size)

    def at_other(t, size=TILE):
        return pl.ds(pl.multiple_of((1 - shard) * own_tokens + t * size, size), size)

    def get(index, source, target):
        return pltpu.make_async_copy(source, target, in_sem.at[index])

    sums_in = [get(i, later.at[skip + i], own.at[i]) for i in range(3)]
    norm_in = [get(3, gin_hbm, gin), get(4, middle_hbm, middle), get(5, cot_hbm, cots)]
    rest_in = [
        get(7, w_attn, wa), get(8, qrot_hbm, qrot), get(9, krot_hbm, krot), get(10, vlow_hbm, vlow),
        get(11, lse_hbm, lse), get(12, mixed_hbm, mixed),
    ]
    for copy in sums_in[:2] + norm_in + sums_in[2:] + rest_in:
        copy.start()
    for side in range(2):
        for chip in range(CHIPS):
            member = 2 * chip + (here.core if side == 0 else 1 - here.core)
            begin = side * side_rows + chip * rows
            get(13, in_one_t.at[here.part(member), :], lefts.at[0, begin : begin + rows, :]).start()

    def bit(value):
        return lax.rem(lax.div(me, value), 2)

    def flipped(*values):
        return me + sum(value - 2 * value * bit(value) for value in values)

    ranks = (here.core + 2 * shard, bit(2) + 2 * bit(4), bit(8))
    partners = (
        ({"dp": flipped(1)}, {"mp": 1 - shard}, {"dp": flipped(1), "mp": 1 - shard}),
        ({"dp": flipped(2)}, {"dp": flipped(4)}, {"dp": flipped(2, 4)}),
        ({"dp": flipped(8)},),
    )

    def rank_of(group, k):
        rank = ranks[group]
        return (rank + 1 - 2 * lax.rem(rank, 2), rank + 2 - 4 * lax.div(rank, 2), 3 - rank)[k]

    barrier = pltpu.get_barrier_semaphore()
    greeted = [p for group in partners for p in group] + [{"dp": n} for n in here.next]
    for target in greeted:
        pl.semaphore_signal(barrier, inc=1, device_id=target, device_id_type=MESH)
    pl.semaphore_wait(barrier, len(greeted))

    def swap_copy(index, src, dst):
        return pltpu.make_async_remote_copy(
            src_ref=src, dst_ref=dst, send_sem=x_send.at[index], recv_sem=x_recv.at[index],
            device_id={"mp": 1 - shard}, device_id_type=MESH,
        )

    some = own_tokens // 2

    def out_swap(index):
        part = slice(index * some, (index + 1) * some)
        return swap_copy(index, osend.at[part, :], orecv.at[part, :])

    half_tiles = own_tokens // TILE

    def attn_swap(t):
        return swap_copy(2 + t, tall.at[at_own(t), :], tall.at[at_own(t), :])

    def attn_got(t):
        return swap_copy(2 + t, tall.at[at_other(t), :], tall.at[at_other(t), :])

    one_swap = swap_copy(2 + half_tiles, dqkv.at[other_rows, :], got)

    def result_copies(job):
        if job < JOBS:
            count, size = pieces[job]
            return [
                pltpu.make_async_copy(
                    stage.at[:, m * size : (m + 1) * size],
                    grads[m].at[:, job * CHUNK : job * CHUNK + size], out_sem.at[m],
                )
                for m in range(count)
            ]
        target = (grad_qkv, grad_out)[job - JOBS]
        return [pltpu.make_async_copy(stage.at[:, 0 : target.shape[1]], target, out_sem.at[0])]

    last_in = get(0, later.at[skip + 3, :, 0 : 3 * tail], own.at[0, :, 0 : 3 * tail])

    def run(point):
        for event in BACK_EVENTS.get(point, "").split():
            job, step = int(event[0]), int(event[1])
            o = p = job % 3
            if step == 0:
                if job == 2:
                    sums_in[2].wait()
                if job == 3:
                    last_in.wait()
                sums.start(o, p, pieces[job])
            elif step < HALF:
                sums.step(o, p, step, pieces[job])
            else:
                if job:
                    for copy in result_copies(job - 1):
                        copy.wait()
                sums.end(o, p, pieces[job], stage)
                for copy in result_copies(job):
                    copy.start()
                if job == 0:
                    last_in.start()

    for i in range(2):
        sums_in[i].wait()
        sums.start(i, i, pieces[i])

    for copy in norm_in:
        copy.wait()
    small[0, :, :] = jnp.zeros_like(small[0])

    @pl.loop(0, half_tiles)
    def _(t):
        part = tile_of(t)
        v = middle[part, :]
        factor = lax.rsqrt(jnp.mean(v * v, axis=-1, keepdims=True) + EPS)
        unit = v * factor
        e = gin[part, :]
        scaled = e * gain_two
        inner = jnp.mean(scaled * unit, axis=-1, keepdims=True)
        total = cots[part, :].astype(F32) + factor * (scaled - unit * inner)
        middle[part, :] = total
        gin[part, :] = v
        tall[at_own(t), :] = total.astype(BF16)
        attn_swap(t).start()
        small[0, 1:2, :] += jnp.sum(e * unit, axis=0, keepdims=True)

    keep = pltpu.make_async_copy(middle, kept, out_sem.at[5])
    keep.start()
    keep.wait()
    middle[...] = jnp.zeros_like(middle)
    chunks = w_down.shape[0]
    top = width // 2

    def down_in(chunk):
        slot = chunk % 2
        weight_to = lefts.at[1, slot * top : (slot + 1) * top, :]
        hidden_to = dqkv.at[slot * own_tokens : (slot + 1) * own_tokens, :]
        if chunk + 1 < chunks:
            parts = [slice(0, 2 * CHUNK)]
        else:
            parts = [slice(h * CHUNK, h * CHUNK + tail) for h in range(2)]
        return [
            pltpu.make_async_copy(source.at[chunk, :, part], target.at[:, part], sem.at[slot, i])
            for i, part in enumerate(parts)
            for source, target, sem in (
                (w_down, weight_to, down_sem), (hiddens, hidden_to, hid_sem)
            )
        ]

    for copy in down_in(0):
        copy.start()
    for chunk in range(chunks):
        if chunk + 1 < chunks:
            for copy in down_in(chunk + 1):
                copy.start()
        for copy in down_in(chunk):
            copy.wait()
        slot, size = chunk % 2, CHUNK if chunk + 1 < chunks else tail
        part = slice(slot * own_tokens, (slot + 1) * own_tokens)
        own_columns, other_columns = (
            pl.ds(pl.multiple_of(side * CHUNK, CHUNK), size) for side in (shard, 1 - shard)
        )
        for h in range(2):
            @pl.loop(0, top // TILE)
            def _(n):
                rows_of = pl.ds(pl.multiple_of(slot * top + n * TILE, TILE), TILE)
                at = pl.ds(pl.multiple_of(h * top + n * TILE, TILE), TILE)
                weight = lefts[1, rows_of, h * CHUNK : h * CHUNK + size]
                middle[:, at] += contract(dqkv[part, other_columns], weight, 1, 1)
                gin[:, at] += contract(dqkv[part, own_columns], weight, 1, 1)

        run(f"w{chunk}")

    osend[...] = middle[...].astype(BF16)
    out_swap(0).start()
    run("w9")

    for copy in rest_in:
        copy.wait()
    for t in range(half_tiles):
        attn_got(t).wait_recv()

    @pl.loop(0, tokens // TILE)
    def _(t):
        gmix[tile_of(t), :] = contract(tall[tile_of(t), :], wa[:, width_qkv:], 1, 0).astype(BF16)

    gk[...] = jnp.zeros_like(gk)
    gv[...] = jnp.zeros_like(gv)

    @pl.loop(0, heads)
    def _(h):
        columns = tile_of(h, HD)
        for i in range(SEQ_LEN // BLOCK):
            low, high = key_range(i)
            part = pl.ds(i * BLOCK, BLOCK)
            query, grad = qrot[part, columns], gmix[part, columns]
            keys = krot[low:high, :]
            scores = contract(keys, query, 1, 1) * SCALE
            seen = visible_keys(start_of(i), low, high, i)
            probs = jnp.where(seen, jnp.exp(scores - lse[h, 0:1, part]), 0.0)
            grad_probs = contract(vlow[low:high, :], grad, 1, 1)
            row_term = jnp.sum(probs * grad_probs, axis=0, keepdims=True)
            grad_scores = (probs * (grad_probs - row_term)).astype(BF16)
            gk[low:high, :] += contract(grad_scores, query, 1, 0)
            gv[low:high, :] += contract(probs.astype(BF16), grad, 1, 0)
            dqkv[part, columns] = turn(
                contract(grad_scores, keys, 0, 0) * SCALE, cos_ref[part, :], -sin_ref[part, :]
            ).astype(BF16)

        for head in range(heads):
            if f"h{head}" in BACK_EVENTS:
                @pl.when(h == head)
                def _():
                    run(f"h{head}")

    dqkv[:, width_q : width_q + HD] = turn(gk[...] * SCALE, cos_ref[...], -sin_ref[...]).astype(BF16)
    dqkv[:, width_q + HD :] = gv[...].astype(BF16)

    one_swap.start()
    out_swap(1).start()
    run("o")

    side_sent = (sent, gmix.at[0:side_rows, :])
    side_got = (sib, qrot.at[0:side_rows, :])

    def side_copy(job, m, columns):
        return pltpu.make_async_remote_copy(
            src_ref=side_sent[job].at[:, columns],
            dst_ref=side_got[job].at[:, columns],
            send_sem=sib_send.at[job, m],
            recv_sem=sib_recv.at[job, m],
            device_id={"dp": here.sibling},
            device_id_type=MESH,
        )

    get(13, lefts.at[0], lefts.at[0]).wait()

    def send_side(job, left, right, pieces):
        for m in range(pieces[0]):
            columns = slice(m * pieces[1], (m + 1) * pieces[1])
            side_sent[job][:, columns] = contract(
                lefts[left, side_rows:, :], right[:, columns], 1, 0
            ).astype(BF16)
            side_copy(job, m, columns).start()

    def own_side(job, left, right, pieces, o):
        for m in range(pieces[0]):
            columns = slice(m * pieces[1], (m + 1) * pieces[1])
            side_copy(job, m, columns).wait()
            own[o, :, columns] = (
                contract(lefts[left, 0:side_rows, :], right[:, columns], 1, 0)
                + side_got[job][:, columns].astype(F32)
            ).astype(BF16)

    send_side(0, 0, dqkv, wide_qkv)
    run("q0")
    own_side(0, 0, dqkv, wide_qkv, 1)
    other_in = get(6, w_other, lefts.at[0])
    other_in.start()
    run("q1")

    for group in range(width // (4 * rows)):
        @pl.loop(0, tokens // TILE)
        def _(t):
            part = tile_of(t)
            turned = tall[part, group * 4 * rows : (group + 1) * 4 * rows].T
            for k in range(4):
                chip, odd = (4 * group + k) // 2, k % 2
                side = odd + here.core - 2 * odd * here.core
                to = pl.ds(pl.multiple_of(side * side_rows + chip * rows, 16), rows)
                lefts[1, to, part] = turned[k * rows : (k + 1) * rows, :]

        run(f"t{group}")

    for t in range(half_tiles):
        attn_swap(t).wait_send()
    hid_in = get(15, hid_hbm, tall)
    hid_in.start()

    fac = gk
    hid_in.wait()

    @pl.loop(0, tokens // TILE)
    def _(t):
        v = tall[tile_of(t), :].astype(F32)
        factor = lax.rsqrt(jnp.mean(v * v, axis=-1, keepdims=True) + EPS)
        fac[tile_of(t), :] = jnp.broadcast_to(factor, (TILE, HD))

    run("f")

    @pl.loop(0, width // TILE)
    def _(n):
        e = contract(dqkv[other_rows, :], wa[tile_of(n), 0:width_qkv], 1, 1)
        unit = tall[other_rows, tile_of(n)].astype(F32) * fac[other_rows, 0:1]
        small[0, 0:1, tile_of(n)] += jnp.sum(e * unit, axis=0, keepdims=True)

    run("g")

    @pl.loop(0, width // TILE)
    def _(n):
        e = contract(dqkv[own_rows, :], wa[tile_of(n), 0:width_qkv], 1, 1)
        middle[:, tile_of(n)] = e
        unit = tall[own_rows, tile_of(n)].astype(F32) * fac[own_rows, 0:1]
        small[0, 0:1, tile_of(n)] += jnp.sum(e * unit, axis=0, keepdims=True)

    @pl.loop(0, tokens // TILE)
    def _(t):
        bias = jnp.sum(dqkv[tile_of(t), :].astype(F32), axis=0, keepdims=True)
        at_query = pl.ds(pl.multiple_of(shard * width_q, HD), width_q)
        small[0, 2:3, at_query] += bias[:, 0:width_q]
        small[0, 3:4, tile_of(shard, HD)] += bias[:, width_q : width_q + HD]
        small[0, 3:4, tile_of(shard + 2, HD)] += bias[:, width_q + HD :]

    run("b")

    def small_copy(group, k):
        return pltpu.make_async_remote_copy(
            src_ref=small.at[group], dst_ref=small_got.at[group, ranks[group]],
            send_sem=s_send.at[group, k], recv_sem=s_recv.at[group, ranks[group]],
            device_id=partners[group][k], device_id_type=MESH,
        )

    def small_start(group):
        for k in range(len(partners[group])):
            small_copy(group, k).start()
        small_got[group, ranks[group]] = small[group]

    def small_end(group):
        count = len(partners[group])
        for k in range(count):
            ref = small_got.at[group, rank_of(group, k)]
            pltpu.make_async_remote_copy(
                src_ref=ref, dst_ref=ref, send_sem=s_send.at[group, k],
                recv_sem=s_recv.at[group, rank_of(group, k)],
                device_id=partners[group][k], device_id_type=MESH,
            ).wait_recv()
            small_copy(group, k).wait_send()
        total = small_got[group, 0]
        for rank in range(1, count + 1):
            total = total + small_got[group, rank]
        small[group + 1] = total

    small_start(0)
    send_side(1, 1, mixed, wide_out)
    run("u0")
    own_side(1, 1, mixed, wide_out, 2)
    small_end(0)
    small_start(1)
    run("u1")

    def layer_rows(index):
        part = slice(index * some, (index + 1) * some)
        out_swap(index).wait()
        orecv[part, :] = (gin[part, :] + orecv[part, :].astype(F32)).astype(BF16)
        copy = pltpu.make_async_copy(
            orecv.at[part, :], layer_out.at[part, :], out_sem.at[(3, 6)[index]]
        )
        copy.start()
        return copy

    def keep_in(index):
        part = slice(index * some, (index + 1) * some)
        return get(14, kept.at[part, :], gin.at[0:some, :])

    layer_copies = [layer_rows(0)]
    keep_in(0).start()
    run("l0")
    small_end(1)
    small_start(2)
    run("l1")
    small_end(2)
    run("l2")
    small_out[...] = small[3]

    one_swap.wait()
    other_in.wait()

    @pl.loop(0, width // TILE)
    def _(n):
        middle[:, tile_of(n)] += contract(got[...], lefts[0, tile_of(n), :], 1, 1)

    for index in range(2):
        part = slice(index * some, (index + 1) * some)
        of = pl.ds(pl.multiple_of(shard * own_tokens + index * some, some), some)
        if index:
            keep_in(index).start()
        keep_in(index).wait()
        factor = fac[of, 0:1]
        unit = tall[of, :].astype(F32) * factor
        scaled = middle[part, :] * gain_one
        inner = jnp.mean(scaled * unit, axis=-1, keepdims=True)
        cots[part, :] = (gin[0:some, :] + factor * (scaled - unit * inner)).astype(BF16)

    input_copy = pltpu.make_async_copy(cots, grad_input, out_sem.at[4])
    input_copy.start()
    layer_copies.append(layer_rows(1))
    run("z1")
    for copy in [input_copy] + layer_copies + result_copies(JOBS + 1):
        copy.wait()


def attention_back(
    later, gin, middle, cot, hiddens, w_down, w_other, forward, cos2, sin2, vector, tail
):
    w_attn, qrot, krot, vlow, lse, mixed, in_one_t, hid_all = forward
    own_tokens, width = cot.shape
    tokens = 2 * own_tokens
    heads = lse.shape[0]
    width_q = heads * HD
    width_qkv = width_q + 2 * HD
    side_rows, wide = later.shape[1:]
    rows = side_rows // CHIPS
    vmem = pl.BlockSpec(memory_space=pltpu.VMEM)
    hbm = pl.BlockSpec(memory_space=pl.ANY)
    dma = pltpu.SemaphoreType.DMA
    shape = jax.ShapeDtypeStruct
    half = (own_tokens, width)
    n_swaps = own_tokens // TILE + 3
    return pl.pallas_call(
        functools.partial(backward_kernel, (rows, heads, later.shape[0] - JOBS, tail)),
        in_specs=[hbm] * 15 + [vmem] * 3,
        out_specs=[hbm, hbm, vmem] + [hbm] * 6,
        out_shape=[
            shape(half, BF16), shape(half, BF16), shape((8, width), F32),
        ] + [shape((rows, (JOBS - 1) * CHUNK + tail), F32)] * 3 + [
            shape((rows, width_qkv), F32), shape((rows, width_q), F32), shape(half, F32),
        ],
        scratch_shapes=[
            pltpu.VMEM((3, side_rows, wide), BF16),
            pltpu.VMEM((3, HALF, 2, rows, wide), BF16),
            pltpu.VMEM((side_rows, width_qkv), BF16),
            pltpu.VMEM((side_rows, width_qkv), BF16),
            pltpu.VMEM((2, width, tokens), BF16),
            pltpu.VMEM(half, F32),
            pltpu.VMEM(half, F32),
            pltpu.VMEM((tokens, width), BF16),
            pltpu.VMEM(w_attn.shape, BF16),
            pltpu.VMEM((tokens, width_q), BF16),
            pltpu.VMEM((tokens, HD), BF16),
            pltpu.VMEM((tokens, HD), BF16),
            pltpu.VMEM(lse.shape, F32),
            pltpu.VMEM((tokens, width_q), BF16),
            pltpu.VMEM((tokens, width_q), BF16),
            pltpu.VMEM((tokens, width_qkv), BF16),
            pltpu.VMEM((tokens, HD), F32),
            pltpu.VMEM((tokens, HD), F32),
            pltpu.VMEM(half, BF16),
            pltpu.VMEM(half, BF16),
            pltpu.VMEM(half, BF16),
            pltpu.VMEM((own_tokens, width_qkv), BF16),
            pltpu.VMEM((rows, wide), F32),
            pltpu.VMEM((4, 8, width), F32),
            pltpu.VMEM((3, 4, 8, width), F32),
            dma((16,)), dma((3, HALF, 2, 3)), dma((3, HALF, 2, 3)), dma((2, 2)), dma((2, 2)),
            dma((n_swaps,)), dma((n_swaps,)), dma((7,)), dma((3, 3)), dma((3, 4)), dma((2, 2)), dma((2, 2)),
        ],
        compiler_params=pltpu.CompilerParams(
            collective_id=3, has_side_effects=True, vmem_limit_bytes=63 * 2**20
        ),
        cost_estimate=pl.CostEstimate(
            flops=10 * heads * tokens * tokens * HD, bytes_accessed=50 * 2**20, transcendentals=0
        ),
        name="attention_back",
    )(
        later, gin, middle, cot, hiddens, w_down, w_other, w_attn, qrot, krot, vlow, lse, mixed, in_one_t,
        hid_all, cos2, sin2, vector,
    )


def finish_kernel(
    layer_in, input_in, first_g, first_u, first_d, last_g, last_u, last_d, qkv_in, out_in, small_in,
    layer_out, grad_input, grad_q, grad_k, grad_v, grad_out, grad_g, grad_u, grad_d, vec_one, vec_two,
    bias_q, bias_k, bias_v,
    layer, grad, gates, ups, downs, qkv, out, in_sem, out_sem,
):
    early = first_g.shape[1]
    moves = [
        (layer_in, layer, layer_out), (input_in, grad, grad_input),
        (first_g, gates.at[:, 0:early], None), (last_g, gates.at[:, early:], None),
        (first_u, ups.at[:, 0:early], None), (last_u, ups.at[:, early:], None),
        (first_d, downs.at[:, 0:early], None), (last_d, downs.at[:, early:], None),
        (qkv_in, qkv, None), (out_in, out, grad_out),
    ]
    loads = [
        pltpu.make_async_copy(source, buffer, in_sem.at[i]) for i, (source, buffer, _) in enumerate(moves)
    ]
    for copy in loads:
        copy.start()
    stores = []

    def store(buffer, target):
        copy = pltpu.make_async_copy(buffer, target, out_sem.at[len(stores)])
        copy.start()
        stores.append(copy)

    for i, (_, buffer, target) in enumerate(moves):
        loads[i].wait()
        if target is not None:
            store(buffer, target)
        if i in (3, 5, 7):
            store(*((gates, grad_g), (ups, grad_u), (downs, grad_d))[i // 2 - 1])
    begin = 0
    for target in (grad_q, grad_k, grad_v):
        store(qkv.at[:, begin : begin + target.shape[1]], target)
        begin += target.shape[1]
    for i, target in enumerate((vec_one, vec_two, bias_q)):
        target[...] = small_in[i : i + 1, :].reshape(target.shape[0])
    wide = bias_k.shape[0]
    bias_k[...] = small_in[3:4, 0:wide].reshape(wide)
    bias_v[...] = small_in[3:4, wide : 2 * wide].reshape(wide)
    for copy in stores:
        copy.wait()


def finish(layer_out, grad_input, first, last, sum_qkv, sum_out, small, width_q):
    vmem = pl.BlockSpec(memory_space=pltpu.VMEM)
    hbm = pl.BlockSpec(memory_space=pl.ANY)
    shape = jax.ShapeDtypeStruct
    rows, width_qkv = sum_qkv.shape
    width_k = (width_qkv - width_q) // 2
    width = layer_out.shape[1]
    ffn = (rows, first[0].shape[1] + last[0].shape[1])
    dma = pltpu.SemaphoreType.DMA
    return pl.pallas_call(
        finish_kernel,
        in_specs=[hbm] * 10 + [vmem],
        out_specs=[hbm] * 9 + [vmem] * 5,
        out_shape=[
            shape(layer_out.shape, BF16), shape(grad_input.shape, BF16),
            shape((rows, width_q), F32), shape((rows, width_k), F32), shape((rows, width_k), F32),
            shape(sum_out.shape, F32), shape(ffn, F32), shape(ffn, F32), shape(ffn, F32),
            shape((width,), F32), shape((width,), F32), shape((2 * width_q,), F32),
            shape((2 * width_k,), F32), shape((2 * width_k,), F32),
        ],
        scratch_shapes=[
            pltpu.VMEM(layer_out.shape, BF16), pltpu.VMEM(grad_input.shape, BF16),
            pltpu.VMEM(ffn, F32), pltpu.VMEM(ffn, F32), pltpu.VMEM(ffn, F32),
            pltpu.VMEM(sum_qkv.shape, F32), pltpu.VMEM(sum_out.shape, F32), dma((10,)), dma((9,)),
        ],
        compiler_params=pltpu.CompilerParams(vmem_limit_bytes=62 * 2**20),
        name="finish",
    )(layer_out, grad_input, *first, *last, sum_qkv, sum_out, small)


def body_fused(
    hidden_in, positions, query_weight, query_bias, key_weight, key_bias, value_weight, value_bias,
    out_weight, gate_weight, up_weight, down_weight, attn_gain, ffn_gain, cotangent,
):
    rows, width_q = query_weight.shape
    heads = width_q // HD
    hidden_units = gate_weight.shape[1]
    own_tokens, width = hidden_in.shape
    half = HD // 2
    lanes = jnp.arange(HD, dtype=jnp.int32)
    freq = jnp.power(ROPE_BASE, -2.0 * (lanes % half).astype(F32) / HD)
    ffn_weights = (gate_weight, up_weight, down_weight.T)
    (w_ffn, w_attn, hidden_all, grad_ffn, in_one_t, qrot, krot, vlow, mixed, lse, middle,
     inputs_two, vector, cos2, sin2, in_two_t, cot_t) = forward_attention(
        hidden_in, cotangent,
        (freq, positions, query_bias, key_bias, value_bias, attn_gain, ffn_gain),
        (query_weight, key_weight, value_weight, out_weight.T, *ffn_weights),
        heads,
    )
    hiddens, w_down, grad_normed_two, later, *first_sums, w_other, _ = feed_forward(
        inputs_two, grad_ffn, in_two_t, cot_t, w_ffn, w_attn, width_q + 2 * HD, ffn_weights
    )
    tail = units_of(-(-hidden_units // CHUNK) - 1, hidden_units)
    layer_out, grad_input, small, *sums = attention_back(
        later, grad_normed_two, middle, cotangent, hiddens, w_down, w_other,
        (w_attn, qrot, krot, vlow, lse, mixed, in_one_t, hidden_all), cos2, sin2, vector, tail,
    )
    (layer_out, grad_input, sum_q, sum_k, sum_v, sum_out, sum_gate, sum_up, sum_down, gain_one,
     gain_two, sum_bias_q, sum_bias_k, sum_bias_v) = finish(
        layer_out, grad_input, first_sums, sums[:3], *sums[3:5], small, width_q
    )
    return (
        layer_out,
        grad_input,
        sum_q,
        sum_bias_q,
        sum_k,
        sum_bias_k,
        sum_v,
        sum_bias_v,
        sum_out.T,
        sum_gate,
        sum_up,
        sum_down.T,
        gain_one,
        gain_two,
    )


def body(*arrays):
    rows = arrays[2].shape[0]
    if lax.axis_size("dp") == 2 * CHIPS and rows % 32 == 0 and -(-arrays[9].shape[1] // CHUNK) == 9:
        return body_fused(*arrays)
    return body_general(*arrays)


def solution(mesh):
    tokens, weight, weight_t = P(("dp", "mp"), None), P("dp", "mp"), P("mp", "dp")
    return jax.shard_map(
        body,
        mesh=mesh,
        in_specs=(
            tokens, P("dp"), weight, P(), weight, P(), weight, P(), weight_t,
            weight, weight, weight_t, P(), P(), tokens,
        ),
        out_specs=(
            tokens, tokens, weight, P(), weight, P(), weight, P(), weight_t,
            weight, weight, weight_t, P(), P(),
        ),
        check_vma=False,
    )
```

```python
import functools
import math

import jax
import jax.numpy as jnp
from jax import lax
from jax.experimental import pallas as pl
from jax.experimental.pallas import tpu as pltpu
from jax.sharding import PartitionSpec as P

HD = 128
SEQ_LEN = 1024
DOC_MAX = 512
EPS = 1e-06
ROPE_BASE = 1000000.0
BLOCK = 256
SCALE = 1.0 / math.sqrt(HD)
F32 = jnp.float32
BF16 = jnp.bfloat16


def contract(left, right, left_dim, right_dim):
    return lax.dot_general(
        left, right, (((left_dim,), (right_dim,)), ((), ())), preferred_element_type=F32
    )


def key_range(block_id):
    low = max(0, block_id * BLOCK - (DOC_MAX - 1)) // BLOCK * BLOCK
    return low, (block_id + 1) * BLOCK


def visible(start_row, low, high, block_id):
    keys = low + lax.broadcasted_iota(jnp.int32, (high - low, BLOCK), 0)
    queries = block_id * BLOCK + lax.broadcasted_iota(jnp.int32, (high - low, BLOCK), 1)
    return (keys >= start_row) & (keys <= queries)


def turn(values, cosines, sines):
    return values * cosines + pltpu.roll(values, HD // 2, 1) * sines


def attend_kernel(
    q_ref, k_ref, v_ref, bq_ref, bk_ref, bv_ref, cos_ref, sin_ref, start_ref,
    mixed_ref, qrot_ref, krot_ref, vlow_ref, lse_ref,
):
    head = pl.program_id(0)

    @pl.when(head == 0)
    def _():
        krot_ref[...] = turn(k_ref[...] + bk_ref[...], cos_ref[...], sin_ref[...]).astype(BF16)
        vlow_ref[...] = (v_ref[...] + bv_ref[...]).astype(BF16)

    qrot_ref[...] = turn(q_ref[...] + bq_ref[...], cos_ref[...], sin_ref[...]).astype(BF16)
    for i in range(SEQ_LEN // BLOCK):
        low, high = key_range(i)
        rows = pl.ds(i * BLOCK, BLOCK)
        start_row = start_ref[0:1, rows]
        scores = contract(krot_ref[low:high, :], qrot_ref[rows, :], 1, 1) * SCALE
        scores = jnp.where(visible(start_row, low, high, i), scores, -1e30)
        top = jnp.max(scores, axis=0, keepdims=True)
        weights = jnp.exp(scores - top)
        total = jnp.sum(weights, axis=0, keepdims=True)
        probs = (weights * (1.0 / total)).astype(BF16)
        mixed_ref[rows, :] = contract(probs, vlow_ref[low:high, :], 0, 0).astype(BF16)
        lse_ref[0, 0:1, rows] = top + jnp.log(total)


def attend(qkv, bias, cos2, sin2, start, heads):
    seq = SEQ_LEN
    full = lambda shape: pl.BlockSpec(shape, lambda h: (0,) * len(shape))
    col = lambda: pl.BlockSpec((seq, HD), lambda h: (0, h))
    at = lambda j: pl.BlockSpec((seq, HD), lambda h: (0, j))
    bat = lambda j: pl.BlockSpec((1, HD), lambda h: (0, j))
    return pl.pallas_call(
        attend_kernel,
        grid=(heads,),
        in_specs=[
            col(), at(heads), at(heads + 1),
            pl.BlockSpec((1, HD), lambda h: (0, h)), bat(heads), bat(heads + 1),
            full((seq, HD)), full((seq, HD)), full((1, seq)),
        ],
        out_specs=[
            col(), col(), full((seq, HD)), full((seq, HD)),
            pl.BlockSpec((1, 8, seq), lambda h: (h, 0, 0)),
        ],
        out_shape=[
            jax.ShapeDtypeStruct((seq, heads * HD), BF16),
            jax.ShapeDtypeStruct((seq, heads * HD), BF16),
            jax.ShapeDtypeStruct((seq, HD), BF16),
            jax.ShapeDtypeStruct((seq, HD), BF16),
            jax.ShapeDtypeStruct((heads, 8, seq), F32),
        ],
        compiler_params=pltpu.CompilerParams(vmem_limit_bytes=40 * 2**20),
        cost_estimate=pl.CostEstimate(
            flops=4 * heads * seq * seq * HD, bytes_accessed=10 * 2**20,
            transcendentals=heads * seq * seq // 2,
        ),
        name="attend",
    )(qkv, qkv, qkv, bias, bias, bias, cos2, sin2, start)


def attend_back_kernel(
    heads, qrot_ref, krot_ref, vlow_ref, lse_ref, grad_ref, cos_ref, sin_ref, start_ref,
    out_ref, gk_ref, gv_ref,
):
    head = pl.program_id(0)

    @pl.when(head == 0)
    def _():
        gk_ref[...] = jnp.zeros_like(gk_ref)
        gv_ref[...] = jnp.zeros_like(gv_ref)

    for i in range(SEQ_LEN // BLOCK):
        low, high = key_range(i)
        rows = pl.ds(i * BLOCK, BLOCK)
        start_row = start_ref[0:1, rows]
        query, grad = qrot_ref[rows, :], grad_ref[rows, :]
        keys = krot_ref[low:high, :]
        scores = contract(keys, query, 1, 1) * SCALE
        probs = jnp.where(
            visible(start_row, low, high, i), jnp.exp(scores - lse_ref[0, 0:1, rows]), 0.0
        )
        grad_probs = contract(vlow_ref[low:high, :], grad, 1, 1)
        row_term = jnp.sum(probs * grad_probs, axis=0, keepdims=True)
        grad_scores = (probs * (grad_probs - row_term)).astype(BF16)
        gk_ref[low:high, :] += contract(grad_scores, query, 1, 0)
        gv_ref[low:high, :] += contract(probs.astype(BF16), grad, 1, 0)
        grad_query = contract(grad_scores, keys, 0, 0) * SCALE
        out_ref[rows, pl.ds(pl.multiple_of(head * HD, HD), HD)] = turn(
            grad_query, cos_ref[rows, :], -sin_ref[rows, :]
        ).astype(BF16)

    @pl.when(head == heads - 1)
    def _():
        out_ref[:, heads * HD : (heads + 1) * HD] = turn(
            gk_ref[...] * SCALE, cos_ref[...], -sin_ref[...]
        ).astype(BF16)
        out_ref[:, (heads + 1) * HD :] = gv_ref[...].astype(BF16)


def attend_back(qrot, krot, vlow, lse, grad_mixed, cos2, sin2, start, heads):
    seq = SEQ_LEN
    full = lambda shape: pl.BlockSpec(shape, lambda h: (0,) * len(shape))
    col = lambda: pl.BlockSpec((seq, HD), lambda h: (0, h))
    return pl.pallas_call(
        functools.partial(attend_back_kernel, heads),
        grid=(heads,),
        in_specs=[
            col(), full((seq, HD)), full((seq, HD)),
            pl.BlockSpec((1, 8, seq), lambda h: (h, 0, 0)), col(),
            full((seq, HD)), full((seq, HD)), full((1, seq)),
        ],
        out_specs=full((seq, (heads + 2) * HD)),
        out_shape=jax.ShapeDtypeStruct((seq, (heads + 2) * HD), BF16),
        scratch_shapes=[pltpu.VMEM((seq, HD), F32), pltpu.VMEM((seq, HD), F32)],
        compiler_params=pltpu.CompilerParams(vmem_limit_bytes=40 * 2**20),
        cost_estimate=pl.CostEstimate(
            flops=10 * heads * seq * seq * HD, bytes_accessed=10 * 2**20,
            transcendentals=heads * seq * seq // 2,
        ),
        name="attend_back",
    )(qrot, krot, vlow, lse, grad_mixed, cos2, sin2, start)


class Ring:
    def __init__(self, members):
        self.members = members
        self.chips = members // 2
        self.half = self.chips // 2
        n = self.chips
        self.path = [2 * r if r < n // 2 else 2 * (n - 1 - r) + 1 for r in range(n)]
        self.offsets = [self.half]
        for k in range(self.half - 1, 0, -1):
            self.offsets += [k, n - k]
        self.offsets += [0]
        self.place = {k: i for i, k in enumerate(self.offsets)}

    def pairs(self, shift):
        n, path = self.chips, self.path
        return [
            (path[r] * 2 + c, path[(r + shift) % n] * 2 + c) for r in range(n) for c in range(2)
        ]

    def up(self, block):
        return lax.ppermute(block, "dp", self.pairs(1))

    def down(self, block):
        return lax.ppermute(block, "dp", self.pairs(-1))

    def across(self, block):
        return lax.ppermute(block, "dp", [(i, i ^ 1) for i in range(self.members)])

    def order(self):
        me = lax.axis_index("dp")
        path = jnp.array(self.path, jnp.int32)
        spot = jnp.zeros((self.chips,), jnp.int32).at[path].set(jnp.arange(self.chips, dtype=jnp.int32))
        mine = spot[me // 2]
        offsets = jnp.array(self.offsets, jnp.int32)
        chips = path[(mine + offsets) % self.chips]
        core = me % 2
        return jnp.concatenate([chips * 2 + core, chips * 2 + (1 - core)])

    def gather(self, block):
        n, h = self.chips, self.half
        rows = block.shape[0]
        got = {0: block}
        for k in range(1, h):
            got[n - k] = self.up(got[(n - k + 1) % n])
            got[k] = self.down(got[k - 1])
        first = self.up(got[h + 1][: rows // 2])
        second = self.down(got[h - 1][rows // 2 :])
        other = {k: self.across(got[k]) for k in got}
        got_half = [first, second]
        other_half = [self.across(first), self.across(second)]
        blocks = []
        for side, halves in ((got, got_half), (other, other_half)):
            for k in self.offsets:
                blocks.append(tuple(halves) if k == h else (side[k],))
        return blocks, first

    def reduce(self, own, rows):
        def term(k):
            begin = self.place[k] * rows
            return jnp.concatenate([o[begin : begin + rows] for o in own], axis=1)

        return self.reduce_terms(term, rows)

    def reduce_terms(self, term, rows):
        n, h = self.chips, self.half
        up = self.up(term(h)[: rows // 2])
        down = self.down(term(h)[rows // 2 :])
        for k in range(h - 1, 0, -1):
            mine_up, mine_down = term(k), term(n - k)
            if k == h - 1:
                sent_up = jnp.concatenate([
                    (up.astype(F32) + mine_up[: rows // 2].astype(F32)).astype(BF16),
                    mine_up[rows // 2 :],
                ])
                sent_down = jnp.concatenate([
                    mine_down[: rows // 2],
                    (down.astype(F32) + mine_down[rows // 2 :].astype(F32)).astype(BF16),
                ])
            else:
                sent_up = (up.astype(F32) + mine_up.astype(F32)).astype(BF16)
                sent_down = (down.astype(F32) + mine_down.astype(F32)).astype(BF16)
            up, down = self.up(sent_up), self.down(sent_down)
        return term(0).astype(F32) + up.astype(F32) + down.astype(F32)


def stack(blocks, begin, stop):
    return jnp.concatenate([part[:, begin:stop] for block in blocks for part in block], axis=0)


def swap(block):
    return lax.ppermute(block, "mp", [(0, 1), (1, 0)])


def rms(values):
    return lax.rsqrt(jnp.mean(values * values, axis=-1, keepdims=True) + EPS)


def after(value, *earlier):
    return lax.optimization_barrier((value, *earlier))[0]


def split_hidden(width, parts):
    tiles = width // HD
    cuts = [round(tiles * i / parts) * HD for i in range(parts + 1)]
    return list(zip(cuts[:-1], cuts[1:]))


def body_general(
    hidden_in, positions, query_weight, query_bias, key_weight, key_bias, value_weight, value_bias,
    out_weight, gate_weight, up_weight, down_weight, attn_gain, ffn_gain, cotangent,
):
    ring = Ring(lax.axis_size("dp"))
    rows = query_weight.shape[0]
    width = rows * ring.members
    side_rows = rows * ring.chips
    heads = query_weight.shape[1] // HD
    width_q = heads * HD
    width_qkv = width_q + 2 * HD
    own_tokens = hidden_in.shape[0]
    shard = lax.axis_index("mp")

    def whole(own, other):
        first = jnp.where(shard == 0, own, other)
        second = jnp.where(shard == 0, other, own)
        return jnp.concatenate([first, second], axis=0)

    def own_half(values):
        return lax.dynamic_slice_in_dim(values, shard * own_tokens, own_tokens, 0)

    def other_half(values):
        return lax.dynamic_slice_in_dim(values, (1 - shard) * own_tokens, own_tokens, 0)

    hidden_other = swap(hidden_in)
    attn_pack = jnp.concatenate([query_weight, key_weight, value_weight, out_weight.T], axis=1)
    attn_blocks, attn_last = ring.gather(attn_pack)
    cotangent_other = swap(after(cotangent, hidden_other))
    down_t = down_weight.T
    spans = split_hidden(gate_weight.shape[1], 2)
    ffn_blocks = []
    last = attn_last
    for begin, stop in spans:
        pack = jnp.concatenate(
            [gate_weight[:, begin:stop], up_weight[:, begin:stop], down_t[:, begin:stop]], axis=1
        )
        blocks, last = ring.gather(after(pack, last))
        ffn_blocks.append(blocks)

    order = ring.order()
    feature = (order[:, None] * rows + jnp.arange(rows, dtype=jnp.int32)[None, :]).reshape(width)
    shuffle = (jnp.arange(width, dtype=jnp.int32)[:, None] == feature[None, :]).astype(BF16)

    def to_order(values):
        return contract(values, shuffle, 1, 0).astype(BF16)

    def from_order(values):
        return contract(values, shuffle, 1, 1).astype(BF16)

    def vector_to_order(values):
        return jnp.sum(jnp.where(shuffle > 0, values[:, None], 0.0), axis=0)

    def vector_from_order(values):
        return jnp.sum(jnp.where(shuffle > 0, values[None, :], 0.0), axis=1)

    gain_attn, gain_ffn = vector_to_order(attn_gain), vector_to_order(ffn_gain)

    hidden_all = to_order(whole(hidden_in, hidden_other))
    resid_all = hidden_all.astype(F32)
    factor_one = rms(resid_all)
    inputs_one = (resid_all * factor_one * gain_attn).astype(BF16)
    half = HD // 2
    freq = jnp.power(ROPE_BASE, -2.0 * jnp.arange(half, dtype=F32) / HD)
    angles = positions.astype(F32)[:, None] * freq[None, :]
    cosines, sines = jnp.cos(angles), jnp.sin(angles)
    cos2 = jnp.concatenate([cosines, cosines], axis=1)
    sin2 = jnp.concatenate([-sines, sines], axis=1)
    start = (jnp.arange(SEQ_LEN, dtype=jnp.int32) - positions)[None, :]
    bias = jnp.concatenate([
        lax.dynamic_slice_in_dim(query_bias, shard * width_q, width_q, 0),
        lax.dynamic_slice_in_dim(key_bias, shard * HD, HD, 0),
        lax.dynamic_slice_in_dim(value_bias, shard * HD, HD, 0),
    ])[None, :]
    qkv_full = stack(attn_blocks, 0, width_qkv)
    out_full = stack(attn_blocks, width_qkv, width_qkv + width_q)
    qkv = contract(inputs_one, qkv_full, 1, 0)
    mixed, qrot, krot, vlow, lse = attend(qkv, bias, cos2, sin2, start, heads)
    out_other = swap(contract(other_half(mixed), out_full, 1, 1).astype(BF16))
    middle = (
        own_half(hidden_all).astype(F32)
        + contract(own_half(mixed), out_full, 1, 1)
        + out_other.astype(F32)
    )
    factor_two = rms(middle)
    in_two_own = (middle * factor_two * gain_ffn).astype(BF16)
    inputs_two = whole(in_two_own, swap(in_two_own))
    grad_ffn = to_order(whole(cotangent, cotangent_other))

    hiddens, grads_gate, grads_up, weights = [], [], [], []
    for (begin, stop), blocks in zip(spans, ffn_blocks):
        wide = stop - begin
        gate_full = stack(blocks, 0, wide)
        up_full = stack(blocks, wide, 2 * wide)
        down_full = stack(blocks, 2 * wide, 3 * wide)
        grad_hidden = contract(grad_ffn, down_full, 1, 0)
        gate = contract(inputs_two, gate_full, 1, 0)
        up = contract(inputs_two, up_full, 1, 0)
        sig = jax.nn.sigmoid(gate)
        swish = gate * sig
        hiddens.append((swish * up).astype(BF16))
        grads_gate.append((grad_hidden * up * sig * (1.0 + gate * (1.0 - sig))).astype(BF16))
        grads_up.append((grad_hidden * swish).astype(BF16))
        weights.append((gate_full, up_full, down_full))

    def side(values, index):
        return values[:, index * side_rows : (index + 1) * side_rows]

    def chip_sum(left, right):
        sent = contract(side(left, 1), right, 0, 0).astype(BF16)
        return (contract(side(left, 0), right, 0, 0) + ring.across(sent).astype(F32)).astype(BF16)

    sums = []
    for index in range(len(spans)):
        own = [
            chip_sum(inputs_two, grads_gate[index]),
            chip_sum(inputs_two, grads_up[index]),
            chip_sum(grad_ffn, hiddens[index]),
        ]
        sums.append(ring.reduce(own, rows))

    def back_two(take):
        total = None
        for (gate_full, up_full, _), g, u in zip(weights, grads_gate, grads_up):
            term = contract(take(g), gate_full, 1, 1) + contract(take(u), up_full, 1, 1)
            total = term if total is None else total + term
        return total

    def forward_out(take):
        total = None
        for (_, _, down_full), h in zip(weights, hiddens):
            term = contract(take(h), down_full, 1, 1)
            total = term if total is None else total + term
        return total

    back_other = swap(back_two(other_half).astype(BF16))
    grad_normed_two = back_two(own_half) + back_other.astype(F32)
    ffn_other = swap(forward_out(other_half).astype(BF16))
    layer_out = from_order(
        (middle + forward_out(own_half) + ffn_other.astype(F32)).astype(BF16)
    )

    unit_two = middle * factor_two
    scaled = grad_normed_two * gain_ffn
    gain_two = jnp.sum(grad_normed_two * unit_two, axis=0)
    inner = jnp.mean(scaled * unit_two, axis=-1, keepdims=True)
    grad_middle = own_half(grad_ffn).astype(F32) + factor_two * (scaled - unit_two * inner)

    grad_attn_own = grad_middle.astype(BF16)
    grad_attn = whole(grad_attn_own, swap(grad_attn_own))
    grad_mixed = contract(grad_attn, out_full, 1, 0).astype(BF16)
    grad_qkv = attend_back(qrot, krot, vlow, lse, grad_mixed, cos2, sin2, start, heads)
    sum_out = ring.reduce([chip_sum(grad_attn, mixed)], rows)
    sum_qkv = ring.reduce([chip_sum(inputs_one, grad_qkv)], rows)

    back_one_other = contract(other_half(grad_qkv), qkv_full, 1, 1)
    one_other = swap(back_one_other.astype(BF16))
    back_one_own = contract(own_half(grad_qkv), qkv_full, 1, 1)
    unit_all = resid_all * factor_one
    unit_one = own_half(unit_all)
    gain_one = jnp.sum(back_one_own * unit_one, axis=0) + jnp.sum(
        back_one_other * other_half(unit_all), axis=0
    )
    grad_normed_one = back_one_own + one_other.astype(F32)
    scaled_one = grad_normed_one * gain_attn
    inner_one = jnp.mean(scaled_one * unit_one, axis=-1, keepdims=True)
    through_one = own_half(factor_one) * (scaled_one - unit_one * inner_one)
    grad_input = from_order((grad_middle + through_one).astype(BF16))

    bias_part = jnp.sum(grad_qkv.astype(F32), axis=0)

    def place(part, total):
        return lax.dynamic_update_slice_in_dim(
            jnp.zeros((total,), F32), part, shard * part.shape[0], 0
        )

    small = jnp.concatenate([
        vector_from_order(gain_one),
        vector_from_order(gain_two),
        place(bias_part[:width_q], query_bias.shape[0]),
        place(bias_part[width_q : width_q + HD], key_bias.shape[0]),
        place(bias_part[width_q + HD :], value_bias.shape[0]),
    ])
    small = small + swap(small)
    bit = 1
    while bit < ring.members:
        small = small + lax.ppermute(small, "dp", [(i, i ^ bit) for i in range(ring.members)])
        bit *= 2
    cuts = [width, width, query_bias.shape[0], key_bias.shape[0], value_bias.shape[0]]
    pieces, begin = [], 0
    for cut in cuts:
        pieces.append(small[begin : begin + cut])
        begin += cut

    def gather_cols(index):
        parts = []
        for (begin, stop), total in zip(spans, sums):
            wide = stop - begin
            parts.append(total[:, index * wide : (index + 1) * wide])
        return jnp.concatenate(parts, axis=1)

    return (
        layer_out,
        grad_input,
        sum_qkv[:, :width_q],
        pieces[2],
        sum_qkv[:, width_q : width_q + HD],
        pieces[3],
        sum_qkv[:, width_q + HD :],
        pieces[4],
        sum_out.T,
        gather_cols(0),
        gather_cols(1),
        gather_cols(2).T,
        pieces[0],
        pieces[1],
    )


CHIPS = 8
HALF = CHIPS // 2
CHUNK = 512
TILE = 256
MESH = pl.DeviceIdType.MESH


class Spot:
    def __init__(self, rows):
        self.rows = rows
        self.me = lax.axis_index("dp")
        self.shard = lax.axis_index("mp")
        self.core = lax.rem(self.me, 2)
        chip = lax.div(self.me, 2)
        line, back = lax.div(chip, 2), lax.rem(chip, 2)
        self.spot = line * (1 - back) + (CHIPS - 1 - line) * back
        self.sibling = self.me + 1 - 2 * self.core
        self.next = (self.chip(1) * 2 + self.core, self.chip(CHIPS - 1) * 2 + self.core)

    def chip(self, offset):
        place = lax.rem(self.spot + offset, CHIPS)
        back = lax.div(place, HALF)
        return (1 - back) * (2 * place) + back * (2 * (CHIPS - 1 - place) + 1)

    def greet(self):
        barrier = pltpu.get_barrier_semaphore()
        for target in (
            {"dp": self.sibling}, {"dp": self.next[0]}, {"dp": self.next[1]}, {"mp": 1 - self.shard}
        ):
            pl.semaphore_signal(barrier, inc=1, device_id=target, device_id_type=MESH)
        pl.semaphore_wait(barrier, 4)

    def part(self, block, half=None):
        begin, size = block * self.rows, self.rows
        if half is not None:
            size = self.rows // 2
            begin = begin + half * size
        return pl.ds(pl.multiple_of(begin, 16), size)


def tile_of(index, size=TILE):
    return pl.ds(pl.multiple_of(index * size, size), size)


def small_inputs(ref, width_qkv, width):
    gains = width_qkv + width, width_qkv + 2 * width

    def start_of(block):
        begin = gains[1] + block * BLOCK
        return ref[0:1, begin : begin + BLOCK]

    return (
        ref[0:1, 0:width_qkv], ref[0:1, width_qkv : gains[0]], ref[0:1, gains[0] : gains[1]], start_of
    )


def visible_keys(start_row, low, high, block_id):
    shape = (high - low, BLOCK)
    keys = low + lax.broadcasted_iota(jnp.int32, shape, 0)
    queries = block_id * BLOCK + lax.broadcasted_iota(jnp.int32, shape, 1)
    return (keys.astype(F32) >= start_row) & (keys <= queries)


class Gather:
    def __init__(self, here, held, home, landed, hop_send, hop_recv, side_send, side_recv, store_sem):
        self.here, self.held, self.home, self.landed = here, held, home, landed
        self.hop_send, self.hop_recv = hop_send, hop_recv
        self.side_send, self.side_recv, self.store_sem = side_send, side_recv, store_sem

    def member(self, step, way, sibling=False):
        here = self.here
        chip = here.chip((CHIPS - step) % CHIPS if way == 0 else step)
        return chip * 2 + (1 - here.core if sibling else here.core)

    def hop(self, unit, step, way, arrival=False):
        half = way if step == HALF else None
        source = self.held(unit, step if arrival else step - 1, way, half)
        target = source if arrival or self.landed(unit) else self.held(unit, step, way, half)
        return pltpu.make_async_remote_copy(
            src_ref=source, dst_ref=target, send_sem=self.hop_send.at[unit, step - 1, way],
            recv_sem=self.hop_recv.at[unit, step - 1, way],
            device_id={"dp": self.here.next[way]}, device_id_type=MESH,
        )

    def index(self, step, way):
        return 0 if step == 0 else 2 * step - 1 + way

    def across(self, unit, step, way, arrival=False):
        half = way if step == HALF else None
        target = self.home(unit, self.member(step, way, sibling=arrival), half)
        source = target if arrival else self.held(unit, step, way, half)
        index = self.index(step, way)
        return pltpu.make_async_remote_copy(
            src_ref=source, dst_ref=target, send_sem=self.side_send.at[unit, index],
            recv_sem=self.side_recv.at[unit, index],
            device_id={"dp": self.here.sibling}, device_id_type=MESH,
        )

    def store(self, unit, step, way):
        half = way if step == HALF else None
        return pltpu.make_async_copy(
            self.held(unit, step, way, half), self.home(unit, self.member(step, way), half),
            self.store_sem.at[unit, self.index(step, way)],
        )

    def start(self, unit):
        for way in range(2):
            self.hop(unit, 1, way).start()
        self.across(unit, 0, 0).start()
        if not self.landed(unit):
            self.store(unit, 0, 0).start()

    def step(self, unit, step):
        for way in range(2):
            self.hop(unit, step - 1, way, arrival=True).wait_recv()
            if step <= HALF:
                self.hop(unit, step, way).start()
            self.across(unit, step - 1, way).start()
            if not self.landed(unit):
                self.store(unit, step - 1, way).start()

    def pieces(self):
        return [(0, 0)] + [(step, way) for step in range(1, HALF + 1) for way in range(2)]

    def end(self, unit):
        for step, way in self.pieces():
            self.across(unit, step, way, arrival=True).wait_recv()

    def sent(self, unit):
        for step, way in self.pieces():
            self.across(unit, step, way).wait_send()
            if step:
                self.hop(unit, step, way).wait_send()
            if not self.landed(unit):
                self.store(unit, step, way).wait()


def units_of(chunk, total):
    return min(CHUNK, total - chunk * CHUNK)


def pack_copies(weights, pack, chunks, sem):
    copies = []
    for i, chunk in enumerate(chunks):
        begin, size = chunk * CHUNK, units_of(chunk, weights[0].shape[1])
        for m, ref in enumerate(weights):
            copies.append(pltpu.make_async_copy(
                ref.at[:, begin : begin + size], pack.at[i, :, m * size : (m + 1) * size],
                sem.at[i, m],
            ))
    return copies


LATER = 3
PAIRS = 2
QUARTERS = 4


def forward_kernel(
    cfg, hid, cot, turns, places, bias_q, bias_k, bias_v, gain_a, gain_f,
    wq, wk, wv, wo, wg, wu, wd,
    w_ffn, w_attn, hid_all, cot_all, in_one_t, qrot, krot, vlow, mixed, lse, middle, in_two, vec_ref,
    cos_ref, sin_ref, in_two_t, cot_t,
    wa, qkv, psend, precv, pack, slots, in_one, cots, turned, turned_cot,
    local_sem, pack_sem, store_sem, hop_send, hop_recv, side_send, side_recv, x_send, x_recv, t_sem,
):
    rows, heads, units = cfg
    own_tokens, width = hid.shape
    tokens = 2 * own_tokens
    width_q = heads * HD
    width_qkv = width_q + 2 * HD
    here = Spot(rows)
    shard = here.shard

    own_rows = pl.ds(pl.multiple_of(shard * own_tokens, TILE), own_tokens)
    other_rows = pl.ds(pl.multiple_of((1 - shard) * own_tokens, TILE), own_tokens)
    quarter = own_tokens // QUARTERS

    def quarter_rows(index, side):
        return pl.ds(pl.multiple_of(side * own_tokens + index * quarter, quarter), quarter)

    mine = here.part(here.me)
    attn_copies, column = [], 0
    for i, ref in enumerate((wq, wk, wv, wo)):
        wide = ref.shape[1]
        attn_copies.append(
            pltpu.make_async_copy(ref, wa.at[mine, column : column + wide], local_sem.at[i])
        )
        column += wide
    ffn_copies = pack_copies((wg, wu, wd), pack, range(PAIRS * units), pack_sem)
    own_copies = [
        pltpu.make_async_copy(hid, hid_all.at[own_rows, :], local_sem.at[4]),
        pltpu.make_async_copy(cot, cots.at[own_rows, :], local_sem.at[5]),
    ]
    for copy in attn_copies + own_copies + ffn_copies:
        copy.start()

    column = 0
    for ref in (bias_q, bias_k, bias_v):
        size = ref.shape[0] // 2
        row = ref[...].reshape(1, 2 * size)
        vec_ref[:, column : column + size] = jnp.where(shard == 0, row[:, :size], row[:, size:])
        column += size
    for ref in (gain_a, gain_f):
        vec_ref[:, column : column + width] = ref[...].reshape(1, width)
        column += width
    vec_ref[:, column : column + tokens] = (
        lax.broadcasted_iota(jnp.int32, (1, tokens), 1) - places[...].reshape(1, tokens)
    ).astype(F32)
    bias, gain_one, gain_two, start_of = small_inputs(vec_ref, width_qkv, width)

    here.greet()

    def swap_copy(index, src, dst):
        return pltpu.make_async_remote_copy(
            src_ref=src, dst_ref=dst, send_sem=x_send.at[index], recv_sem=x_recv.at[index],
            device_id={"mp": 1 - shard}, device_id_type=MESH,
        )

    hid_swap = (swap_copy(0, hid, hid_all.at[own_rows, :]), swap_copy(0, hid, hid_all.at[other_rows, :]))
    mix_swap = swap_copy(1, psend, precv)
    two_swap = (
        swap_copy(2, in_two.at[own_rows, :], in_two.at[own_rows, :]),
        swap_copy(2, in_two.at[other_rows, :], in_two.at[other_rows, :]),
    )

    def cot_swap(index, arrival=False):
        ref = cots.at[quarter_rows(index, 1 - shard if arrival else shard), :]
        return swap_copy(3 + index, ref, ref)

    def home(unit, member, half):
        part = here.part(member, half)
        if unit == 0:
            return wa.at[part, :]
        return w_ffn.at[(unit - 1) * PAIRS : unit * PAIRS, part, :]

    def held(unit, step, way, half):
        if unit == 0:
            return home(0, gather.member(step, way), half)
        part = slice(0, rows) if half is None else slice(half * rows // 2, (half + 1) * rows // 2)
        if step == 0:
            return pack.at[(unit - 1) * PAIRS : unit * PAIRS, part, :]
        slot = 2 * HALF - 2 if step == HALF else 2 * (step - 1) + way
        return slots.at[unit - 1, slot, :, part, :]

    gather = Gather(
        here, held, home, lambda unit: unit == 0, hop_send, hop_recv, side_send, side_recv, store_sem
    )
    ffn_units = range(1, units + 1)

    hid_swap[0].start()
    for copy in attn_copies:
        copy.wait()
    gather.start(0)
    at = jnp.broadcast_to(places[...].reshape(1, tokens).astype(F32), (HD, tokens)).T
    angles = at * turns[...].reshape(1, HD)
    cos_ref[...] = jnp.cos(angles)
    lanes = lax.broadcasted_iota(jnp.int32, (tokens, HD), 1)
    sin_ref[...] = jnp.where(lanes < HD // 2, -1.0, 1.0) * jnp.sin(angles)

    for step in range(2, HALF + 1):
        gather.step(0, step)
    for copy in ffn_copies:
        copy.wait()
    for unit in ffn_units:
        gather.start(unit)
    gather.step(0, HALF + 1)

    for copy in own_copies:
        copy.wait()
    hid_swap[1].wait_recv()
    for index in range(QUARTERS - 1):
        cot_swap(index).start()

    @pl.loop(0, tokens // TILE)
    def _(t):
        v = hid_all[tile_of(t), :].astype(F32)
        factor = lax.rsqrt(jnp.mean(v * v, axis=-1, keepdims=True) + EPS)
        in_one[tile_of(t), :] = (v * factor * gain_one).astype(BF16)

    gather.end(0)
    wa_out = pltpu.make_async_copy(wa, w_attn, local_sem.at[6])
    wa_out.start()

    @pl.loop(0, tokens // TILE)
    def _(t):
        part = tile_of(t)
        qkv[part, :] = contract(in_one[part, :], wa[:, 0:width_qkv], 1, 0) + bias
        cosines, sines = cos_ref[part, :], sin_ref[part, :]
        for h in range(heads):
            columns = slice(h * HD, (h + 1) * HD)
            qrot[part, columns] = turn(qkv[part, columns], cosines, sines).astype(BF16)
        krot[part, :] = turn(qkv[part, width_q : width_q + HD], cosines, sines).astype(BF16)
        vlow[part, :] = qkv[part, width_q + HD :].astype(BF16)

    def attend(blocks):
        @pl.loop(0, heads)
        def _(h):
            columns = tile_of(h, HD)
            for i in blocks:
                low, high = key_range(i)
                part = pl.ds(i * BLOCK, BLOCK)
                scores = contract(krot[low:high, :], qrot[part, columns], 1, 1) * SCALE
                scores = jnp.where(visible_keys(start_of(i), low, high, i), scores, -1e30)
                top = jnp.max(scores, axis=0, keepdims=True)
                weights = jnp.exp(scores - top)
                total = jnp.sum(weights, axis=0, keepdims=True)
                probs = (weights * (1.0 / total)).astype(BF16)
                mixed[part, columns] = contract(probs, vlow[low:high, :], 0, 0).astype(BF16)
                lse[h, 0:1, part] = top + jnp.log(total)

    halves = (range(own_tokens // BLOCK), range(own_tokens // BLOCK, tokens // BLOCK))
    for index in range(2):
        @pl.when(shard == index)
        def _():
            attend(halves[1 - index])

    @pl.loop(0, width // TILE)
    def _(n):
        weight = wa[tile_of(n), width_qkv:]
        psend[:, tile_of(n)] = contract(mixed[other_rows, :], weight, 1, 1).astype(BF16)

    mix_swap.start()
    for index in range(2):
        @pl.when(shard == index)
        def _():
            attend(halves[index])

    @pl.loop(0, width // TILE)
    def _(n):
        weight = wa[tile_of(n), width_qkv:]
        middle[:, tile_of(n)] = (
            contract(mixed[own_rows, :], weight, 1, 1) + hid[:, tile_of(n)].astype(F32)
        )

    for unit in ffn_units:
        gather.step(unit, 2)

    def transpose(source, target, first, begin, count):
        @pl.loop(0, width // TILE)
        def _(n):
            for t in range(count):
                part = pl.ds(pl.multiple_of(begin + t * TILE, TILE), TILE)
                target[tile_of(n), part] = source[part, tile_of(n)].T

    transpose(in_one, turned, 0, 0, tokens // TILE)
    one_turned = pltpu.make_async_copy(turned, in_one_t, t_sem.at[0])
    one_turned.start()
    mine_begin, theirs_begin = shard * own_tokens, (1 - shard) * own_tokens
    transpose(cots, turned_cot, 0, mine_begin, own_tokens // TILE)
    for index in range(QUARTERS // 2):
        cot_swap(index, arrival=True).wait_recv()
    transpose(cots, turned_cot, 0, theirs_begin, own_tokens // TILE // 2)

    mix_swap.wait_recv()

    @pl.loop(0, own_tokens // TILE)
    def _(t):
        part = tile_of(t)
        v = middle[part, :] + precv[part, :].astype(F32)
        middle[part, :] = v
        factor = lax.rsqrt(jnp.mean(v * v, axis=-1, keepdims=True) + EPS)
        to = pl.ds(pl.multiple_of(shard * own_tokens + t * TILE, TILE), TILE)
        in_two[to, :] = (v * factor * gain_two).astype(BF16)

    two_swap[0].start()
    cot_swap(QUARTERS - 1).start()
    one_turned.wait()
    for unit in ffn_units:
        gather.step(unit, 3)
    transpose(in_two, turned, 0, mine_begin, own_tokens // TILE)
    for unit in list(ffn_units)[:1]:
        gather.step(unit, 4)
    two_swap[1].wait_recv()
    transpose(in_two, turned, 0, theirs_begin, own_tokens // TILE)
    two_turned = pltpu.make_async_copy(turned, in_two_t, t_sem.at[1])
    two_turned.start()
    for unit in list(ffn_units)[1:]:
        gather.step(unit, 4)
    for index in range(QUARTERS // 2, QUARTERS):
        cot_swap(index, arrival=True).wait_recv()
    transpose(cots, turned_cot, 0, theirs_begin + own_tokens // 2, own_tokens // TILE // 2)
    cot_copies = [
        pltpu.make_async_copy(cots, cot_all, t_sem.at[2]),
        pltpu.make_async_copy(turned_cot, cot_t, t_sem.at[3]),
    ]
    for copy in cot_copies:
        copy.start()
    for unit in ffn_units:
        gather.step(unit, 5)
    for unit in ffn_units:
        gather.end(unit)
    for unit in range(units + 1):
        gather.sent(unit)
    hid_swap[0].wait_send()
    mix_swap.wait_send()
    two_swap[0].wait_send()
    for index in range(QUARTERS):
        cot_swap(index).wait_send()
    for copy in [wa_out, two_turned] + cot_copies:
        copy.wait()


def forward_attention(hidden_in, cotangent, vectors, weights, heads):
    own_tokens, width = hidden_in.shape
    tokens = 2 * own_tokens
    rows = weights[0].shape[0]
    chunks = -(-weights[4].shape[1] // CHUNK)
    units = (chunks - LATER) // PAIRS
    early = units * PAIRS
    width_q = heads * HD
    width_attn = 2 * width_q + 2 * HD
    wide = 3 * CHUNK
    vmem = pl.BlockSpec(memory_space=pltpu.VMEM)
    hbm = pl.BlockSpec(memory_space=pl.ANY)
    dma = pltpu.SemaphoreType.DMA
    shape = jax.ShapeDtypeStruct
    pieces = 2 * HALF + 1
    return pl.pallas_call(
        functools.partial(forward_kernel, (rows, heads, units)),
        in_specs=[vmem, hbm] + [vmem] * 7 + [hbm] * 7,
        out_specs=[hbm, hbm, vmem, hbm, hbm] + [vmem] * 10 + [hbm, hbm],
        out_shape=[
            shape((early, width, wide), BF16),
            shape((width, width_attn), BF16),
            shape((tokens, width), BF16),
            shape((tokens, width), BF16),
            shape((width, tokens), BF16),
            shape((tokens, width_q), BF16),
            shape((tokens, HD), BF16),
            shape((tokens, HD), BF16),
            shape((tokens, width_q), BF16),
            shape((heads, 8, tokens), F32),
            shape((own_tokens, width), F32),
            shape((tokens, width), BF16),
            shape((1, width_q + 2 * HD + 2 * width + tokens), F32),
            shape((tokens, HD), F32),
            shape((tokens, HD), F32),
            shape((width, tokens), BF16),
            shape((width, tokens), BF16),
        ],
        scratch_shapes=[
            pltpu.VMEM((width, width_attn), BF16),
            pltpu.VMEM((tokens, width_q + 2 * HD), F32),
            pltpu.VMEM((own_tokens, width), BF16),
            pltpu.VMEM((own_tokens, width), BF16),
            pltpu.VMEM((early, rows, wide), BF16),
            pltpu.VMEM((units, 2 * HALF - 1, PAIRS, rows, wide), BF16),
            pltpu.VMEM((tokens, width), BF16),
            pltpu.VMEM((tokens, width), BF16),
            pltpu.VMEM((width, tokens), BF16),
            pltpu.VMEM((width, tokens), BF16),
            dma((7,)), dma((early, 3)), dma((units + 1, pieces)),
            dma((units + 1, HALF, 2)), dma((units + 1, HALF, 2)),
            dma((units + 1, pieces)), dma((units + 1, pieces)),
            dma((3 + QUARTERS,)), dma((3 + QUARTERS,)), dma((4,)),
        ],
        compiler_params=pltpu.CompilerParams(
            collective_id=1, has_side_effects=True, vmem_limit_bytes=63 * 2**20
        ),
        cost_estimate=pl.CostEstimate(
            flops=6 * tokens * width * width_attn, bytes_accessed=120 * 2**20, transcendentals=0
        ),
        name="forward_attention",
    )(hidden_in, cotangent, *vectors, *weights)


class Sums:
    def __init__(self, here, own, places, send_sem, recv_sem):
        self.here, self.own, self.places = here, own, places
        self.send_sem, self.recv_sem = send_sem, recv_sem

    def chip(self, step, way):
        distance = HALF - step
        return self.here.chip(distance if way == 0 else CHIPS - distance)

    def copy(self, o, p, step, way, m, columns):
        here, rows = self.here, self.here.rows
        return pltpu.make_async_remote_copy(
            src_ref=self.own.at[o, here.part(self.chip(step, way), way if step == 0 else None), columns],
            dst_ref=self.places.at[p, step, way, 0 : rows // 2 if step == 0 else rows, columns],
            send_sem=self.send_sem.at[p, step, way, m],
            recv_sem=self.recv_sem.at[p, step, way, m],
            device_id={"dp": here.next[way]},
            device_id_type=MESH,
        )

    def columns(self, pieces, m):
        count, size = pieces
        return pl.ds(pl.multiple_of(m * size, HD), size)

    def start(self, o, p, pieces):
        @pl.loop(0, pieces[0])
        def _(m):
            for way in range(2):
                self.copy(o, p, 0, way, m, self.columns(pieces, m)).start()

    def step(self, o, p, step, pieces):
        here, own = self.here, self.own

        @pl.loop(0, pieces[0])
        def _(m):
            columns = self.columns(pieces, m)
            for way in range(2):
                self.copy(o, p, step - 1, way, m, columns).wait()
            for way in range(2):
                part = here.part(self.chip(step, way), way if step == 1 else None)
                size = here.rows // 2 if step == 1 else here.rows
                own[o, part, columns] = (
                    own[o, part, columns].astype(F32)
                    + self.places[p, step - 1, way, 0:size, columns].astype(F32)
                ).astype(BF16)
                self.copy(o, p, step, way, m, columns).start()

    def end(self, o, p, pieces, target):
        own, last = self.own, HALF - 1
        part = self.here.part(self.here.chip(0))

        @pl.loop(0, pieces[0])
        def _(m):
            columns = self.columns(pieces, m)
            for way in range(2):
                self.copy(o, p, last, way, m, columns).wait()
            target[:, columns] = (
                own[o, part, columns].astype(F32)
                + self.places[p, last, 0, :, columns].astype(F32)
                + self.places[p, last, 1, :, columns].astype(F32)
            )


EVENTS = {
    (0, "a"): "G11 G21",
    (0, "c"): "G02",
    (0, "f"): "G12",
    (1, "a"): "R00",
    (1, "b"): "G22",
    (1, "e"): "G03",
    (2, "a"): "R10",
    (2, "b"): "G13",
    (2, "c"): "R01 G23",
    (3, "a"): "G04 R11",
    (3, "c"): "G14",
    (4, "a"): "R02",
    (4, "b"): "G24",
    (4, "c"): "G05",
    (4, "e"): "R12",
    (4, "f"): "G15",
    (5, "a"): "R03 R20",
    (5, "c"): "G25 R13",
    (6, "0a"): "R04 R21",
    (6, "1a"): "R14 R22",
    (6, "1b"): "R30",
    (6, "2b"): "R23",
    (7, "0a"): "R31",
    (7, "1a"): "R24 R32 R40",
    (7, "2a"): "R33",
    (7, "2b"): "R41",
    (8, "1a"): "R34 R42",
    (8, "1b"): "R43",
    (8, "2b"): "R44",
}
SETS = 3


def ffn_kernel(
    cfg, in2_hbm, cot_hbm, in2t_hbm, cott_hbm, w_ffn, w_attn, wg, wu, wd,
    hiddens, w_down, gin_own, later, grad_g, grad_u, grad_d, w_other, w_late,
    in2, cot, in2t, cott, wbuf, acts, gin, own, sent, sib, ring, stage, pack,
    in_sem, w_sem, sib_send, sib_recv, ring_send, ring_recv, out_sem, g_sem, end_sem, free_sem,
    pack_sem, store_sem, hop_send, hop_recv, side_send, side_recv, park_sem, fetch_sem, hid_sem, down_sem,
):
    rows, chunks, total = cfg
    grads = (grad_g, grad_u, grad_d)
    tokens, width = in2.shape
    side_rows = CHIPS * rows
    own_tokens = tokens // 2
    first = chunks - LATER
    rings = first - 1
    here = Spot(rows)
    shard = here.shard
    sums = Sums(here, own, ring, ring_send, ring_recv)
    ring_pieces = (3, CHUNK)
    own_rows = pl.ds(pl.multiple_of(shard * own_tokens, TILE), own_tokens)
    other_rows = pl.ds(pl.multiple_of((1 - shard) * own_tokens, TILE), own_tokens)

    def size_of(i):
        return units_of(first + i, total)

    def load(chunk, s):
        return pltpu.make_async_copy(w_ffn.at[chunk], wbuf.at[s], w_sem.at[s])

    def load_late(i, s):
        columns = slice(0, 3 * size_of(i))
        return pltpu.make_async_copy(w_late.at[i, :, columns], wbuf.at[s, :, columns], w_sem.at[s])

    def down_copies(chunk, s, size=CHUNK):
        top = width // 2
        return [
            pltpu.make_async_copy(
                wbuf.at[s, h * top : (h + 1) * top, 2 * size : 3 * size],
                w_down.at[chunk, :, h * CHUNK : h * CHUNK + size], down_sem.at[s, h],
            )
            for h in range(2)
        ]

    def hidden_copies(index, chunk, size=CHUNK):
        return [
            pltpu.make_async_copy(
                acts.at[index, h * own_tokens : (h + 1) * own_tokens, 2 * size : 3 * size],
                hiddens.at[chunk, :, h * CHUNK : h * CHUNK + size], hid_sem.at[index, h],
            )
            for h in range(2)
        ]

    def home(unit, member, half):
        return w_late.at[unit, here.part(member, half), 0 : 3 * size_of(unit)]

    def held(unit, step, way, half):
        size = rows if half is None else rows // 2
        columns = slice(0, 3 * size_of(unit))
        if step == 0:
            return pack.at[unit, :, columns]
        slot = 2 * (step - 1) + way
        whole = 2 * HALF - 2
        if unit < 2:
            buffer, begin = 1 + unit, (whole if step == HALF else slot) * rows
            offset = 0
            if half is not None:
                offset = half * size
        else:
            base = (whole + 1) * rows
            if step == HALF:
                buffer, begin, offset = 1 + way, base + whole // 2 * rows, 0
            else:
                buffer, begin = 1 + slot // (whole // 2), base + slot % (whole // 2) * rows
                offset = 0 if half is None else half * size
        return acts.at[buffer, begin + offset : begin + offset + size, columns]

    gather = Gather(
        here, held, home, lambda unit: False, hop_send, hop_recv, side_send, side_recv, store_sem
    )
    own_blocks = pack_copies((wg, wu, wd), pack, range(first, chunks), pack_sem)

    inputs = [
        pltpu.make_async_copy(in2_hbm, in2, in_sem.at[0]),
        pltpu.make_async_copy(cot_hbm, cot, in_sem.at[1]),
    ]
    turned = []
    for i, (source, target) in enumerate(((in2t_hbm, in2t), (cott_hbm, cott))):
        for side in range(2):
            for chip in range(CHIPS):
                member = 2 * chip + (here.core if side == 0 else 1 - here.core)
                begin = side * side_rows + chip * rows
                turned.append(pltpu.make_async_copy(
                    source.at[here.part(member), :], target.at[begin : begin + rows, :],
                    in_sem.at[2 + i],
                ))
    for copy in own_blocks + [load(0, 0)] + inputs:
        copy.start()
    here.greet()
    for copy in own_blocks:
        copy.wait()
    gather.start(0)

    def result_copies(chunk):
        return [
            pltpu.make_async_copy(
                stage.at[:, m * CHUNK : (m + 1) * CHUNK],
                grads[m].at[:, tile_of(chunk, CHUNK)],
                out_sem.at[m],
            )
            for m in range(3)
        ]

    def fetch(chunk):
        return pltpu.make_async_copy(
            later.at[chunk - SETS], own.at[chunk % SETS], fetch_sem.at[chunk % SETS]
        )

    def park(chunk, p, early, size=CHUNK):
        columns = slice(0, 3 * size)
        target = own.at[chunk] if early else later.at[chunk - SETS, :, columns]
        return pltpu.make_async_copy(sib.at[p, :, columns], target, park_sem.at[p])

    def ring_event(chunk, step):
        o, p = chunk % SETS, chunk % 2
        if step == 0:
            if chunk >= SETS:
                fetch(chunk).wait()
            sums.start(o, p, ring_pieces)
        elif step < HALF:
            sums.step(o, p, step, ring_pieces)
        else:
            if chunk:
                for copy in result_copies(chunk - 1):
                    copy.wait()
            sums.end(o, p, ring_pieces, stage)
            for copy in result_copies(chunk):
                copy.start()
            if chunk + SETS < rings:
                fetch(chunk + SETS).start()

    def run(events):
        for event in events.split():
            index, step = int(event[1]), int(event[2])
            if event[0] == "R":
                ring_event(index, step)
            elif step == 1:
                gather.start(index)
            else:
                gather.step(index, step)

    def sib_copy(p, m, size):
        columns = slice(m * size, (m + 1) * size)
        return pltpu.make_async_remote_copy(
            src_ref=sent.at[:, columns],
            dst_ref=sib.at[p, :, columns],
            send_sem=sib_send.at[m],
            recv_sem=sib_recv.at[p, m],
            device_id={"dp": here.sibling},
            device_id_type=MESH,
        )

    def weight_copy():
        return pltpu.make_async_remote_copy(
            src_ref=w_attn.at[:, 0 : w_other.shape[1]], dst_ref=w_other,
            send_sem=g_sem.at[2], recv_sem=g_sem.at[3],
            device_id={"mp": 1 - shard}, device_id_type=MESH,
        )

    def gin_copy():
        return pltpu.make_async_remote_copy(
            src_ref=in2.at[other_rows, :], dst_ref=cot.at[own_rows, :],
            send_sem=g_sem.at[0], recv_sem=g_sem.at[1],
            device_id={"mp": 1 - shard}, device_id_type=MESH,
        )

    def forward(index, part, s, size=CHUNK):
        for begin in range(0, size, TILE):
            stop = min(begin + TILE, size)
            gates, ups, downs = (slice(m * size + begin, m * size + stop) for m in range(3))
            gate = contract(in2[part, :], wbuf[s, :, gates], 1, 0)
            up = contract(in2[part, :], wbuf[s, :, ups], 1, 0)
            grad = contract(cot[part, :], wbuf[s, :, downs], 1, 0)
            sig = 0.5 * jnp.tanh(0.5 * gate) + 0.5
            swish = gate * sig
            acts[index, part, downs] = (swish * up).astype(BF16)
            acts[index, part, gates] = (grad * up * (sig + swish - swish * sig)).astype(BF16)
            acts[index, part, ups] = (grad * swish).astype(BF16)

    def back_gin(index, part, s, size=CHUNK):
        @pl.loop(0, width // TILE)
        def _(n):
            gin[part, tile_of(n)] += contract(
                acts[index, part, 0 : 2 * size], wbuf[s, tile_of(n), 0 : 2 * size], 1, 1
            )

    def weight_grads(index, p, between, size=CHUNK):
        for m, left in enumerate((in2t, in2t, cott)):
            columns = slice(m * size, (m + 1) * size)
            sent[:, columns] = contract(
                left[side_rows:, :], acts[index, :, columns], 1, 0
            ).astype(BF16)
            sib_copy(p, m, size).start()
        between()
        for m, left in enumerate((in2t, in2t, cott)):
            columns = slice(m * size, (m + 1) * size)
            sib_copy(p, m, size).wait()
            sib[p, :, columns] = (
                contract(left[0:side_rows, :], acts[index, :, columns], 1, 0)
                + sib[p, :, columns].astype(F32)
            ).astype(BF16)

    gin[...] = jnp.zeros_like(gin)
    for copy in inputs:
        copy.wait()
    for copy in turned:
        copy.start()

    def at_point(j, point):
        for chunk in range(first):
            if (chunk, point) in EVENTS:
                @pl.when(j == chunk)
                def _():
                    run(EVENTS[chunk, point])

    weight_copy().start()

    def start(copies):
        for copy in copies:
            copy.start()

    def wait(copies):
        for copy in copies:
            copy.wait()

    @pl.loop(0, first)
    def _(j):
        p = lax.rem(j, 2)
        load(j, p).wait()
        start(down_copies(j, p))

        @pl.when(j >= 1)
        def _():
            wait(down_copies(j - 1, 1 - p))
            wait(hidden_copies(0, j - 1))

        @pl.when(j + 1 < first)
        def _():
            load(j + 1, 1 - p).start()

        @pl.when(j == first - 1)
        def _():
            gather.end(0)
            gather.sent(0)
            load_late(0, 1 - p).start()

        forward(0, slice(0, own_tokens), p)

        @pl.when((j >= 1) & (j <= SETS))
        def _():
            park(j - 1, 1 - p, True).wait()

        @pl.when(j > SETS)
        def _():
            park(j - 1, 1 - p, False).wait()

        at_point(j, "a")
        forward(0, slice(own_tokens, tokens), p)
        start(hidden_copies(0, j))
        at_point(j, "b")
        back_gin(0, slice(0, tokens), p)
        at_point(j, "c")

        @pl.when(j == 0)
        def _():
            for i, ref in enumerate((in2t, cott)):
                pltpu.make_async_copy(ref, ref, in_sem.at[2 + i]).wait()

        weight_grads(0, p, lambda: at_point(j, "e"))

        @pl.when(j < SETS)
        def _():
            park(j, p, True).start()

        @pl.when(j >= SETS)
        def _():
            park(j, p, False).start()

        at_point(j, "f")

    wait(hidden_copies(0, first - 1))
    wait(down_copies(first - 1, (first - 1) % 2))
    for unit in range(1, LATER):
        gather.end(unit)
        gather.sent(unit)

    for half in range(2):
        part = (other_rows, own_rows)[half]
        for i in range(LATER):
            size = size_of(i)
            turn = half * LATER + i
            s = (first + turn) % 2
            load_late(i, s).wait()
            if half == 0:
                start(down_copies(first + i, s, size))
            if 0 < turn <= LATER:
                wait(down_copies(first + turn - 1, 1 - s, size_of(turn - 1)))
            if turn + 1 < 2 * LATER:
                load_late((i + 1) % LATER, 1 - s).start()
            forward(i, part, s, size)
            if half == 1:
                start(hidden_copies(i, first + i, size))
            run(EVENTS.get((first + half, f"{i}a"), ""))
            back_gin(i, part, s, size)
            run(EVENTS.get((first + half, f"{i}b"), ""))
        if half == 0:
            pl.semaphore_signal(
                free_sem, inc=1, device_id={"mp": 1 - shard}, device_id_type=MESH
            )

            @pl.loop(0, own_tokens // TILE)
            def _(t):
                of = pl.ds(pl.multiple_of((1 - shard) * own_tokens + t * TILE, TILE), TILE)
                in2[of, :] = gin[of, :].astype(BF16)

            pl.semaphore_wait(free_sem, 1)
            gin_copy().start()

    for i in range(LATER):
        chunk, size = first + i, size_of(i)
        p = chunk % 2
        park(chunk - 1, 1 - p, False).wait()
        weight_grads(i, p, lambda: run(EVENTS.get((first + 2, f"{i}a"), "")), size)
        park(chunk, p, False, size).start()
        run(EVENTS.get((first + 2, f"{i}b"), ""))
    gin_copy().wait()

    @pl.loop(0, own_tokens // TILE)
    def _(t):
        of = pl.ds(pl.multiple_of(shard * own_tokens + t * TILE, TILE), TILE)
        at = pl.ds(pl.multiple_of((1 - shard) * own_tokens + t * TILE, TILE), TILE)
        gin[of, :] = gin[of, :] + cot[at, :].astype(F32)

    gin_out = pltpu.make_async_copy(gin.at[own_rows, :], gin_own, end_sem.at[0])
    gin_out.start()
    weight_copy().wait()
    last_park = park(chunks - 1, (chunks - 1) % 2, False, size_of(LATER - 1))
    for copy in [gin_out, last_park] + result_copies(rings - 1):
        copy.wait()
    for i in range(LATER):
        wait(hidden_copies(i, first + i, size_of(i)))


def feed_forward(inputs_two, grad_ffn, in_two_t, cot_t, w_ffn, w_attn, width_qkv, weights):
    tokens, width = inputs_two.shape
    rows = weights[0].shape[0]
    chunks = w_ffn.shape[0] + LATER
    pieces = 2 * HALF + 1
    hbm = pl.BlockSpec(memory_space=pl.ANY)
    side_rows, wide = CHIPS * rows, 3 * CHUNK
    dma = pltpu.SemaphoreType.DMA
    shape = jax.ShapeDtypeStruct
    half = (tokens // 2, width)
    return pl.pallas_call(
        functools.partial(ffn_kernel, (rows, chunks, weights[0].shape[1])),
        in_specs=[hbm] * 9,
        out_specs=[hbm] * 9,
        out_shape=[
            shape((chunks, tokens // 2, 2 * CHUNK), BF16),
            shape((chunks, width // 2, 2 * CHUNK), BF16), shape(half, F32),
            shape((chunks - SETS, side_rows, wide), BF16),
        ] + [shape((rows, (chunks - LATER - 1) * CHUNK), F32)] * 3 + [
            shape((width, width_qkv), BF16),
            shape((LATER, width, wide), BF16),
        ],
        scratch_shapes=[
            pltpu.VMEM((tokens, width), BF16),
            pltpu.VMEM((tokens, width), BF16),
            pltpu.VMEM((width, tokens), BF16),
            pltpu.VMEM((width, tokens), BF16),
            pltpu.VMEM((2, width, wide), BF16),
            pltpu.VMEM((LATER, tokens, wide), BF16),
            pltpu.VMEM((tokens, width), F32),
            pltpu.VMEM((SETS, side_rows, wide), BF16),
            pltpu.VMEM((side_rows, wide), BF16),
            pltpu.VMEM((2, side_rows, wide), BF16),
            pltpu.VMEM((2, HALF, 2, rows, wide), BF16),
            pltpu.VMEM((rows, wide), F32),
            pltpu.VMEM((LATER, rows, wide), BF16),
            dma((4,)), dma((2,)), dma((3,)), dma((2, 3)),
            dma((2, HALF, 2, 3)), dma((2, HALF, 2, 3)), dma((3,)), dma((4,)), dma((1,)),
            pltpu.SemaphoreType.REGULAR,
            dma((LATER, 3)), dma((LATER, pieces)), dma((LATER, HALF, 2)), dma((LATER, HALF, 2)),
            dma((LATER, pieces)), dma((LATER, pieces)), dma((2,)), dma((SETS,)), dma((LATER, 2)), dma((2, 2)),
        ],
        compiler_params=pltpu.CompilerParams(
            collective_id=2, has_side_effects=True, vmem_limit_bytes=63 * 2**20
        ),
        cost_estimate=pl.CostEstimate(
            flops=18 * tokens * width * chunks * CHUNK, bytes_accessed=80 * 2**20,
            transcendentals=tokens * chunks * CHUNK,
        ),
        name="feed_forward",
    )(inputs_two, grad_ffn, in_two_t, cot_t, w_ffn, w_attn, *weights)


JOBS = 1 + LATER


BACK_EVENTS = {
    "w0": "01 11",
    "w1": "20",
    "w2": "02",
    "w4": "12",
    "w6": "21",
    "w8": "03",
    "w9": "13",
    "h0": "22",
    "h3": "04",
    "h4": "30",
    "h5": "14",
    "o": "23 31",
    "q1": "40",
    "t1": "24",
    "t2": "32",
    "t3": "41",
    "g": "33",
    "b": "42",
    "u1": "50 34 43",
    "l0": "51",
    "l2": "44 52 53",
    "z1": "54",
}


def backward_kernel(
    cfg, later, gin_hbm, middle_hbm, cot_hbm, hiddens, w_down, w_other, w_attn, qrot_hbm, krot_hbm,
    vlow_hbm, lse_hbm, mixed_hbm, in_one_t, hid_hbm, cos_ref, sin_ref, vec_ref,
    layer_out, grad_input, small_out, grad_g, grad_u, grad_d, grad_qkv, grad_out, kept,
    own, ring, sent, sib, lefts, gin, middle, tall, wa, qrot, krot, vlow, lse, mixed,
    gmix, dqkv, gk, gv, osend, orecv, cots, got, stage, small, small_got,
    in_sem, ring_send, ring_recv, sib_send, sib_recv, x_send, x_recv, out_sem, s_send, s_recv, down_sem, hid_sem,
):
    rows, heads, skip, tail = cfg
    grads = (grad_g, grad_u, grad_d)
    own_tokens, width = gin.shape
    tokens = 2 * own_tokens
    width_q = heads * HD
    width_qkv = width_q + 2 * HD
    side_rows = CHIPS * rows
    _, gain_one, gain_two, start_of = small_inputs(vec_ref, width_qkv, width)
    here = Spot(rows)
    shard, me = here.shard, here.me
    sums = Sums(here, own, ring, ring_send, ring_recv)
    wide_qkv, wide_out = (2, width_qkv // 2), (2, width_q // 2)
    pieces = [(1, 3 * CHUNK)] * (JOBS - 1) + [(1, 3 * tail), (1, width_qkv), (1, width_q)]
    own_rows = pl.ds(pl.multiple_of(shard * own_tokens, TILE), own_tokens)
    other_rows = pl.ds(pl.multiple_of((1 - shard) * own_tokens, TILE), own_tokens)

    def at_own(t, size=TILE):
        return pl.ds(pl.multiple_of(shard * own_tokens + t * size, size), size)

    def at_other(t, size=TILE):
        return pl.ds(pl.multiple_of((1 - shard) * own_tokens + t * size, size), size)

    def get(index, source, target):
        return pltpu.make_async_copy(source, target, in_sem.at[index])

    sums_in = [get(i, later.at[skip + i], own.at[i]) for i in range(3)]
    norm_in = [get(3, gin_hbm, gin), get(4, middle_hbm, middle), get(5, cot_hbm, cots)]
    rest_in = [
        get(7, w_attn, wa), get(8, qrot_hbm, qrot), get(9, krot_hbm, krot), get(10, vlow_hbm, vlow),
        get(11, lse_hbm, lse), get(12, mixed_hbm, mixed),
    ]
    for copy in sums_in[:2] + norm_in + sums_in[2:] + rest_in:
        copy.start()
    for side in range(2):
        for chip in range(CHIPS):
            member = 2 * chip + (here.core if side == 0 else 1 - here.core)
            begin = side * side_rows + chip * rows
            get(13, in_one_t.at[here.part(member), :], lefts.at[0, begin : begin + rows, :]).start()

    def bit(value):
        return lax.rem(lax.div(me, value), 2)

    def flipped(*values):
        return me + sum(value - 2 * value * bit(value) for value in values)

    ranks = (here.core + 2 * shard, bit(2) + 2 * bit(4), bit(8))
    partners = (
        ({"dp": flipped(1)}, {"mp": 1 - shard}, {"dp": flipped(1), "mp": 1 - shard}),
        ({"dp": flipped(2)}, {"dp": flipped(4)}, {"dp": flipped(2, 4)}),
        ({"dp": flipped(8)},),
    )

    def rank_of(group, k):
        rank = ranks[group]
        return (rank + 1 - 2 * lax.rem(rank, 2), rank + 2 - 4 * lax.div(rank, 2), 3 - rank)[k]

    barrier = pltpu.get_barrier_semaphore()
    greeted = [p for group in partners for p in group] + [{"dp": n} for n in here.next]
    for target in greeted:
        pl.semaphore_signal(barrier, inc=1, device_id=target, device_id_type=MESH)
    pl.semaphore_wait(barrier, len(greeted))

    def swap_copy(index, src, dst):
        return pltpu.make_async_remote_copy(
            src_ref=src, dst_ref=dst, send_sem=x_send.at[index], recv_sem=x_recv.at[index],
            device_id={"mp": 1 - shard}, device_id_type=MESH,
        )

    some = own_tokens // 2

    def out_swap(index):
        part = slice(index * some, (index + 1) * some)
        return swap_copy(index, osend.at[part, :], orecv.at[part, :])

    half_tiles = own_tokens // TILE

    def attn_swap(t):
        return swap_copy(2 + t, tall.at[at_own(t), :], tall.at[at_own(t), :])

    def attn_got(t):
        return swap_copy(2 + t, tall.at[at_other(t), :], tall.at[at_other(t), :])

    one_swap = swap_copy(2 + half_tiles, dqkv.at[other_rows, :], got)

    def result_copies(job):
        if job < JOBS:
            size = CHUNK if job + 1 < JOBS else tail
            return [
                pltpu.make_async_copy(
                    stage.at[:, m * size : (m + 1) * size],
                    grads[m].at[:, job * CHUNK : job * CHUNK + size], out_sem.at[m],
                )
                for m in range(3)
            ]
        target = (grad_qkv, grad_out)[job - JOBS]
        return [pltpu.make_async_copy(stage.at[:, 0 : target.shape[1]], target, out_sem.at[0])]

    last_in = get(0, later.at[skip + 3, :, 0 : 3 * tail], own.at[0, :, 0 : 3 * tail])

    def run(point):
        for event in BACK_EVENTS.get(point, "").split():
            job, step = int(event[0]), int(event[1])
            o = p = job % 3
            if step == 0:
                if job == 2:
                    sums_in[2].wait()
                if job == 3:
                    last_in.wait()
                sums.start(o, p, pieces[job])
            elif step < HALF:
                sums.step(o, p, step, pieces[job])
            else:
                if job:
                    for copy in result_copies(job - 1):
                        copy.wait()
                sums.end(o, p, pieces[job], stage)
                for copy in result_copies(job):
                    copy.start()
                if job == 0:
                    last_in.start()

    for i in range(2):
        sums_in[i].wait()
        sums.start(i, i, pieces[i])

    for copy in norm_in:
        copy.wait()
    small[0, :, :] = jnp.zeros_like(small[0])

    @pl.loop(0, half_tiles)
    def _(t):
        part = tile_of(t)
        v = middle[part, :]
        factor = lax.rsqrt(jnp.mean(v * v, axis=-1, keepdims=True) + EPS)
        unit = v * factor
        e = gin[part, :]
        scaled = e * gain_two
        inner = jnp.mean(scaled * unit, axis=-1, keepdims=True)
        total = cots[part, :].astype(F32) + factor * (scaled - unit * inner)
        middle[part, :] = total
        gin[part, :] = v
        tall[at_own(t), :] = total.astype(BF16)
        attn_swap(t).start()
        small[0, 1:2, :] += jnp.sum(e * unit, axis=0, keepdims=True)

    keep = pltpu.make_async_copy(middle, kept, out_sem.at[5])
    keep.start()
    keep.wait()
    middle[...] = jnp.zeros_like(middle)
    chunks = w_down.shape[0]
    top = width // 2

    def down_in(chunk):
        slot = chunk % 2
        weight_to = lefts.at[1, slot * top : (slot + 1) * top, :]
        hidden_to = dqkv.at[slot * own_tokens : (slot + 1) * own_tokens, :]
        if chunk + 1 < chunks:
            parts = [slice(0, 2 * CHUNK)]
        else:
            parts = [slice(h * CHUNK, h * CHUNK + tail) for h in range(2)]
        return [
            pltpu.make_async_copy(source.at[chunk, :, part], target.at[:, part], sem.at[slot, i])
            for i, part in enumerate(parts)
            for source, target, sem in (
                (w_down, weight_to, down_sem), (hiddens, hidden_to, hid_sem)
            )
        ]

    for copy in down_in(0):
        copy.start()
    for chunk in range(chunks):
        if chunk + 1 < chunks:
            for copy in down_in(chunk + 1):
                copy.start()
        for copy in down_in(chunk):
            copy.wait()
        slot, size = chunk % 2, CHUNK if chunk + 1 < chunks else tail
        part = slice(slot * own_tokens, (slot + 1) * own_tokens)
        own_columns, other_columns = (
            pl.ds(pl.multiple_of(side * CHUNK, CHUNK), size) for side in (shard, 1 - shard)
        )
        for h in range(2):
            @pl.loop(0, top // TILE)
            def _(n):
                rows_of = pl.ds(pl.multiple_of(slot * top + n * TILE, TILE), TILE)
                at = pl.ds(pl.multiple_of(h * top + n * TILE, TILE), TILE)
                weight = lefts[1, rows_of, h * CHUNK : h * CHUNK + size]
                middle[:, at] += contract(dqkv[part, other_columns], weight, 1, 1)
                gin[:, at] += contract(dqkv[part, own_columns], weight, 1, 1)

        run(f"w{chunk}")

    osend[...] = middle[...].astype(BF16)
    out_swap(0).start()
    run("w9")

    for copy in rest_in:
        copy.wait()
    for t in range(half_tiles):
        attn_got(t).wait_recv()

    @pl.loop(0, tokens // TILE)
    def _(t):
        gmix[tile_of(t), :] = contract(tall[tile_of(t), :], wa[:, width_qkv:], 1, 0).astype(BF16)

    gk[...] = jnp.zeros_like(gk)
    gv[...] = jnp.zeros_like(gv)

    @pl.loop(0, heads)
    def _(h):
        columns = tile_of(h, HD)
        for i in range(SEQ_LEN // BLOCK):
            low, high = key_range(i)
            part = pl.ds(i * BLOCK, BLOCK)
            query, grad = qrot[part, columns], gmix[part, columns]
            keys = krot[low:high, :]
            scores = contract(keys, query, 1, 1) * SCALE
            seen = visible_keys(start_of(i), low, high, i)
            probs = jnp.where(seen, jnp.exp(scores - lse[h, 0:1, part]), 0.0)
            grad_probs = contract(vlow[low:high, :], grad, 1, 1)
            row_term = jnp.sum(probs * grad_probs, axis=0, keepdims=True)
            grad_scores = (probs * (grad_probs - row_term)).astype(BF16)
            gk[low:high, :] += contract(grad_scores, query, 1, 0)
            gv[low:high, :] += contract(probs.astype(BF16), grad, 1, 0)
            dqkv[part, columns] = turn(
                contract(grad_scores, keys, 0, 0) * SCALE, cos_ref[part, :], -sin_ref[part, :]
            ).astype(BF16)

        for head in range(heads):
            if f"h{head}" in BACK_EVENTS:
                @pl.when(h == head)
                def _():
                    run(f"h{head}")

    dqkv[:, width_q : width_q + HD] = turn(gk[...] * SCALE, cos_ref[...], -sin_ref[...]).astype(BF16)
    dqkv[:, width_q + HD :] = gv[...].astype(BF16)

    one_swap.start()
    out_swap(1).start()
    run("o")

    side_sent = (sent, gmix.at[0:side_rows, :])
    side_got = (sib, qrot.at[0:side_rows, :])

    def side_copy(job, m, columns):
        return pltpu.make_async_remote_copy(
            src_ref=side_sent[job].at[:, columns],
            dst_ref=side_got[job].at[:, columns],
            send_sem=sib_send.at[job, m],
            recv_sem=sib_recv.at[job, m],
            device_id={"dp": here.sibling},
            device_id_type=MESH,
        )

    get(13, lefts.at[0], lefts.at[0]).wait()

    def send_side(job, left, right, pieces):
        for m in range(pieces[0]):
            columns = slice(m * pieces[1], (m + 1) * pieces[1])
            side_sent[job][:, columns] = contract(
                lefts[left, side_rows:, :], right[:, columns], 1, 0
            ).astype(BF16)
            side_copy(job, m, columns).start()

    def own_side(job, left, right, pieces, o):
        for m in range(pieces[0]):
            columns = slice(m * pieces[1], (m + 1) * pieces[1])
            side_copy(job, m, columns).wait()
            own[o, :, columns] = (
                contract(lefts[left, 0:side_rows, :], right[:, columns], 1, 0)
                + side_got[job][:, columns].astype(F32)
            ).astype(BF16)

    send_side(0, 0, dqkv, wide_qkv)
    run("q0")
    own_side(0, 0, dqkv, wide_qkv, 1)
    other_in = get(6, w_other, lefts.at[0])
    other_in.start()
    run("q1")

    for group in range(width // (4 * rows)):
        @pl.loop(0, tokens // TILE)
        def _(t):
            part = tile_of(t)
            turned = tall[part, group * 4 * rows : (group + 1) * 4 * rows].T
            for k in range(4):
                chip, odd = (4 * group + k) // 2, k % 2
                side = odd + here.core - 2 * odd * here.core
                to = pl.ds(pl.multiple_of(side * side_rows + chip * rows, 16), rows)
                lefts[1, to, part] = turned[k * rows : (k + 1) * rows, :]

        run(f"t{group}")

    for t in range(half_tiles):
        attn_swap(t).wait_send()
    hid_in = get(15, hid_hbm, tall)
    hid_in.start()

    fac = gk
    hid_in.wait()

    @pl.loop(0, tokens // TILE)
    def _(t):
        v = tall[tile_of(t), :].astype(F32)
        factor = lax.rsqrt(jnp.mean(v * v, axis=-1, keepdims=True) + EPS)
        fac[tile_of(t), :] = jnp.broadcast_to(factor, (TILE, HD))

    run("f")

    @pl.loop(0, width // TILE)
    def _(n):
        e = contract(dqkv[other_rows, :], wa[tile_of(n), 0:width_qkv], 1, 1)
        unit = tall[other_rows, tile_of(n)].astype(F32) * fac[other_rows, 0:1]
        small[0, 0:1, tile_of(n)] += jnp.sum(e * unit, axis=0, keepdims=True)

    run("g")

    @pl.loop(0, width // TILE)
    def _(n):
        e = contract(dqkv[own_rows, :], wa[tile_of(n), 0:width_qkv], 1, 1)
        middle[:, tile_of(n)] = e
        unit = tall[own_rows, tile_of(n)].astype(F32) * fac[own_rows, 0:1]
        small[0, 0:1, tile_of(n)] += jnp.sum(e * unit, axis=0, keepdims=True)

    @pl.loop(0, tokens // TILE)
    def _(t):
        bias = jnp.sum(dqkv[tile_of(t), :].astype(F32), axis=0, keepdims=True)
        at_query = pl.ds(pl.multiple_of(shard * width_q, HD), width_q)
        small[0, 2:3, at_query] += bias[:, 0:width_q]
        small[0, 3:4, tile_of(shard, HD)] += bias[:, width_q : width_q + HD]
        small[0, 3:4, tile_of(shard + 2, HD)] += bias[:, width_q + HD :]

    run("b")

    def small_copy(group, k):
        return pltpu.make_async_remote_copy(
            src_ref=small.at[group], dst_ref=small_got.at[group, ranks[group]],
            send_sem=s_send.at[group, k], recv_sem=s_recv.at[group, ranks[group]],
            device_id=partners[group][k], device_id_type=MESH,
        )

    def small_start(group):
        for k in range(len(partners[group])):
            small_copy(group, k).start()
        small_got[group, ranks[group]] = small[group]

    def small_end(group):
        count = len(partners[group])
        for k in range(count):
            ref = small_got.at[group, rank_of(group, k)]
            pltpu.make_async_remote_copy(
                src_ref=ref, dst_ref=ref, send_sem=s_send.at[group, k],
                recv_sem=s_recv.at[group, rank_of(group, k)],
                device_id=partners[group][k], device_id_type=MESH,
            ).wait_recv()
            small_copy(group, k).wait_send()
        total = small_got[group, 0]
        for rank in range(1, count + 1):
            total = total + small_got[group, rank]
        small[group + 1] = total

    small_start(0)
    send_side(1, 1, mixed, wide_out)
    run("u0")
    own_side(1, 1, mixed, wide_out, 2)
    small_end(0)
    small_start(1)
    run("u1")

    def layer_rows(index):
        part = slice(index * some, (index + 1) * some)
        out_swap(index).wait()
        orecv[part, :] = (gin[part, :] + orecv[part, :].astype(F32)).astype(BF16)
        copy = pltpu.make_async_copy(
            orecv.at[part, :], layer_out.at[part, :], out_sem.at[(3, 6)[index]]
        )
        copy.start()
        return copy

    def keep_in(index):
        part = slice(index * some, (index + 1) * some)
        return get(14, kept.at[part, :], gin.at[0:some, :])

    layer_copies = [layer_rows(0)]
    keep_in(0).start()
    run("l0")
    small_end(1)
    small_start(2)
    run("l1")
    small_end(2)
    run("l2")
    small_out[...] = small[3]

    one_swap.wait()
    other_in.wait()

    @pl.loop(0, width // TILE)
    def _(n):
        middle[:, tile_of(n)] += contract(got[...], lefts[0, tile_of(n), :], 1, 1)

    for index in range(2):
        part = slice(index * some, (index + 1) * some)
        of = pl.ds(pl.multiple_of(shard * own_tokens + index * some, some), some)
        if index:
            keep_in(index).start()
        keep_in(index).wait()
        factor = fac[of, 0:1]
        unit = tall[of, :].astype(F32) * factor
        scaled = middle[part, :] * gain_one
        inner = jnp.mean(scaled * unit, axis=-1, keepdims=True)
        cots[part, :] = (gin[0:some, :] + factor * (scaled - unit * inner)).astype(BF16)

    input_copy = pltpu.make_async_copy(cots, grad_input, out_sem.at[4])
    input_copy.start()
    layer_copies.append(layer_rows(1))
    run("z1")
    for copy in [input_copy] + layer_copies + result_copies(JOBS + 1):
        copy.wait()


def attention_back(
    later, gin, middle, cot, hiddens, w_down, w_other, forward, cos2, sin2, vector, tail
):
    w_attn, qrot, krot, vlow, lse, mixed, in_one_t, hid_all = forward
    own_tokens, width = cot.shape
    tokens = 2 * own_tokens
    heads = lse.shape[0]
    width_q = heads * HD
    width_qkv = width_q + 2 * HD
    side_rows, wide = later.shape[1:]
    rows = side_rows // CHIPS
    vmem = pl.BlockSpec(memory_space=pltpu.VMEM)
    hbm = pl.BlockSpec(memory_space=pl.ANY)
    dma = pltpu.SemaphoreType.DMA
    shape = jax.ShapeDtypeStruct
    half = (own_tokens, width)
    n_swaps = own_tokens // TILE + 3
    return pl.pallas_call(
        functools.partial(backward_kernel, (rows, heads, later.shape[0] - JOBS, tail)),
        in_specs=[hbm] * 15 + [vmem] * 3,
        out_specs=[hbm, hbm, vmem] + [hbm] * 6,
        out_shape=[
            shape(half, BF16), shape(half, BF16), shape((8, width), F32),
        ] + [shape((rows, (JOBS - 1) * CHUNK + tail), F32)] * 3 + [
            shape((rows, width_qkv), F32), shape((rows, width_q), F32), shape(half, F32),
        ],
        scratch_shapes=[
            pltpu.VMEM((3, side_rows, wide), BF16),
            pltpu.VMEM((3, HALF, 2, rows, wide), BF16),
            pltpu.VMEM((side_rows, width_qkv), BF16),
            pltpu.VMEM((side_rows, width_qkv), BF16),
            pltpu.VMEM((2, width, tokens), BF16),
            pltpu.VMEM(half, F32),
            pltpu.VMEM(half, F32),
            pltpu.VMEM((tokens, width), BF16),
            pltpu.VMEM(w_attn.shape, BF16),
            pltpu.VMEM((tokens, width_q), BF16),
            pltpu.VMEM((tokens, HD), BF16),
            pltpu.VMEM((tokens, HD), BF16),
            pltpu.VMEM(lse.shape, F32),
            pltpu.VMEM((tokens, width_q), BF16),
            pltpu.VMEM((tokens, width_q), BF16),
            pltpu.VMEM((tokens, width_qkv), BF16),
            pltpu.VMEM((tokens, HD), F32),
            pltpu.VMEM((tokens, HD), F32),
            pltpu.VMEM(half, BF16),
            pltpu.VMEM(half, BF16),
            pltpu.VMEM(half, BF16),
            pltpu.VMEM((own_tokens, width_qkv), BF16),
            pltpu.VMEM((rows, wide), F32),
            pltpu.VMEM((4, 8, width), F32),
            pltpu.VMEM((3, 4, 8, width), F32),
            dma((16,)), dma((3, HALF, 2, 3)), dma((3, HALF, 2, 3)), dma((2, 2)), dma((2, 2)),
            dma((n_swaps,)), dma((n_swaps,)), dma((7,)), dma((3, 3)), dma((3, 4)), dma((2, 2)), dma((2, 2)),
        ],
        compiler_params=pltpu.CompilerParams(
            collective_id=3, has_side_effects=True, vmem_limit_bytes=63 * 2**20
        ),
        cost_estimate=pl.CostEstimate(
            flops=10 * heads * tokens * tokens * HD, bytes_accessed=50 * 2**20, transcendentals=0
        ),
        name="attention_back",
    )(
        later, gin, middle, cot, hiddens, w_down, w_other, w_attn, qrot, krot, vlow, lse, mixed, in_one_t,
        hid_all, cos2, sin2, vector,
    )


def finish_kernel(
    layer_in, input_in, first_g, first_u, first_d, last_g, last_u, last_d, qkv_in, out_in, small_in,
    layer_out, grad_input, grad_q, grad_k, grad_v, grad_out, grad_g, grad_u, grad_d, vec_one, vec_two,
    bias_q, bias_k, bias_v,
    layer, grad, gates, ups, downs, qkv, out, in_sem, out_sem,
):
    early = first_g.shape[1]
    moves = [
        (layer_in, layer, layer_out), (input_in, grad, grad_input),
        (first_g, gates.at[:, 0:early], None), (last_g, gates.at[:, early:], None),
        (first_u, ups.at[:, 0:early], None), (last_u, ups.at[:, early:], None),
        (first_d, downs.at[:, 0:early], None), (last_d, downs.at[:, early:], None),
        (qkv_in, qkv, None), (out_in, out, grad_out),
    ]
    loads = [
        pltpu.make_async_copy(source, buffer, in_sem.at[i]) for i, (source, buffer, _) in enumerate(moves)
    ]
    for copy in loads:
        copy.start()
    stores = []

    def store(buffer, target):
        copy = pltpu.make_async_copy(buffer, target, out_sem.at[len(stores)])
        copy.start()
        stores.append(copy)

    for i, (_, buffer, target) in enumerate(moves):
        loads[i].wait()
        if target is not None:
            store(buffer, target)
        if i in (3, 5, 7):
            store(*((gates, grad_g), (ups, grad_u), (downs, grad_d))[i // 2 - 1])
    begin = 0
    for target in (grad_q, grad_k, grad_v):
        store(qkv.at[:, begin : begin + target.shape[1]], target)
        begin += target.shape[1]
    for i, target in enumerate((vec_one, vec_two, bias_q)):
        target[...] = small_in[i : i + 1, :].reshape(target.shape[0])
    wide = bias_k.shape[0]
    bias_k[...] = small_in[3:4, 0:wide].reshape(wide)
    bias_v[...] = small_in[3:4, wide : 2 * wide].reshape(wide)
    for copy in stores:
        copy.wait()


def finish(layer_out, grad_input, first, last, sum_qkv, sum_out, small, width_q):
    vmem = pl.BlockSpec(memory_space=pltpu.VMEM)
    hbm = pl.BlockSpec(memory_space=pl.ANY)
    shape = jax.ShapeDtypeStruct
    rows, width_qkv = sum_qkv.shape
    width_k = (width_qkv - width_q) // 2
    width = layer_out.shape[1]
    ffn = (rows, first[0].shape[1] + last[0].shape[1])
    dma = pltpu.SemaphoreType.DMA
    return pl.pallas_call(
        finish_kernel,
        in_specs=[hbm] * 10 + [vmem],
        out_specs=[hbm] * 9 + [vmem] * 5,
        out_shape=[
            shape(layer_out.shape, BF16), shape(grad_input.shape, BF16),
            shape((rows, width_q), F32), shape((rows, width_k), F32), shape((rows, width_k), F32),
            shape(sum_out.shape, F32), shape(ffn, F32), shape(ffn, F32), shape(ffn, F32),
            shape((width,), F32), shape((width,), F32), shape((2 * width_q,), F32),
            shape((2 * width_k,), F32), shape((2 * width_k,), F32),
        ],
        scratch_shapes=[
            pltpu.VMEM(layer_out.shape, BF16), pltpu.VMEM(grad_input.shape, BF16),
            pltpu.VMEM(ffn, F32), pltpu.VMEM(ffn, F32), pltpu.VMEM(ffn, F32),
            pltpu.VMEM(sum_qkv.shape, F32), pltpu.VMEM(sum_out.shape, F32), dma((10,)), dma((9,)),
        ],
        compiler_params=pltpu.CompilerParams(vmem_limit_bytes=62 * 2**20),
        name="finish",
    )(layer_out, grad_input, *first, *last, sum_qkv, sum_out, small)


def body_fused(
    hidden_in, positions, query_weight, query_bias, key_weight, key_bias, value_weight, value_bias,
    out_weight, gate_weight, up_weight, down_weight, attn_gain, ffn_gain, cotangent,
):
    rows, width_q = query_weight.shape
    heads = width_q // HD
    hidden_units = gate_weight.shape[1]
    own_tokens, width = hidden_in.shape
    half = HD // 2
    lanes = jnp.arange(HD, dtype=jnp.int32)
    freq = jnp.power(ROPE_BASE, -2.0 * (lanes % half).astype(F32) / HD)
    ffn_weights = (gate_weight, up_weight, down_weight.T)
    (w_ffn, w_attn, hidden_all, grad_ffn, in_one_t, qrot, krot, vlow, mixed, lse, middle,
     inputs_two, vector, cos2, sin2, in_two_t, cot_t) = forward_attention(
        hidden_in, cotangent,
        (freq, positions, query_bias, key_bias, value_bias, attn_gain, ffn_gain),
        (query_weight, key_weight, value_weight, out_weight.T, *ffn_weights),
        heads,
    )
    hiddens, w_down, grad_normed_two, later, *first_sums, w_other, _ = feed_forward(
        inputs_two, grad_ffn, in_two_t, cot_t, w_ffn, w_attn, width_q + 2 * HD, ffn_weights
    )
    tail = units_of(-(-hidden_units // CHUNK) - 1, hidden_units)
    layer_out, grad_input, small, *sums = attention_back(
        later, grad_normed_two, middle, cotangent, hiddens, w_down, w_other,
        (w_attn, qrot, krot, vlow, lse, mixed, in_one_t, hidden_all), cos2, sin2, vector, tail,
    )
    (layer_out, grad_input, sum_q, sum_k, sum_v, sum_out, sum_gate, sum_up, sum_down, gain_one,
     gain_two, sum_bias_q, sum_bias_k, sum_bias_v) = finish(
        layer_out, grad_input, first_sums, sums[:3], *sums[3:5], small, width_q
    )
    return (
        layer_out,
        grad_input,
        sum_q,
        sum_bias_q,
        sum_k,
        sum_bias_k,
        sum_v,
        sum_bias_v,
        sum_out.T,
        sum_gate,
        sum_up,
        sum_down.T,
        gain_one,
        gain_two,
    )


def body(*arrays):
    rows = arrays[2].shape[0]
    if lax.axis_size("dp") == 2 * CHIPS and rows % 32 == 0 and -(-arrays[9].shape[1] // CHUNK) == 9:
        return body_fused(*arrays)
    return body_general(*arrays)


def solution(mesh):
    tokens, weight, weight_t = P(("dp", "mp"), None), P("dp", "mp"), P("mp", "dp")
    return jax.shard_map(
        body,
        mesh=mesh,
        in_specs=(
            tokens, P("dp"), weight, P(), weight, P(), weight, P(), weight_t,
            weight, weight, weight_t, P(), P(), tokens,
        ),
        out_specs=(
            tokens, tokens, weight, P(), weight, P(), weight, P(), weight_t,
            weight, weight, weight_t, P(), P(),
        ),
        check_vma=False,
    )
```

```python
import functools
import math

import jax
import jax.numpy as jnp
from jax import lax
from jax.experimental import pallas as pl
from jax.experimental.pallas import tpu as pltpu
from jax.sharding import PartitionSpec as P

HD = 128
SEQ_LEN = 1024
DOC_MAX = 512
EPS = 1e-06
ROPE_BASE = 1000000.0
BLOCK = 256
SCALE = 1.0 / math.sqrt(HD)
F32 = jnp.float32
BF16 = jnp.bfloat16


def contract(left, right, left_dim, right_dim):
    return lax.dot_general(
        left, right, (((left_dim,), (right_dim,)), ((), ())), preferred_element_type=F32
    )


def key_range(block_id):
    low = max(0, block_id * BLOCK - (DOC_MAX - 1)) // BLOCK * BLOCK
    return low, (block_id + 1) * BLOCK


def visible(start_row, low, high, block_id):
    keys = low + lax.broadcasted_iota(jnp.int32, (high - low, BLOCK), 0)
    queries = block_id * BLOCK + lax.broadcasted_iota(jnp.int32, (high - low, BLOCK), 1)
    return (keys >= start_row) & (keys <= queries)


def turn(values, cosines, sines):
    return values * cosines + pltpu.roll(values, HD // 2, 1) * sines


def attend_kernel(
    q_ref, k_ref, v_ref, bq_ref, bk_ref, bv_ref, cos_ref, sin_ref, start_ref,
    mixed_ref, qrot_ref, krot_ref, vlow_ref, lse_ref,
):
    head = pl.program_id(0)

    @pl.when(head == 0)
    def _():
        krot_ref[...] = turn(k_ref[...] + bk_ref[...], cos_ref[...], sin_ref[...]).astype(BF16)
        vlow_ref[...] = (v_ref[...] + bv_ref[...]).astype(BF16)

    qrot_ref[...] = turn(q_ref[...] + bq_ref[...], cos_ref[...], sin_ref[...]).astype(BF16)
    for i in range(SEQ_LEN // BLOCK):
        low, high = key_range(i)
        rows = pl.ds(i * BLOCK, BLOCK)
        start_row = start_ref[0:1, rows]
        scores = contract(krot_ref[low:high, :], qrot_ref[rows, :], 1, 1) * SCALE
        scores = jnp.where(visible(start_row, low, high, i), scores, -1e30)
        top = jnp.max(scores, axis=0, keepdims=True)
        weights = jnp.exp(scores - top)
        total = jnp.sum(weights, axis=0, keepdims=True)
        probs = (weights * (1.0 / total)).astype(BF16)
        mixed_ref[rows, :] = contract(probs, vlow_ref[low:high, :], 0, 0).astype(BF16)
        lse_ref[0, 0:1, rows] = top + jnp.log(total)


def attend(qkv, bias, cos2, sin2, start, heads):
    seq = SEQ_LEN
    full = lambda shape: pl.BlockSpec(shape, lambda h: (0,) * len(shape))
    col = lambda: pl.BlockSpec((seq, HD), lambda h: (0, h))
    at = lambda j: pl.BlockSpec((seq, HD), lambda h: (0, j))
    bat = lambda j: pl.BlockSpec((1, HD), lambda h: (0, j))
    return pl.pallas_call(
        attend_kernel,
        grid=(heads,),
        in_specs=[
            col(), at(heads), at(heads + 1),
            pl.BlockSpec((1, HD), lambda h: (0, h)), bat(heads), bat(heads + 1),
            full((seq, HD)), full((seq, HD)), full((1, seq)),
        ],
        out_specs=[
            col(), col(), full((seq, HD)), full((seq, HD)),
            pl.BlockSpec((1, 8, seq), lambda h: (h, 0, 0)),
        ],
        out_shape=[
            jax.ShapeDtypeStruct((seq, heads * HD), BF16),
            jax.ShapeDtypeStruct((seq, heads * HD), BF16),
            jax.ShapeDtypeStruct((seq, HD), BF16),
            jax.ShapeDtypeStruct((seq, HD), BF16),
            jax.ShapeDtypeStruct((heads, 8, seq), F32),
        ],
        compiler_params=pltpu.CompilerParams(vmem_limit_bytes=40 * 2**20),
        cost_estimate=pl.CostEstimate(
            flops=4 * heads * seq * seq * HD, bytes_accessed=10 * 2**20,
            transcendentals=heads * seq * seq // 2,
        ),
        name="attend",
    )(qkv, qkv, qkv, bias, bias, bias, cos2, sin2, start)


def attend_back_kernel(
    heads, qrot_ref, krot_ref, vlow_ref, lse_ref, grad_ref, cos_ref, sin_ref, start_ref,
    out_ref, gk_ref, gv_ref,
):
    head = pl.program_id(0)

    @pl.when(head == 0)
    def _():
        gk_ref[...] = jnp.zeros_like(gk_ref)
        gv_ref[...] = jnp.zeros_like(gv_ref)

    for i in range(SEQ_LEN // BLOCK):
        low, high = key_range(i)
        rows = pl.ds(i * BLOCK, BLOCK)
        start_row = start_ref[0:1, rows]
        query, grad = qrot_ref[rows, :], grad_ref[rows, :]
        keys = krot_ref[low:high, :]
        scores = contract(keys, query, 1, 1) * SCALE
        probs = jnp.where(
            visible(start_row, low, high, i), jnp.exp(scores - lse_ref[0, 0:1, rows]), 0.0
        )
        grad_probs = contract(vlow_ref[low:high, :], grad, 1, 1)
        row_term = jnp.sum(probs * grad_probs, axis=0, keepdims=True)
        grad_scores = (probs * (grad_probs - row_term)).astype(BF16)
        gk_ref[low:high, :] += contract(grad_scores, query, 1, 0)
        gv_ref[low:high, :] += contract(probs.astype(BF16), grad, 1, 0)
        grad_query = contract(grad_scores, keys, 0, 0) * SCALE
        out_ref[rows, pl.ds(pl.multiple_of(head * HD, HD), HD)] = turn(
            grad_query, cos_ref[rows, :], -sin_ref[rows, :]
        ).astype(BF16)

    @pl.when(head == heads - 1)
    def _():
        out_ref[:, heads * HD : (heads + 1) * HD] = turn(
            gk_ref[...] * SCALE, cos_ref[...], -sin_ref[...]
        ).astype(BF16)
        out_ref[:, (heads + 1) * HD :] = gv_ref[...].astype(BF16)


def attend_back(qrot, krot, vlow, lse, grad_mixed, cos2, sin2, start, heads):
    seq = SEQ_LEN
    full = lambda shape: pl.BlockSpec(shape, lambda h: (0,) * len(shape))
    col = lambda: pl.BlockSpec((seq, HD), lambda h: (0, h))
    return pl.pallas_call(
        functools.partial(attend_back_kernel, heads),
        grid=(heads,),
        in_specs=[
            col(), full((seq, HD)), full((seq, HD)),
            pl.BlockSpec((1, 8, seq), lambda h: (h, 0, 0)), col(),
            full((seq, HD)), full((seq, HD)), full((1, seq)),
        ],
        out_specs=full((seq, (heads + 2) * HD)),
        out_shape=jax.ShapeDtypeStruct((seq, (heads + 2) * HD), BF16),
        scratch_shapes=[pltpu.VMEM((seq, HD), F32), pltpu.VMEM((seq, HD), F32)],
        compiler_params=pltpu.CompilerParams(vmem_limit_bytes=40 * 2**20),
        cost_estimate=pl.CostEstimate(
            flops=10 * heads * seq * seq * HD, bytes_accessed=10 * 2**20,
            transcendentals=heads * seq * seq // 2,
        ),
        name="attend_back",
    )(qrot, krot, vlow, lse, grad_mixed, cos2, sin2, start)


class Ring:
    def __init__(self, members):
        self.members = members
        self.chips = members // 2
        self.half = self.chips // 2
        n = self.chips
        self.path = [2 * r if r < n // 2 else 2 * (n - 1 - r) + 1 for r in range(n)]
        self.offsets = [self.half]
        for k in range(self.half - 1, 0, -1):
            self.offsets += [k, n - k]
        self.offsets += [0]
        self.place = {k: i for i, k in enumerate(self.offsets)}

    def pairs(self, shift):
        n, path = self.chips, self.path
        return [
            (path[r] * 2 + c, path[(r + shift) % n] * 2 + c) for r in range(n) for c in range(2)
        ]

    def up(self, block):
        return lax.ppermute(block, "dp", self.pairs(1))

    def down(self, block):
        return lax.ppermute(block, "dp", self.pairs(-1))

    def across(self, block):
        return lax.ppermute(block, "dp", [(i, i ^ 1) for i in range(self.members)])

    def order(self):
        me = lax.axis_index("dp")
        path = jnp.array(self.path, jnp.int32)
        spot = jnp.zeros((self.chips,), jnp.int32).at[path].set(jnp.arange(self.chips, dtype=jnp.int32))
        mine = spot[me // 2]
        offsets = jnp.array(self.offsets, jnp.int32)
        chips = path[(mine + offsets) % self.chips]
        core = me % 2
        return jnp.concatenate([chips * 2 + core, chips * 2 + (1 - core)])

    def gather(self, block):
        n, h = self.chips, self.half
        rows = block.shape[0]
        got = {0: block}
        for k in range(1, h):
            got[n - k] = self.up(got[(n - k + 1) % n])
            got[k] = self.down(got[k - 1])
        first = self.up(got[h + 1][: rows // 2])
        second = self.down(got[h - 1][rows // 2 :])
        other = {k: self.across(got[k]) for k in got}
        got_half = [first, second]
        other_half = [self.across(first), self.across(second)]
        blocks = []
        for side, halves in ((got, got_half), (other, other_half)):
            for k in self.offsets:
                blocks.append(tuple(halves) if k == h else (side[k],))
        return blocks, first

    def reduce(self, own, rows):
        def term(k):
            begin = self.place[k] * rows
            return jnp.concatenate([o[begin : begin + rows] for o in own], axis=1)

        return self.reduce_terms(term, rows)

    def reduce_terms(self, term, rows):
        n, h = self.chips, self.half
        up = self.up(term(h)[: rows // 2])
        down = self.down(term(h)[rows // 2 :])
        for k in range(h - 1, 0, -1):
            mine_up, mine_down = term(k), term(n - k)
            if k == h - 1:
                sent_up = jnp.concatenate([
                    (up.astype(F32) + mine_up[: rows // 2].astype(F32)).astype(BF16),
                    mine_up[rows // 2 :],
                ])
                sent_down = jnp.concatenate([
                    mine_down[: rows // 2],
                    (down.astype(F32) + mine_down[rows // 2 :].astype(F32)).astype(BF16),
                ])
            else:
                sent_up = (up.astype(F32) + mine_up.astype(F32)).astype(BF16)
                sent_down = (down.astype(F32) + mine_down.astype(F32)).astype(BF16)
            up, down = self.up(sent_up), self.down(sent_down)
        return term(0).astype(F32) + up.astype(F32) + down.astype(F32)


def stack(blocks, begin, stop):
    return jnp.concatenate([part[:, begin:stop] for block in blocks for part in block], axis=0)


def swap(block):
    return lax.ppermute(block, "mp", [(0, 1), (1, 0)])


def rms(values):
    return lax.rsqrt(jnp.mean(values * values, axis=-1, keepdims=True) + EPS)


def after(value, *earlier):
    return lax.optimization_barrier((value, *earlier))[0]


def split_hidden(width, parts):
    tiles = width // HD
    cuts = [round(tiles * i / parts) * HD for i in range(parts + 1)]
    return list(zip(cuts[:-1], cuts[1:]))


def body_general(
    hidden_in, positions, query_weight, query_bias, key_weight, key_bias, value_weight, value_bias,
    out_weight, gate_weight, up_weight, down_weight, attn_gain, ffn_gain, cotangent,
):
    ring = Ring(lax.axis_size("dp"))
    rows = query_weight.shape[0]
    width = rows * ring.members
    side_rows = rows * ring.chips
    heads = query_weight.shape[1] // HD
    width_q = heads * HD
    width_qkv = width_q + 2 * HD
    own_tokens = hidden_in.shape[0]
    shard = lax.axis_index("mp")

    def whole(own, other):
        first = jnp.where(shard == 0, own, other)
        second = jnp.where(shard == 0, other, own)
        return jnp.concatenate([first, second], axis=0)

    def own_half(values):
        return lax.dynamic_slice_in_dim(values, shard * own_tokens, own_tokens, 0)

    def other_half(values):
        return lax.dynamic_slice_in_dim(values, (1 - shard) * own_tokens, own_tokens, 0)

    hidden_other = swap(hidden_in)
    attn_pack = jnp.concatenate([query_weight, key_weight, value_weight, out_weight.T], axis=1)
    attn_blocks, attn_last = ring.gather(attn_pack)
    cotangent_other = swap(after(cotangent, hidden_other))
    down_t = down_weight.T
    spans = split_hidden(gate_weight.shape[1], 2)
    ffn_blocks = []
    last = attn_last
    for begin, stop in spans:
        pack = jnp.concatenate(
            [gate_weight[:, begin:stop], up_weight[:, begin:stop], down_t[:, begin:stop]], axis=1
        )
        blocks, last = ring.gather(after(pack, last))
        ffn_blocks.append(blocks)

    order = ring.order()
    feature = (order[:, None] * rows + jnp.arange(rows, dtype=jnp.int32)[None, :]).reshape(width)
    shuffle = (jnp.arange(width, dtype=jnp.int32)[:, None] == feature[None, :]).astype(BF16)

    def to_order(values):
        return contract(values, shuffle, 1, 0).astype(BF16)

    def from_order(values):
        return contract(values, shuffle, 1, 1).astype(BF16)

    def vector_to_order(values):
        return jnp.sum(jnp.where(shuffle > 0, values[:, None], 0.0), axis=0)

    def vector_from_order(values):
        return jnp.sum(jnp.where(shuffle > 0, values[None, :], 0.0), axis=1)

    gain_attn, gain_ffn = vector_to_order(attn_gain), vector_to_order(ffn_gain)

    hidden_all = to_order(whole(hidden_in, hidden_other))
    resid_all = hidden_all.astype(F32)
    factor_one = rms(resid_all)
    inputs_one = (resid_all * factor_one * gain_attn).astype(BF16)
    half = HD // 2
    freq = jnp.power(ROPE_BASE, -2.0 * jnp.arange(half, dtype=F32) / HD)
    angles = positions.astype(F32)[:, None] * freq[None, :]
    cosines, sines = jnp.cos(angles), jnp.sin(angles)
    cos2 = jnp.concatenate([cosines, cosines], axis=1)
    sin2 = jnp.concatenate([-sines, sines], axis=1)
    start = (jnp.arange(SEQ_LEN, dtype=jnp.int32) - positions)[None, :]
    bias = jnp.concatenate([
        lax.dynamic_slice_in_dim(query_bias, shard * width_q, width_q, 0),
        lax.dynamic_slice_in_dim(key_bias, shard * HD, HD, 0),
        lax.dynamic_slice_in_dim(value_bias, shard * HD, HD, 0),
    ])[None, :]
    qkv_full = stack(attn_blocks, 0, width_qkv)
    out_full = stack(attn_blocks, width_qkv, width_qkv + width_q)
    qkv = contract(inputs_one, qkv_full, 1, 0)
    mixed, qrot, krot, vlow, lse = attend(qkv, bias, cos2, sin2, start, heads)
    out_other = swap(contract(other_half(mixed), out_full, 1, 1).astype(BF16))
    middle = (
        own_half(hidden_all).astype(F32)
        + contract(own_half(mixed), out_full, 1, 1)
        + out_other.astype(F32)
    )
    factor_two = rms(middle)
    in_two_own = (middle * factor_two * gain_ffn).astype(BF16)
    inputs_two = whole(in_two_own, swap(in_two_own))
    grad_ffn = to_order(whole(cotangent, cotangent_other))

    hiddens, grads_gate, grads_up, weights = [], [], [], []
    for (begin, stop), blocks in zip(spans, ffn_blocks):
        wide = stop - begin
        gate_full = stack(blocks, 0, wide)
        up_full = stack(blocks, wide, 2 * wide)
        down_full = stack(blocks, 2 * wide, 3 * wide)
        grad_hidden = contract(grad_ffn, down_full, 1, 0)
        gate = contract(inputs_two, gate_full, 1, 0)
        up = contract(inputs_two, up_full, 1, 0)
        sig = jax.nn.sigmoid(gate)
        swish = gate * sig
        hiddens.append((swish * up).astype(BF16))
        grads_gate.append((grad_hidden * up * sig * (1.0 + gate * (1.0 - sig))).astype(BF16))
        grads_up.append((grad_hidden * swish).astype(BF16))
        weights.append((gate_full, up_full, down_full))

    def side(values, index):
        return values[:, index * side_rows : (index + 1) * side_rows]

    def chip_sum(left, right):
        sent = contract(side(left, 1), right, 0, 0).astype(BF16)
        return (contract(side(left, 0), right, 0, 0) + ring.across(sent).astype(F32)).astype(BF16)

    sums = []
    for index in range(len(spans)):
        own = [
            chip_sum(inputs_two, grads_gate[index]),
            chip_sum(inputs_two, grads_up[index]),
            chip_sum(grad_ffn, hiddens[index]),
        ]
        sums.append(ring.reduce(own, rows))

    def back_two(take):
        total = None
        for (gate_full, up_full, _), g, u in zip(weights, grads_gate, grads_up):
            term = contract(take(g), gate_full, 1, 1) + contract(take(u), up_full, 1, 1)
            total = term if total is None else total + term
        return total

    def forward_out(take):
        total = None
        for (_, _, down_full), h in zip(weights, hiddens):
            term = contract(take(h), down_full, 1, 1)
            total = term if total is None else total + term
        return total

    back_other = swap(back_two(other_half).astype(BF16))
    grad_normed_two = back_two(own_half) + back_other.astype(F32)
    ffn_other = swap(forward_out(other_half).astype(BF16))
    layer_out = from_order(
        (middle + forward_out(own_half) + ffn_other.astype(F32)).astype(BF16)
    )

    unit_two = middle * factor_two
    scaled = grad_normed_two * gain_ffn
    gain_two = jnp.sum(grad_normed_two * unit_two, axis=0)
    inner = jnp.mean(scaled * unit_two, axis=-1, keepdims=True)
    grad_middle = own_half(grad_ffn).astype(F32) + factor_two * (scaled - unit_two * inner)

    grad_attn_own = grad_middle.astype(BF16)
    grad_attn = whole(grad_attn_own, swap(grad_attn_own))
    grad_mixed = contract(grad_attn, out_full, 1, 0).astype(BF16)
    grad_qkv = attend_back(qrot, krot, vlow, lse, grad_mixed, cos2, sin2, start, heads)
    sum_out = ring.reduce([chip_sum(grad_attn, mixed)], rows)
    sum_qkv = ring.reduce([chip_sum(inputs_one, grad_qkv)], rows)

    back_one_other = contract(other_half(grad_qkv), qkv_full, 1, 1)
    one_other = swap(back_one_other.astype(BF16))
    back_one_own = contract(own_half(grad_qkv), qkv_full, 1, 1)
    unit_all = resid_all * factor_one
    unit_one = own_half(unit_all)
    gain_one = jnp.sum(back_one_own * unit_one, axis=0) + jnp.sum(
        back_one_other * other_half(unit_all), axis=0
    )
    grad_normed_one = back_one_own + one_other.astype(F32)
    scaled_one = grad_normed_one * gain_attn
    inner_one = jnp.mean(scaled_one * unit_one, axis=-1, keepdims=True)
    through_one = own_half(factor_one) * (scaled_one - unit_one * inner_one)
    grad_input = from_order((grad_middle + through_one).astype(BF16))

    bias_part = jnp.sum(grad_qkv.astype(F32), axis=0)

    def place(part, total):
        return lax.dynamic_update_slice_in_dim(
            jnp.zeros((total,), F32), part, shard * part.shape[0], 0
        )

    small = jnp.concatenate([
        vector_from_order(gain_one),
        vector_from_order(gain_two),
        place(bias_part[:width_q], query_bias.shape[0]),
        place(bias_part[width_q : width_q + HD], key_bias.shape[0]),
        place(bias_part[width_q + HD :], value_bias.shape[0]),
    ])
    small = small + swap(small)
    bit = 1
    while bit < ring.members:
        small = small + lax.ppermute(small, "dp", [(i, i ^ bit) for i in range(ring.members)])
        bit *= 2
    cuts = [width, width, query_bias.shape[0], key_bias.shape[0], value_bias.shape[0]]
    pieces, begin = [], 0
    for cut in cuts:
        pieces.append(small[begin : begin + cut])
        begin += cut

    def gather_cols(index):
        parts = []
        for (begin, stop), total in zip(spans, sums):
            wide = stop - begin
            parts.append(total[:, index * wide : (index + 1) * wide])
        return jnp.concatenate(parts, axis=1)

    return (
        layer_out,
        grad_input,
        sum_qkv[:, :width_q],
        pieces[2],
        sum_qkv[:, width_q : width_q + HD],
        pieces[3],
        sum_qkv[:, width_q + HD :],
        pieces[4],
        sum_out.T,
        gather_cols(0),
        gather_cols(1),
        gather_cols(2).T,
        pieces[0],
        pieces[1],
    )


CHIPS = 8
HALF = CHIPS // 2
CHUNK = 512
TILE = 256
MESH = pl.DeviceIdType.MESH


class Spot:
    def __init__(self, rows):
        self.rows = rows
        self.me = lax.axis_index("dp")
        self.shard = lax.axis_index("mp")
        self.core = lax.rem(self.me, 2)
        chip = lax.div(self.me, 2)
        line, back = lax.div(chip, 2), lax.rem(chip, 2)
        self.spot = line * (1 - back) + (CHIPS - 1 - line) * back
        self.sibling = self.me + 1 - 2 * self.core
        self.next = (self.chip(1) * 2 + self.core, self.chip(CHIPS - 1) * 2 + self.core)

    def chip(self, offset):
        place = lax.rem(self.spot + offset, CHIPS)
        back = lax.div(place, HALF)
        return (1 - back) * (2 * place) + back * (2 * (CHIPS - 1 - place) + 1)

    def greet(self):
        barrier = pltpu.get_barrier_semaphore()
        for target in (
            {"dp": self.sibling}, {"dp": self.next[0]}, {"dp": self.next[1]}, {"mp": 1 - self.shard}
        ):
            pl.semaphore_signal(barrier, inc=1, device_id=target, device_id_type=MESH)
        pl.semaphore_wait(barrier, 4)

    def part(self, block, half=None):
        begin, size = block * self.rows, self.rows
        if half is not None:
            size = self.rows // 2
            begin = begin + half * size
        return pl.ds(pl.multiple_of(begin, 16), size)


def tile_of(index, size=TILE):
    return pl.ds(pl.multiple_of(index * size, size), size)


def small_inputs(ref, width_qkv, width):
    gains = width_qkv + width, width_qkv + 2 * width

    def start_of(block):
        begin = gains[1] + block * BLOCK
        return ref[0:1, begin : begin + BLOCK]

    return (
        ref[0:1, 0:width_qkv], ref[0:1, width_qkv : gains[0]], ref[0:1, gains[0] : gains[1]], start_of
    )


def visible_keys(start_row, low, high, block_id):
    shape = (high - low, BLOCK)
    keys = low + lax.broadcasted_iota(jnp.int32, shape, 0)
    queries = block_id * BLOCK + lax.broadcasted_iota(jnp.int32, shape, 1)
    return (keys.astype(F32) >= start_row) & (keys <= queries)


class Gather:
    def __init__(self, here, held, home, landed, hop_send, hop_recv, side_send, side_recv, store_sem):
        self.here, self.held, self.home, self.landed = here, held, home, landed
        self.hop_send, self.hop_recv = hop_send, hop_recv
        self.side_send, self.side_recv, self.store_sem = side_send, side_recv, store_sem

    def member(self, step, way, sibling=False):
        here = self.here
        chip = here.chip((CHIPS - step) % CHIPS if way == 0 else step)
        return chip * 2 + (1 - here.core if sibling else here.core)

    def hop(self, unit, step, way, arrival=False):
        half = way if step == HALF else None
        source = self.held(unit, step if arrival else step - 1, way, half)
        target = source if arrival or self.landed(unit) else self.held(unit, step, way, half)
        return pltpu.make_async_remote_copy(
            src_ref=source, dst_ref=target, send_sem=self.hop_send.at[unit, step - 1, way],
            recv_sem=self.hop_recv.at[unit, step - 1, way],
            device_id={"dp": self.here.next[way]}, device_id_type=MESH,
        )

    def index(self, step, way):
        return 0 if step == 0 else 2 * step - 1 + way

    def across(self, unit, step, way, arrival=False):
        half = way if step == HALF else None
        target = self.home(unit, self.member(step, way, sibling=arrival), half)
        source = target if arrival else self.held(unit, step, way, half)
        index = self.index(step, way)
        return pltpu.make_async_remote_copy(
            src_ref=source, dst_ref=target, send_sem=self.side_send.at[unit, index],
            recv_sem=self.side_recv.at[unit, index],
            device_id={"dp": self.here.sibling}, device_id_type=MESH,
        )

    def store(self, unit, step, way):
        half = way if step == HALF else None
        return pltpu.make_async_copy(
            self.held(unit, step, way, half), self.home(unit, self.member(step, way), half),
            self.store_sem.at[unit, self.index(step, way)],
        )

    def start(self, unit):
        for way in range(2):
            self.hop(unit, 1, way).start()
        self.across(unit, 0, 0).start()
        if not self.landed(unit):
            self.store(unit, 0, 0).start()

    def step(self, unit, step):
        for way in range(2):
            self.hop(unit, step - 1, way, arrival=True).wait_recv()
            if step <= HALF:
                self.hop(unit, step, way).start()
            self.across(unit, step - 1, way).start()
            if not self.landed(unit):
                self.store(unit, step - 1, way).start()

    def pieces(self):
        return [(0, 0)] + [(step, way) for step in range(1, HALF + 1) for way in range(2)]

    def end(self, unit):
        for step, way in self.pieces():
            self.across(unit, step, way, arrival=True).wait_recv()

    def sent(self, unit):
        for step, way in self.pieces():
            self.across(unit, step, way).wait_send()
            if step:
                self.hop(unit, step, way).wait_send()
            if not self.landed(unit):
                self.store(unit, step, way).wait()


def units_of(chunk, total):
    return min(CHUNK, total - chunk * CHUNK)


def pack_copies(weights, pack, chunks, sem):
    copies = []
    for i, chunk in enumerate(chunks):
        begin, size = chunk * CHUNK, units_of(chunk, weights[0].shape[1])
        for m, ref in enumerate(weights):
            copies.append(pltpu.make_async_copy(
                ref.at[:, begin : begin + size], pack.at[i, :, m * size : (m + 1) * size],
                sem.at[i, m],
            ))
    return copies


LATER = 3
PAIRS = 2
QUARTERS = 4


def forward_kernel(
    cfg, hid, cot, turns, places, bias_q, bias_k, bias_v, gain_a, gain_f,
    wq, wk, wv, wo, wg, wu, wd,
    w_ffn, w_attn, hid_all, cot_all, in_one_t, qrot, krot, vlow, mixed, lse, middle, in_two, vec_ref,
    cos_ref, sin_ref, in_two_t, cot_t,
    wa, qkv, psend, precv, pack, slots, in_one, cots, turned, turned_cot,
    local_sem, pack_sem, store_sem, hop_send, hop_recv, side_send, side_recv, x_send, x_recv, t_sem,
):
    rows, heads, units = cfg
    own_tokens, width = hid.shape
    tokens = 2 * own_tokens
    width_q = heads * HD
    width_qkv = width_q + 2 * HD
    here = Spot(rows)
    shard = here.shard

    own_rows = pl.ds(pl.multiple_of(shard * own_tokens, TILE), own_tokens)
    other_rows = pl.ds(pl.multiple_of((1 - shard) * own_tokens, TILE), own_tokens)
    quarter = own_tokens // QUARTERS

    def quarter_rows(index, side):
        return pl.ds(pl.multiple_of(side * own_tokens + index * quarter, quarter), quarter)

    mine = here.part(here.me)
    attn_copies, column = [], 0
    for i, ref in enumerate((wq, wk, wv, wo)):
        wide = ref.shape[1]
        attn_copies.append(
            pltpu.make_async_copy(ref, wa.at[mine, column : column + wide], local_sem.at[i])
        )
        column += wide
    ffn_copies = pack_copies((wg, wu, wd), pack, range(PAIRS * units), pack_sem)
    own_copies = [
        pltpu.make_async_copy(hid, hid_all.at[own_rows, :], local_sem.at[4]),
        pltpu.make_async_copy(cot, cots.at[own_rows, :], local_sem.at[5]),
    ]
    for copy in attn_copies + own_copies + ffn_copies:
        copy.start()

    column = 0
    for ref in (bias_q, bias_k, bias_v):
        size = ref.shape[0] // 2
        row = ref[...].reshape(1, 2 * size)
        vec_ref[:, column : column + size] = jnp.where(shard == 0, row[:, :size], row[:, size:])
        column += size
    for ref in (gain_a, gain_f):
        vec_ref[:, column : column + width] = ref[...].reshape(1, width)
        column += width
    vec_ref[:, column : column + tokens] = (
        lax.broadcasted_iota(jnp.int32, (1, tokens), 1) - places[...].reshape(1, tokens)
    ).astype(F32)
    bias, gain_one, gain_two, start_of = small_inputs(vec_ref, width_qkv, width)

    here.greet()

    def swap_copy(index, src, dst):
        return pltpu.make_async_remote_copy(
            src_ref=src, dst_ref=dst, send_sem=x_send.at[index], recv_sem=x_recv.at[index],
            device_id={"mp": 1 - shard}, device_id_type=MESH,
        )

    hid_swap = (swap_copy(0, hid, hid_all.at[own_rows, :]), swap_copy(0, hid, hid_all.at[other_rows, :]))
    mix_swap = swap_copy(1, psend, precv)
    two_swap = (
        swap_copy(2, in_two.at[own_rows, :], in_two.at[own_rows, :]),
        swap_copy(2, in_two.at[other_rows, :], in_two.at[other_rows, :]),
    )

    def cot_swap(index, arrival=False):
        ref = cots.at[quarter_rows(index, 1 - shard if arrival else shard), :]
        return swap_copy(3 + index, ref, ref)

    def home(unit, member, half):
        part = here.part(member, half)
        if unit == 0:
            return wa.at[part, :]
        return w_ffn.at[(unit - 1) * PAIRS : unit * PAIRS, part, :]

    def held(unit, step, way, half):
        if unit == 0:
            return home(0, gather.member(step, way), half)
        part = slice(0, rows) if half is None else slice(half * rows // 2, (half + 1) * rows // 2)
        if step == 0:
            return pack.at[(unit - 1) * PAIRS : unit * PAIRS, part, :]
        slot = 2 * HALF - 2 if step == HALF else 2 * (step - 1) + way
        return slots.at[unit - 1, slot, :, part, :]

    gather = Gather(
        here, held, home, lambda unit: unit == 0, hop_send, hop_recv, side_send, side_recv, store_sem
    )
    ffn_units = range(1, units + 1)

    hid_swap[0].start()
    for copy in attn_copies:
        copy.wait()
    gather.start(0)
    at = jnp.broadcast_to(places[...].reshape(1, tokens).astype(F32), (HD, tokens)).T
    angles = at * turns[...].reshape(1, HD)
    cos_ref[...] = jnp.cos(angles)
    lanes = lax.broadcasted_iota(jnp.int32, (tokens, HD), 1)
    sin_ref[...] = jnp.where(lanes < HD // 2, -1.0, 1.0) * jnp.sin(angles)

    for step in range(2, HALF + 1):
        gather.step(0, step)
    for copy in ffn_copies:
        copy.wait()
    for unit in ffn_units:
        gather.start(unit)
    gather.step(0, HALF + 1)

    for copy in own_copies:
        copy.wait()
    hid_swap[1].wait_recv()
    for index in range(QUARTERS - 1):
        cot_swap(index).start()

    @pl.loop(0, tokens // TILE)
    def _(t):
        v = hid_all[tile_of(t), :].astype(F32)
        factor = lax.rsqrt(jnp.mean(v * v, axis=-1, keepdims=True) + EPS)
        in_one[tile_of(t), :] = (v * factor * gain_one).astype(BF16)

    gather.end(0)
    wa_out = pltpu.make_async_copy(wa, w_attn, local_sem.at[6])
    wa_out.start()

    @pl.loop(0, tokens // TILE)
    def _(t):
        part = tile_of(t)
        qkv[part, :] = contract(in_one[part, :], wa[:, 0:width_qkv], 1, 0) + bias
        cosines, sines = cos_ref[part, :], sin_ref[part, :]
        for h in range(heads):
            columns = slice(h * HD, (h + 1) * HD)
            qrot[part, columns] = turn(qkv[part, columns], cosines, sines).astype(BF16)
        krot[part, :] = turn(qkv[part, width_q : width_q + HD], cosines, sines).astype(BF16)
        vlow[part, :] = qkv[part, width_q + HD :].astype(BF16)

    def attend(blocks):
        @pl.loop(0, heads)
        def _(h):
            columns = tile_of(h, HD)
            for i in blocks:
                low, high = key_range(i)
                part = pl.ds(i * BLOCK, BLOCK)
                scores = contract(krot[low:high, :], qrot[part, columns], 1, 1) * SCALE
                scores = jnp.where(visible_keys(start_of(i), low, high, i), scores, -1e30)
                top = jnp.max(scores, axis=0, keepdims=True)
                weights = jnp.exp(scores - top)
                total = jnp.sum(weights, axis=0, keepdims=True)
                probs = (weights * (1.0 / total)).astype(BF16)
                mixed[part, columns] = contract(probs, vlow[low:high, :], 0, 0).astype(BF16)
                lse[h, 0:1, part] = top + jnp.log(total)

    halves = (range(own_tokens // BLOCK), range(own_tokens // BLOCK, tokens // BLOCK))
    for index in range(2):
        @pl.when(shard == index)
        def _():
            attend(halves[1 - index])

    @pl.loop(0, width // TILE)
    def _(n):
        weight = wa[tile_of(n), width_qkv:]
        psend[:, tile_of(n)] = contract(mixed[other_rows, :], weight, 1, 1).astype(BF16)

    mix_swap.start()
    for index in range(2):
        @pl.when(shard == index)
        def _():
            attend(halves[index])

    @pl.loop(0, width // TILE)
    def _(n):
        weight = wa[tile_of(n), width_qkv:]
        middle[:, tile_of(n)] = (
            contract(mixed[own_rows, :], weight, 1, 1) + hid[:, tile_of(n)].astype(F32)
        )

    for unit in ffn_units:
        gather.step(unit, 2)

    def transpose(source, target, first, begin, count):
        @pl.loop(0, width // TILE)
        def _(n):
            for t in range(count):
                part = pl.ds(pl.multiple_of(begin + t * TILE, TILE), TILE)
                target[tile_of(n), part] = source[part, tile_of(n)].T

    transpose(in_one, turned, 0, 0, tokens // TILE)
    one_turned = pltpu.make_async_copy(turned, in_one_t, t_sem.at[0])
    one_turned.start()
    mine_begin, theirs_begin = shard * own_tokens, (1 - shard) * own_tokens
    transpose(cots, turned_cot, 0, mine_begin, own_tokens // TILE)
    for index in range(QUARTERS // 2):
        cot_swap(index, arrival=True).wait_recv()
    transpose(cots, turned_cot, 0, theirs_begin, own_tokens // TILE // 2)

    mix_swap.wait_recv()

    @pl.loop(0, own_tokens // TILE)
    def _(t):
        part = tile_of(t)
        v = middle[part, :] + precv[part, :].astype(F32)
        middle[part, :] = v
        factor = lax.rsqrt(jnp.mean(v * v, axis=-1, keepdims=True) + EPS)
        to = pl.ds(pl.multiple_of(shard * own_tokens + t * TILE, TILE), TILE)
        in_two[to, :] = (v * factor * gain_two).astype(BF16)

    two_swap[0].start()
    cot_swap(QUARTERS - 1).start()
    one_turned.wait()
    for unit in ffn_units:
        gather.step(unit, 3)
    transpose(in_two, turned, 0, mine_begin, own_tokens // TILE)
    for unit in list(ffn_units)[:1]:
        gather.step(unit, 4)
    two_swap[1].wait_recv()
    transpose(in_two, turned, 0, theirs_begin, own_tokens // TILE)
    two_turned = pltpu.make_async_copy(turned, in_two_t, t_sem.at[1])
    two_turned.start()
    for unit in list(ffn_units)[1:]:
        gather.step(unit, 4)
    for index in range(QUARTERS // 2, QUARTERS):
        cot_swap(index, arrival=True).wait_recv()
    transpose(cots, turned_cot, 0, theirs_begin + own_tokens // 2, own_tokens // TILE // 2)
    cot_copies = [
        pltpu.make_async_copy(cots, cot_all, t_sem.at[2]),
        pltpu.make_async_copy(turned_cot, cot_t, t_sem.at[3]),
    ]
    for copy in cot_copies:
        copy.start()
    for unit in ffn_units:
        gather.step(unit, 5)
    for unit in ffn_units:
        gather.end(unit)
    for unit in range(units + 1):
        gather.sent(unit)
    hid_swap[0].wait_send()
    mix_swap.wait_send()
    two_swap[0].wait_send()
    for index in range(QUARTERS):
        cot_swap(index).wait_send()
    for copy in [wa_out, two_turned] + cot_copies:
        copy.wait()


def forward_attention(hidden_in, cotangent, vectors, weights, heads):
    own_tokens, width = hidden_in.shape
    tokens = 2 * own_tokens
    rows = weights[0].shape[0]
    chunks = -(-weights[4].shape[1] // CHUNK)
    units = (chunks - LATER) // PAIRS
    early = units * PAIRS
    width_q = heads * HD
    width_attn = 2 * width_q + 2 * HD
    wide = 3 * CHUNK
    vmem = pl.BlockSpec(memory_space=pltpu.VMEM)
    hbm = pl.BlockSpec(memory_space=pl.ANY)
    dma = pltpu.SemaphoreType.DMA
    shape = jax.ShapeDtypeStruct
    pieces = 2 * HALF + 1
    return pl.pallas_call(
        functools.partial(forward_kernel, (rows, heads, units)),
        in_specs=[vmem, hbm] + [vmem] * 7 + [hbm] * 7,
        out_specs=[hbm, hbm, vmem, hbm, hbm] + [vmem] * 10 + [hbm, hbm],
        out_shape=[
            shape((early, width, wide), BF16),
            shape((width, width_attn), BF16),
            shape((tokens, width), BF16),
            shape((tokens, width), BF16),
            shape((width, tokens), BF16),
            shape((tokens, width_q), BF16),
            shape((tokens, HD), BF16),
            shape((tokens, HD), BF16),
            shape((tokens, width_q), BF16),
            shape((heads, 8, tokens), F32),
            shape((own_tokens, width), F32),
            shape((tokens, width), BF16),
            shape((1, width_q + 2 * HD + 2 * width + tokens), F32),
            shape((tokens, HD), F32),
            shape((tokens, HD), F32),
            shape((width, tokens), BF16),
            shape((width, tokens), BF16),
        ],
        scratch_shapes=[
            pltpu.VMEM((width, width_attn), BF16),
            pltpu.VMEM((tokens, width_q + 2 * HD), F32),
            pltpu.VMEM((own_tokens, width), BF16),
            pltpu.VMEM((own_tokens, width), BF16),
            pltpu.VMEM((early, rows, wide), BF16),
            pltpu.VMEM((units, 2 * HALF - 1, PAIRS, rows, wide), BF16),
            pltpu.VMEM((tokens, width), BF16),
            pltpu.VMEM((tokens, width), BF16),
            pltpu.VMEM((width, tokens), BF16),
            pltpu.VMEM((width, tokens), BF16),
            dma((7,)), dma((early, 3)), dma((units + 1, pieces)),
            dma((units + 1, HALF, 2)), dma((units + 1, HALF, 2)),
            dma((units + 1, pieces)), dma((units + 1, pieces)),
            dma((3 + QUARTERS,)), dma((3 + QUARTERS,)), dma((4,)),
        ],
        compiler_params=pltpu.CompilerParams(
            collective_id=1, has_side_effects=True, vmem_limit_bytes=63 * 2**20
        ),
        cost_estimate=pl.CostEstimate(
            flops=6 * tokens * width * width_attn, bytes_accessed=120 * 2**20, transcendentals=0
        ),
        name="forward_attention",
    )(hidden_in, cotangent, *vectors, *weights)


class Sums:
    def __init__(self, here, own, places, send_sem, recv_sem):
        self.here, self.own, self.places = here, own, places
        self.send_sem, self.recv_sem = send_sem, recv_sem

    def chip(self, step, way):
        distance = HALF - step
        return self.here.chip(distance if way == 0 else CHIPS - distance)

    def copy(self, o, p, step, way, m, columns):
        here, rows = self.here, self.here.rows
        return pltpu.make_async_remote_copy(
            src_ref=self.own.at[o, here.part(self.chip(step, way), way if step == 0 else None), columns],
            dst_ref=self.places.at[p, step, way, 0 : rows // 2 if step == 0 else rows, columns],
            send_sem=self.send_sem.at[p, step, way, m],
            recv_sem=self.recv_sem.at[p, step, way, m],
            device_id={"dp": here.next[way]},
            device_id_type=MESH,
        )

    def columns(self, pieces, m):
        count, size = pieces
        return pl.ds(pl.multiple_of(m * size, HD), size)

    def start(self, o, p, pieces):
        @pl.loop(0, pieces[0])
        def _(m):
            for way in range(2):
                self.copy(o, p, 0, way, m, self.columns(pieces, m)).start()

    def step(self, o, p, step, pieces):
        here, own = self.here, self.own

        @pl.loop(0, pieces[0])
        def _(m):
            columns = self.columns(pieces, m)
            for way in range(2):
                self.copy(o, p, step - 1, way, m, columns).wait()
            for way in range(2):
                part = here.part(self.chip(step, way), way if step == 1 else None)
                size = here.rows // 2 if step == 1 else here.rows
                own[o, part, columns] = (
                    own[o, part, columns].astype(F32)
                    + self.places[p, step - 1, way, 0:size, columns].astype(F32)
                ).astype(BF16)
                self.copy(o, p, step, way, m, columns).start()

    def end(self, o, p, pieces, target):
        own, last = self.own, HALF - 1
        part = self.here.part(self.here.chip(0))

        @pl.loop(0, pieces[0])
        def _(m):
            columns = self.columns(pieces, m)
            for way in range(2):
                self.copy(o, p, last, way, m, columns).wait()
            target[:, columns] = (
                own[o, part, columns].astype(F32)
                + self.places[p, last, 0, :, columns].astype(F32)
                + self.places[p, last, 1, :, columns].astype(F32)
            )


EVENTS = {
    (0, "a"): "G11 G21",
    (0, "c"): "G02",
    (0, "f"): "G12",
    (1, "a"): "R00",
    (1, "b"): "G22",
    (1, "e"): "G03",
    (2, "a"): "R10",
    (2, "b"): "G13",
    (2, "c"): "R01 G23",
    (3, "a"): "G04 R11",
    (3, "c"): "G14",
    (4, "a"): "R02",
    (4, "b"): "G24",
    (4, "c"): "G05",
    (4, "e"): "R12",
    (4, "f"): "G15",
    (5, "a"): "R03 R20",
    (5, "c"): "G25 R13",
    (6, "0a"): "R04 R21",
    (6, "1a"): "R14 R22",
    (6, "1b"): "R30",
    (6, "2b"): "R23",
    (7, "0a"): "R31",
    (7, "1a"): "R24 R32 R40",
    (7, "2a"): "R33",
    (7, "2b"): "R41",
    (8, "1a"): "R34 R42",
    (8, "1b"): "R43",
    (8, "2b"): "R44",
}
SETS = 3


def ffn_kernel(
    cfg, in2_hbm, cot_hbm, in2t_hbm, cott_hbm, w_ffn, w_attn, wg, wu, wd,
    hiddens, w_down, gin_own, later, grad_g, grad_u, grad_d, w_other, w_late,
    in2, cot, in2t, cott, wbuf, acts, gin, own, sent, sib, ring, stage, pack,
    in_sem, w_sem, sib_send, sib_recv, ring_send, ring_recv, out_sem, g_sem, end_sem, free_sem,
    pack_sem, store_sem, hop_send, hop_recv, side_send, side_recv, park_sem, fetch_sem, hid_sem, down_sem,
):
    rows, chunks, total = cfg
    grads = (grad_g, grad_u, grad_d)
    tokens, width = in2.shape
    side_rows = CHIPS * rows
    own_tokens = tokens // 2
    first = chunks - LATER
    rings = first - 1
    here = Spot(rows)
    shard = here.shard
    sums = Sums(here, own, ring, ring_send, ring_recv)
    ring_pieces = (3, CHUNK)
    own_rows = pl.ds(pl.multiple_of(shard * own_tokens, TILE), own_tokens)
    other_rows = pl.ds(pl.multiple_of((1 - shard) * own_tokens, TILE), own_tokens)

    def size_of(i):
        return units_of(first + i, total)

    def load(chunk, s):
        return pltpu.make_async_copy(w_ffn.at[chunk], wbuf.at[s], w_sem.at[s])

    def load_late(i, s):
        columns = slice(0, 3 * size_of(i))
        return pltpu.make_async_copy(w_late.at[i, :, columns], wbuf.at[s, :, columns], w_sem.at[s])

    def down_copies(chunk, s, size=CHUNK):
        top = width // 2
        return [
            pltpu.make_async_copy(
                wbuf.at[s, h * top : (h + 1) * top, 2 * size : 3 * size],
                w_down.at[chunk, :, h * CHUNK : h * CHUNK + size], down_sem.at[s, h],
            )
            for h in range(2)
        ]

    def hidden_copies(index, chunk, size=CHUNK):
        return [pltpu.make_async_copy(
            acts.at[index, :, 2 * size : 3 * size], hiddens.at[chunk, :, 0:size], hid_sem.at[index]
        )]

    def home(unit, member, half):
        return w_late.at[unit, here.part(member, half), 0 : 3 * size_of(unit)]

    def held(unit, step, way, half):
        size = rows if half is None else rows // 2
        columns = slice(0, 3 * size_of(unit))
        if step == 0:
            return pack.at[unit, :, columns]
        slot = 2 * (step - 1) + way
        whole = 2 * HALF - 2
        if unit < 2:
            buffer, begin = 1 + unit, (whole if step == HALF else slot) * rows
            offset = 0
            if half is not None:
                offset = half * size
        else:
            base = (whole + 1) * rows
            if step == HALF:
                buffer, begin, offset = 1 + way, base + whole // 2 * rows, 0
            else:
                buffer, begin = 1 + slot // (whole // 2), base + slot % (whole // 2) * rows
                offset = 0 if half is None else half * size
        return acts.at[buffer, begin + offset : begin + offset + size, columns]

    gather = Gather(
        here, held, home, lambda unit: False, hop_send, hop_recv, side_send, side_recv, store_sem
    )
    own_blocks = pack_copies((wg, wu, wd), pack, range(first, chunks), pack_sem)

    inputs = [
        pltpu.make_async_copy(in2_hbm, in2, in_sem.at[0]),
        pltpu.make_async_copy(cot_hbm, cot, in_sem.at[1]),
    ]
    turned = []
    for i, (source, target) in enumerate(((in2t_hbm, in2t), (cott_hbm, cott))):
        for side in range(2):
            for chip in range(CHIPS):
                member = 2 * chip + (here.core if side == 0 else 1 - here.core)
                begin = side * side_rows + chip * rows
                turned.append(pltpu.make_async_copy(
                    source.at[here.part(member), :], target.at[begin : begin + rows, :],
                    in_sem.at[2 + i],
                ))
    for copy in own_blocks + [load(0, 0)] + inputs:
        copy.start()
    here.greet()
    for copy in own_blocks:
        copy.wait()
    gather.start(0)

    def result_copies(chunk):
        return [
            pltpu.make_async_copy(
                stage.at[:, m * CHUNK : (m + 1) * CHUNK],
                grads[m].at[:, tile_of(chunk, CHUNK)],
                out_sem.at[m],
            )
            for m in range(3)
        ]

    def fetch(chunk):
        return pltpu.make_async_copy(
            later.at[chunk - SETS], own.at[chunk % SETS], fetch_sem.at[chunk % SETS]
        )

    def park(chunk, p, early, size=CHUNK):
        columns = slice(0, 3 * size)
        target = own.at[chunk] if early else later.at[chunk - SETS, :, columns]
        return pltpu.make_async_copy(sib.at[p, :, columns], target, park_sem.at[p])

    def ring_event(chunk, step):
        o, p = chunk % SETS, chunk % 2
        if step == 0:
            if chunk >= SETS:
                fetch(chunk).wait()
            sums.start(o, p, ring_pieces)
        elif step < HALF:
            sums.step(o, p, step, ring_pieces)
        else:
            if chunk:
                for copy in result_copies(chunk - 1):
                    copy.wait()
            sums.end(o, p, ring_pieces, stage)
            for copy in result_copies(chunk):
                copy.start()
            if chunk + SETS < rings:
                fetch(chunk + SETS).start()

    def run(events):
        for event in events.split():
            index, step = int(event[1]), int(event[2])
            if event[0] == "R":
                ring_event(index, step)
            elif step == 1:
                gather.start(index)
            else:
                gather.step(index, step)

    def sib_copy(p, m, size):
        columns = slice(m * size, (m + 1) * size)
        return pltpu.make_async_remote_copy(
            src_ref=sent.at[:, columns],
            dst_ref=sib.at[p, :, columns],
            send_sem=sib_send.at[m],
            recv_sem=sib_recv.at[p, m],
            device_id={"dp": here.sibling},
            device_id_type=MESH,
        )

    def weight_copy():
        return pltpu.make_async_remote_copy(
            src_ref=w_attn.at[:, 0 : w_other.shape[1]], dst_ref=w_other,
            send_sem=g_sem.at[2], recv_sem=g_sem.at[3],
            device_id={"mp": 1 - shard}, device_id_type=MESH,
        )

    def gin_copy():
        return pltpu.make_async_remote_copy(
            src_ref=in2.at[other_rows, :], dst_ref=cot.at[own_rows, :],
            send_sem=g_sem.at[0], recv_sem=g_sem.at[1],
            device_id={"mp": 1 - shard}, device_id_type=MESH,
        )

    def forward(index, part, s, size=CHUNK):
        for begin in range(0, size, TILE):
            stop = min(begin + TILE, size)
            gates, ups, downs = (slice(m * size + begin, m * size + stop) for m in range(3))
            gate = contract(in2[part, :], wbuf[s, :, gates], 1, 0)
            up = contract(in2[part, :], wbuf[s, :, ups], 1, 0)
            grad = contract(cot[part, :], wbuf[s, :, downs], 1, 0)
            sig = 0.5 * jnp.tanh(0.5 * gate) + 0.5
            swish = gate * sig
            acts[index, part, downs] = (swish * up).astype(BF16)
            acts[index, part, gates] = (grad * up * (sig + swish - swish * sig)).astype(BF16)
            acts[index, part, ups] = (grad * swish).astype(BF16)

    def back_gin(index, part, s, size=CHUNK):
        @pl.loop(0, width // TILE)
        def _(n):
            gin[part, tile_of(n)] += contract(
                acts[index, part, 0 : 2 * size], wbuf[s, tile_of(n), 0 : 2 * size], 1, 1
            )

    def weight_grads(index, p, between, size=CHUNK):
        for m, left in enumerate((in2t, in2t, cott)):
            columns = slice(m * size, (m + 1) * size)
            sent[:, columns] = contract(
                left[side_rows:, :], acts[index, :, columns], 1, 0
            ).astype(BF16)
            sib_copy(p, m, size).start()
        between()
        for m, left in enumerate((in2t, in2t, cott)):
            columns = slice(m * size, (m + 1) * size)
            sib_copy(p, m, size).wait()
            sib[p, :, columns] = (
                contract(left[0:side_rows, :], acts[index, :, columns], 1, 0)
                + sib[p, :, columns].astype(F32)
            ).astype(BF16)

    gin[...] = jnp.zeros_like(gin)
    for copy in inputs:
        copy.wait()
    for copy in turned:
        copy.start()

    def at_point(j, point):
        for chunk in range(first):
            if (chunk, point) in EVENTS:
                @pl.when(j == chunk)
                def _():
                    run(EVENTS[chunk, point])

    weight_copy().start()

    def start(copies):
        for copy in copies:
            copy.start()

    def wait(copies):
        for copy in copies:
            copy.wait()

    @pl.loop(0, first)
    def _(j):
        p = lax.rem(j, 2)
        load(j, p).wait()
        start(down_copies(j, p))

        @pl.when(j >= 1)
        def _():
            wait(down_copies(j - 1, 1 - p))
            wait(hidden_copies(0, j - 1))

        @pl.when(j + 1 < first)
        def _():
            load(j + 1, 1 - p).start()

        @pl.when(j == first - 1)
        def _():
            gather.end(0)
            gather.sent(0)
            load_late(0, 1 - p).start()

        forward(0, slice(0, own_tokens), p)

        @pl.when((j >= 1) & (j <= SETS))
        def _():
            park(j - 1, 1 - p, True).wait()

        @pl.when(j > SETS)
        def _():
            park(j - 1, 1 - p, False).wait()

        at_point(j, "a")
        forward(0, slice(own_tokens, tokens), p)
        start(hidden_copies(0, j))
        at_point(j, "b")
        back_gin(0, slice(0, tokens), p)
        at_point(j, "c")

        @pl.when(j == 0)
        def _():
            for i, ref in enumerate((in2t, cott)):
                pltpu.make_async_copy(ref, ref, in_sem.at[2 + i]).wait()

        weight_grads(0, p, lambda: at_point(j, "e"))

        @pl.when(j < SETS)
        def _():
            park(j, p, True).start()

        @pl.when(j >= SETS)
        def _():
            park(j, p, False).start()

        at_point(j, "f")

    wait(hidden_copies(0, first - 1))
    wait(down_copies(first - 1, (first - 1) % 2))
    for unit in range(1, LATER):
        gather.end(unit)
        gather.sent(unit)

    for half in range(2):
        part = (other_rows, own_rows)[half]
        for i in range(LATER):
            size = size_of(i)
            turn = half * LATER + i
            s = (first + turn) % 2
            load_late(i, s).wait()
            if half == 0:
                start(down_copies(first + i, s, size))
            if 0 < turn <= LATER:
                wait(down_copies(first + turn - 1, 1 - s, size_of(turn - 1)))
            if turn + 1 < 2 * LATER:
                load_late((i + 1) % LATER, 1 - s).start()
            forward(i, part, s, size)
            if half == 1:
                start(hidden_copies(i, first + i, size))
            run(EVENTS.get((first + half, f"{i}a"), ""))
            back_gin(i, part, s, size)
            run(EVENTS.get((first + half, f"{i}b"), ""))
        if half == 0:
            pl.semaphore_signal(
                free_sem, inc=1, device_id={"mp": 1 - shard}, device_id_type=MESH
            )

            @pl.loop(0, own_tokens // TILE)
            def _(t):
                of = pl.ds(pl.multiple_of((1 - shard) * own_tokens + t * TILE, TILE), TILE)
                in2[of, :] = gin[of, :].astype(BF16)

            pl.semaphore_wait(free_sem, 1)
            gin_copy().start()

    for i in range(LATER):
        chunk, size = first + i, size_of(i)
        p = chunk % 2
        park(chunk - 1, 1 - p, False).wait()
        weight_grads(i, p, lambda: run(EVENTS.get((first + 2, f"{i}a"), "")), size)
        park(chunk, p, False, size).start()
        run(EVENTS.get((first + 2, f"{i}b"), ""))
    gin_copy().wait()

    @pl.loop(0, own_tokens // TILE)
    def _(t):
        of = pl.ds(pl.multiple_of(shard * own_tokens + t * TILE, TILE), TILE)
        at = pl.ds(pl.multiple_of((1 - shard) * own_tokens + t * TILE, TILE), TILE)
        gin[of, :] = gin[of, :] + cot[at, :].astype(F32)

    gin_out = pltpu.make_async_copy(gin.at[own_rows, :], gin_own, end_sem.at[0])
    gin_out.start()
    weight_copy().wait()
    last_park = park(chunks - 1, (chunks - 1) % 2, False, size_of(LATER - 1))
    for copy in [gin_out, last_park] + result_copies(rings - 1):
        copy.wait()
    for i in range(LATER):
        wait(hidden_copies(i, first + i, size_of(i)))


def feed_forward(inputs_two, grad_ffn, in_two_t, cot_t, w_ffn, w_attn, width_qkv, weights):
    tokens, width = inputs_two.shape
    rows = weights[0].shape[0]
    chunks = w_ffn.shape[0] + LATER
    pieces = 2 * HALF + 1
    hbm = pl.BlockSpec(memory_space=pl.ANY)
    side_rows, wide = CHIPS * rows, 3 * CHUNK
    dma = pltpu.SemaphoreType.DMA
    shape = jax.ShapeDtypeStruct
    half = (tokens // 2, width)
    return pl.pallas_call(
        functools.partial(ffn_kernel, (rows, chunks, weights[0].shape[1])),
        in_specs=[hbm] * 9,
        out_specs=[hbm] * 9,
        out_shape=[
            shape((chunks, tokens, CHUNK), BF16),
            shape((chunks, width // 2, 2 * CHUNK), BF16), shape(half, F32),
            shape((chunks - SETS, side_rows, wide), BF16),
        ] + [shape((rows, (chunks - LATER - 1) * CHUNK), F32)] * 3 + [
            shape((width, width_qkv), BF16),
            shape((LATER, width, wide), BF16),
        ],
        scratch_shapes=[
            pltpu.VMEM((tokens, width), BF16),
            pltpu.VMEM((tokens, width), BF16),
            pltpu.VMEM((width, tokens), BF16),
            pltpu.VMEM((width, tokens), BF16),
            pltpu.VMEM((2, width, wide), BF16),
            pltpu.VMEM((LATER, tokens, wide), BF16),
            pltpu.VMEM((tokens, width), F32),
            pltpu.VMEM((SETS, side_rows, wide), BF16),
            pltpu.VMEM((side_rows, wide), BF16),
            pltpu.VMEM((2, side_rows, wide), BF16),
            pltpu.VMEM((2, HALF, 2, rows, wide), BF16),
            pltpu.VMEM((rows, wide), F32),
            pltpu.VMEM((LATER, rows, wide), BF16),
            dma((4,)), dma((2,)), dma((3,)), dma((2, 3)),
            dma((2, HALF, 2, 3)), dma((2, HALF, 2, 3)), dma((3,)), dma((4,)), dma((1,)),
            pltpu.SemaphoreType.REGULAR,
            dma((LATER, 3)), dma((LATER, pieces)), dma((LATER, HALF, 2)), dma((LATER, HALF, 2)),
            dma((LATER, pieces)), dma((LATER, pieces)), dma((2,)), dma((SETS,)), dma((LATER,)), dma((2, 2)),
        ],
        compiler_params=pltpu.CompilerParams(
            collective_id=2, has_side_effects=True, vmem_limit_bytes=63 * 2**20
        ),
        cost_estimate=pl.CostEstimate(
            flops=18 * tokens * width * chunks * CHUNK, bytes_accessed=80 * 2**20,
            transcendentals=tokens * chunks * CHUNK,
        ),
        name="feed_forward",
    )(inputs_two, grad_ffn, in_two_t, cot_t, w_ffn, w_attn, *weights)


JOBS = 1 + LATER


BACK_EVENTS = {
    "w0": "01 11",
    "w1": "20",
    "w2": "02",
    "w4": "12",
    "w6": "21",
    "w8": "03",
    "w9": "13",
    "h0": "22",
    "h3": "04",
    "h4": "30",
    "h5": "14",
    "o": "23 31",
    "q1": "40",
    "t1": "24",
    "t2": "32",
    "t3": "41",
    "g": "33",
    "b": "42",
    "u1": "50 34 43",
    "l0": "51",
    "l2": "44 52 53",
    "z1": "54",
}


def backward_kernel(
    cfg, later, gin_hbm, middle_hbm, cot_hbm, hiddens, w_down, w_other, w_attn, qrot_hbm, krot_hbm,
    vlow_hbm, lse_hbm, mixed_hbm, in_one_t, hid_hbm, cos_ref, sin_ref, vec_ref,
    layer_out, grad_input, small_out, grad_g, grad_u, grad_d, grad_qkv, grad_out, kept,
    own, ring, sent, sib, lefts, gin, middle, tall, wa, qrot, krot, vlow, lse, mixed,
    gmix, dqkv, gk, gv, osend, orecv, cots, got, stage, small, small_got,
    in_sem, ring_send, ring_recv, sib_send, sib_recv, x_send, x_recv, out_sem, s_send, s_recv, down_sem, hid_sem,
):
    rows, heads, skip, tail = cfg
    grads = (grad_g, grad_u, grad_d)
    own_tokens, width = gin.shape
    tokens = 2 * own_tokens
    width_q = heads * HD
    width_qkv = width_q + 2 * HD
    side_rows = CHIPS * rows
    _, gain_one, gain_two, start_of = small_inputs(vec_ref, width_qkv, width)
    here = Spot(rows)
    shard, me = here.shard, here.me
    sums = Sums(here, own, ring, ring_send, ring_recv)
    wide_qkv, wide_out = (2, width_qkv // 2), (2, width_q // 2)
    pieces = [(1, 3 * CHUNK)] * (JOBS - 1) + [(1, 3 * tail), (1, width_qkv), (1, width_q)]
    own_rows = pl.ds(pl.multiple_of(shard * own_tokens, TILE), own_tokens)
    other_rows = pl.ds(pl.multiple_of((1 - shard) * own_tokens, TILE), own_tokens)

    def at_own(t, size=TILE):
        return pl.ds(pl.multiple_of(shard * own_tokens + t * size, size), size)

    def at_other(t, size=TILE):
        return pl.ds(pl.multiple_of((1 - shard) * own_tokens + t * size, size), size)

    def get(index, source, target):
        return pltpu.make_async_copy(source, target, in_sem.at[index])

    sums_in = [get(i, later.at[skip + i], own.at[i]) for i in range(3)]
    norm_in = [get(3, gin_hbm, gin), get(4, middle_hbm, middle), get(5, cot_hbm, cots)]
    rest_in = [
        get(7, w_attn, wa), get(8, qrot_hbm, qrot), get(9, krot_hbm, krot), get(10, vlow_hbm, vlow),
        get(11, lse_hbm, lse), get(12, mixed_hbm, mixed),
    ]
    for copy in sums_in[:2] + norm_in + sums_in[2:] + rest_in:
        copy.start()
    for side in range(2):
        for chip in range(CHIPS):
            member = 2 * chip + (here.core if side == 0 else 1 - here.core)
            begin = side * side_rows + chip * rows
            get(13, in_one_t.at[here.part(member), :], lefts.at[0, begin : begin + rows, :]).start()

    def bit(value):
        return lax.rem(lax.div(me, value), 2)

    def flipped(*values):
        return me + sum(value - 2 * value * bit(value) for value in values)

    ranks = (here.core + 2 * shard, bit(2) + 2 * bit(4), bit(8))
    partners = (
        ({"dp": flipped(1)}, {"mp": 1 - shard}, {"dp": flipped(1), "mp": 1 - shard}),
        ({"dp": flipped(2)}, {"dp": flipped(4)}, {"dp": flipped(2, 4)}),
        ({"dp": flipped(8)},),
    )

    def rank_of(group, k):
        rank = ranks[group]
        return (rank + 1 - 2 * lax.rem(rank, 2), rank + 2 - 4 * lax.div(rank, 2), 3 - rank)[k]

    barrier = pltpu.get_barrier_semaphore()
    greeted = [p for group in partners for p in group] + [{"dp": n} for n in here.next]
    for target in greeted:
        pl.semaphore_signal(barrier, inc=1, device_id=target, device_id_type=MESH)
    pl.semaphore_wait(barrier, len(greeted))

    def swap_copy(index, src, dst):
        return pltpu.make_async_remote_copy(
            src_ref=src, dst_ref=dst, send_sem=x_send.at[index], recv_sem=x_recv.at[index],
            device_id={"mp": 1 - shard}, device_id_type=MESH,
        )

    some = own_tokens // 2

    def out_swap(index):
        part = slice(index * some, (index + 1) * some)
        return swap_copy(index, osend.at[part, :], orecv.at[part, :])

    half_tiles = own_tokens // TILE

    def attn_swap(t):
        return swap_copy(2 + t, tall.at[at_own(t), :], tall.at[at_own(t), :])

    def attn_got(t):
        return swap_copy(2 + t, tall.at[at_other(t), :], tall.at[at_other(t), :])

    one_swap = swap_copy(2 + half_tiles, dqkv.at[other_rows, :], got)

    def result_copies(job):
        if job < JOBS:
            size = CHUNK if job + 1 < JOBS else tail
            return [
                pltpu.make_async_copy(
                    stage.at[:, m * size : (m + 1) * size],
                    grads[m].at[:, job * CHUNK : job * CHUNK + size], out_sem.at[m],
                )
                for m in range(3)
            ]
        target = (grad_qkv, grad_out)[job - JOBS]
        return [pltpu.make_async_copy(stage.at[:, 0 : target.shape[1]], target, out_sem.at[0])]

    last_in = get(0, later.at[skip + 3, :, 0 : 3 * tail], own.at[0, :, 0 : 3 * tail])

    def run(point):
        for event in BACK_EVENTS.get(point, "").split():
            job, step = int(event[0]), int(event[1])
            o = p = job % 3
            if step == 0:
                if job == 2:
                    sums_in[2].wait()
                if job == 3:
                    last_in.wait()
                sums.start(o, p, pieces[job])
            elif step < HALF:
                sums.step(o, p, step, pieces[job])
            else:
                if job:
                    for copy in result_copies(job - 1):
                        copy.wait()
                sums.end(o, p, pieces[job], stage)
                for copy in result_copies(job):
                    copy.start()
                if job == 0:
                    last_in.start()

    for i in range(2):
        sums_in[i].wait()
        sums.start(i, i, pieces[i])

    for copy in norm_in:
        copy.wait()
    small[0, :, :] = jnp.zeros_like(small[0])

    @pl.loop(0, half_tiles)
    def _(t):
        part = tile_of(t)
        v = middle[part, :]
        factor = lax.rsqrt(jnp.mean(v * v, axis=-1, keepdims=True) + EPS)
        unit = v * factor
        e = gin[part, :]
        scaled = e * gain_two
        inner = jnp.mean(scaled * unit, axis=-1, keepdims=True)
        total = cots[part, :].astype(F32) + factor * (scaled - unit * inner)
        middle[part, :] = total
        tall[at_own(t), :] = total.astype(BF16)
        attn_swap(t).start()
        small[0, 1:2, :] += jnp.sum(e * unit, axis=0, keepdims=True)

    keep = pltpu.make_async_copy(middle, kept, out_sem.at[5])
    keep.start()
    gin[...] = jnp.zeros_like(gin)
    keep.wait()
    middle[...] = jnp.zeros_like(middle)
    chunks = w_down.shape[0]
    top = width // 2

    def down_in(chunk):
        slot = chunk % 2
        weight_to = lefts.at[1, slot * top : (slot + 1) * top, :]
        size = CHUNK if chunk + 1 < chunks else tail
        if chunk + 1 < chunks:
            parts = [slice(0, 2 * CHUNK)]
        else:
            parts = [slice(h * CHUNK, h * CHUNK + tail) for h in range(2)]
        copies = [
            pltpu.make_async_copy(
                w_down.at[chunk, :, part], weight_to.at[:, part], down_sem.at[slot, i]
            )
            for i, part in enumerate(parts)
        ]
        return copies + [pltpu.make_async_copy(
            hiddens.at[chunk, :, 0:size], dqkv.at[:, slot * CHUNK : slot * CHUNK + size],
            hid_sem.at[slot],
        )]

    for copy in down_in(0):
        copy.start()
    for chunk in range(chunks):
        if chunk + 1 < chunks:
            for copy in down_in(chunk + 1):
                copy.start()
        for copy in down_in(chunk):
            copy.wait()
        slot, size = chunk % 2, CHUNK if chunk + 1 < chunks else tail
        part = slice(slot * CHUNK, slot * CHUNK + size)
        for h in range(2):
            @pl.loop(0, top // TILE)
            def _(n):
                rows_of = pl.ds(pl.multiple_of(slot * top + n * TILE, TILE), TILE)
                at = pl.ds(pl.multiple_of(h * top + n * TILE, TILE), TILE)
                weight = lefts[1, rows_of, h * CHUNK : h * CHUNK + size]
                product = contract(dqkv[:, part], weight, 1, 1)
                middle[:, at] += product[0:own_tokens, :]
                gin[:, at] += product[own_tokens:, :]

        run(f"w{chunk}")

    @pl.loop(0, half_tiles)
    def _(t):
        one, two = middle[tile_of(t), :], gin[tile_of(t), :]
        osend[tile_of(t), :] = jnp.where(shard == 0, two, one).astype(BF16)
        gin[tile_of(t), :] = jnp.where(shard == 0, one, two)

    out_swap(0).start()
    middle_in = get(4, middle_hbm, middle)
    middle_in.start()
    run("w9")
    middle_in.wait()

    @pl.loop(0, half_tiles)
    def _(t):
        gin[tile_of(t), :] += middle[tile_of(t), :]

    for copy in rest_in:
        copy.wait()
    for t in range(half_tiles):
        attn_got(t).wait_recv()

    @pl.loop(0, tokens // TILE)
    def _(t):
        gmix[tile_of(t), :] = contract(tall[tile_of(t), :], wa[:, width_qkv:], 1, 0).astype(BF16)

    gk[...] = jnp.zeros_like(gk)
    gv[...] = jnp.zeros_like(gv)

    @pl.loop(0, heads)
    def _(h):
        columns = tile_of(h, HD)
        for i in range(SEQ_LEN // BLOCK):
            low, high = key_range(i)
            part = pl.ds(i * BLOCK, BLOCK)
            query, grad = qrot[part, columns], gmix[part, columns]
            keys = krot[low:high, :]
            scores = contract(keys, query, 1, 1) * SCALE
            seen = visible_keys(start_of(i), low, high, i)
            probs = jnp.where(seen, jnp.exp(scores - lse[h, 0:1, part]), 0.0)
            grad_probs = contract(vlow[low:high, :], grad, 1, 1)
            row_term = jnp.sum(probs * grad_probs, axis=0, keepdims=True)
            grad_scores = (probs * (grad_probs - row_term)).astype(BF16)
            gk[low:high, :] += contract(grad_scores, query, 1, 0)
            gv[low:high, :] += contract(probs.astype(BF16), grad, 1, 0)
            dqkv[part, columns] = turn(
                contract(grad_scores, keys, 0, 0) * SCALE, cos_ref[part, :], -sin_ref[part, :]
            ).astype(BF16)

        for head in range(heads):
            if f"h{head}" in BACK_EVENTS:
                @pl.when(h == head)
                def _():
                    run(f"h{head}")

    dqkv[:, width_q : width_q + HD] = turn(gk[...] * SCALE, cos_ref[...], -sin_ref[...]).astype(BF16)
    dqkv[:, width_q + HD :] = gv[...].astype(BF16)

    one_swap.start()
    out_swap(1).start()
    run("o")

    side_sent = (sent, gmix.at[0:side_rows, :])
    side_got = (sib, qrot.at[0:side_rows, :])

    def side_copy(job, m, columns):
        return pltpu.make_async_remote_copy(
            src_ref=side_sent[job].at[:, columns],
            dst_ref=side_got[job].at[:, columns],
            send_sem=sib_send.at[job, m],
            recv_sem=sib_recv.at[job, m],
            device_id={"dp": here.sibling},
            device_id_type=MESH,
        )

    get(13, lefts.at[0], lefts.at[0]).wait()

    def send_side(job, left, right, pieces):
        for m in range(pieces[0]):
            columns = slice(m * pieces[1], (m + 1) * pieces[1])
            side_sent[job][:, columns] = contract(
                lefts[left, side_rows:, :], right[:, columns], 1, 0
            ).astype(BF16)
            side_copy(job, m, columns).start()

    def own_side(job, left, right, pieces, o):
        for m in range(pieces[0]):
            columns = slice(m * pieces[1], (m + 1) * pieces[1])
            side_copy(job, m, columns).wait()
            own[o, :, columns] = (
                contract(lefts[left, 0:side_rows, :], right[:, columns], 1, 0)
                + side_got[job][:, columns].astype(F32)
            ).astype(BF16)

    send_side(0, 0, dqkv, wide_qkv)
    run("q0")
    own_side(0, 0, dqkv, wide_qkv, 1)
    other_in = get(6, w_other, lefts.at[0])
    other_in.start()
    run("q1")

    for group in range(width // (4 * rows)):
        @pl.loop(0, tokens // TILE)
        def _(t):
            part = tile_of(t)
            turned = tall[part, group * 4 * rows : (group + 1) * 4 * rows].T
            for k in range(4):
                chip, odd = (4 * group + k) // 2, k % 2
                side = odd + here.core - 2 * odd * here.core
                to = pl.ds(pl.multiple_of(side * side_rows + chip * rows, 16), rows)
                lefts[1, to, part] = turned[k * rows : (k + 1) * rows, :]

        run(f"t{group}")

    for t in range(half_tiles):
        attn_swap(t).wait_send()
    hid_in = get(15, hid_hbm, tall)
    hid_in.start()

    fac = gk
    hid_in.wait()

    @pl.loop(0, tokens // TILE)
    def _(t):
        v = tall[tile_of(t), :].astype(F32)
        factor = lax.rsqrt(jnp.mean(v * v, axis=-1, keepdims=True) + EPS)
        fac[tile_of(t), :] = jnp.broadcast_to(factor, (TILE, HD))

    run("f")

    @pl.loop(0, width // TILE)
    def _(n):
        e = contract(dqkv[other_rows, :], wa[tile_of(n), 0:width_qkv], 1, 1)
        unit = tall[other_rows, tile_of(n)].astype(F32) * fac[other_rows, 0:1]
        small[0, 0:1, tile_of(n)] += jnp.sum(e * unit, axis=0, keepdims=True)

    run("g")

    @pl.loop(0, width // TILE)
    def _(n):
        e = contract(dqkv[own_rows, :], wa[tile_of(n), 0:width_qkv], 1, 1)
        middle[:, tile_of(n)] = e
        unit = tall[own_rows, tile_of(n)].astype(F32) * fac[own_rows, 0:1]
        small[0, 0:1, tile_of(n)] += jnp.sum(e * unit, axis=0, keepdims=True)

    @pl.loop(0, tokens // TILE)
    def _(t):
        bias = jnp.sum(dqkv[tile_of(t), :].astype(F32), axis=0, keepdims=True)
        at_query = pl.ds(pl.multiple_of(shard * width_q, HD), width_q)
        small[0, 2:3, at_query] += bias[:, 0:width_q]
        small[0, 3:4, tile_of(shard, HD)] += bias[:, width_q : width_q + HD]
        small[0, 3:4, tile_of(shard + 2, HD)] += bias[:, width_q + HD :]

    run("b")

    def small_copy(group, k):
        return pltpu.make_async_remote_copy(
            src_ref=small.at[group], dst_ref=small_got.at[group, ranks[group]],
            send_sem=s_send.at[group, k], recv_sem=s_recv.at[group, ranks[group]],
            device_id=partners[group][k], device_id_type=MESH,
        )

    def small_start(group):
        for k in range(len(partners[group])):
            small_copy(group, k).start()
        small_got[group, ranks[group]] = small[group]

    def small_end(group):
        count = len(partners[group])
        for k in range(count):
            ref = small_got.at[group, rank_of(group, k)]
            pltpu.make_async_remote_copy(
                src_ref=ref, dst_ref=ref, send_sem=s_send.at[group, k],
                recv_sem=s_recv.at[group, rank_of(group, k)],
                device_id=partners[group][k], device_id_type=MESH,
            ).wait_recv()
            small_copy(group, k).wait_send()
        total = small_got[group, 0]
        for rank in range(1, count + 1):
            total = total + small_got[group, rank]
        small[group + 1] = total

    small_start(0)
    send_side(1, 1, mixed, wide_out)
    run("u0")
    own_side(1, 1, mixed, wide_out, 2)
    small_end(0)
    small_start(1)
    run("u1")

    def layer_rows(index):
        part = slice(index * some, (index + 1) * some)
        out_swap(index).wait()
        orecv[part, :] = (gin[part, :] + orecv[part, :].astype(F32)).astype(BF16)
        copy = pltpu.make_async_copy(
            orecv.at[part, :], layer_out.at[part, :], out_sem.at[(3, 6)[index]]
        )
        copy.start()
        return copy

    def keep_in(index):
        part = slice(index * some, (index + 1) * some)
        return get(14, kept.at[part, :], gin.at[0:some, :])

    layer_copies = [layer_rows(0)]
    keep_in(0).start()
    run("l0")
    small_end(1)
    small_start(2)
    run("l1")
    small_end(2)
    run("l2")
    small_out[...] = small[3]

    one_swap.wait()
    other_in.wait()

    @pl.loop(0, width // TILE)
    def _(n):
        middle[:, tile_of(n)] += contract(got[...], lefts[0, tile_of(n), :], 1, 1)

    for index in range(2):
        part = slice(index * some, (index + 1) * some)
        of = pl.ds(pl.multiple_of(shard * own_tokens + index * some, some), some)
        if index:
            keep_in(index).start()
        keep_in(index).wait()
        factor = fac[of, 0:1]
        unit = tall[of, :].astype(F32) * factor
        scaled = middle[part, :] * gain_one
        inner = jnp.mean(scaled * unit, axis=-1, keepdims=True)
        cots[part, :] = (gin[0:some, :] + factor * (scaled - unit * inner)).astype(BF16)

    input_copy = pltpu.make_async_copy(cots, grad_input, out_sem.at[4])
    input_copy.start()
    layer_copies.append(layer_rows(1))
    run("z1")
    for copy in [input_copy] + layer_copies + result_copies(JOBS + 1):
        copy.wait()


def attention_back(
    later, gin, middle, cot, hiddens, w_down, w_other, forward, cos2, sin2, vector, tail
):
    w_attn, qrot, krot, vlow, lse, mixed, in_one_t, hid_all = forward
    own_tokens, width = cot.shape
    tokens = 2 * own_tokens
    heads = lse.shape[0]
    width_q = heads * HD
    width_qkv = width_q + 2 * HD
    side_rows, wide = later.shape[1:]
    rows = side_rows // CHIPS
    vmem = pl.BlockSpec(memory_space=pltpu.VMEM)
    hbm = pl.BlockSpec(memory_space=pl.ANY)
    dma = pltpu.SemaphoreType.DMA
    shape = jax.ShapeDtypeStruct
    half = (own_tokens, width)
    n_swaps = own_tokens // TILE + 3
    return pl.pallas_call(
        functools.partial(backward_kernel, (rows, heads, later.shape[0] - JOBS, tail)),
        in_specs=[hbm] * 15 + [vmem] * 3,
        out_specs=[hbm, hbm, vmem] + [hbm] * 6,
        out_shape=[
            shape(half, BF16), shape(half, BF16), shape((8, width), F32),
        ] + [shape((rows, (JOBS - 1) * CHUNK + tail), F32)] * 3 + [
            shape((rows, width_qkv), F32), shape((rows, width_q), F32), shape(half, F32),
        ],
        scratch_shapes=[
            pltpu.VMEM((3, side_rows, wide), BF16),
            pltpu.VMEM((3, HALF, 2, rows, wide), BF16),
            pltpu.VMEM((side_rows, width_qkv), BF16),
            pltpu.VMEM((side_rows, width_qkv), BF16),
            pltpu.VMEM((2, width, tokens), BF16),
            pltpu.VMEM(half, F32),
            pltpu.VMEM(half, F32),
            pltpu.VMEM((tokens, width), BF16),
            pltpu.VMEM(w_attn.shape, BF16),
            pltpu.VMEM((tokens, width_q), BF16),
            pltpu.VMEM((tokens, HD), BF16),
            pltpu.VMEM((tokens, HD), BF16),
            pltpu.VMEM(lse.shape, F32),
            pltpu.VMEM((tokens, width_q), BF16),
            pltpu.VMEM((tokens, width_q), BF16),
            pltpu.VMEM((tokens, width_qkv), BF16),
            pltpu.VMEM((tokens, HD), F32),
            pltpu.VMEM((tokens, HD), F32),
            pltpu.VMEM(half, BF16),
            pltpu.VMEM(half, BF16),
            pltpu.VMEM(half, BF16),
            pltpu.VMEM((own_tokens, width_qkv), BF16),
            pltpu.VMEM((rows, wide), F32),
            pltpu.VMEM((4, 8, width), F32),
            pltpu.VMEM((3, 4, 8, width), F32),
            dma((16,)), dma((3, HALF, 2, 3)), dma((3, HALF, 2, 3)), dma((2, 2)), dma((2, 2)),
            dma((n_swaps,)), dma((n_swaps,)), dma((7,)), dma((3, 3)), dma((3, 4)), dma((2, 2)), dma((2,)),
        ],
        compiler_params=pltpu.CompilerParams(
            collective_id=3, has_side_effects=True, vmem_limit_bytes=63 * 2**20
        ),
        cost_estimate=pl.CostEstimate(
            flops=10 * heads * tokens * tokens * HD, bytes_accessed=50 * 2**20, transcendentals=0
        ),
        name="attention_back",
    )(
        later, gin, middle, cot, hiddens, w_down, w_other, w_attn, qrot, krot, vlow, lse, mixed, in_one_t,
        hid_all, cos2, sin2, vector,
    )


def finish_kernel(
    layer_in, input_in, first_g, first_u, first_d, last_g, last_u, last_d, qkv_in, out_in, small_in,
    layer_out, grad_input, grad_q, grad_k, grad_v, grad_out, grad_g, grad_u, grad_d, vec_one, vec_two,
    bias_q, bias_k, bias_v,
    layer, grad, gates, ups, downs, qkv, out, in_sem, out_sem,
):
    early = first_g.shape[1]
    moves = [
        (layer_in, layer, layer_out), (input_in, grad, grad_input),
        (first_g, gates.at[:, 0:early], None), (last_g, gates.at[:, early:], None),
        (first_u, ups.at[:, 0:early], None), (last_u, ups.at[:, early:], None),
        (first_d, downs.at[:, 0:early], None), (last_d, downs.at[:, early:], None),
        (qkv_in, qkv, None), (out_in, out, grad_out),
    ]
    loads = [
        pltpu.make_async_copy(source, buffer, in_sem.at[i]) for i, (source, buffer, _) in enumerate(moves)
    ]
    for copy in loads:
        copy.start()
    stores = []

    def store(buffer, target):
        copy = pltpu.make_async_copy(buffer, target, out_sem.at[len(stores)])
        copy.start()
        stores.append(copy)

    for i, (_, buffer, target) in enumerate(moves):
        loads[i].wait()
        if target is not None:
            store(buffer, target)
        if i in (3, 5, 7):
            store(*((gates, grad_g), (ups, grad_u), (downs, grad_d))[i // 2 - 1])
    begin = 0
    for target in (grad_q, grad_k, grad_v):
        store(qkv.at[:, begin : begin + target.shape[1]], target)
        begin += target.shape[1]
    for i, target in enumerate((vec_one, vec_two, bias_q)):
        target[...] = small_in[i : i + 1, :].reshape(target.shape[0])
    wide = bias_k.shape[0]
    bias_k[...] = small_in[3:4, 0:wide].reshape(wide)
    bias_v[...] = small_in[3:4, wide : 2 * wide].reshape(wide)
    for copy in stores:
        copy.wait()


def finish(layer_out, grad_input, first, last, sum_qkv, sum_out, small, width_q):
    vmem = pl.BlockSpec(memory_space=pltpu.VMEM)
    hbm = pl.BlockSpec(memory_space=pl.ANY)
    shape = jax.ShapeDtypeStruct
    rows, width_qkv = sum_qkv.shape
    width_k = (width_qkv - width_q) // 2
    width = layer_out.shape[1]
    ffn = (rows, first[0].shape[1] + last[0].shape[1])
    dma = pltpu.SemaphoreType.DMA
    return pl.pallas_call(
        finish_kernel,
        in_specs=[hbm] * 10 + [vmem],
        out_specs=[hbm] * 9 + [vmem] * 5,
        out_shape=[
            shape(layer_out.shape, BF16), shape(grad_input.shape, BF16),
            shape((rows, width_q), F32), shape((rows, width_k), F32), shape((rows, width_k), F32),
            shape(sum_out.shape, F32), shape(ffn, F32), shape(ffn, F32), shape(ffn, F32),
            shape((width,), F32), shape((width,), F32), shape((2 * width_q,), F32),
            shape((2 * width_k,), F32), shape((2 * width_k,), F32),
        ],
        scratch_shapes=[
            pltpu.VMEM(layer_out.shape, BF16), pltpu.VMEM(grad_input.shape, BF16),
            pltpu.VMEM(ffn, F32), pltpu.VMEM(ffn, F32), pltpu.VMEM(ffn, F32),
            pltpu.VMEM(sum_qkv.shape, F32), pltpu.VMEM(sum_out.shape, F32), dma((10,)), dma((9,)),
        ],
        compiler_params=pltpu.CompilerParams(vmem_limit_bytes=62 * 2**20),
        name="finish",
    )(layer_out, grad_input, *first, *last, sum_qkv, sum_out, small)


def body_fused(
    hidden_in, positions, query_weight, query_bias, key_weight, key_bias, value_weight, value_bias,
    out_weight, gate_weight, up_weight, down_weight, attn_gain, ffn_gain, cotangent,
):
    rows, width_q = query_weight.shape
    heads = width_q // HD
    hidden_units = gate_weight.shape[1]
    own_tokens, width = hidden_in.shape
    half = HD // 2
    lanes = jnp.arange(HD, dtype=jnp.int32)
    freq = jnp.power(ROPE_BASE, -2.0 * (lanes % half).astype(F32) / HD)
    ffn_weights = (gate_weight, up_weight, down_weight.T)
    (w_ffn, w_attn, hidden_all, grad_ffn, in_one_t, qrot, krot, vlow, mixed, lse, middle,
     inputs_two, vector, cos2, sin2, in_two_t, cot_t) = forward_attention(
        hidden_in, cotangent,
        (freq, positions, query_bias, key_bias, value_bias, attn_gain, ffn_gain),
        (query_weight, key_weight, value_weight, out_weight.T, *ffn_weights),
        heads,
    )
    hiddens, w_down, grad_normed_two, later, *first_sums, w_other, _ = feed_forward(
        inputs_two, grad_ffn, in_two_t, cot_t, w_ffn, w_attn, width_q + 2 * HD, ffn_weights
    )
    tail = units_of(-(-hidden_units // CHUNK) - 1, hidden_units)
    layer_out, grad_input, small, *sums = attention_back(
        later, grad_normed_two, middle, cotangent, hiddens, w_down, w_other,
        (w_attn, qrot, krot, vlow, lse, mixed, in_one_t, hidden_all), cos2, sin2, vector, tail,
    )
    (layer_out, grad_input, sum_q, sum_k, sum_v, sum_out, sum_gate, sum_up, sum_down, gain_one,
     gain_two, sum_bias_q, sum_bias_k, sum_bias_v) = finish(
        layer_out, grad_input, first_sums, sums[:3], *sums[3:5], small, width_q
    )
    return (
        layer_out,
        grad_input,
        sum_q,
        sum_bias_q,
        sum_k,
        sum_bias_k,
        sum_v,
        sum_bias_v,
        sum_out.T,
        sum_gate,
        sum_up,
        sum_down.T,
        gain_one,
        gain_two,
    )


def body(*arrays):
    rows = arrays[2].shape[0]
    if lax.axis_size("dp") == 2 * CHIPS and rows % 32 == 0 and -(-arrays[9].shape[1] // CHUNK) == 9:
        return body_fused(*arrays)
    return body_general(*arrays)


def solution(mesh):
    tokens, weight, weight_t = P(("dp", "mp"), None), P("dp", "mp"), P("mp", "dp")
    return jax.shard_map(
        body,
        mesh=mesh,
        in_specs=(
            tokens, P("dp"), weight, P(), weight, P(), weight, P(), weight_t,
            weight, weight, weight_t, P(), P(), tokens,
        ),
        out_specs=(
            tokens, tokens, weight, P(), weight, P(), weight, P(), weight_t,
            weight, weight, weight_t, P(), P(),
        ),
        check_vma=False,
    )
```

```python
import functools
import math

import jax
import jax.numpy as jnp
from jax import lax
from jax.experimental import pallas as pl
from jax.experimental.pallas import tpu as pltpu
from jax.sharding import PartitionSpec as P

HD = 128
SEQ_LEN = 1024
DOC_MAX = 512
EPS = 1e-06
ROPE_BASE = 1000000.0
BLOCK = 256
SCALE = 1.0 / math.sqrt(HD)
F32 = jnp.float32
BF16 = jnp.bfloat16


def contract(left, right, left_dim, right_dim):
    return lax.dot_general(
        left, right, (((left_dim,), (right_dim,)), ((), ())), preferred_element_type=F32
    )


def key_range(block_id):
    low = max(0, block_id * BLOCK - (DOC_MAX - 1)) // BLOCK * BLOCK
    return low, (block_id + 1) * BLOCK


def visible(start_row, low, high, block_id):
    keys = low + lax.broadcasted_iota(jnp.int32, (high - low, BLOCK), 0)
    queries = block_id * BLOCK + lax.broadcasted_iota(jnp.int32, (high - low, BLOCK), 1)
    return (keys >= start_row) & (keys <= queries)


def turn(values, cosines, sines):
    return values * cosines + pltpu.roll(values, HD // 2, 1) * sines


def attend_kernel(
    q_ref, k_ref, v_ref, bq_ref, bk_ref, bv_ref, cos_ref, sin_ref, start_ref,
    mixed_ref, qrot_ref, krot_ref, vlow_ref, lse_ref,
):
    head = pl.program_id(0)

    @pl.when(head == 0)
    def _():
        krot_ref[...] = turn(k_ref[...] + bk_ref[...], cos_ref[...], sin_ref[...]).astype(BF16)
        vlow_ref[...] = (v_ref[...] + bv_ref[...]).astype(BF16)

    qrot_ref[...] = turn(q_ref[...] + bq_ref[...], cos_ref[...], sin_ref[...]).astype(BF16)
    for i in range(SEQ_LEN // BLOCK):
        low, high = key_range(i)
        rows = pl.ds(i * BLOCK, BLOCK)
        start_row = start_ref[0:1, rows]
        scores = contract(krot_ref[low:high, :], qrot_ref[rows, :], 1, 1) * SCALE
        scores = jnp.where(visible(start_row, low, high, i), scores, -1e30)
        top = jnp.max(scores, axis=0, keepdims=True)
        weights = jnp.exp(scores - top)
        total = jnp.sum(weights, axis=0, keepdims=True)
        probs = (weights * (1.0 / total)).astype(BF16)
        mixed_ref[rows, :] = contract(probs, vlow_ref[low:high, :], 0, 0).astype(BF16)
        lse_ref[0, 0:1, rows] = top + jnp.log(total)


def attend(qkv, bias, cos2, sin2, start, heads):
    seq = SEQ_LEN
    full = lambda shape: pl.BlockSpec(shape, lambda h: (0,) * len(shape))
    col = lambda: pl.BlockSpec((seq, HD), lambda h: (0, h))
    at = lambda j: pl.BlockSpec((seq, HD), lambda h: (0, j))
    bat = lambda j: pl.BlockSpec((1, HD), lambda h: (0, j))
    return pl.pallas_call(
        attend_kernel,
        grid=(heads,),
        in_specs=[
            col(), at(heads), at(heads + 1),
            pl.BlockSpec((1, HD), lambda h: (0, h)), bat(heads), bat(heads + 1),
            full((seq, HD)), full((seq, HD)), full((1, seq)),
        ],
        out_specs=[
            col(), col(), full((seq, HD)), full((seq, HD)),
            pl.BlockSpec((1, 8, seq), lambda h: (h, 0, 0)),
        ],
        out_shape=[
            jax.ShapeDtypeStruct((seq, heads * HD), BF16),
            jax.ShapeDtypeStruct((seq, heads * HD), BF16),
            jax.ShapeDtypeStruct((seq, HD), BF16),
            jax.ShapeDtypeStruct((seq, HD), BF16),
            jax.ShapeDtypeStruct((heads, 8, seq), F32),
        ],
        compiler_params=pltpu.CompilerParams(vmem_limit_bytes=40 * 2**20),
        cost_estimate=pl.CostEstimate(
            flops=4 * heads * seq * seq * HD, bytes_accessed=10 * 2**20,
            transcendentals=heads * seq * seq // 2,
        ),
        name="attend",
    )(qkv, qkv, qkv, bias, bias, bias, cos2, sin2, start)


def attend_back_kernel(
    heads, qrot_ref, krot_ref, vlow_ref, lse_ref, grad_ref, cos_ref, sin_ref, start_ref,
    out_ref, gk_ref, gv_ref,
):
    head = pl.program_id(0)

    @pl.when(head == 0)
    def _():
        gk_ref[...] = jnp.zeros_like(gk_ref)
        gv_ref[...] = jnp.zeros_like(gv_ref)

    for i in range(SEQ_LEN // BLOCK):
        low, high = key_range(i)
        rows = pl.ds(i * BLOCK, BLOCK)
        start_row = start_ref[0:1, rows]
        query, grad = qrot_ref[rows, :], grad_ref[rows, :]
        keys = krot_ref[low:high, :]
        scores = contract(keys, query, 1, 1) * SCALE
        probs = jnp.where(
            visible(start_row, low, high, i), jnp.exp(scores - lse_ref[0, 0:1, rows]), 0.0
        )
        grad_probs = contract(vlow_ref[low:high, :], grad, 1, 1)
        row_term = jnp.sum(probs * grad_probs, axis=0, keepdims=True)
        grad_scores = (probs * (grad_probs - row_term)).astype(BF16)
        gk_ref[low:high, :] += contract(grad_scores, query, 1, 0)
        gv_ref[low:high, :] += contract(probs.astype(BF16), grad, 1, 0)
        grad_query = contract(grad_scores, keys, 0, 0) * SCALE
        out_ref[rows, pl.ds(pl.multiple_of(head * HD, HD), HD)] = turn(
            grad_query, cos_ref[rows, :], -sin_ref[rows, :]
        ).astype(BF16)

    @pl.when(head == heads - 1)
    def _():
        out_ref[:, heads * HD : (heads + 1) * HD] = turn(
            gk_ref[...] * SCALE, cos_ref[...], -sin_ref[...]
        ).astype(BF16)
        out_ref[:, (heads + 1) * HD :] = gv_ref[...].astype(BF16)


def attend_back(qrot, krot, vlow, lse, grad_mixed, cos2, sin2, start, heads):
    seq = SEQ_LEN
    full = lambda shape: pl.BlockSpec(shape, lambda h: (0,) * len(shape))
    col = lambda: pl.BlockSpec((seq, HD), lambda h: (0, h))
    return pl.pallas_call(
        functools.partial(attend_back_kernel, heads),
        grid=(heads,),
        in_specs=[
            col(), full((seq, HD)), full((seq, HD)),
            pl.BlockSpec((1, 8, seq), lambda h: (h, 0, 0)), col(),
            full((seq, HD)), full((seq, HD)), full((1, seq)),
        ],
        out_specs=full((seq, (heads + 2) * HD)),
        out_shape=jax.ShapeDtypeStruct((seq, (heads + 2) * HD), BF16),
        scratch_shapes=[pltpu.VMEM((seq, HD), F32), pltpu.VMEM((seq, HD), F32)],
        compiler_params=pltpu.CompilerParams(vmem_limit_bytes=40 * 2**20),
        cost_estimate=pl.CostEstimate(
            flops=10 * heads * seq * seq * HD, bytes_accessed=10 * 2**20,
            transcendentals=heads * seq * seq // 2,
        ),
        name="attend_back",
    )(qrot, krot, vlow, lse, grad_mixed, cos2, sin2, start)


class Ring:
    def __init__(self, members):
        self.members = members
        self.chips = members // 2
        self.half = self.chips // 2
        n = self.chips
        self.path = [2 * r if r < n // 2 else 2 * (n - 1 - r) + 1 for r in range(n)]
        self.offsets = [self.half]
        for k in range(self.half - 1, 0, -1):
            self.offsets += [k, n - k]
        self.offsets += [0]
        self.place = {k: i for i, k in enumerate(self.offsets)}

    def pairs(self, shift):
        n, path = self.chips, self.path
        return [
            (path[r] * 2 + c, path[(r + shift) % n] * 2 + c) for r in range(n) for c in range(2)
        ]

    def up(self, block):
        return lax.ppermute(block, "dp", self.pairs(1))

    def down(self, block):
        return lax.ppermute(block, "dp", self.pairs(-1))

    def across(self, block):
        return lax.ppermute(block, "dp", [(i, i ^ 1) for i in range(self.members)])

    def order(self):
        me = lax.axis_index("dp")
        path = jnp.array(self.path, jnp.int32)
        spot = jnp.zeros((self.chips,), jnp.int32).at[path].set(jnp.arange(self.chips, dtype=jnp.int32))
        mine = spot[me // 2]
        offsets = jnp.array(self.offsets, jnp.int32)
        chips = path[(mine + offsets) % self.chips]
        core = me % 2
        return jnp.concatenate([chips * 2 + core, chips * 2 + (1 - core)])

    def gather(self, block):
        n, h = self.chips, self.half
        rows = block.shape[0]
        got = {0: block}
        for k in range(1, h):
            got[n - k] = self.up(got[(n - k + 1) % n])
            got[k] = self.down(got[k - 1])
        first = self.up(got[h + 1][: rows // 2])
        second = self.down(got[h - 1][rows // 2 :])
        other = {k: self.across(got[k]) for k in got}
        got_half = [first, second]
        other_half = [self.across(first), self.across(second)]
        blocks = []
        for side, halves in ((got, got_half), (other, other_half)):
            for k in self.offsets:
                blocks.append(tuple(halves) if k == h else (side[k],))
        return blocks, first

    def reduce(self, own, rows):
        def term(k):
            begin = self.place[k] * rows
            return jnp.concatenate([o[begin : begin + rows] for o in own], axis=1)

        return self.reduce_terms(term, rows)

    def reduce_terms(self, term, rows):
        n, h = self.chips, self.half
        up = self.up(term(h)[: rows // 2])
        down = self.down(term(h)[rows // 2 :])
        for k in range(h - 1, 0, -1):
            mine_up, mine_down = term(k), term(n - k)
            if k == h - 1:
                sent_up = jnp.concatenate([
                    (up.astype(F32) + mine_up[: rows // 2].astype(F32)).astype(BF16),
                    mine_up[rows // 2 :],
                ])
                sent_down = jnp.concatenate([
                    mine_down[: rows // 2],
                    (down.astype(F32) + mine_down[rows // 2 :].astype(F32)).astype(BF16),
                ])
            else:
                sent_up = (up.astype(F32) + mine_up.astype(F32)).astype(BF16)
                sent_down = (down.astype(F32) + mine_down.astype(F32)).astype(BF16)
            up, down = self.up(sent_up), self.down(sent_down)
        return term(0).astype(F32) + up.astype(F32) + down.astype(F32)


def stack(blocks, begin, stop):
    return jnp.concatenate([part[:, begin:stop] for block in blocks for part in block], axis=0)


def swap(block):
    return lax.ppermute(block, "mp", [(0, 1), (1, 0)])


def rms(values):
    return lax.rsqrt(jnp.mean(values * values, axis=-1, keepdims=True) + EPS)


def after(value, *earlier):
    return lax.optimization_barrier((value, *earlier))[0]


def split_hidden(width, parts):
    tiles = width // HD
    cuts = [round(tiles * i / parts) * HD for i in range(parts + 1)]
    return list(zip(cuts[:-1], cuts[1:]))


def body_general(
    hidden_in, positions, query_weight, query_bias, key_weight, key_bias, value_weight, value_bias,
    out_weight, gate_weight, up_weight, down_weight, attn_gain, ffn_gain, cotangent,
):
    ring = Ring(lax.axis_size("dp"))
    rows = query_weight.shape[0]
    width = rows * ring.members
    side_rows = rows * ring.chips
    heads = query_weight.shape[1] // HD
    width_q = heads * HD
    width_qkv = width_q + 2 * HD
    own_tokens = hidden_in.shape[0]
    shard = lax.axis_index("mp")

    def whole(own, other):
        first = jnp.where(shard == 0, own, other)
        second = jnp.where(shard == 0, other, own)
        return jnp.concatenate([first, second], axis=0)

    def own_half(values):
        return lax.dynamic_slice_in_dim(values, shard * own_tokens, own_tokens, 0)

    def other_half(values):
        return lax.dynamic_slice_in_dim(values, (1 - shard) * own_tokens, own_tokens, 0)

    hidden_other = swap(hidden_in)
    attn_pack = jnp.concatenate([query_weight, key_weight, value_weight, out_weight.T], axis=1)
    attn_blocks, attn_last = ring.gather(attn_pack)
    cotangent_other = swap(after(cotangent, hidden_other))
    down_t = down_weight.T
    spans = split_hidden(gate_weight.shape[1], 2)
    ffn_blocks = []
    last = attn_last
    for begin, stop in spans:
        pack = jnp.concatenate(
            [gate_weight[:, begin:stop], up_weight[:, begin:stop], down_t[:, begin:stop]], axis=1
        )
        blocks, last = ring.gather(after(pack, last))
        ffn_blocks.append(blocks)

    order = ring.order()
    feature = (order[:, None] * rows + jnp.arange(rows, dtype=jnp.int32)[None, :]).reshape(width)
    shuffle = (jnp.arange(width, dtype=jnp.int32)[:, None] == feature[None, :]).astype(BF16)

    def to_order(values):
        return contract(values, shuffle, 1, 0).astype(BF16)

    def from_order(values):
        return contract(values, shuffle, 1, 1).astype(BF16)

    def vector_to_order(values):
        return jnp.sum(jnp.where(shuffle > 0, values[:, None], 0.0), axis=0)

    def vector_from_order(values):
        return jnp.sum(jnp.where(shuffle > 0, values[None, :], 0.0), axis=1)

    gain_attn, gain_ffn = vector_to_order(attn_gain), vector_to_order(ffn_gain)

    hidden_all = to_order(whole(hidden_in, hidden_other))
    resid_all = hidden_all.astype(F32)
    factor_one = rms(resid_all)
    inputs_one = (resid_all * factor_one * gain_attn).astype(BF16)
    half = HD // 2
    freq = jnp.power(ROPE_BASE, -2.0 * jnp.arange(half, dtype=F32) / HD)
    angles = positions.astype(F32)[:, None] * freq[None, :]
    cosines, sines = jnp.cos(angles), jnp.sin(angles)
    cos2 = jnp.concatenate([cosines, cosines], axis=1)
    sin2 = jnp.concatenate([-sines, sines], axis=1)
    start = (jnp.arange(SEQ_LEN, dtype=jnp.int32) - positions)[None, :]
    bias = jnp.concatenate([
        lax.dynamic_slice_in_dim(query_bias, shard * width_q, width_q, 0),
        lax.dynamic_slice_in_dim(key_bias, shard * HD, HD, 0),
        lax.dynamic_slice_in_dim(value_bias, shard * HD, HD, 0),
    ])[None, :]
    qkv_full = stack(attn_blocks, 0, width_qkv)
    out_full = stack(attn_blocks, width_qkv, width_qkv + width_q)
    qkv = contract(inputs_one, qkv_full, 1, 0)
    mixed, qrot, krot, vlow, lse = attend(qkv, bias, cos2, sin2, start, heads)
    out_other = swap(contract(other_half(mixed), out_full, 1, 1).astype(BF16))
    middle = (
        own_half(hidden_all).astype(F32)
        + contract(own_half(mixed), out_full, 1, 1)
        + out_other.astype(F32)
    )
    factor_two = rms(middle)
    in_two_own = (middle * factor_two * gain_ffn).astype(BF16)
    inputs_two = whole(in_two_own, swap(in_two_own))
    grad_ffn = to_order(whole(cotangent, cotangent_other))

    hiddens, grads_gate, grads_up, weights = [], [], [], []
    for (begin, stop), blocks in zip(spans, ffn_blocks):
        wide = stop - begin
        gate_full = stack(blocks, 0, wide)
        up_full = stack(blocks, wide, 2 * wide)
        down_full = stack(blocks, 2 * wide, 3 * wide)
        grad_hidden = contract(grad_ffn, down_full, 1, 0)
        gate = contract(inputs_two, gate_full, 1, 0)
        up = contract(inputs_two, up_full, 1, 0)
        sig = jax.nn.sigmoid(gate)
        swish = gate * sig
        hiddens.append((swish * up).astype(BF16))
        grads_gate.append((grad_hidden * up * sig * (1.0 + gate * (1.0 - sig))).astype(BF16))
        grads_up.append((grad_hidden * swish).astype(BF16))
        weights.append((gate_full, up_full, down_full))

    def side(values, index):
        return values[:, index * side_rows : (index + 1) * side_rows]

    def chip_sum(left, right):
        sent = contract(side(left, 1), right, 0, 0).astype(BF16)
        return (contract(side(left, 0), right, 0, 0) + ring.across(sent).astype(F32)).astype(BF16)

    sums = []
    for index in range(len(spans)):
        own = [
            chip_sum(inputs_two, grads_gate[index]),
            chip_sum(inputs_two, grads_up[index]),
            chip_sum(grad_ffn, hiddens[index]),
        ]
        sums.append(ring.reduce(own, rows))

    def back_two(take):
        total = None
        for (gate_full, up_full, _), g, u in zip(weights, grads_gate, grads_up):
            term = contract(take(g), gate_full, 1, 1) + contract(take(u), up_full, 1, 1)
            total = term if total is None else total + term
        return total

    def forward_out(take):
        total = None
        for (_, _, down_full), h in zip(weights, hiddens):
            term = contract(take(h), down_full, 1, 1)
            total = term if total is None else total + term
        return total

    back_other = swap(back_two(other_half).astype(BF16))
    grad_normed_two = back_two(own_half) + back_other.astype(F32)
    ffn_other = swap(forward_out(other_half).astype(BF16))
    layer_out = from_order(
        (middle + forward_out(own_half) + ffn_other.astype(F32)).astype(BF16)
    )

    unit_two = middle * factor_two
    scaled = grad_normed_two * gain_ffn
    gain_two = jnp.sum(grad_normed_two * unit_two, axis=0)
    inner = jnp.mean(scaled * unit_two, axis=-1, keepdims=True)
    grad_middle = own_half(grad_ffn).astype(F32) + factor_two * (scaled - unit_two * inner)

    grad_attn_own = grad_middle.astype(BF16)
    grad_attn = whole(grad_attn_own, swap(grad_attn_own))
    grad_mixed = contract(grad_attn, out_full, 1, 0).astype(BF16)
    grad_qkv = attend_back(qrot, krot, vlow, lse, grad_mixed, cos2, sin2, start, heads)
    sum_out = ring.reduce([chip_sum(grad_attn, mixed)], rows)
    sum_qkv = ring.reduce([chip_sum(inputs_one, grad_qkv)], rows)

    back_one_other = contract(other_half(grad_qkv), qkv_full, 1, 1)
    one_other = swap(back_one_other.astype(BF16))
    back_one_own = contract(own_half(grad_qkv), qkv_full, 1, 1)
    unit_all = resid_all * factor_one
    unit_one = own_half(unit_all)
    gain_one = jnp.sum(back_one_own * unit_one, axis=0) + jnp.sum(
        back_one_other * other_half(unit_all), axis=0
    )
    grad_normed_one = back_one_own + one_other.astype(F32)
    scaled_one = grad_normed_one * gain_attn
    inner_one = jnp.mean(scaled_one * unit_one, axis=-1, keepdims=True)
    through_one = own_half(factor_one) * (scaled_one - unit_one * inner_one)
    grad_input = from_order((grad_middle + through_one).astype(BF16))

    bias_part = jnp.sum(grad_qkv.astype(F32), axis=0)

    def place(part, total):
        return lax.dynamic_update_slice_in_dim(
            jnp.zeros((total,), F32), part, shard * part.shape[0], 0
        )

    small = jnp.concatenate([
        vector_from_order(gain_one),
        vector_from_order(gain_two),
        place(bias_part[:width_q], query_bias.shape[0]),
        place(bias_part[width_q : width_q + HD], key_bias.shape[0]),
        place(bias_part[width_q + HD :], value_bias.shape[0]),
    ])
    small = small + swap(small)
    bit = 1
    while bit < ring.members:
        small = small + lax.ppermute(small, "dp", [(i, i ^ bit) for i in range(ring.members)])
        bit *= 2
    cuts = [width, width, query_bias.shape[0], key_bias.shape[0], value_bias.shape[0]]
    pieces, begin = [], 0
    for cut in cuts:
        pieces.append(small[begin : begin + cut])
        begin += cut

    def gather_cols(index):
        parts = []
        for (begin, stop), total in zip(spans, sums):
            wide = stop - begin
            parts.append(total[:, index * wide : (index + 1) * wide])
        return jnp.concatenate(parts, axis=1)

    return (
        layer_out,
        grad_input,
        sum_qkv[:, :width_q],
        pieces[2],
        sum_qkv[:, width_q : width_q + HD],
        pieces[3],
        sum_qkv[:, width_q + HD :],
        pieces[4],
        sum_out.T,
        gather_cols(0),
        gather_cols(1),
        gather_cols(2).T,
        pieces[0],
        pieces[1],
    )


CHIPS = 8
HALF = CHIPS // 2
CHUNK = 512
TILE = 256
MESH = pl.DeviceIdType.MESH


class Spot:
    def __init__(self, rows):
        self.rows = rows
        self.me = lax.axis_index("dp")
        self.shard = lax.axis_index("mp")
        self.core = lax.rem(self.me, 2)
        chip = lax.div(self.me, 2)
        line, back = lax.div(chip, 2), lax.rem(chip, 2)
        self.spot = line * (1 - back) + (CHIPS - 1 - line) * back
        self.sibling = self.me + 1 - 2 * self.core
        self.next = (self.chip(1) * 2 + self.core, self.chip(CHIPS - 1) * 2 + self.core)

    def chip(self, offset):
        place = lax.rem(self.spot + offset, CHIPS)
        back = lax.div(place, HALF)
        return (1 - back) * (2 * place) + back * (2 * (CHIPS - 1 - place) + 1)

    def greet(self):
        barrier = pltpu.get_barrier_semaphore()
        for target in (
            {"dp": self.sibling}, {"dp": self.next[0]}, {"dp": self.next[1]}, {"mp": 1 - self.shard}
        ):
            pl.semaphore_signal(barrier, inc=1, device_id=target, device_id_type=MESH)
        pl.semaphore_wait(barrier, 4)

    def part(self, block, half=None):
        begin, size = block * self.rows, self.rows
        if half is not None:
            size = self.rows // 2
            begin = begin + half * size
        return pl.ds(pl.multiple_of(begin, 16), size)


def tile_of(index, size=TILE):
    return pl.ds(pl.multiple_of(index * size, size), size)


def small_inputs(ref, width_qkv, width):
    gains = width_qkv + width, width_qkv + 2 * width

    def start_of(block):
        begin = gains[1] + block * BLOCK
        return ref[0:1, begin : begin + BLOCK]

    return (
        ref[0:1, 0:width_qkv], ref[0:1, width_qkv : gains[0]], ref[0:1, gains[0] : gains[1]], start_of
    )


def visible_keys(start_row, low, high, block_id):
    shape = (high - low, BLOCK)
    keys = low + lax.broadcasted_iota(jnp.int32, shape, 0)
    queries = block_id * BLOCK + lax.broadcasted_iota(jnp.int32, shape, 1)
    return (keys.astype(F32) >= start_row) & (keys <= queries)


class Gather:
    def __init__(self, here, held, home, landed, hop_send, hop_recv, side_send, side_recv, store_sem):
        self.here, self.held, self.home, self.landed = here, held, home, landed
        self.hop_send, self.hop_recv = hop_send, hop_recv
        self.side_send, self.side_recv, self.store_sem = side_send, side_recv, store_sem

    def member(self, step, way, sibling=False):
        here = self.here
        chip = here.chip((CHIPS - step) % CHIPS if way == 0 else step)
        return chip * 2 + (1 - here.core if sibling else here.core)

    def hop(self, unit, step, way, arrival=False):
        half = way if step == HALF else None
        source = self.held(unit, step if arrival else step - 1, way, half)
        target = source if arrival or self.landed(unit) else self.held(unit, step, way, half)
        return pltpu.make_async_remote_copy(
            src_ref=source, dst_ref=target, send_sem=self.hop_send.at[unit, step - 1, way],
            recv_sem=self.hop_recv.at[unit, step - 1, way],
            device_id={"dp": self.here.next[way]}, device_id_type=MESH,
        )

    def index(self, step, way):
        return 0 if step == 0 else 2 * step - 1 + way

    def across(self, unit, step, way, arrival=False):
        half = way if step == HALF else None
        target = self.home(unit, self.member(step, way, sibling=arrival), half)
        source = target if arrival else self.held(unit, step, way, half)
        index = self.index(step, way)
        return pltpu.make_async_remote_copy(
            src_ref=source, dst_ref=target, send_sem=self.side_send.at[unit, index],
            recv_sem=self.side_recv.at[unit, index],
            device_id={"dp": self.here.sibling}, device_id_type=MESH,
        )

    def store(self, unit, step, way):
        half = way if step == HALF else None
        return pltpu.make_async_copy(
            self.held(unit, step, way, half), self.home(unit, self.member(step, way), half),
            self.store_sem.at[unit, self.index(step, way)],
        )

    def start(self, unit):
        for way in range(2):
            self.hop(unit, 1, way).start()
        self.across(unit, 0, 0).start()
        if not self.landed(unit):
            self.store(unit, 0, 0).start()

    def step(self, unit, step):
        for way in range(2):
            self.hop(unit, step - 1, way, arrival=True).wait_recv()
            if step <= HALF:
                self.hop(unit, step, way).start()
            self.across(unit, step - 1, way).start()
            if not self.landed(unit):
                self.store(unit, step - 1, way).start()

    def pieces(self):
        return [(0, 0)] + [(step, way) for step in range(1, HALF + 1) for way in range(2)]

    def end(self, unit):
        for step, way in self.pieces():
            self.across(unit, step, way, arrival=True).wait_recv()

    def sent(self, unit):
        for step, way in self.pieces():
            self.across(unit, step, way).wait_send()
            if step:
                self.hop(unit, step, way).wait_send()
            if not self.landed(unit):
                self.store(unit, step, way).wait()


def units_of(chunk, total):
    return min(CHUNK, total - chunk * CHUNK)


def pack_copies(weights, pack, chunks, sem):
    copies = []
    for i, chunk in enumerate(chunks):
        begin, size = chunk * CHUNK, units_of(chunk, weights[0].shape[1])
        for m, ref in enumerate(weights):
            copies.append(pltpu.make_async_copy(
                ref.at[:, begin : begin + size], pack.at[i, :, m * size : (m + 1) * size],
                sem.at[i, m],
            ))
    return copies


LATER = 3
PAIRS = 2
QUARTERS = 4


def forward_kernel(
    cfg, hid, cot, turns, places, bias_q, bias_k, bias_v, gain_a, gain_f,
    wq, wk, wv, wo, wg, wu, wd,
    w_ffn, w_attn, hid_all, cot_all, in_one_t, qrot, krot, vlow, mixed, lse, middle, in_two, vec_ref,
    cos_ref, sin_ref, in_two_t, cot_t,
    wa, qkv, psend, precv, pack, slots, in_one, cots, turned, turned_cot,
    local_sem, pack_sem, store_sem, hop_send, hop_recv, side_send, side_recv, x_send, x_recv, t_sem,
):
    rows, heads, units = cfg
    own_tokens, width = hid.shape
    tokens = 2 * own_tokens
    width_q = heads * HD
    width_qkv = width_q + 2 * HD
    here = Spot(rows)
    shard = here.shard

    own_rows = pl.ds(pl.multiple_of(shard * own_tokens, TILE), own_tokens)
    other_rows = pl.ds(pl.multiple_of((1 - shard) * own_tokens, TILE), own_tokens)
    quarter = own_tokens // QUARTERS

    def quarter_rows(index, side):
        return pl.ds(pl.multiple_of(side * own_tokens + index * quarter, quarter), quarter)

    mine = here.part(here.me)
    attn_copies, column = [], 0
    for i, ref in enumerate((wq, wk, wv, wo)):
        wide = ref.shape[1]
        attn_copies.append(
            pltpu.make_async_copy(ref, wa.at[mine, column : column + wide], local_sem.at[i])
        )
        column += wide
    ffn_copies = pack_copies((wg, wu, wd), pack, range(PAIRS * units), pack_sem)
    own_copies = [
        pltpu.make_async_copy(hid, hid_all.at[own_rows, :], local_sem.at[4]),
        pltpu.make_async_copy(cot, cots.at[own_rows, :], local_sem.at[5]),
    ]
    for copy in attn_copies + own_copies + ffn_copies:
        copy.start()

    column = 0
    for ref in (bias_q, bias_k, bias_v):
        size = ref.shape[0] // 2
        row = ref[...].reshape(1, 2 * size)
        vec_ref[:, column : column + size] = jnp.where(shard == 0, row[:, :size], row[:, size:])
        column += size
    for ref in (gain_a, gain_f):
        vec_ref[:, column : column + width] = ref[...].reshape(1, width)
        column += width
    vec_ref[:, column : column + tokens] = (
        lax.broadcasted_iota(jnp.int32, (1, tokens), 1) - places[...].reshape(1, tokens)
    ).astype(F32)
    bias, gain_one, gain_two, start_of = small_inputs(vec_ref, width_qkv, width)

    here.greet()

    def swap_copy(index, src, dst):
        return pltpu.make_async_remote_copy(
            src_ref=src, dst_ref=dst, send_sem=x_send.at[index], recv_sem=x_recv.at[index],
            device_id={"mp": 1 - shard}, device_id_type=MESH,
        )

    hid_swap = (swap_copy(0, hid, hid_all.at[own_rows, :]), swap_copy(0, hid, hid_all.at[other_rows, :]))
    mix_swap = swap_copy(1, psend, precv)
    two_swap = (
        swap_copy(2, in_two.at[own_rows, :], in_two.at[own_rows, :]),
        swap_copy(2, in_two.at[other_rows, :], in_two.at[other_rows, :]),
    )

    def cot_swap(index, arrival=False):
        ref = cots.at[quarter_rows(index, 1 - shard if arrival else shard), :]
        return swap_copy(3 + index, ref, ref)

    def home(unit, member, half):
        part = here.part(member, half)
        if unit == 0:
            return wa.at[part, :]
        return w_ffn.at[(unit - 1) * PAIRS : unit * PAIRS, part, :]

    def held(unit, step, way, half):
        if unit == 0:
            return home(0, gather.member(step, way), half)
        part = slice(0, rows) if half is None else slice(half * rows // 2, (half + 1) * rows // 2)
        if step == 0:
            return pack.at[(unit - 1) * PAIRS : unit * PAIRS, part, :]
        slot = 2 * HALF - 2 if step == HALF else 2 * (step - 1) + way
        return slots.at[unit - 1, slot, :, part, :]

    gather = Gather(
        here, held, home, lambda unit: unit == 0, hop_send, hop_recv, side_send, side_recv, store_sem
    )
    ffn_units = range(1, units + 1)

    hid_swap[0].start()
    for copy in attn_copies:
        copy.wait()
    gather.start(0)
    at = jnp.broadcast_to(places[...].reshape(1, tokens).astype(F32), (HD, tokens)).T
    angles = at * turns[...].reshape(1, HD)
    cos_ref[...] = jnp.cos(angles)
    lanes = lax.broadcasted_iota(jnp.int32, (tokens, HD), 1)
    sin_ref[...] = jnp.where(lanes < HD // 2, -1.0, 1.0) * jnp.sin(angles)

    for step in range(2, HALF + 1):
        gather.step(0, step)
    for copy in ffn_copies:
        copy.wait()
    for unit in ffn_units:
        gather.start(unit)
    gather.step(0, HALF + 1)

    for copy in own_copies:
        copy.wait()
    hid_swap[1].wait_recv()
    for index in range(QUARTERS - 1):
        cot_swap(index).start()

    @pl.loop(0, tokens // TILE)
    def _(t):
        v = hid_all[tile_of(t), :].astype(F32)
        factor = lax.rsqrt(jnp.mean(v * v, axis=-1, keepdims=True) + EPS)
        in_one[tile_of(t), :] = (v * factor * gain_one).astype(BF16)

    gather.end(0)
    wa_out = pltpu.make_async_copy(wa, w_attn, local_sem.at[6])
    wa_out.start()

    @pl.loop(0, tokens // TILE)
    def _(t):
        part = tile_of(t)
        qkv[part, :] = contract(in_one[part, :], wa[:, 0:width_qkv], 1, 0) + bias
        cosines, sines = cos_ref[part, :], sin_ref[part, :]
        for h in range(heads):
            columns = slice(h * HD, (h + 1) * HD)
            qrot[part, columns] = turn(qkv[part, columns], cosines, sines).astype(BF16)
        krot[part, :] = turn(qkv[part, width_q : width_q + HD], cosines, sines).astype(BF16)
        vlow[part, :] = qkv[part, width_q + HD :].astype(BF16)

    def attend(blocks):
        @pl.loop(0, heads)
        def _(h):
            columns = tile_of(h, HD)
            for i in blocks:
                low, high = key_range(i)
                part = pl.ds(i * BLOCK, BLOCK)
                scores = contract(krot[low:high, :], qrot[part, columns], 1, 1) * SCALE
                scores = jnp.where(visible_keys(start_of(i), low, high, i), scores, -1e30)
                top = jnp.max(scores, axis=0, keepdims=True)
                weights = jnp.exp(scores - top)
                total = jnp.sum(weights, axis=0, keepdims=True)
                probs = (weights * (1.0 / total)).astype(BF16)
                mixed[part, columns] = contract(probs, vlow[low:high, :], 0, 0).astype(BF16)
                lse[h, 0:1, part] = top + jnp.log(total)

    halves = (range(own_tokens // BLOCK), range(own_tokens // BLOCK, tokens // BLOCK))
    for index in range(2):
        @pl.when(shard == index)
        def _():
            attend(halves[1 - index])

    @pl.loop(0, width // TILE)
    def _(n):
        weight = wa[tile_of(n), width_qkv:]
        psend[:, tile_of(n)] = contract(mixed[other_rows, :], weight, 1, 1).astype(BF16)

    mix_swap.start()
    for index in range(2):
        @pl.when(shard == index)
        def _():
            attend(halves[index])

    @pl.loop(0, width // TILE)
    def _(n):
        weight = wa[tile_of(n), width_qkv:]
        middle[:, tile_of(n)] = (
            contract(mixed[own_rows, :], weight, 1, 1) + hid[:, tile_of(n)].astype(F32)
        )

    for unit in ffn_units:
        gather.step(unit, 2)

    def transpose(source, target, first, begin, count):
        @pl.loop(0, width // TILE)
        def _(n):
            for t in range(count):
                part = pl.ds(pl.multiple_of(begin + t * TILE, TILE), TILE)
                target[tile_of(n), part] = source[part, tile_of(n)].T

    transpose(in_one, turned, 0, 0, tokens // TILE)
    one_turned = pltpu.make_async_copy(turned, in_one_t, t_sem.at[0])
    one_turned.start()
    mine_begin, theirs_begin = shard * own_tokens, (1 - shard) * own_tokens
    transpose(cots, turned_cot, 0, mine_begin, own_tokens // TILE)
    for index in range(QUARTERS // 2):
        cot_swap(index, arrival=True).wait_recv()
    transpose(cots, turned_cot, 0, theirs_begin, own_tokens // TILE // 2)

    mix_swap.wait_recv()

    @pl.loop(0, own_tokens // TILE)
    def _(t):
        part = tile_of(t)
        v = middle[part, :] + precv[part, :].astype(F32)
        middle[part, :] = v
        factor = lax.rsqrt(jnp.mean(v * v, axis=-1, keepdims=True) + EPS)
        to = pl.ds(pl.multiple_of(shard * own_tokens + t * TILE, TILE), TILE)
        in_two[to, :] = (v * factor * gain_two).astype(BF16)

    two_swap[0].start()
    cot_swap(QUARTERS - 1).start()
    one_turned.wait()
    for unit in ffn_units:
        gather.step(unit, 3)
    transpose(in_two, turned, 0, mine_begin, own_tokens // TILE)
    for unit in list(ffn_units)[:1]:
        gather.step(unit, 4)
    two_swap[1].wait_recv()
    transpose(in_two, turned, 0, theirs_begin, own_tokens // TILE)
    two_turned = pltpu.make_async_copy(turned, in_two_t, t_sem.at[1])
    two_turned.start()
    for unit in list(ffn_units)[1:]:
        gather.step(unit, 4)
    for index in range(QUARTERS // 2, QUARTERS):
        cot_swap(index, arrival=True).wait_recv()
    transpose(cots, turned_cot, 0, theirs_begin + own_tokens // 2, own_tokens // TILE // 2)
    cot_copies = [
        pltpu.make_async_copy(cots, cot_all, t_sem.at[2]),
        pltpu.make_async_copy(turned_cot, cot_t, t_sem.at[3]),
    ]
    for copy in cot_copies:
        copy.start()
    for unit in ffn_units:
        gather.step(unit, 5)
    for unit in ffn_units:
        gather.end(unit)
    for unit in range(units + 1):
        gather.sent(unit)
    hid_swap[0].wait_send()
    mix_swap.wait_send()
    two_swap[0].wait_send()
    for index in range(QUARTERS):
        cot_swap(index).wait_send()
    for copy in [wa_out, two_turned] + cot_copies:
        copy.wait()


def forward_attention(hidden_in, cotangent, vectors, weights, heads):
    own_tokens, width = hidden_in.shape
    tokens = 2 * own_tokens
    rows = weights[0].shape[0]
    chunks = -(-weights[4].shape[1] // CHUNK)
    units = (chunks - LATER) // PAIRS
    early = units * PAIRS
    width_q = heads * HD
    width_attn = 2 * width_q + 2 * HD
    wide = 3 * CHUNK
    vmem = pl.BlockSpec(memory_space=pltpu.VMEM)
    hbm = pl.BlockSpec(memory_space=pl.ANY)
    dma = pltpu.SemaphoreType.DMA
    shape = jax.ShapeDtypeStruct
    pieces = 2 * HALF + 1
    return pl.pallas_call(
        functools.partial(forward_kernel, (rows, heads, units)),
        in_specs=[vmem, hbm] + [vmem] * 7 + [hbm] * 7,
        out_specs=[hbm, hbm, vmem, hbm, hbm] + [vmem] * 10 + [hbm, hbm],
        out_shape=[
            shape((early, width, wide), BF16),
            shape((width, width_attn), BF16),
            shape((tokens, width), BF16),
            shape((tokens, width), BF16),
            shape((width, tokens), BF16),
            shape((tokens, width_q), BF16),
            shape((tokens, HD), BF16),
            shape((tokens, HD), BF16),
            shape((tokens, width_q), BF16),
            shape((heads, 8, tokens), F32),
            shape((own_tokens, width), F32),
            shape((tokens, width), BF16),
            shape((1, width_q + 2 * HD + 2 * width + tokens), F32),
            shape((tokens, HD), F32),
            shape((tokens, HD), F32),
            shape((width, tokens), BF16),
            shape((width, tokens), BF16),
        ],
        scratch_shapes=[
            pltpu.VMEM((width, width_attn), BF16),
            pltpu.VMEM((tokens, width_q + 2 * HD), F32),
            pltpu.VMEM((own_tokens, width), BF16),
            pltpu.VMEM((own_tokens, width), BF16),
            pltpu.VMEM((early, rows, wide), BF16),
            pltpu.VMEM((units, 2 * HALF - 1, PAIRS, rows, wide), BF16),
            pltpu.VMEM((tokens, width), BF16),
            pltpu.VMEM((tokens, width), BF16),
            pltpu.VMEM((width, tokens), BF16),
            pltpu.VMEM((width, tokens), BF16),
            dma((7,)), dma((early, 3)), dma((units + 1, pieces)),
            dma((units + 1, HALF, 2)), dma((units + 1, HALF, 2)),
            dma((units + 1, pieces)), dma((units + 1, pieces)),
            dma((3 + QUARTERS,)), dma((3 + QUARTERS,)), dma((4,)),
        ],
        compiler_params=pltpu.CompilerParams(
            collective_id=1, has_side_effects=True, vmem_limit_bytes=63 * 2**20
        ),
        cost_estimate=pl.CostEstimate(
            flops=6 * tokens * width * width_attn, bytes_accessed=120 * 2**20, transcendentals=0
        ),
        name="forward_attention",
    )(hidden_in, cotangent, *vectors, *weights)


class Sums:
    def __init__(self, here, own, places, send_sem, recv_sem):
        self.here, self.own, self.places = here, own, places
        self.send_sem, self.recv_sem = send_sem, recv_sem

    def chip(self, step, way):
        distance = HALF - step
        return self.here.chip(distance if way == 0 else CHIPS - distance)

    def copy(self, o, p, step, way, m, columns):
        here, rows = self.here, self.here.rows
        return pltpu.make_async_remote_copy(
            src_ref=self.own.at[o, here.part(self.chip(step, way), way if step == 0 else None), columns],
            dst_ref=self.places.at[p, step, way, 0 : rows // 2 if step == 0 else rows, columns],
            send_sem=self.send_sem.at[p, step, way, m],
            recv_sem=self.recv_sem.at[p, step, way, m],
            device_id={"dp": here.next[way]},
            device_id_type=MESH,
        )

    def columns(self, pieces, m):
        count, size = pieces
        return pl.ds(pl.multiple_of(m * size, HD), size)

    def start(self, o, p, pieces):
        @pl.loop(0, pieces[0])
        def _(m):
            for way in range(2):
                self.copy(o, p, 0, way, m, self.columns(pieces, m)).start()

    def step(self, o, p, step, pieces):
        here, own = self.here, self.own

        @pl.loop(0, pieces[0])
        def _(m):
            columns = self.columns(pieces, m)
            for way in range(2):
                self.copy(o, p, step - 1, way, m, columns).wait()
            for way in range(2):
                part = here.part(self.chip(step, way), way if step == 1 else None)
                size = here.rows // 2 if step == 1 else here.rows
                own[o, part, columns] = (
                    own[o, part, columns].astype(F32)
                    + self.places[p, step - 1, way, 0:size, columns].astype(F32)
                ).astype(BF16)
                self.copy(o, p, step, way, m, columns).start()

    def end(self, o, p, pieces, target):
        own, last = self.own, HALF - 1
        part = self.here.part(self.here.chip(0))

        @pl.loop(0, pieces[0])
        def _(m):
            columns = self.columns(pieces, m)
            for way in range(2):
                self.copy(o, p, last, way, m, columns).wait()
            target[:, columns] = (
                own[o, part, columns].astype(F32)
                + self.places[p, last, 0, :, columns].astype(F32)
                + self.places[p, last, 1, :, columns].astype(F32)
            )


EVENTS = {
    (0, "a"): "G11 G21",
    (0, "c"): "G02",
    (0, "f"): "G12",
    (1, "a"): "R00",
    (1, "b"): "G22",
    (1, "e"): "G03",
    (2, "a"): "R10",
    (2, "b"): "G13",
    (2, "c"): "R01 G23",
    (3, "a"): "G04 R11",
    (3, "c"): "G14",
    (4, "a"): "R02",
    (4, "b"): "G24",
    (4, "c"): "G05",
    (4, "e"): "R12",
    (4, "f"): "G15",
    (5, "a"): "R03 R20",
    (5, "c"): "G25 R13",
    (6, "0a"): "R04 R21",
    (6, "1a"): "R14 R22",
    (6, "1b"): "R30",
    (6, "2b"): "R23",
    (7, "0a"): "R31",
    (7, "1a"): "R24 R32 R40",
    (7, "2a"): "R33",
    (7, "2b"): "R41",
    (8, "1a"): "R34 R42",
    (8, "1b"): "R43",
    (8, "2b"): "R44",
}
SETS = 3


def ffn_kernel(
    cfg, in2_hbm, cot_hbm, in2t_hbm, cott_hbm, w_ffn, w_attn, wg, wu, wd,
    hiddens, w_down, gin_own, later, grad_g, grad_u, grad_d, w_other, w_late,
    in2, cot, in2t, cott, wbuf, acts, gin, own, sent, sib, ring, stage, pack,
    in_sem, w_sem, sib_send, sib_recv, ring_send, ring_recv, out_sem, g_sem, end_sem, free_sem,
    pack_sem, store_sem, hop_send, hop_recv, side_send, side_recv, park_sem, fetch_sem, hid_sem, down_sem,
):
    rows, chunks, total = cfg
    grads = (grad_g, grad_u, grad_d)
    tokens, width = in2.shape
    side_rows = CHIPS * rows
    own_tokens = tokens // 2
    first = chunks - LATER
    rings = first - 1
    here = Spot(rows)
    shard = here.shard
    sums = Sums(here, own, ring, ring_send, ring_recv)
    ring_pieces = (3, CHUNK)
    own_rows = pl.ds(pl.multiple_of(shard * own_tokens, TILE), own_tokens)
    other_rows = pl.ds(pl.multiple_of((1 - shard) * own_tokens, TILE), own_tokens)

    def size_of(i):
        return units_of(first + i, total)

    def load(chunk, s):
        return pltpu.make_async_copy(w_ffn.at[chunk], wbuf.at[s], w_sem.at[s])

    def load_late(i, s):
        columns = slice(0, 3 * size_of(i))
        return pltpu.make_async_copy(w_late.at[i, :, columns], wbuf.at[s, :, columns], w_sem.at[s])

    def down_copies(chunk, s, size=CHUNK):
        top = width // 2
        return [
            pltpu.make_async_copy(
                wbuf.at[s, h * top : (h + 1) * top, 2 * size : 3 * size],
                w_down.at[chunk, :, h * CHUNK : h * CHUNK + size], down_sem.at[s, h],
            )
            for h in range(2)
        ]

    def hidden_copies(index, chunk, size=CHUNK):
        return [pltpu.make_async_copy(
            acts.at[index, :, 2 * size : 3 * size], hiddens.at[chunk, :, 0:size], hid_sem.at[index]
        )]

    def home(unit, member, half):
        return w_late.at[unit, here.part(member, half), 0 : 3 * size_of(unit)]

    def held(unit, step, way, half):
        size = rows if half is None else rows // 2
        columns = slice(0, 3 * size_of(unit))
        if step == 0:
            return pack.at[unit, :, columns]
        slot = 2 * (step - 1) + way
        whole = 2 * HALF - 2
        if unit < 2:
            buffer, begin = 1 + unit, (whole if step == HALF else slot) * rows
            offset = 0
            if half is not None:
                offset = half * size
        else:
            base = (whole + 1) * rows
            if step == HALF:
                buffer, begin, offset = 1 + way, base + whole // 2 * rows, 0
            else:
                buffer, begin = 1 + slot // (whole // 2), base + slot % (whole // 2) * rows
                offset = 0 if half is None else half * size
        return acts.at[buffer, begin + offset : begin + offset + size, columns]

    gather = Gather(
        here, held, home, lambda unit: False, hop_send, hop_recv, side_send, side_recv, store_sem
    )
    own_blocks = pack_copies((wg, wu, wd), pack, range(first, chunks), pack_sem)

    inputs = [
        pltpu.make_async_copy(in2_hbm, in2, in_sem.at[0]),
        pltpu.make_async_copy(cot_hbm, cot, in_sem.at[1]),
    ]
    turned = []
    for i, (source, target) in enumerate(((in2t_hbm, in2t), (cott_hbm, cott))):
        for side in range(2):
            for chip in range(CHIPS):
                member = 2 * chip + (here.core if side == 0 else 1 - here.core)
                begin = side * side_rows + chip * rows
                turned.append(pltpu.make_async_copy(
                    source.at[here.part(member), :], target.at[begin : begin + rows, :],
                    in_sem.at[2 + i],
                ))
    for copy in own_blocks + [load(0, 0)] + inputs:
        copy.start()
    here.greet()
    for copy in own_blocks:
        copy.wait()
    gather.start(0)

    def result_copies(chunk):
        return [
            pltpu.make_async_copy(
                stage.at[:, m * CHUNK : (m + 1) * CHUNK],
                grads[m].at[:, tile_of(chunk, CHUNK)],
                out_sem.at[m],
            )
            for m in range(3)
        ]

    def fetch(chunk):
        return pltpu.make_async_copy(
            later.at[chunk - SETS], own.at[chunk % SETS], fetch_sem.at[chunk % SETS]
        )

    def park(chunk, p, early, size=CHUNK):
        columns = slice(0, 3 * size)
        target = own.at[chunk] if early else later.at[chunk - SETS, :, columns]
        return pltpu.make_async_copy(sib.at[p, :, columns], target, park_sem.at[p])

    def ring_event(chunk, step):
        o, p = chunk % SETS, chunk % 2
        if step == 0:
            if chunk >= SETS:
                fetch(chunk).wait()
            sums.start(o, p, ring_pieces)
        elif step < HALF:
            sums.step(o, p, step, ring_pieces)
        else:
            if chunk:
                for copy in result_copies(chunk - 1):
                    copy.wait()
            sums.end(o, p, ring_pieces, stage)
            for copy in result_copies(chunk):
                copy.start()
            if chunk + SETS < rings:
                fetch(chunk + SETS).start()

    def run(events):
        for event in events.split():
            index, step = int(event[1]), int(event[2])
            if event[0] == "R":
                ring_event(index, step)
            elif step == 1:
                gather.start(index)
            else:
                gather.step(index, step)

    def sib_copy(p, m, size):
        columns = slice(m * size, (m + 1) * size)
        return pltpu.make_async_remote_copy(
            src_ref=sent.at[:, columns],
            dst_ref=sib.at[p, :, columns],
            send_sem=sib_send.at[m],
            recv_sem=sib_recv.at[p, m],
            device_id={"dp": here.sibling},
            device_id_type=MESH,
        )

    def weight_copy():
        return pltpu.make_async_remote_copy(
            src_ref=w_attn.at[:, 0 : w_other.shape[1]], dst_ref=w_other,
            send_sem=g_sem.at[2], recv_sem=g_sem.at[3],
            device_id={"mp": 1 - shard}, device_id_type=MESH,
        )

    def gin_copy():
        return pltpu.make_async_remote_copy(
            src_ref=in2.at[other_rows, :], dst_ref=cot.at[own_rows, :],
            send_sem=g_sem.at[0], recv_sem=g_sem.at[1],
            device_id={"mp": 1 - shard}, device_id_type=MESH,
        )

    def forward(index, part, s, size=CHUNK):
        for begin in range(0, size, TILE):
            stop = min(begin + TILE, size)
            gates, ups, downs = (slice(m * size + begin, m * size + stop) for m in range(3))
            gate = contract(in2[part, :], wbuf[s, :, gates], 1, 0)
            up = contract(in2[part, :], wbuf[s, :, ups], 1, 0)
            grad = contract(cot[part, :], wbuf[s, :, downs], 1, 0)
            sig = 0.5 * jnp.tanh(0.5 * gate) + 0.5
            swish = gate * sig
            acts[index, part, downs] = (swish * up).astype(BF16)
            acts[index, part, gates] = (grad * up * (sig + swish - swish * sig)).astype(BF16)
            acts[index, part, ups] = (grad * swish).astype(BF16)

    def back_gin(index, part, s, size=CHUNK):
        @pl.loop(0, width // TILE)
        def _(n):
            gin[part, tile_of(n)] += contract(
                acts[index, part, 0 : 2 * size], wbuf[s, tile_of(n), 0 : 2 * size], 1, 1
            )

    def weight_grads(index, p, between, size=CHUNK):
        for m, left in enumerate((in2t, in2t, cott)):
            columns = slice(m * size, (m + 1) * size)
            sent[:, columns] = contract(
                left[side_rows:, :], acts[index, :, columns], 1, 0
            ).astype(BF16)
            sib_copy(p, m, size).start()
        between()
        for m, left in enumerate((in2t, in2t, cott)):
            columns = slice(m * size, (m + 1) * size)
            sib_copy(p, m, size).wait()
            sib[p, :, columns] = (
                contract(left[0:side_rows, :], acts[index, :, columns], 1, 0)
                + sib[p, :, columns].astype(F32)
            ).astype(BF16)

    gin[...] = jnp.zeros_like(gin)
    for copy in inputs:
        copy.wait()
    for copy in turned:
        copy.start()

    def at_point(j, point):
        for chunk in range(first):
            if (chunk, point) in EVENTS:
                @pl.when(j == chunk)
                def _():
                    run(EVENTS[chunk, point])

    weight_copy().start()

    def start(copies):
        for copy in copies:
            copy.start()

    def wait(copies):
        for copy in copies:
            copy.wait()

    @pl.loop(0, first)
    def _(j):
        p = lax.rem(j, 2)
        load(j, p).wait()
        start(down_copies(j, p))

        @pl.when(j >= 1)
        def _():
            wait(down_copies(j - 1, 1 - p))
            wait(hidden_copies(0, j - 1))

        @pl.when(j + 1 < first)
        def _():
            load(j + 1, 1 - p).start()

        @pl.when(j == first - 1)
        def _():
            gather.end(0)
            gather.sent(0)
            load_late(0, 1 - p).start()

        forward(0, slice(0, own_tokens), p)

        @pl.when((j >= 1) & (j <= SETS))
        def _():
            park(j - 1, 1 - p, True).wait()

        @pl.when(j > SETS)
        def _():
            park(j - 1, 1 - p, False).wait()

        at_point(j, "a")
        forward(0, slice(own_tokens, tokens), p)
        start(hidden_copies(0, j))
        at_point(j, "b")
        back_gin(0, slice(0, tokens), p)
        at_point(j, "c")

        @pl.when(j == 0)
        def _():
            for i, ref in enumerate((in2t, cott)):
                pltpu.make_async_copy(ref, ref, in_sem.at[2 + i]).wait()

        weight_grads(0, p, lambda: at_point(j, "e"))

        @pl.when(j < SETS)
        def _():
            park(j, p, True).start()

        @pl.when(j >= SETS)
        def _():
            park(j, p, False).start()

        at_point(j, "f")

    wait(hidden_copies(0, first - 1))
    wait(down_copies(first - 1, (first - 1) % 2))
    for unit in range(1, LATER):
        gather.end(unit)
        gather.sent(unit)

    for half in range(2):
        part = (other_rows, own_rows)[half]
        for i in range(LATER):
            size = size_of(i)
            turn = half * LATER + i
            s = (first + turn) % 2
            load_late(i, s).wait()
            if half == 0:
                start(down_copies(first + i, s, size))
            if 0 < turn <= LATER:
                wait(down_copies(first + turn - 1, 1 - s, size_of(turn - 1)))
            if turn + 1 < 2 * LATER:
                load_late((i + 1) % LATER, 1 - s).start()
            forward(i, part, s, size)
            if half == 1:
                start(hidden_copies(i, first + i, size))
            run(EVENTS.get((first + half, f"{i}a"), ""))
            back_gin(i, part, s, size)
            run(EVENTS.get((first + half, f"{i}b"), ""))
        if half == 0:
            pl.semaphore_signal(
                free_sem, inc=1, device_id={"mp": 1 - shard}, device_id_type=MESH
            )

            @pl.loop(0, own_tokens // TILE)
            def _(t):
                of = pl.ds(pl.multiple_of((1 - shard) * own_tokens + t * TILE, TILE), TILE)
                in2[of, :] = gin[of, :].astype(BF16)

            pl.semaphore_wait(free_sem, 1)
            gin_copy().start()

    for i in range(LATER):
        chunk, size = first + i, size_of(i)
        p = chunk % 2
        park(chunk - 1, 1 - p, False).wait()
        weight_grads(i, p, lambda: run(EVENTS.get((first + 2, f"{i}a"), "")), size)
        park(chunk, p, False, size).start()
        run(EVENTS.get((first + 2, f"{i}b"), ""))
    gin_copy().wait()

    @pl.loop(0, own_tokens // TILE)
    def _(t):
        of = pl.ds(pl.multiple_of(shard * own_tokens + t * TILE, TILE), TILE)
        at = pl.ds(pl.multiple_of((1 - shard) * own_tokens + t * TILE, TILE), TILE)
        gin[of, :] = gin[of, :] + cot[at, :].astype(F32)

    gin_out = pltpu.make_async_copy(gin.at[own_rows, :], gin_own, end_sem.at[0])
    gin_out.start()
    weight_copy().wait()
    last_park = park(chunks - 1, (chunks - 1) % 2, False, size_of(LATER - 1))
    for copy in [gin_out, last_park] + result_copies(rings - 1):
        copy.wait()
    for i in range(LATER):
        wait(hidden_copies(i, first + i, size_of(i)))


def feed_forward(inputs_two, grad_ffn, in_two_t, cot_t, w_ffn, w_attn, width_qkv, weights):
    tokens, width = inputs_two.shape
    rows = weights[0].shape[0]
    chunks = w_ffn.shape[0] + LATER
    pieces = 2 * HALF + 1
    hbm = pl.BlockSpec(memory_space=pl.ANY)
    side_rows, wide = CHIPS * rows, 3 * CHUNK
    dma = pltpu.SemaphoreType.DMA
    shape = jax.ShapeDtypeStruct
    half = (tokens // 2, width)
    return pl.pallas_call(
        functools.partial(ffn_kernel, (rows, chunks, weights[0].shape[1])),
        in_specs=[hbm] * 9,
        out_specs=[hbm] * 9,
        out_shape=[
            shape((chunks, tokens, CHUNK), BF16),
            shape((chunks, width // 2, 2 * CHUNK), BF16), shape(half, F32),
            shape((chunks - SETS, side_rows, wide), BF16),
        ] + [shape((rows, (chunks - LATER - 1) * CHUNK), F32)] * 3 + [
            shape((width, width_qkv), BF16),
            shape((LATER, width, wide), BF16),
        ],
        scratch_shapes=[
            pltpu.VMEM((tokens, width), BF16),
            pltpu.VMEM((tokens, width), BF16),
            pltpu.VMEM((width, tokens), BF16),
            pltpu.VMEM((width, tokens), BF16),
            pltpu.VMEM((2, width, wide), BF16),
            pltpu.VMEM((LATER, tokens, wide), BF16),
            pltpu.VMEM((tokens, width), F32),
            pltpu.VMEM((SETS, side_rows, wide), BF16),
            pltpu.VMEM((side_rows, wide), BF16),
            pltpu.VMEM((2, side_rows, wide), BF16),
            pltpu.VMEM((2, HALF, 2, rows, wide), BF16),
            pltpu.VMEM((rows, wide), F32),
            pltpu.VMEM((LATER, rows, wide), BF16),
            dma((4,)), dma((2,)), dma((3,)), dma((2, 3)),
            dma((2, HALF, 2, 3)), dma((2, HALF, 2, 3)), dma((3,)), dma((4,)), dma((1,)),
            pltpu.SemaphoreType.REGULAR,
            dma((LATER, 3)), dma((LATER, pieces)), dma((LATER, HALF, 2)), dma((LATER, HALF, 2)),
            dma((LATER, pieces)), dma((LATER, pieces)), dma((2,)), dma((SETS,)), dma((LATER,)), dma((2, 2)),
        ],
        compiler_params=pltpu.CompilerParams(
            collective_id=2, has_side_effects=True, vmem_limit_bytes=63 * 2**20
        ),
        cost_estimate=pl.CostEstimate(
            flops=18 * tokens * width * chunks * CHUNK, bytes_accessed=80 * 2**20,
            transcendentals=tokens * chunks * CHUNK,
        ),
        name="feed_forward",
    )(inputs_two, grad_ffn, in_two_t, cot_t, w_ffn, w_attn, *weights)


JOBS = 1 + LATER


BACK_EVENTS = {
    "w0": "01 11",
    "w1": "20",
    "w2": "02",
    "w4": "12",
    "w6": "21",
    "w8": "03",
    "w9": "13",
    "h0": "22",
    "h3": "04",
    "h4": "30",
    "h5": "14",
    "o": "23 31",
    "q1": "40",
    "t1": "24",
    "t2": "32",
    "t3": "41",
    "u0": "33",
    "u1": "50",
    "f": "42",
    "g": "34 51",
    "b": "43",
    "l0": "52",
    "l1": "44",
    "l2": "53",
    "z1": "54",
}


def backward_kernel(
    cfg, later, gin_hbm, middle_hbm, cot_hbm, hiddens, w_down, w_other, w_attn, qrot_hbm, krot_hbm,
    vlow_hbm, lse_hbm, mixed_hbm, in_one_t, hid_hbm, cos_ref, sin_ref, vec_ref,
    layer_out, grad_input, small_out, grad_g, grad_u, grad_d, grad_qkv, grad_out, kept,
    own, ring, sent, sib, lefts, gin, middle, tall, wa, qrot, krot, vlow, lse, mixed,
    gmix, dqkv, gk, gv, osend, orecv, cots, got, stage, small, small_got,
    in_sem, ring_send, ring_recv, sib_send, sib_recv, x_send, x_recv, out_sem, s_send, s_recv, down_sem, hid_sem,
):
    rows, heads, skip, tail = cfg
    grads = (grad_g, grad_u, grad_d)
    own_tokens, width = gin.shape
    tokens = 2 * own_tokens
    width_q = heads * HD
    width_qkv = width_q + 2 * HD
    side_rows = CHIPS * rows
    _, gain_one, gain_two, start_of = small_inputs(vec_ref, width_qkv, width)
    here = Spot(rows)
    shard, me = here.shard, here.me
    sums = Sums(here, own, ring, ring_send, ring_recv)
    wide_qkv, wide_out = (2, width_qkv // 2), (2, width_q // 2)
    pieces = [(1, 3 * CHUNK)] * (JOBS - 1) + [(1, 3 * tail), (1, width_qkv), (1, width_q)]
    own_rows = pl.ds(pl.multiple_of(shard * own_tokens, TILE), own_tokens)
    other_rows = pl.ds(pl.multiple_of((1 - shard) * own_tokens, TILE), own_tokens)

    def at_own(t, size=TILE):
        return pl.ds(pl.multiple_of(shard * own_tokens + t * size, size), size)

    def at_other(t, size=TILE):
        return pl.ds(pl.multiple_of((1 - shard) * own_tokens + t * size, size), size)

    def get(index, source, target):
        return pltpu.make_async_copy(source, target, in_sem.at[index])

    sums_in = [get(i, later.at[skip + i], own.at[i]) for i in range(3)]
    norm_in = [get(3, gin_hbm, gin), get(4, middle_hbm, middle), get(5, cot_hbm, cots)]
    rest_in = [
        get(7, w_attn, wa), get(8, qrot_hbm, qrot), get(9, krot_hbm, krot), get(10, vlow_hbm, vlow),
        get(11, lse_hbm, lse), get(12, mixed_hbm, mixed),
    ]
    for copy in sums_in[:2] + norm_in + sums_in[2:] + rest_in:
        copy.start()
    for side in range(2):
        for chip in range(CHIPS):
            member = 2 * chip + (here.core if side == 0 else 1 - here.core)
            begin = side * side_rows + chip * rows
            get(13, in_one_t.at[here.part(member), :], lefts.at[0, begin : begin + rows, :]).start()

    def bit(value):
        return lax.rem(lax.div(me, value), 2)

    def flipped(*values):
        return me + sum(value - 2 * value * bit(value) for value in values)

    ranks = (here.core + 2 * shard, bit(2) + 2 * bit(4), bit(8))
    partners = (
        ({"dp": flipped(1)}, {"mp": 1 - shard}, {"dp": flipped(1), "mp": 1 - shard}),
        ({"dp": flipped(2)}, {"dp": flipped(4)}, {"dp": flipped(2, 4)}),
        ({"dp": flipped(8)},),
    )

    def rank_of(group, k):
        rank = ranks[group]
        return (rank + 1 - 2 * lax.rem(rank, 2), rank + 2 - 4 * lax.div(rank, 2), 3 - rank)[k]

    barrier = pltpu.get_barrier_semaphore()
    greeted = [p for group in partners for p in group] + [{"dp": n} for n in here.next]
    for target in greeted:
        pl.semaphore_signal(barrier, inc=1, device_id=target, device_id_type=MESH)
    pl.semaphore_wait(barrier, len(greeted))

    def swap_copy(index, src, dst):
        return pltpu.make_async_remote_copy(
            src_ref=src, dst_ref=dst, send_sem=x_send.at[index], recv_sem=x_recv.at[index],
            device_id={"mp": 1 - shard}, device_id_type=MESH,
        )

    some = own_tokens // 2

    def out_swap(index):
        part = slice(index * some, (index + 1) * some)
        return swap_copy(index, osend.at[part, :], orecv.at[part, :])

    half_tiles = own_tokens // TILE

    def attn_swap(t):
        return swap_copy(2 + t, tall.at[at_own(t), :], tall.at[at_own(t), :])

    def attn_got(t):
        return swap_copy(2 + t, tall.at[at_other(t), :], tall.at[at_other(t), :])

    one_swap = swap_copy(2 + half_tiles, dqkv.at[other_rows, :], got)

    def result_copies(job):
        if job < JOBS:
            size = CHUNK if job + 1 < JOBS else tail
            return [
                pltpu.make_async_copy(
                    stage.at[:, m * size : (m + 1) * size],
                    grads[m].at[:, job * CHUNK : job * CHUNK + size], out_sem.at[m],
                )
                for m in range(3)
            ]
        target = (grad_qkv, grad_out)[job - JOBS]
        return [pltpu.make_async_copy(stage.at[:, 0 : target.shape[1]], target, out_sem.at[0])]

    last_in = get(0, later.at[skip + 3, :, 0 : 3 * tail], own.at[0, :, 0 : 3 * tail])

    def run(point):
        for event in BACK_EVENTS.get(point, "").split():
            job, step = int(event[0]), int(event[1])
            o = p = job % 3
            if step == 0:
                if job == 2:
                    sums_in[2].wait()
                if job == 3:
                    last_in.wait()
                sums.start(o, p, pieces[job])
            elif step < HALF:
                sums.step(o, p, step, pieces[job])
            else:
                if job:
                    for copy in result_copies(job - 1):
                        copy.wait()
                sums.end(o, p, pieces[job], stage)
                for copy in result_copies(job):
                    copy.start()
                if job == 0:
                    last_in.start()

    for i in range(2):
        sums_in[i].wait()
        sums.start(i, i, pieces[i])

    for copy in norm_in:
        copy.wait()
    small[0, :, :] = jnp.zeros_like(small[0])

    @pl.loop(0, half_tiles)
    def _(t):
        part = tile_of(t)
        v = middle[part, :]
        factor = lax.rsqrt(jnp.mean(v * v, axis=-1, keepdims=True) + EPS)
        unit = v * factor
        e = gin[part, :]
        scaled = e * gain_two
        inner = jnp.mean(scaled * unit, axis=-1, keepdims=True)
        total = cots[part, :].astype(F32) + factor * (scaled - unit * inner)
        middle[part, :] = total
        tall[at_own(t), :] = total.astype(BF16)
        attn_swap(t).start()
        small[0, 1:2, :] += jnp.sum(e * unit, axis=0, keepdims=True)

    keep = pltpu.make_async_copy(middle, kept, out_sem.at[5])
    keep.start()
    gin[...] = jnp.zeros_like(gin)
    keep.wait()
    middle[...] = jnp.zeros_like(middle)
    chunks = w_down.shape[0]
    top = width // 2

    def down_in(chunk):
        slot = chunk % 2
        weight_to = lefts.at[1, slot * top : (slot + 1) * top, :]
        size = CHUNK if chunk + 1 < chunks else tail
        if chunk + 1 < chunks:
            parts = [slice(0, 2 * CHUNK)]
        else:
            parts = [slice(h * CHUNK, h * CHUNK + tail) for h in range(2)]
        copies = [
            pltpu.make_async_copy(
                w_down.at[chunk, :, part], weight_to.at[:, part], down_sem.at[slot, i]
            )
            for i, part in enumerate(parts)
        ]
        return copies + [pltpu.make_async_copy(
            hiddens.at[chunk, :, 0:size], dqkv.at[:, slot * CHUNK : slot * CHUNK + size],
            hid_sem.at[slot],
        )]

    for copy in down_in(0):
        copy.start()
    for chunk in range(chunks):
        if chunk + 1 < chunks:
            for copy in down_in(chunk + 1):
                copy.start()
        for copy in down_in(chunk):
            copy.wait()
        slot, size = chunk % 2, CHUNK if chunk + 1 < chunks else tail
        part = slice(slot * CHUNK, slot * CHUNK + size)
        for h in range(2):
            @pl.loop(0, top // TILE)
            def _(n):
                rows_of = pl.ds(pl.multiple_of(slot * top + n * TILE, TILE), TILE)
                at = pl.ds(pl.multiple_of(h * top + n * TILE, TILE), TILE)
                weight = lefts[1, rows_of, h * CHUNK : h * CHUNK + size]
                product = contract(dqkv[:, part], weight, 1, 1)
                middle[:, at] += product[0:own_tokens, :]
                gin[:, at] += product[own_tokens:, :]

        run(f"w{chunk}")

    @pl.loop(0, half_tiles)
    def _(t):
        one, two = middle[tile_of(t), :], gin[tile_of(t), :]
        osend[tile_of(t), :] = jnp.where(shard == 0, two, one).astype(BF16)
        gin[tile_of(t), :] = jnp.where(shard == 0, one, two)

    out_swap(0).start()
    middle_in = get(4, middle_hbm, middle)
    middle_in.start()
    run("w9")
    middle_in.wait()

    @pl.loop(0, half_tiles)
    def _(t):
        gin[tile_of(t), :] += middle[tile_of(t), :]

    for copy in rest_in:
        copy.wait()
    for t in range(half_tiles):
        attn_got(t).wait_recv()

    @pl.loop(0, tokens // TILE)
    def _(t):
        gmix[tile_of(t), :] = contract(tall[tile_of(t), :], wa[:, width_qkv:], 1, 0).astype(BF16)

    gk[...] = jnp.zeros_like(gk)
    gv[...] = jnp.zeros_like(gv)

    @pl.loop(0, heads)
    def _(h):
        columns = tile_of(h, HD)
        for i in range(SEQ_LEN // BLOCK):
            low, high = key_range(i)
            part = pl.ds(i * BLOCK, BLOCK)
            query, grad = qrot[part, columns], gmix[part, columns]
            keys = krot[low:high, :]
            scores = contract(keys, query, 1, 1) * SCALE
            seen = visible_keys(start_of(i), low, high, i)
            probs = jnp.where(seen, jnp.exp(scores - lse[h, 0:1, part]), 0.0)
            grad_probs = contract(vlow[low:high, :], grad, 1, 1)
            row_term = jnp.sum(probs * grad_probs, axis=0, keepdims=True)
            grad_scores = (probs * (grad_probs - row_term)).astype(BF16)
            gk[low:high, :] += contract(grad_scores, query, 1, 0)
            gv[low:high, :] += contract(probs.astype(BF16), grad, 1, 0)
            dqkv[part, columns] = turn(
                contract(grad_scores, keys, 0, 0) * SCALE, cos_ref[part, :], -sin_ref[part, :]
            ).astype(BF16)

        for head in range(heads):
            if f"h{head}" in BACK_EVENTS:
                @pl.when(h == head)
                def _():
                    run(f"h{head}")

    dqkv[:, width_q : width_q + HD] = turn(gk[...] * SCALE, cos_ref[...], -sin_ref[...]).astype(BF16)
    dqkv[:, width_q + HD :] = gv[...].astype(BF16)

    one_swap.start()
    out_swap(1).start()
    run("o")

    side_sent = (sent, gmix.at[0:side_rows, :])
    side_got = (sib, qrot.at[0:side_rows, :])

    def side_copy(job, m, columns):
        return pltpu.make_async_remote_copy(
            src_ref=side_sent[job].at[:, columns],
            dst_ref=side_got[job].at[:, columns],
            send_sem=sib_send.at[job, m],
            recv_sem=sib_recv.at[job, m],
            device_id={"dp": here.sibling},
            device_id_type=MESH,
        )

    get(13, lefts.at[0], lefts.at[0]).wait()

    def send_side(job, left, right, pieces):
        for m in range(pieces[0]):
            columns = slice(m * pieces[1], (m + 1) * pieces[1])
            side_sent[job][:, columns] = contract(
                lefts[left, side_rows:, :], right[:, columns], 1, 0
            ).astype(BF16)
            side_copy(job, m, columns).start()

    def own_side(job, left, right, pieces, o):
        for m in range(pieces[0]):
            columns = slice(m * pieces[1], (m + 1) * pieces[1])
            side_copy(job, m, columns).wait()
            own[o, :, columns] = (
                contract(lefts[left, 0:side_rows, :], right[:, columns], 1, 0)
                + side_got[job][:, columns].astype(F32)
            ).astype(BF16)

    send_side(0, 0, dqkv, wide_qkv)
    run("q0")
    own_side(0, 0, dqkv, wide_qkv, 1)
    other_in = get(6, w_other, lefts.at[0])
    other_in.start()
    run("q1")

    for group in range(width // (4 * rows)):
        @pl.loop(0, tokens // TILE)
        def _(t):
            part = tile_of(t)
            turned = tall[part, group * 4 * rows : (group + 1) * 4 * rows].T
            for k in range(4):
                chip, odd = (4 * group + k) // 2, k % 2
                side = odd + here.core - 2 * odd * here.core
                to = pl.ds(pl.multiple_of(side * side_rows + chip * rows, 16), rows)
                lefts[1, to, part] = turned[k * rows : (k + 1) * rows, :]

        run(f"t{group}")

    for t in range(half_tiles):
        attn_swap(t).wait_send()
    hid_in = get(15, hid_hbm, tall)
    hid_in.start()
    send_side(1, 1, mixed, wide_out)
    run("u0")
    own_side(1, 1, mixed, wide_out, 2)
    run("u1")

    fac = gk
    hid_in.wait()

    @pl.loop(0, tokens // TILE)
    def _(t):
        v = tall[tile_of(t), :].astype(F32)
        factor = lax.rsqrt(jnp.mean(v * v, axis=-1, keepdims=True) + EPS)
        fac[tile_of(t), :] = jnp.broadcast_to(factor, (TILE, HD))

    run("f")

    @pl.loop(0, width // TILE)
    def _(n):
        e = contract(dqkv[other_rows, :], wa[tile_of(n), 0:width_qkv], 1, 1)
        unit = tall[other_rows, tile_of(n)].astype(F32) * fac[other_rows, 0:1]
        small[0, 0:1, tile_of(n)] += jnp.sum(e * unit, axis=0, keepdims=True)

    run("g")

    @pl.loop(0, width // TILE)
    def _(n):
        e = contract(dqkv[own_rows, :], wa[tile_of(n), 0:width_qkv], 1, 1)
        middle[:, tile_of(n)] = e
        unit = tall[own_rows, tile_of(n)].astype(F32) * fac[own_rows, 0:1]
        small[0, 0:1, tile_of(n)] += jnp.sum(e * unit, axis=0, keepdims=True)

    @pl.loop(0, tokens // TILE)
    def _(t):
        bias = jnp.sum(dqkv[tile_of(t), :].astype(F32), axis=0, keepdims=True)
        at_query = pl.ds(pl.multiple_of(shard * width_q, HD), width_q)
        small[0, 2:3, at_query] += bias[:, 0:width_q]
        small[0, 3:4, tile_of(shard, HD)] += bias[:, width_q : width_q + HD]
        small[0, 3:4, tile_of(shard + 2, HD)] += bias[:, width_q + HD :]

    run("b")

    def small_copy(group, k):
        return pltpu.make_async_remote_copy(
            src_ref=small.at[group], dst_ref=small_got.at[group, ranks[group]],
            send_sem=s_send.at[group, k], recv_sem=s_recv.at[group, ranks[group]],
            device_id=partners[group][k], device_id_type=MESH,
        )

    def small_start(group):
        for k in range(len(partners[group])):
            small_copy(group, k).start()
        small_got[group, ranks[group]] = small[group]

    def small_end(group):
        count = len(partners[group])
        for k in range(count):
            ref = small_got.at[group, rank_of(group, k)]
            pltpu.make_async_remote_copy(
                src_ref=ref, dst_ref=ref, send_sem=s_send.at[group, k],
                recv_sem=s_recv.at[group, rank_of(group, k)],
                device_id=partners[group][k], device_id_type=MESH,
            ).wait_recv()
            small_copy(group, k).wait_send()
        total = small_got[group, 0]
        for rank in range(1, count + 1):
            total = total + small_got[group, rank]
        small[group + 1] = total

    small_start(0)

    def layer_rows(index):
        part = slice(index * some, (index + 1) * some)
        out_swap(index).wait()
        orecv[part, :] = (gin[part, :] + orecv[part, :].astype(F32)).astype(BF16)
        copy = pltpu.make_async_copy(
            orecv.at[part, :], layer_out.at[part, :], out_sem.at[(3, 6)[index]]
        )
        copy.start()
        return copy

    def keep_in(index):
        part = slice(index * some, (index + 1) * some)
        return get(14, kept.at[part, :], gin.at[0:some, :])

    layer_copies = [layer_rows(0)]
    keep_in(0).start()
    small_end(0)
    small_start(1)
    run("l0")
    small_end(1)
    small_start(2)
    run("l1")
    small_end(2)
    run("l2")
    small_out[...] = small[3]

    one_swap.wait()
    other_in.wait()

    @pl.loop(0, width // TILE)
    def _(n):
        middle[:, tile_of(n)] += contract(got[...], lefts[0, tile_of(n), :], 1, 1)

    for index in range(2):
        part = slice(index * some, (index + 1) * some)
        of = pl.ds(pl.multiple_of(shard * own_tokens + index * some, some), some)
        if index:
            keep_in(index).start()
        keep_in(index).wait()
        factor = fac[of, 0:1]
        unit = tall[of, :].astype(F32) * factor
        scaled = middle[part, :] * gain_one
        inner = jnp.mean(scaled * unit, axis=-1, keepdims=True)
        cots[part, :] = (gin[0:some, :] + factor * (scaled - unit * inner)).astype(BF16)

    input_copy = pltpu.make_async_copy(cots, grad_input, out_sem.at[4])
    input_copy.start()
    layer_copies.append(layer_rows(1))
    run("z1")
    for copy in [input_copy] + layer_copies + result_copies(JOBS + 1):
        copy.wait()


def attention_back(
    later, gin, middle, cot, hiddens, w_down, w_other, forward, cos2, sin2, vector, tail
):
    w_attn, qrot, krot, vlow, lse, mixed, in_one_t, hid_all = forward
    own_tokens, width = cot.shape
    tokens = 2 * own_tokens
    heads = lse.shape[0]
    width_q = heads * HD
    width_qkv = width_q + 2 * HD
    side_rows, wide = later.shape[1:]
    rows = side_rows // CHIPS
    vmem = pl.BlockSpec(memory_space=pltpu.VMEM)
    hbm = pl.BlockSpec(memory_space=pl.ANY)
    dma = pltpu.SemaphoreType.DMA
    shape = jax.ShapeDtypeStruct
    half = (own_tokens, width)
    n_swaps = own_tokens // TILE + 3
    return pl.pallas_call(
        functools.partial(backward_kernel, (rows, heads, later.shape[0] - JOBS, tail)),
        in_specs=[hbm] * 15 + [vmem] * 3,
        out_specs=[hbm, hbm, vmem] + [hbm] * 6,
        out_shape=[
            shape(half, BF16), shape(half, BF16), shape((8, width), F32),
        ] + [shape((rows, (JOBS - 1) * CHUNK + tail), F32)] * 3 + [
            shape((rows, width_qkv), F32), shape((rows, width_q), F32), shape(half, F32),
        ],
        scratch_shapes=[
            pltpu.VMEM((3, side_rows, wide), BF16),
            pltpu.VMEM((3, HALF, 2, rows, wide), BF16),
            pltpu.VMEM((side_rows, width_qkv), BF16),
            pltpu.VMEM((side_rows, width_qkv), BF16),
            pltpu.VMEM((2, width, tokens), BF16),
            pltpu.VMEM(half, F32),
            pltpu.VMEM(half, F32),
            pltpu.VMEM((tokens, width), BF16),
            pltpu.VMEM(w_attn.shape, BF16),
            pltpu.VMEM((tokens, width_q), BF16),
            pltpu.VMEM((tokens, HD), BF16),
            pltpu.VMEM((tokens, HD), BF16),
            pltpu.VMEM(lse.shape, F32),
            pltpu.VMEM((tokens, width_q), BF16),
            pltpu.VMEM((tokens, width_q), BF16),
            pltpu.VMEM((tokens, width_qkv), BF16),
            pltpu.VMEM((tokens, HD), F32),
            pltpu.VMEM((tokens, HD), F32),
            pltpu.VMEM(half, BF16),
            pltpu.VMEM(half, BF16),
            pltpu.VMEM(half, BF16),
            pltpu.VMEM((own_tokens, width_qkv), BF16),
            pltpu.VMEM((rows, wide), F32),
            pltpu.VMEM((4, 8, width), F32),
            pltpu.VMEM((3, 4, 8, width), F32),
            dma((16,)), dma((3, HALF, 2, 3)), dma((3, HALF, 2, 3)), dma((2, 2)), dma((2, 2)),
            dma((n_swaps,)), dma((n_swaps,)), dma((7,)), dma((3, 3)), dma((3, 4)), dma((2, 2)), dma((2,)),
        ],
        compiler_params=pltpu.CompilerParams(
            collective_id=3, has_side_effects=True, vmem_limit_bytes=63 * 2**20
        ),
        cost_estimate=pl.CostEstimate(
            flops=10 * heads * tokens * tokens * HD, bytes_accessed=50 * 2**20, transcendentals=0
        ),
        name="attention_back",
    )(
        later, gin, middle, cot, hiddens, w_down, w_other, w_attn, qrot, krot, vlow, lse, mixed, in_one_t,
        hid_all, cos2, sin2, vector,
    )


def finish_kernel(
    layer_in, input_in, first_g, first_u, first_d, last_g, last_u, last_d, qkv_in, out_in, small_in,
    layer_out, grad_input, grad_q, grad_k, grad_v, grad_out, grad_g, grad_u, grad_d, vec_one, vec_two,
    bias_q, bias_k, bias_v,
    layer, grad, gates, ups, downs, qkv, out, in_sem, out_sem,
):
    early = first_g.shape[1]
    moves = [
        (layer_in, layer, layer_out), (input_in, grad, grad_input),
        (first_g, gates.at[:, 0:early], None), (last_g, gates.at[:, early:], None),
        (first_u, ups.at[:, 0:early], None), (last_u, ups.at[:, early:], None),
        (first_d, downs.at[:, 0:early], None), (last_d, downs.at[:, early:], None),
        (qkv_in, qkv, None), (out_in, out, grad_out),
    ]
    loads = [
        pltpu.make_async_copy(source, buffer, in_sem.at[i]) for i, (source, buffer, _) in enumerate(moves)
    ]
    for copy in loads:
        copy.start()
    stores = []

    def store(buffer, target):
        copy = pltpu.make_async_copy(buffer, target, out_sem.at[len(stores)])
        copy.start()
        stores.append(copy)

    for i, (_, buffer, target) in enumerate(moves):
        loads[i].wait()
        if target is not None:
            store(buffer, target)
        if i in (3, 5, 7):
            store(*((gates, grad_g), (ups, grad_u), (downs, grad_d))[i // 2 - 1])
    begin = 0
    for target in (grad_q, grad_k, grad_v):
        store(qkv.at[:, begin : begin + target.shape[1]], target)
        begin += target.shape[1]
    for i, target in enumerate((vec_one, vec_two, bias_q)):
        target[...] = small_in[i : i + 1, :].reshape(target.shape[0])
    wide = bias_k.shape[0]
    bias_k[...] = small_in[3:4, 0:wide].reshape(wide)
    bias_v[...] = small_in[3:4, wide : 2 * wide].reshape(wide)
    for copy in stores:
        copy.wait()


def finish(layer_out, grad_input, first, last, sum_qkv, sum_out, small, width_q):
    vmem = pl.BlockSpec(memory_space=pltpu.VMEM)
    hbm = pl.BlockSpec(memory_space=pl.ANY)
    shape = jax.ShapeDtypeStruct
    rows, width_qkv = sum_qkv.shape
    width_k = (width_qkv - width_q) // 2
    width = layer_out.shape[1]
    ffn = (rows, first[0].shape[1] + last[0].shape[1])
    dma = pltpu.SemaphoreType.DMA
    return pl.pallas_call(
        finish_kernel,
        in_specs=[hbm] * 10 + [vmem],
        out_specs=[hbm] * 9 + [vmem] * 5,
        out_shape=[
            shape(layer_out.shape, BF16), shape(grad_input.shape, BF16),
            shape((rows, width_q), F32), shape((rows, width_k), F32), shape((rows, width_k), F32),
            shape(sum_out.shape, F32), shape(ffn, F32), shape(ffn, F32), shape(ffn, F32),
            shape((width,), F32), shape((width,), F32), shape((2 * width_q,), F32),
            shape((2 * width_k,), F32), shape((2 * width_k,), F32),
        ],
        scratch_shapes=[
            pltpu.VMEM(layer_out.shape, BF16), pltpu.VMEM(grad_input.shape, BF16),
            pltpu.VMEM(ffn, F32), pltpu.VMEM(ffn, F32), pltpu.VMEM(ffn, F32),
            pltpu.VMEM(sum_qkv.shape, F32), pltpu.VMEM(sum_out.shape, F32), dma((10,)), dma((9,)),
        ],
        compiler_params=pltpu.CompilerParams(vmem_limit_bytes=62 * 2**20),
        name="finish",
    )(layer_out, grad_input, *first, *last, sum_qkv, sum_out, small)


def body_fused(
    hidden_in, positions, query_weight, query_bias, key_weight, key_bias, value_weight, value_bias,
    out_weight, gate_weight, up_weight, down_weight, attn_gain, ffn_gain, cotangent,
):
    rows, width_q = query_weight.shape
    heads = width_q // HD
    hidden_units = gate_weight.shape[1]
    own_tokens, width = hidden_in.shape
    half = HD // 2
    lanes = jnp.arange(HD, dtype=jnp.int32)
    freq = jnp.power(ROPE_BASE, -2.0 * (lanes % half).astype(F32) / HD)
    ffn_weights = (gate_weight, up_weight, down_weight.T)
    (w_ffn, w_attn, hidden_all, grad_ffn, in_one_t, qrot, krot, vlow, mixed, lse, middle,
     inputs_two, vector, cos2, sin2, in_two_t, cot_t) = forward_attention(
        hidden_in, cotangent,
        (freq, positions, query_bias, key_bias, value_bias, attn_gain, ffn_gain),
        (query_weight, key_weight, value_weight, out_weight.T, *ffn_weights),
        heads,
    )
    hiddens, w_down, grad_normed_two, later, *first_sums, w_other, _ = feed_forward(
        inputs_two, grad_ffn, in_two_t, cot_t, w_ffn, w_attn, width_q + 2 * HD, ffn_weights
    )
    tail = units_of(-(-hidden_units // CHUNK) - 1, hidden_units)
    layer_out, grad_input, small, *sums = attention_back(
        later, grad_normed_two, middle, cotangent, hiddens, w_down, w_other,
        (w_attn, qrot, krot, vlow, lse, mixed, in_one_t, hidden_all), cos2, sin2, vector, tail,
    )
    (layer_out, grad_input, sum_q, sum_k, sum_v, sum_out, sum_gate, sum_up, sum_down, gain_one,
     gain_two, sum_bias_q, sum_bias_k, sum_bias_v) = finish(
        layer_out, grad_input, first_sums, sums[:3], *sums[3:5], small, width_q
    )
    return (
        layer_out,
        grad_input,
        sum_q,
        sum_bias_q,
        sum_k,
        sum_bias_k,
        sum_v,
        sum_bias_v,
        sum_out.T,
        sum_gate,
        sum_up,
        sum_down.T,
        gain_one,
        gain_two,
    )


def body(*arrays):
    rows = arrays[2].shape[0]
    if lax.axis_size("dp") == 2 * CHIPS and rows % 32 == 0 and -(-arrays[9].shape[1] // CHUNK) == 9:
        return body_fused(*arrays)
    return body_general(*arrays)


def solution(mesh):
    tokens, weight, weight_t = P(("dp", "mp"), None), P("dp", "mp"), P("mp", "dp")
    return jax.shard_map(
        body,
        mesh=mesh,
        in_specs=(
            tokens, P("dp"), weight, P(), weight, P(), weight, P(), weight_t,
            weight, weight, weight_t, P(), P(), tokens,
        ),
        out_specs=(
            tokens, tokens, weight, P(), weight, P(), weight, P(), weight_t,
            weight, weight, weight_t, P(), P(),
        ),
        check_vma=False,
    )
```
